32 devices in a mesh: wide: 16 (over z, x, core), narrow: 2 (over y).
Axes of the slice: x: 2, y: 2, z: 4, core: 2. Of those that a mesh axis runs over, the one named last changes fastest.
Arguments:
- tokens: bfloat16 [1088, 24576], P('narrow', 'wide'), may hold values from -6 to 6
- piece_starts: int32 [16, 2], P('wide'), may hold values from 0 to 1280, as said below
- ln1_gain: bfloat16 [1088], P('narrow'), may hold values from 0.5 to 1.5
- ln1_bias: bfloat16 [1088], P('narrow'), may hold values from -2 to 2
- w_qkv: bfloat16 [1088, 3, 1088], P('wide', None, 'narrow'), may hold values from -0.1875 to 0.1875
- bias_qv: bfloat16 [2, 1088], P(None, 'narrow'), may hold values from -2 to 2
- w_out: bfloat16 [1088, 1088], P('wide', 'narrow'), may hold values from -0.75 to 0.75
- bias_out: bfloat16 [1088], P('narrow'), may hold values from -2 to 2
- ln2_gain: bfloat16 [1088], P('narrow'), may hold values from 0.5 to 1.5
- ln2_bias: bfloat16 [1088], P('narrow'), may hold values from -2 to 2
- w_up: bfloat16 [1088, 4352], P('wide', 'narrow'), may hold values from -0.1875 to 0.1875
- bias_up: bfloat16 [4352], P('narrow'), may hold values from -2 to 2
- w_down: bfloat16 [4352, 1088], P('narrow', 'wide'), may hold values from -0.09375 to 0.09375
- bias_down: bfloat16 [1088], P('narrow'), may hold values from -2 to 2
- cotangent: bfloat16 [1088, 24576], P('narrow', 'wide'), may hold values from -6 to 6
Outputs:
- output: bfloat16 [1088, 24576], P('narrow', 'wide')
- grad_tokens: float32 [1088, 24576], P('narrow', 'wide')
- grad_ln1_gain: float32 [1088], P('narrow')
- grad_ln1_bias: float32 [1088], P('narrow')
- grad_w_qkv: float32 [1088, 3, 1088], P('wide', None, 'narrow')
- grad_bias_qv: float32 [2, 1088], P(None, 'narrow')
- grad_w_out: float32 [1088, 1088], P('wide', 'narrow')
- grad_bias_out: float32 [1088], P('narrow')
- grad_ln2_gain: float32 [1088], P('narrow')
- grad_ln2_bias: float32 [1088], P('narrow')
- grad_w_up: float32 [1088, 4352], P('wide', 'narrow')
- grad_bias_up: float32 [4352], P('narrow')
- grad_w_down: float32 [4352, 1088], P('narrow', 'wide')
- grad_bias_down: float32 [1088], P('narrow')
The draws below stay inside these ranges and needn't reach their ends.
Inputs may be any that keep to these rules, and one draw needn't show every extreme that they name: `piece_starts`: each sequence has 2 picture pieces of 256 tokens; their starts rise along the sequence, the pieces do not intersect and lie inside the sequence.
All inputs are finite; a program needn't handle non-finite values.
Results may differ from the reference program's by a relative error of at most 0.011.
Values may be sent and summed in bfloat16 or wider, within the bound.
No kernel may reach another device: no remote copies, remote signals or barrier semaphores. Data moves between devices by JAX's collectives and lax.ppermute only.
A program may use at most 512 MiB of HBM per device.

```python
import jax
import jax.numpy as jnp
from jax import lax

D = 1088
HEADS = 17
FF = 4352
LEN = 1536
PIECE = 256
PIECES = 2
SEQS = 16
TOKENS = 24576


def draw_piece_starts(key, part):
    key = jax.random.fold_in(key, 11)
    key_offs, key_first, key_last = jax.random.split(key, 3)
    slot_size = LEN // PIECES
    offsets = jax.random.randint(key_offs, (SEQS, PIECES), 0, slot_size - PIECE + 1)
    starts = jnp.arange(PIECES, dtype=jnp.int32)[None, :] * slot_size + offsets
    first_seq = jax.random.randint(key_first, (), 0, SEQS)
    last_seq = (first_seq + 1 + jax.random.randint(key_last, (), 0, SEQS - 1)) % SEQS
    row_ids = jnp.arange(SEQS, dtype=jnp.int32)[:, None]
    col_ids = jnp.arange(PIECES, dtype=jnp.int32)[None, :]
    starts = jnp.where((row_ids == first_seq) & (col_ids == 0), 0, starts)
    starts = jnp.where((row_ids == last_seq) & (col_ids == PIECES - 1), LEN - PIECE, starts)
    return starts.astype(jnp.int32)


def spiked(entries, rng, source, target, blocks, factor):
    owner, partner = [(jnp.arange(entries.shape[axis_at]) // (entries.shape[axis_at] // blocks)).reshape([-1 if axis == axis_at else 1 for axis in range(entries.ndim)]) for axis_at in (source, target)]
    chosen = jax.random.permutation(rng, blocks)[partner]
    strong = (owner == chosen) | (owner == (partner + blocks // 2) % blocks)
    return jnp.where(strong, factor * entries, entries)


def levels(key, extent, cuts, smallest, largest):
    factor_of, own = 1.0, jax.random.fold_in(key, 6)
    for dim, blocks in cuts:
        steps = jnp.exp(jax.random.uniform(jax.random.fold_in(own, dim), (blocks,), jnp.float32, smallest / len(cuts), largest / len(cuts)))
        factor_of = factor_of * jnp.repeat(steps, extent[dim] // blocks).reshape([-1 if axis == dim else 1 for axis in range(len(extent))])
    return factor_of


def noise(key, dims, deviation, limit, cuts=(), kind=jnp.bfloat16):
    values = jax.random.normal(key, dims, jnp.float32) * deviation
    if len(cuts) > 0:
        values = levels(key, dims, cuts, -0.22, 0.18) * values
    return jnp.clip(values, min=-limit, max=limit).astype(kind)


def noise_with(stream_key, shape, scale, limit, cuts, heavy, kind=jnp.bfloat16):
    entries = scale * jax.random.normal(stream_key, shape, jnp.float32)
    if cuts:
        entries = entries * levels(stream_key, shape, cuts, -0.22, 0.18)
    return jnp.clip(spiked(entries, jax.random.fold_in(stream_key, 3), *heavy), -limit, limit).astype(kind)


def setup_inputs(seed: int = 0) -> dict:
    keys = jax.random.split(jax.random.key(seed), 16)
    tokens = noise(keys[0], (D, TOKENS), 1.0, 6.0, ((0, 2), (1, 16)))
    piece_starts = draw_piece_starts(jax.random.fold_in(keys[15], 71), 0)
    ln1_gain = jnp.clip(1.0 + 0.1 * jax.random.normal(keys[2], (D,), jnp.float32), 0.5, 1.5).astype(jnp.bfloat16)
    ln1_bias = noise(keys[3], (D,), 0.3, 2.0, ((0, 2),))
    w_qkv = noise(keys[4], (D, 3, D), D ** -0.5, 0.1875, ((0, 16), (2, 2)))
    bias_qv = noise(keys[5], (2, D), 0.3, 2.0, ((1, 2),))
    w_out = noise(keys[6], (D, D), (D // 16) ** -0.5, 0.75, ((0, 16), (1, 2)))
    bias_out = noise(keys[7], (D,), 0.3, 2.0, ((0, 2),))
    ln2_gain = jnp.clip(1.0 + 0.1 * jax.random.normal(keys[8], (D,), jnp.float32), 0.5, 1.5).astype(jnp.bfloat16)
    ln2_bias = noise(keys[9], (D,), 0.3, 2.0, ((0, 2),))
    w_up = noise(keys[10], (D, FF), D ** -0.5, 0.1875, ((0, 16), (1, 2)))
    bias_up = noise(keys[11], (FF,), 0.3, 2.0, ((0, 2),))
    w_down = noise(keys[12], (FF, D), FF ** -0.5, 0.09375, ((0, 2), (1, 16)))
    bias_down = noise(keys[13], (D,), 0.3, 2.0, ((0, 2),))
    cotangent = noise_with(keys[14], (D, TOKENS), 1.0, 6.0, ((0, 2), (1, 16)), (1, 0, 16, 2.0))
    return {"tokens": tokens, "piece_starts": piece_starts, "ln1_gain": ln1_gain, "ln1_bias": ln1_bias, "w_qkv": w_qkv, "bias_qv": bias_qv, "w_out": w_out, "bias_out": bias_out, "ln2_gain": ln2_gain, "ln2_bias": ln2_bias, "w_up": w_up, "bias_up": bias_up, "w_down": w_down, "bias_down": bias_down, "cotangent": cotangent}


EPSILON = 1e-05
PRECISE = lax.Precision.HIGHEST

@jax.custom_vjp
def low(v):
    return lax.optimization_barrier(v.astype(jnp.bfloat16)).astype(jnp.float32)

@jax.custom_vjp
def low_back(v):
    return v

def low_keep(v):
    return (low(v), None)

def low_pass(kept, grad):
    return (grad,)

def back_keep(v):
    return (v, None)

def back_low(kept, grad):
    return (low(grad),)
low.defvjp(low_keep, low_pass)
low_back.defvjp(back_keep, back_low)

def round_both(value):
    return low(low_back(value))

def normalize(row_data, gain_vec, shift_vec):
    centre = lax.optimization_barrier(jnp.mean(row_data, axis=-1, keepdims=True))
    centred = row_data - centre
    spread = lax.optimization_barrier(jnp.mean(centred * centred, axis=-1, keepdims=True))
    return centred * lax.rsqrt(spread + EPSILON) * gain_vec + shift_vec

def visible_mask(starts, length):
    positions = jnp.arange(length, dtype=jnp.int32)
    inside = (positions[:, None] >= starts[None, :]) & (positions[:, None] < starts[None, :] + PIECE)
    shared = jnp.any(inside[:, None, :] & inside[None, :, :], axis=-1)
    return (positions[None, :] <= positions[:, None]) | shared

def split_heads(matrix):
    return matrix.reshape(matrix.shape[0], HEADS, D // HEADS).transpose(1, 0, 2)

def head_attention(triple, visible):
    query_rows, key_rows, value_rows = triple
    scores = low_back((D // HEADS) ** (-0.5) * jnp.dot(query_rows, key_rows.T, precision=PRECISE))
    masked = jnp.where(visible, scores, -1e+30)
    row_top = lax.optimization_barrier(jnp.max(masked, axis=-1, keepdims=True))
    weights = jnp.exp(masked - row_top)
    probs = low(weights / lax.optimization_barrier(jnp.sum(weights, axis=-1, keepdims=True)))
    return jnp.dot(probs, value_rows, precision=PRECISE)

def layer(row_data, starts, params):
    gain_one, shift_one, w_qkv, bias_qv, w_out, bias_out, gain_two, shift_two, w_up, bias_up, w_down, bias_down = params
    length = row_data.shape[0]
    h_one = low(normalize(row_data, gain_one, shift_one))
    mixed = jnp.einsum('td,dcf->tcf', h_one, w_qkv, precision=PRECISE)
    query_all = round_both(mixed[:, 0] + bias_qv[0])
    key_all = round_both(mixed[:, 1])
    value_all = round_both(mixed[:, 2] + bias_qv[1])
    visible = visible_mask(starts, length)

    def one_head(triple):
        return head_attention(triple, visible)
    context = lax.map(jax.checkpoint(one_head), (split_heads(query_all), split_heads(key_all), split_heads(value_all)))
    context = round_both(context.transpose(1, 0, 2).reshape(length, D))
    projected = round_both(jnp.dot(context, w_out, precision=PRECISE) + bias_out)
    mid_rows = row_data + projected
    h_two = low(normalize(mid_rows, gain_two, shift_two))
    up_pre = low_back(jnp.dot(h_two, w_up, precision=PRECISE) + bias_up)
    act_value = low(jax.nn.gelu(up_pre, approximate=True))
    down_sum = low_back(jnp.dot(act_value, w_down, precision=PRECISE) + bias_down)
    return mid_rows + down_sum

def reference(tokens, piece_starts, ln1_gain, ln1_bias, w_qkv, bias_qv, w_out, bias_out, ln2_gain, ln2_bias, w_up, bias_up, w_down, bias_down, cotangent):
    params = tuple((argument.astype(jnp.float32) for argument in (ln1_gain, ln1_bias, w_qkv, bias_qv, w_out, bias_out, ln2_gain, ln2_bias, w_up, bias_up, w_down, bias_down)))
    row_blocks = tokens.astype(jnp.float32).T.reshape(SEQS, LEN, D)
    grad_blocks = cotangent.astype(jnp.float32).T.reshape(SEQS, LEN, D)

    def per_sequence(totals, sequence):
        row_data, starts, grad_rows = sequence

        def forward(inputs, weights):
            return layer(inputs, starts, weights)
        result, pull_back = jax.vjp(forward, row_data, params)
        grad_input, grad_params = pull_back(grad_rows)
        return (jax.tree.map(jnp.add, totals, grad_params), (result.astype(jnp.bfloat16), grad_input))
    zero_grads = jax.tree.map(jnp.zeros_like, params)
    totals, (outputs, grad_inputs) = lax.scan(per_sequence, zero_grads, (row_blocks, piece_starts, grad_blocks))
    return (outputs.reshape(TOKENS, D).T, grad_inputs.reshape(TOKENS, D).T, totals[0], totals[1], totals[2], totals[3], totals[4], totals[5], totals[6], totals[7], totals[8], totals[9], totals[10], totals[11])
```

```python
import functools
from functools import partial

import jax
import jax.numpy as jnp
from jax import lax
from jax.experimental import pallas as pl
from jax.experimental.pallas import tpu as pltpu
from jax.sharding import PartitionSpec as P

HEADS = 17
PIECE = 256


EPSILON = 1e-05


def normalize(row_data, gain_vec, shift_vec):
    centre = jnp.mean(row_data, axis=-1, keepdims=True)
    centred = row_data - centre
    spread = jnp.mean(centred * centred, axis=-1, keepdims=True)
    return centred * lax.rsqrt(spread + EPSILON) * gain_vec + shift_vec


def norm_back(row_data, gain_vec, shift_vec, grad_rows):
    unused, pull_back = jax.vjp(normalize, row_data, gain_vec, shift_vec)
    return pull_back(grad_rows)


def full_rows(partial_rows):
    return lax.psum(partial_rows, "narrow")


def visible_mask(starts, query_pos, key_pos):
    query_in = (query_pos[:, None] >= starts[None, :]) & (
        query_pos[:, None] < starts[None, :] + PIECE
    )
    key_in = (key_pos[:, None] >= starts[None, :]) & (key_pos[:, None] < starts[None, :] + PIECE)
    shared = jnp.any(query_in[:, None, :] & key_in[None, :, :], axis=-1)
    return (key_pos[None, :] <= query_pos[:, None]) | shared


def to_heads(matrix):
    return matrix.reshape(matrix.shape[0], HEADS, matrix.shape[1] // HEADS)


def attention_scores(query_rows, key_full, visible, score_scale):
    raw = (
        jnp.einsum(
            "qhd,khd->hqk",
            to_heads(query_rows),
            to_heads(key_full),
            preferred_element_type=jnp.float32,
        )
        * score_scale
    )
    return jnp.where(visible[None], raw, -1e30)


def any_mesh(
    tokens,
    piece_starts,
    ln1_gain,
    ln1_bias,
    w_qkv,
    bias_qv,
    w_out,
    bias_out,
    ln2_gain,
    ln2_bias,
    w_up,
    bias_up,
    w_down,
    bias_down,
    cotangent,
):
    narrow_size = lax.axis_size("narrow")
    narrow_rank = lax.axis_index("narrow")
    col_width, length = tokens.shape
    full_width = col_width * narrow_size
    queries = length // narrow_size
    score_scale = (full_width // HEADS) ** (-0.5)
    col_start = narrow_rank * col_width
    row_start = narrow_rank * queries

    def own_cols(matrix):
        return lax.dynamic_slice_in_dim(matrix, col_start, col_width, matrix.ndim - 1)

    x_cols, dy_cols, gain_one, shift_one, gain_two, shift_two = (
        lax.all_gather(tokens, "narrow", axis=0, tiled=True),
        lax.all_gather(cotangent, "narrow", axis=0, tiled=True),
        lax.all_gather(ln1_gain, "narrow", axis=0, tiled=True),
        lax.all_gather(ln1_bias, "narrow", axis=0, tiled=True),
        lax.all_gather(ln2_gain, "narrow", axis=0, tiled=True),
        lax.all_gather(ln2_bias, "narrow", axis=0, tiled=True),
    )
    x_rows = x_cols.T
    dy_rows = dy_cols.T
    qkv_cols, out_cols, up_cols, down_rows = (
        lax.all_gather(w_qkv, "wide", axis=0, tiled=True),
        lax.all_gather(w_out, "wide", axis=0, tiled=True),
        lax.all_gather(w_up, "wide", axis=0, tiled=True),
        lax.all_gather(w_down, "wide", axis=1, tiled=True),
    )
    gain_one = gain_one.astype(jnp.float32)
    shift_one = shift_one.astype(jnp.float32)
    gain_two = gain_two.astype(jnp.float32)
    shift_two = shift_two.astype(jnp.float32)
    x_full = x_rows.astype(jnp.float32)
    h_one = normalize(x_full, gain_one, shift_one).astype(jnp.bfloat16)
    mixed = jnp.einsum("td,dcf->tcf", h_one, qkv_cols, preferred_element_type=jnp.float32)
    bias_cols = bias_qv.astype(jnp.float32)
    query_cols = (mixed[:, 0] + bias_cols[0]).astype(jnp.bfloat16)
    key_cols = mixed[:, 1].astype(jnp.bfloat16)
    value_cols = (mixed[:, 2] + bias_cols[1]).astype(jnp.bfloat16)
    query_full, key_full, value_full = (
        lax.all_gather(query_cols, "narrow", axis=1, tiled=True),
        lax.all_gather(key_cols, "narrow", axis=1, tiled=True),
        lax.all_gather(value_cols, "narrow", axis=1, tiled=True),
    )
    query_rows = lax.dynamic_slice_in_dim(query_full, row_start, queries, 0)
    query_pos = row_start + jnp.arange(queries, dtype=jnp.int32)
    key_pos = jnp.arange(length, dtype=jnp.int32)
    visible = visible_mask(piece_starts[0], query_pos, key_pos)
    masked = attention_scores(query_rows, key_full, visible, score_scale)
    row_top = jnp.max(masked, axis=-1, keepdims=True)
    weights = jnp.exp(masked - row_top)
    row_total = jnp.sum(weights, axis=-1, keepdims=True)
    log_total = row_top + jnp.log(row_total)
    probs_low = (weights / row_total).astype(jnp.bfloat16)
    context = jnp.einsum(
        "hqk,khd->qhd", probs_low, to_heads(value_full), preferred_element_type=jnp.float32
    )
    context = context.reshape(queries, full_width).astype(jnp.bfloat16)
    context_full = lax.all_gather(context, "narrow", axis=0, tiled=True)
    projected = jnp.dot(
        context_full, out_cols, preferred_element_type=jnp.float32
    ) + bias_out.astype(jnp.float32)
    projected_low = projected.astype(jnp.bfloat16)
    projected_full = lax.all_gather(projected_low, "narrow", axis=1, tiled=True)
    mid_full = x_full + projected_full.astype(jnp.float32)
    mid_rows = tokens.T.astype(jnp.float32) + projected_low.astype(jnp.float32)
    h_two = normalize(mid_full, gain_two, shift_two).astype(jnp.bfloat16)
    up_pre = jnp.dot(h_two, up_cols, preferred_element_type=jnp.float32) + bias_up.astype(
        jnp.float32
    )
    act_value, gelu_pull = jax.vjp(partial(jax.nn.gelu, approximate=True), up_pre)
    act_low = act_value.astype(jnp.bfloat16)
    partial_down = jnp.dot(act_low, down_rows, preferred_element_type=jnp.float32)
    down_sum = lax.psum_scatter(
        partial_down.astype(jnp.bfloat16), "narrow", scatter_dimension=1, tiled=True
    ).astype(jnp.float32)
    output = (mid_rows + (down_sum + bias_down.astype(jnp.float32))).astype(jnp.bfloat16)
    grad_out = cotangent.T.astype(jnp.float32)
    grad_bias_down = jnp.sum(grad_out, axis=0)
    grad_w_down = jnp.einsum("tf,td->fd", act_low, dy_rows, preferred_element_type=jnp.float32)
    grad_act = jnp.einsum("td,fd->tf", dy_rows, down_rows, preferred_element_type=jnp.float32)
    grad_up = gelu_pull(grad_act)[0].astype(jnp.bfloat16)
    grad_bias_up = jnp.sum(grad_up.astype(jnp.float32), axis=0)
    grad_w_up = jnp.einsum("td,tf->df", h_two, grad_up, preferred_element_type=jnp.float32)
    grad_h_two = full_rows(
        jnp.einsum("tf,df->td", grad_up, up_cols, preferred_element_type=jnp.float32)
    )
    grad_mid_full, grad_gain_two, grad_shift_two = norm_back(
        mid_full, gain_two, shift_two, grad_h_two
    )
    grad_mid = grad_out + own_cols(grad_mid_full)
    grad_projected = grad_mid.astype(jnp.bfloat16)
    grad_bias_out = jnp.sum(grad_projected.astype(jnp.float32), axis=0)
    grad_w_out = jnp.einsum(
        "td,tc->dc", context_full, grad_projected, preferred_element_type=jnp.float32
    )
    grad_context = lax.psum_scatter(
        jnp.einsum("tc,dc->td", grad_projected, out_cols, preferred_element_type=jnp.float32),
        "narrow",
        scatter_dimension=0,
        tiled=True,
    ).astype(jnp.bfloat16)
    weights_back = jnp.exp(masked - log_total)
    context_heads = to_heads(grad_context)
    grad_probs = jnp.einsum(
        "qhd,khd->hqk", context_heads, to_heads(value_full), preferred_element_type=jnp.float32
    )
    centre = jnp.sum(weights_back * grad_probs, axis=-1, keepdims=True)
    grad_scores = (weights_back * (grad_probs - centre)).astype(jnp.bfloat16)
    grad_query = jnp.einsum(
        "hqk,khd->qhd", grad_scores, to_heads(key_full), preferred_element_type=jnp.float32
    )
    grad_query = grad_query.reshape(queries, full_width) * score_scale
    probs_back = weights_back.astype(jnp.bfloat16)
    grad_key = jnp.einsum(
        "hqk,qhd->khd", grad_scores, to_heads(query_rows), preferred_element_type=jnp.float32
    )
    grad_key = grad_key.reshape(length, full_width) * score_scale
    grad_value = jnp.einsum(
        "hqk,qhd->khd", probs_back, context_heads, preferred_element_type=jnp.float32
    )
    grad_value = grad_value.reshape(length, full_width)
    placed = jnp.zeros((length, full_width), jnp.float32)
    placed = lax.dynamic_update_slice_in_dim(placed, grad_query, row_start, 0)
    stacked = jnp.stack((placed, grad_key, grad_value), axis=1)
    grad_mixed = lax.psum_scatter(stacked, "narrow", scatter_dimension=2, tiled=True).astype(
        jnp.bfloat16
    )
    grad_mixed_f = grad_mixed.astype(jnp.float32)
    grad_bias_qv = jnp.stack(
        (jnp.sum(grad_mixed_f[:, 0], axis=0), jnp.sum(grad_mixed_f[:, 2], axis=0))
    )
    grad_w_qkv = jnp.einsum("td,tcf->dcf", h_one, grad_mixed, preferred_element_type=jnp.float32)
    grad_h_one = full_rows(
        jnp.einsum("tcf,dcf->td", grad_mixed, qkv_cols, preferred_element_type=jnp.float32)
    )
    grad_x_full, grad_gain_one, grad_shift_one = norm_back(x_full, gain_one, shift_one, grad_h_one)
    grad_tokens = grad_mid + own_cols(grad_x_full)
    sum_w_qkv, sum_w_out, sum_w_up, sum_w_down = (
        lax.psum_scatter(grad_w_qkv, "wide", scatter_dimension=0, tiled=True),
        lax.psum_scatter(grad_w_out, "wide", scatter_dimension=0, tiled=True),
        lax.psum_scatter(grad_w_up, "wide", scatter_dimension=0, tiled=True),
        lax.psum_scatter(grad_w_down, "wide", scatter_dimension=1, tiled=True),
    )
    (
        sum_gain_one,
        sum_shift_one,
        sum_bias_qv,
        sum_bias_out,
        sum_gain_two,
        sum_shift_two,
        sum_bias_up,
        sum_bias_down,
    ) = lax.psum(
        (
            own_cols(grad_gain_one),
            own_cols(grad_shift_one),
            grad_bias_qv,
            grad_bias_out,
            own_cols(grad_gain_two),
            own_cols(grad_shift_two),
            grad_bias_up,
            grad_bias_down,
        ),
        "wide",
    )
    return (
        output.T,
        grad_tokens.T,
        sum_gain_one,
        sum_shift_one,
        sum_w_qkv,
        sum_bias_qv,
        sum_w_out,
        sum_bias_out,
        sum_gain_two,
        sum_shift_two,
        sum_w_up,
        sum_bias_up,
        sum_w_down,
        sum_bias_down,
    )


F32 = jnp.float32
BF16 = jnp.bfloat16
HEAD = 64
TILE = 256
MLP_TILE = 256
VMEM = 56 << 20


def dot(a, b, dim_a, dim_b):
    return lax.dot_general(a, b, (((dim_a,), (dim_b,)), ((), ())), preferred_element_type=F32)


def fill_bias(starts_ref, bias, length):
    for i in range(length // TILE):
        low = i * TILE
        rows = min(2 * TILE, length - low)
        key = low + lax.broadcasted_iota(jnp.int32, (rows, TILE), 0)
        query = low + lax.broadcasted_iota(jnp.int32, (rows, TILE), 1)
        seen = key <= query
        for p in range(starts_ref.shape[0]):
            s = starts_ref[p]
            seen = seen | (
                (key >= s) & (key < s + PIECE) & (query >= s) & (query < s + PIECE)
            )
        bias[i, :rows, :] = jnp.where(seen, 0.0, -1e30)


def score_parts(key_rows, query, bias, i, length):
    low = i * TILE
    high = min(low + 2 * TILE, length)
    parts = []
    if low > 0:
        parts.append(dot(key_rows[:low], query, 1, 0))
    parts.append(dot(key_rows[low:high], query, 1, 0) + bias[i, : high - low, :])
    return parts


def attend_kernel(starts_ref, q_ref, k_ref, v_ref, c_ref, l_ref, bias, key_rows):
    length = q_ref.shape[1]

    @pl.when(pl.program_id(0) == 0)
    def _():
        fill_bias(starts_ref, bias, length)

    key_rows[...] = k_ref[...].T
    for i in range(length // TILE):
        here = pl.ds(i * TILE, TILE)
        query = q_ref[:, here] * jnp.asarray(HEAD**-0.5, BF16)
        parts = score_parts(key_rows, query, bias, i, length)
        top = functools.reduce(jnp.maximum, [jnp.max(s, axis=0, keepdims=True) for s in parts])
        total, acc, at = 0.0, 0.0, 0
        for s in parts:
            p = jnp.exp(s - top)
            total = total + jnp.sum(p, axis=0, keepdims=True)
            acc = acc + dot(v_ref[:, at : at + s.shape[0]], p.astype(BF16), 1, 0)
            at += s.shape[0]
        c_ref[:, here] = (acc / total).astype(BF16)
        l_ref[0, :, here] = top + jnp.log(total)


def attend_back_kernel(
    starts_ref, q_ref, k_ref, v_ref, d_ref, l_ref, dq_ref, dk_ref, dv_ref,
    bias, key_rows, value_rows, query_rows, grad_rows, key_sum, value_sum,
):
    length = q_ref.shape[1]
    scale = jnp.asarray(HEAD**-0.5, BF16)

    @pl.when(pl.program_id(0) == 0)
    def _():
        fill_bias(starts_ref, bias, length)

    key_rows[...] = k_ref[...].T
    value_rows[...] = v_ref[...].T
    grad_rows[...] = d_ref[...].T
    query_rows[...] = (q_ref[...] * scale).T
    tiles = length // TILE
    for i in reversed(range(tiles)):
        here = pl.ds(i * TILE, TILE)
        grad = d_ref[:, here]
        parts = score_parts(key_rows, q_ref[:, here] * scale, bias, i, length)
        lse = l_ref[0, :, here]
        at, centre, pairs = 0, 0.0, []
        for s in parts:
            p = jnp.exp(s - lse)
            gp = dot(value_rows[at : at + s.shape[0]], grad, 1, 0)
            centre = centre + jnp.sum(p * gp, axis=0, keepdims=True)
            pairs.append((p, gp))
            at += s.shape[0]
        at, dq = 0, 0.0
        for p, gp in pairs:
            span = slice(at, at + p.shape[0])
            gs = (p * (gp - centre)).astype(BF16)
            dq = dq + dot(k_ref[:, span], gs, 1, 0)
            dk = dot(gs, query_rows[here], 1, 0)
            dv = dot(p.astype(BF16), grad_rows[here], 1, 0)
            if i == tiles - 1:
                key_sum[span], value_sum[span] = dk, dv
            else:
                key_sum[span] += dk
                value_sum[span] += dv
            at += p.shape[0]
        dq_ref[:, here] = (dq * HEAD**-0.5).astype(BF16)
    dk_ref[...] = key_sum[...].T.astype(BF16)
    dv_ref[...] = value_sum[...].T.astype(BF16)


def head_block(length):
    return pl.BlockSpec((HEAD, length), lambda h, s: (h, 0))


def attend(starts, query, key, value):
    rows, length = query.shape
    heads = rows // HEAD
    block = head_block(length)
    return pl.pallas_call(
        attend_kernel,
        grid_spec=pltpu.PrefetchScalarGridSpec(
            num_scalar_prefetch=1,
            grid=(heads,),
            in_specs=[block] * 3,
            out_specs=[block, pl.BlockSpec((1, 1, length), lambda h, s: (h, 0, 0))],
            scratch_shapes=[
                pltpu.VMEM((length // TILE, 2 * TILE, TILE), F32),
                pltpu.VMEM((length, HEAD), BF16),
            ],
        ),
        out_shape=[
            jax.ShapeDtypeStruct((rows, length), BF16),
            jax.ShapeDtypeStruct((heads, 1, length), F32),
        ],
        compiler_params=pltpu.CompilerParams(vmem_limit_bytes=VMEM),
        cost_estimate=pl.CostEstimate(
            flops=35 * 10**6 * 1000 * heads // 9, bytes_accessed=rows * length * 8, transcendentals=0
        ),
        name="attend",
    )(starts, query, key, value)


def attend_back(starts, query, key, value, grad, lse):
    rows, length = query.shape
    heads = rows // HEAD
    block = head_block(length)
    narrow_rows = pltpu.VMEM((length, HEAD), BF16)
    sums = pltpu.VMEM((length, HEAD), F32)
    return pl.pallas_call(
        attend_back_kernel,
        grid_spec=pltpu.PrefetchScalarGridSpec(
            num_scalar_prefetch=1,
            grid=(heads,),
            in_specs=[block] * 4 + [pl.BlockSpec((1, 1, length), lambda h, s: (h, 0, 0))],
            out_specs=[block] * 3,
            scratch_shapes=[pltpu.VMEM((length // TILE, 2 * TILE, TILE), F32)]
            + [narrow_rows] * 4
            + [sums] * 2,
        ),
        out_shape=[jax.ShapeDtypeStruct((rows, length), BF16)] * 3,
        compiler_params=pltpu.CompilerParams(vmem_limit_bytes=VMEM),
        cost_estimate=pl.CostEstimate(
            flops=60 * 10**6 * 1000 * heads // 9, bytes_accessed=rows * length * 14, transcendentals=0
        ),
        name="attend_back",
    )(starts, query, key, value, grad, lse)


def feed_kernel(h_ref, g_ref, up_ref, down_ref, bias_ref, act_ref, gup_ref, out_ref, gh_ref, gb_ref):
    root = (2 / jnp.pi) ** 0.5
    u = dot(h_ref[...], up_ref[...], 0, 0) + bias_ref[...]
    grad_act = dot(g_ref[...], down_ref[...], 0, 0)
    square = u * u
    t = jnp.tanh(root * u * (1 + 0.044715 * square))
    half = 0.5 * (1 + t)
    act = (u * half).astype(BF16)
    slope = half + 0.5 * u * (1 - t * t) * (root * (1 + 3 * 0.044715 * square))
    gup = (grad_act * slope).astype(BF16)
    act_ref[...] = act
    gup_ref[...] = gup
    out_ref[...] = dot(down_ref[...], act, 1, 1).astype(BF16)
    gh_ref[...] = dot(up_ref[...], gup, 1, 1).astype(BF16)
    sums = jnp.sum(gup.astype(F32), axis=0, keepdims=True)

    @pl.when(pl.program_id(0) == 0)
    def _():
        gb_ref[...] = sums

    @pl.when(pl.program_id(0) > 0)
    def _():
        gb_ref[...] += sums


def feed(h_two, grad_out, up, down, bias_up):
    depth, length = h_two.shape
    hidden = up.shape[1]
    tokens = pl.BlockSpec((depth, MLP_TILE), lambda i: (0, i))
    wide_rows = pl.BlockSpec((MLP_TILE, hidden), lambda i: (i, 0))
    weights = pl.BlockSpec((depth, hidden), lambda i: (0, 0))
    vector = pl.BlockSpec((1, hidden), lambda i: (0, 0))
    return pl.pallas_call(
        feed_kernel,
        grid=(length // MLP_TILE,),
        in_specs=[tokens, tokens, weights, weights, vector],
        out_specs=[wide_rows, wide_rows, tokens, tokens, vector],
        out_shape=[
            jax.ShapeDtypeStruct((length, hidden), BF16),
            jax.ShapeDtypeStruct((length, hidden), BF16),
            jax.ShapeDtypeStruct((depth, length), BF16),
            jax.ShapeDtypeStruct((depth, length), BF16),
            jax.ShapeDtypeStruct((1, hidden), F32),
        ],
        compiler_params=pltpu.CompilerParams(vmem_limit_bytes=VMEM),
        cost_estimate=pl.CostEstimate(
            flops=8 * depth * length * hidden, bytes_accessed=40 << 20, transcendentals=0
        ),
        name="feed",
    )(h_two, grad_out, up, down, bias_up)


def pair_plan(
    tokens,
    piece_starts,
    ln1_gain,
    ln1_bias,
    w_qkv,
    bias_qv,
    w_out,
    bias_out,
    ln2_gain,
    ln2_bias,
    w_up,
    bias_up,
    w_down,
    bias_down,
    cotangent,
):
    rank = lax.axis_index("narrow")
    first = rank == 0
    wide = lax.axis_index("wide")
    wide_size = lax.axis_size("wide")
    own, length = tokens.shape
    depth = 2 * own
    whole = own // HEAD * HEAD
    rest = own - whole
    share = length // 2
    block = depth // wide_size
    hidden = w_up.shape[1]

    def swap(a):
        return lax.ppermute(a, "narrow", [(0, 1), (1, 0)])

    def flip(a, bit):
        return lax.ppermute(a, "wide", [(i, i ^ bit) for i in range(wide_size)])

    def by_bit(bit, a, b):
        return jnp.where(wide & bit == 0, a, b)

    def mine_first(a, b, axis):
        return jnp.where(first, jnp.concatenate((a, b), axis), jnp.concatenate((b, a), axis))

    bits = []
    bit = wide_size // 2
    while bit > 1:
        bits.append(bit)
        bit //= 2

    def gather_rows(a, b, local):
        got = flip(by_bit(1, b, a), 1)
        kept = by_bit(1, a, b)
        cur = by_bit(1, jnp.concatenate((kept, got), 0), jnp.concatenate((got, kept), 0))
        for level, bit in enumerate(bits):
            got = flip(cur, bit)
            low = wide & bit == 0
            if local and level == 0:
                low = low == first
            a_shape = cur.shape[:level] + (1,) + cur.shape[level:]
            mine, other = cur.reshape(a_shape), got.reshape(a_shape)
            cur = jnp.where(
                low,
                jnp.concatenate((mine, other), level),
                jnp.concatenate((other, mine), level),
            )
        cur = cur.reshape(depth, cur.shape[-1])
        got = flip(cur, 1)
        return by_bit(1, cur, got), by_bit(1, got, cur)

    def scatter_rows(a, b, local):
        cols = a.shape[1]
        got = flip(by_bit(1, b, a), 1)
        cur = (by_bit(1, a, b).astype(F32) + got.astype(F32)).astype(BF16)
        cur = cur.reshape((2,) * len(bits) + (2 * block, cols))
        for level in reversed(range(len(bits))):
            bit = bits[level]
            index = (wide & bit != 0).astype(jnp.int32)
            if local and level == 0:
                index = index ^ rank
            keep = lax.dynamic_index_in_dim(cur, index, level, keepdims=False)
            send = lax.dynamic_index_in_dim(cur, 1 - index, level, keepdims=False)
            cur = keep.astype(F32) + flip(send, bit).astype(F32)
            if level > 0:
                cur = cur.astype(BF16)
        core = wide & 1
        cur = cur.reshape(2, block, cols)
        keep = lax.dynamic_index_in_dim(cur, core, 0, keepdims=False)
        got = flip(lax.dynamic_index_in_dim(cur, 1 - core, 0, keepdims=False), 1)
        return by_bit(1, keep, got), by_bit(1, got, keep)

    def all_sum(a):
        for bit in [1] + bits[::-1]:
            a = a + flip(a, bit)
        return a

    own_vectors = jnp.stack((ln1_gain, ln1_bias, ln2_gain, ln2_bias, bias_out))
    vectors = jnp.concatenate((own_vectors, swap(own_vectors)), 1).astype(F32)[:, :, None]
    gain_one, shift_one, gain_two, shift_two, bias_full = [vectors[i] for i in range(5)]
    x = jnp.concatenate((tokens, swap(tokens)), 0)

    def heads_first(a):
        return jnp.where(first, a, jnp.concatenate((a[..., rest:], a[..., :rest]), -1))

    def heads_back(a):
        return jnp.where(first, a, jnp.concatenate((a[..., whole:], a[..., :whole]), -1))

    qkv_shard = heads_first(w_qkv).reshape(block, 3 * own)
    half_cols = -(-3 * own // 256) * 128
    skip = 3 * own - half_cols
    qkv_a, qkv_b = gather_rows(qkv_shard[:, :half_cols], qkv_shard[:, skip:], True)
    qkv = jnp.concatenate((qkv_a, qkv_b[:, half_cols - skip :]), 1)
    dy = jnp.concatenate((cotangent, swap(cotangent)), 0)
    out_a, out_b = gather_rows(w_out, swap(w_out), False)
    out_nat = jnp.concatenate((out_a, out_b), 1)
    up, down = gather_rows(w_up, w_down.T, True)

    x_full = x.astype(F32)
    mean_one = jnp.mean(x_full, axis=0, keepdims=True)
    x_mid = x_full - mean_one
    inv_one = lax.rsqrt(jnp.mean(x_mid * x_mid, axis=0, keepdims=True) + EPSILON)
    h_one = (x_mid * inv_one * gain_one + shift_one).astype(BF16)
    mixed = dot(qkv, h_one, 0, 0)
    bias_local = heads_first(bias_qv).astype(F32)[:, :, None]
    query = (mixed[:own] + bias_local[0]).astype(BF16)
    key = mixed[own : 2 * own].astype(BF16)
    value = (mixed[2 * own :] + bias_local[1]).astype(BF16)
    other = swap(jnp.concatenate((query[whole:], key[whole:], value[whole:]), 0))
    query = jnp.concatenate((query, other[:rest]), 0)
    key = jnp.concatenate((key, other[rest : 2 * rest]), 0)
    value = jnp.concatenate((value, other[2 * rest :]), 0)
    starts = piece_starts[0]
    context, lse = attend(starts, query, key, value)
    context = jnp.concatenate((context, swap(context[:whole])), 0)

    def to_context_order(a):
        turned = jnp.concatenate(
            (a[own + rest :], a[own : own + rest], a[whole:own], a[:whole]), 0
        )
        return jnp.where(first, a, turned)

    out_w = to_context_order(out_nat)
    projected = (dot(out_w, context, 0, 0) + bias_full).astype(BF16)
    mid = x_full + projected.astype(F32)
    mean_two = jnp.mean(mid, axis=0, keepdims=True)
    mid_c = mid - mean_two
    inv_two = lax.rsqrt(jnp.mean(mid_c * mid_c, axis=0, keepdims=True) + EPSILON)
    h_two = (mid_c * inv_two * gain_two + shift_two).astype(BF16)
    act, grad_up, down_part, gh_part, grad_bias_up = feed(
        h_two, dy, up, down, bias_up.astype(F32)[None]
    )

    here, there = rank * share, (1 - rank) * share

    def take(a, start):
        return lax.dynamic_slice_in_dim(a, start, share, 1)

    away = take(gh_part, there)
    away = swap(jnp.concatenate((away[own:], away[:own]), 0))
    gh_two = take(gh_part, here).astype(F32) + away.astype(F32)
    mid_half = take(x, here).astype(F32) + take(projected, here).astype(F32)
    inv_half = take(inv_two, here)
    hat = (mid_half - take(mean_two, here)) * inv_half
    e = gh_two * gain_two
    grad_mid = take(dy, here).astype(F32) + inv_half * (
        e
        - jnp.mean(e, axis=0, keepdims=True)
        - hat * jnp.mean(e * hat, axis=0, keepdims=True)
    )
    grad_two = jnp.stack((jnp.sum(gh_two * hat, axis=1), jnp.sum(gh_two, axis=1)))
    gp = grad_mid.astype(BF16)
    grad_context = dot(out_w, gp, 1, 0).astype(BF16)
    away = jnp.concatenate(
        (grad_context[own + rest :], grad_context[own : own + rest], grad_context[whole:own]), 0
    )
    grad_context = mine_first(grad_context[: own + rest], swap(away), 1)
    gp_own = mine_first(gp[:own], swap(gp[own:]), 1)
    down_sum = down_part[:own].astype(F32) + swap(down_part[own:]).astype(F32)
    output = (
        tokens.astype(F32)
        + projected[:own].astype(F32)
        + (down_sum + bias_down.astype(F32)[:, None])
    ).astype(BF16)
    grad_w_up = dot(h_two, grad_up, 1, 0).astype(BF16)
    grad_w_down = dot(dy, act, 1, 0).astype(BF16)
    sum_w_up, sum_w_down = scatter_rows(grad_w_up, grad_w_down, True)
    grad_w_out = to_context_order(dot(context, gp_own, 1, 1).astype(BF16))
    sum_w_out = jnp.concatenate(
        scatter_rows(grad_w_out[:, : own // 2], grad_w_out[:, own // 2 :], False), 1
    )
    dq, dk, dv = attend_back(starts, query, key, value, grad_context, lse)
    dq, dk, dv = dq[:own], dk[:own], dv[:own]
    grad_mixed = jnp.concatenate((dq, dk, dv), 0)
    gh_one = dot(qkv, grad_mixed, 1, 0)
    grad_qkv_a = dot(h_one, grad_mixed[:half_cols], 1, 1).astype(BF16)
    grad_qkv_b = dot(h_one, grad_mixed[skip:], 1, 1).astype(BF16)
    sum_a, sum_b = scatter_rows(grad_qkv_a, grad_qkv_b, True)
    sum_w_qkv = jnp.concatenate((sum_a, sum_b[:, half_cols - skip :]), 1)
    sum_w_qkv = heads_back(sum_w_qkv.reshape(block, 3, own))
    gh_one = gh_one[:own] + swap(gh_one[own:].astype(BF16)).astype(F32)
    hat = (tokens.astype(F32) - mean_one) * inv_one
    e = gh_one * gain_one[:own]
    stats = jnp.concatenate(
        (jnp.sum(e, axis=0, keepdims=True), jnp.sum(e * hat, axis=0, keepdims=True)), 0
    )
    stats = (stats + swap(stats)) / depth
    grad_tokens = gp_own.astype(F32) + inv_one * (e - stats[:1] - hat * stats[1:])

    grad_two = grad_two[:, :own] + swap(grad_two[:, own:])
    parts = [
        jnp.sum(gh_one * hat, axis=1),
        jnp.sum(gh_one, axis=1),
        jnp.sum(dq.astype(F32), axis=1),
        jnp.sum(dv.astype(F32), axis=1),
        jnp.sum(gp_own.astype(F32), axis=1),
        grad_two[0],
        grad_two[1],
        jnp.sum(cotangent.astype(F32), axis=1),
        grad_bias_up[0],
    ]
    sums = all_sum(jnp.concatenate(parts).reshape(-1, 128)).reshape(-1)
    small = [sums[i * own : (i + 1) * own] for i in range(8)]
    return (
        output,
        grad_tokens,
        small[0],
        small[1],
        sum_w_qkv,
        heads_back(jnp.stack((small[2], small[3]))),
        sum_w_out,
        small[4],
        small[5],
        small[6],
        sum_w_up,
        sums[8 * own :],
        sum_w_down.T,
        small[7],
    )


def solution(mesh):
    in_specs = (
        P("narrow", "wide"),
        P("wide", None),
        P("narrow"),
        P("narrow"),
        P("wide", None, "narrow"),
        P(None, "narrow"),
        P("wide", "narrow"),
        P("narrow"),
        P("narrow"),
        P("narrow"),
        P("wide", "narrow"),
        P("narrow"),
        P("narrow", "wide"),
        P("narrow"),
        P("narrow", "wide"),
    )
    out_specs = (
        P("narrow", "wide"),
        P("narrow", "wide"),
        P("narrow"),
        P("narrow"),
        P("wide", None, "narrow"),
        P(None, "narrow"),
        P("wide", "narrow"),
        P("narrow"),
        P("narrow"),
        P("narrow"),
        P("wide", "narrow"),
        P("narrow"),
        P("narrow", "wide"),
        P("narrow"),
    )
    paired = mesh.shape["narrow"] == 2 and mesh.shape["wide"] == 16
    return jax.shard_map(
        pair_plan if paired else any_mesh, mesh=mesh, in_specs=in_specs, out_specs=out_specs, check_vma=False
    )
```

```python
import functools
from functools import partial

import jax
import jax.numpy as jnp
from jax import lax
from jax.experimental import pallas as pl
from jax.experimental.pallas import tpu as pltpu
from jax.sharding import PartitionSpec as P

HEADS = 17
PIECE = 256


EPSILON = 1e-05


def normalize(row_data, gain_vec, shift_vec):
    centre = jnp.mean(row_data, axis=-1, keepdims=True)
    centred = row_data - centre
    spread = jnp.mean(centred * centred, axis=-1, keepdims=True)
    return centred * lax.rsqrt(spread + EPSILON) * gain_vec + shift_vec


def norm_back(row_data, gain_vec, shift_vec, grad_rows):
    unused, pull_back = jax.vjp(normalize, row_data, gain_vec, shift_vec)
    return pull_back(grad_rows)


def full_rows(partial_rows):
    return lax.psum(partial_rows, "narrow")


def visible_mask(starts, query_pos, key_pos):
    query_in = (query_pos[:, None] >= starts[None, :]) & (
        query_pos[:, None] < starts[None, :] + PIECE
    )
    key_in = (key_pos[:, None] >= starts[None, :]) & (key_pos[:, None] < starts[None, :] + PIECE)
    shared = jnp.any(query_in[:, None, :] & key_in[None, :, :], axis=-1)
    return (key_pos[None, :] <= query_pos[:, None]) | shared


def to_heads(matrix):
    return matrix.reshape(matrix.shape[0], HEADS, matrix.shape[1] // HEADS)


def attention_scores(query_rows, key_full, visible, score_scale):
    raw = (
        jnp.einsum(
            "qhd,khd->hqk",
            to_heads(query_rows),
            to_heads(key_full),
            preferred_element_type=jnp.float32,
        )
        * score_scale
    )
    return jnp.where(visible[None], raw, -1e30)


def any_mesh(
    tokens,
    piece_starts,
    ln1_gain,
    ln1_bias,
    w_qkv,
    bias_qv,
    w_out,
    bias_out,
    ln2_gain,
    ln2_bias,
    w_up,
    bias_up,
    w_down,
    bias_down,
    cotangent,
):
    narrow_size = lax.axis_size("narrow")
    narrow_rank = lax.axis_index("narrow")
    col_width, length = tokens.shape
    full_width = col_width * narrow_size
    queries = length // narrow_size
    score_scale = (full_width // HEADS) ** (-0.5)
    col_start = narrow_rank * col_width
    row_start = narrow_rank * queries

    def own_cols(matrix):
        return lax.dynamic_slice_in_dim(matrix, col_start, col_width, matrix.ndim - 1)

    x_cols, dy_cols, gain_one, shift_one, gain_two, shift_two = (
        lax.all_gather(tokens, "narrow", axis=0, tiled=True),
        lax.all_gather(cotangent, "narrow", axis=0, tiled=True),
        lax.all_gather(ln1_gain, "narrow", axis=0, tiled=True),
        lax.all_gather(ln1_bias, "narrow", axis=0, tiled=True),
        lax.all_gather(ln2_gain, "narrow", axis=0, tiled=True),
        lax.all_gather(ln2_bias, "narrow", axis=0, tiled=True),
    )
    x_rows = x_cols.T
    dy_rows = dy_cols.T
    qkv_cols, out_cols, up_cols, down_rows = (
        lax.all_gather(w_qkv, "wide", axis=0, tiled=True),
        lax.all_gather(w_out, "wide", axis=0, tiled=True),
        lax.all_gather(w_up, "wide", axis=0, tiled=True),
        lax.all_gather(w_down, "wide", axis=1, tiled=True),
    )
    gain_one = gain_one.astype(jnp.float32)
    shift_one = shift_one.astype(jnp.float32)
    gain_two = gain_two.astype(jnp.float32)
    shift_two = shift_two.astype(jnp.float32)
    x_full = x_rows.astype(jnp.float32)
    h_one = normalize(x_full, gain_one, shift_one).astype(jnp.bfloat16)
    mixed = jnp.einsum("td,dcf->tcf", h_one, qkv_cols, preferred_element_type=jnp.float32)
    bias_cols = bias_qv.astype(jnp.float32)
    query_cols = (mixed[:, 0] + bias_cols[0]).astype(jnp.bfloat16)
    key_cols = mixed[:, 1].astype(jnp.bfloat16)
    value_cols = (mixed[:, 2] + bias_cols[1]).astype(jnp.bfloat16)
    query_full, key_full, value_full = (
        lax.all_gather(query_cols, "narrow", axis=1, tiled=True),
        lax.all_gather(key_cols, "narrow", axis=1, tiled=True),
        lax.all_gather(value_cols, "narrow", axis=1, tiled=True),
    )
    query_rows = lax.dynamic_slice_in_dim(query_full, row_start, queries, 0)
    query_pos = row_start + jnp.arange(queries, dtype=jnp.int32)
    key_pos = jnp.arange(length, dtype=jnp.int32)
    visible = visible_mask(piece_starts[0], query_pos, key_pos)
    masked = attention_scores(query_rows, key_full, visible, score_scale)
    row_top = jnp.max(masked, axis=-1, keepdims=True)
    weights = jnp.exp(masked - row_top)
    row_total = jnp.sum(weights, axis=-1, keepdims=True)
    log_total = row_top + jnp.log(row_total)
    probs_low = (weights / row_total).astype(jnp.bfloat16)
    context = jnp.einsum(
        "hqk,khd->qhd", probs_low, to_heads(value_full), preferred_element_type=jnp.float32
    )
    context = context.reshape(queries, full_width).astype(jnp.bfloat16)
    context_full = lax.all_gather(context, "narrow", axis=0, tiled=True)
    projected = jnp.dot(
        context_full, out_cols, preferred_element_type=jnp.float32
    ) + bias_out.astype(jnp.float32)
    projected_low = projected.astype(jnp.bfloat16)
    projected_full = lax.all_gather(projected_low, "narrow", axis=1, tiled=True)
    mid_full = x_full + projected_full.astype(jnp.float32)
    mid_rows = tokens.T.astype(jnp.float32) + projected_low.astype(jnp.float32)
    h_two = normalize(mid_full, gain_two, shift_two).astype(jnp.bfloat16)
    up_pre = jnp.dot(h_two, up_cols, preferred_element_type=jnp.float32) + bias_up.astype(
        jnp.float32
    )
    act_value, gelu_pull = jax.vjp(partial(jax.nn.gelu, approximate=True), up_pre)
    act_low = act_value.astype(jnp.bfloat16)
    partial_down = jnp.dot(act_low, down_rows, preferred_element_type=jnp.float32)
    down_sum = lax.psum_scatter(
        partial_down.astype(jnp.bfloat16), "narrow", scatter_dimension=1, tiled=True
    ).astype(jnp.float32)
    output = (mid_rows + (down_sum + bias_down.astype(jnp.float32))).astype(jnp.bfloat16)
    grad_out = cotangent.T.astype(jnp.float32)
    grad_bias_down = jnp.sum(grad_out, axis=0)
    grad_w_down = jnp.einsum("tf,td->fd", act_low, dy_rows, preferred_element_type=jnp.float32)
    grad_act = jnp.einsum("td,fd->tf", dy_rows, down_rows, preferred_element_type=jnp.float32)
    grad_up = gelu_pull(grad_act)[0].astype(jnp.bfloat16)
    grad_bias_up = jnp.sum(grad_up.astype(jnp.float32), axis=0)
    grad_w_up = jnp.einsum("td,tf->df", h_two, grad_up, preferred_element_type=jnp.float32)
    grad_h_two = full_rows(
        jnp.einsum("tf,df->td", grad_up, up_cols, preferred_element_type=jnp.float32)
    )
    grad_mid_full, grad_gain_two, grad_shift_two = norm_back(
        mid_full, gain_two, shift_two, grad_h_two
    )
    grad_mid = grad_out + own_cols(grad_mid_full)
    grad_projected = grad_mid.astype(jnp.bfloat16)
    grad_bias_out = jnp.sum(grad_projected.astype(jnp.float32), axis=0)
    grad_w_out = jnp.einsum(
        "td,tc->dc", context_full, grad_projected, preferred_element_type=jnp.float32
    )
    grad_context = lax.psum_scatter(
        jnp.einsum("tc,dc->td", grad_projected, out_cols, preferred_element_type=jnp.float32),
        "narrow",
        scatter_dimension=0,
        tiled=True,
    ).astype(jnp.bfloat16)
    weights_back = jnp.exp(masked - log_total)
    context_heads = to_heads(grad_context)
    grad_probs = jnp.einsum(
        "qhd,khd->hqk", context_heads, to_heads(value_full), preferred_element_type=jnp.float32
    )
    centre = jnp.sum(weights_back * grad_probs, axis=-1, keepdims=True)
    grad_scores = (weights_back * (grad_probs - centre)).astype(jnp.bfloat16)
    grad_query = jnp.einsum(
        "hqk,khd->qhd", grad_scores, to_heads(key_full), preferred_element_type=jnp.float32
    )
    grad_query = grad_query.reshape(queries, full_width) * score_scale
    probs_back = weights_back.astype(jnp.bfloat16)
    grad_key = jnp.einsum(
        "hqk,qhd->khd", grad_scores, to_heads(query_rows), preferred_element_type=jnp.float32
    )
    grad_key = grad_key.reshape(length, full_width) * score_scale
    grad_value = jnp.einsum(
        "hqk,qhd->khd", probs_back, context_heads, preferred_element_type=jnp.float32
    )
    grad_value = grad_value.reshape(length, full_width)
    placed = jnp.zeros((length, full_width), jnp.float32)
    placed = lax.dynamic_update_slice_in_dim(placed, grad_query, row_start, 0)
    stacked = jnp.stack((placed, grad_key, grad_value), axis=1)
    grad_mixed = lax.psum_scatter(stacked, "narrow", scatter_dimension=2, tiled=True).astype(
        jnp.bfloat16
    )
    grad_mixed_f = grad_mixed.astype(jnp.float32)
    grad_bias_qv = jnp.stack(
        (jnp.sum(grad_mixed_f[:, 0], axis=0), jnp.sum(grad_mixed_f[:, 2], axis=0))
    )
    grad_w_qkv = jnp.einsum("td,tcf->dcf", h_one, grad_mixed, preferred_element_type=jnp.float32)
    grad_h_one = full_rows(
        jnp.einsum("tcf,dcf->td", grad_mixed, qkv_cols, preferred_element_type=jnp.float32)
    )
    grad_x_full, grad_gain_one, grad_shift_one = norm_back(x_full, gain_one, shift_one, grad_h_one)
    grad_tokens = grad_mid + own_cols(grad_x_full)
    sum_w_qkv, sum_w_out, sum_w_up, sum_w_down = (
        lax.psum_scatter(grad_w_qkv, "wide", scatter_dimension=0, tiled=True),
        lax.psum_scatter(grad_w_out, "wide", scatter_dimension=0, tiled=True),
        lax.psum_scatter(grad_w_up, "wide", scatter_dimension=0, tiled=True),
        lax.psum_scatter(grad_w_down, "wide", scatter_dimension=1, tiled=True),
    )
    (
        sum_gain_one,
        sum_shift_one,
        sum_bias_qv,
        sum_bias_out,
        sum_gain_two,
        sum_shift_two,
        sum_bias_up,
        sum_bias_down,
    ) = lax.psum(
        (
            own_cols(grad_gain_one),
            own_cols(grad_shift_one),
            grad_bias_qv,
            grad_bias_out,
            own_cols(grad_gain_two),
            own_cols(grad_shift_two),
            grad_bias_up,
            grad_bias_down,
        ),
        "wide",
    )
    return (
        output.T,
        grad_tokens.T,
        sum_gain_one,
        sum_shift_one,
        sum_w_qkv,
        sum_bias_qv,
        sum_w_out,
        sum_bias_out,
        sum_gain_two,
        sum_shift_two,
        sum_w_up,
        sum_bias_up,
        sum_w_down,
        sum_bias_down,
    )


F32 = jnp.float32
BF16 = jnp.bfloat16
HEAD = 64
TILE = 256
VMEM = 60 << 20
LANES = 128
PACE = 0.15


def dot(a, b, dim_a, dim_b):
    return lax.dot_general(a, b, (((dim_a,), (dim_b,)), ((), ())), preferred_element_type=F32)


def after(value, *others):
    return lax.optimization_barrier((value,) + others)[0]


def cost(flops, moved):
    return pl.CostEstimate(flops=int(PACE * flops), bytes_accessed=int(moved), transcendentals=0)


def params():
    return pltpu.CompilerParams(vmem_limit_bytes=VMEM)


def lane_sums(a):
    return functools.reduce(
        jnp.add, [a[:, i : i + LANES] for i in range(0, a.shape[1], LANES)]
    )


def row_sums(acc):
    return jnp.concatenate(
        [
            jnp.sum(acc[:, i : i + LANES].T, axis=0, keepdims=True)
            for i in range(0, acc.shape[1], LANES)
        ],
        0,
    )


def rows_at(start, size):
    return pl.ds(pl.multiple_of(start, HEAD // 2), size)


def first_step():
    return pl.program_id(0) == 0


def last_step():
    return pl.program_id(0) == pl.num_programs(0) - 1


def unit(rows, a, b):
    mine = rows == 0
    return jnp.where(mine, a, b), jnp.where(mine, b, a)


def bias_kernel(starts_ref, bias_ref):
    length = bias_ref.shape[0] * TILE
    for i in range(length // TILE):
        low = i * TILE
        rows = min(2 * TILE, length - low)
        key = low + lax.broadcasted_iota(jnp.int32, (rows, TILE), 0)
        query = low + lax.broadcasted_iota(jnp.int32, (rows, TILE), 1)
        seen = key <= query
        for p in range(starts_ref.shape[0]):
            s = starts_ref[p]
            seen = seen | (
                (key >= s) & (key < s + PIECE) & (query >= s) & (query < s + PIECE)
            )
        bias_ref[i, :rows, :] = jnp.where(seen, 0.0, -1e30)


def mask_bias(starts, length):
    shape = (length // TILE, 2 * TILE, TILE)
    return pl.pallas_call(
        bias_kernel,
        in_specs=[pl.BlockSpec(memory_space=pltpu.SMEM)],
        out_specs=pl.BlockSpec(memory_space=pltpu.VMEM),
        out_shape=jax.ShapeDtypeStruct(shape, F32),
        compiler_params=params(),
        name="mask_bias",
    )(starts)


def score_parts(key_rows, query, bias, i, length):
    low = i * TILE
    high = min(low + 2 * TILE, length)
    parts = []
    if low > 0:
        parts.append(dot(key_rows[:low], query, 1, 0))
    parts.append(dot(key_rows[low:high], query, 1, 0) + bias[i, : high - low, :])
    return parts


def attend_kernel(bias, x_ref, c_ref, l_ref, key_rows):
    length = x_ref.shape[2]
    key_rows[...] = x_ref[1].T
    for i in range(length // TILE):
        here = pl.ds(i * TILE, TILE)
        query = x_ref[0, :, here] * jnp.asarray(HEAD**-0.5, BF16)
        parts = score_parts(key_rows, query, bias, i, length)
        top = functools.reduce(jnp.maximum, [jnp.max(s, axis=0, keepdims=True) for s in parts])
        total, acc, at = 0.0, 0.0, 0
        for s in parts:
            p = jnp.exp(s - top)
            total = total + jnp.sum(p, axis=0, keepdims=True)
            acc = acc + dot(x_ref[2, :, at : at + s.shape[0]], p.astype(BF16), 1, 0)
            at += s.shape[0]
        c_ref[:, here] = (acc / total).astype(BF16)
        l_ref[0, :, here] = top + jnp.log(total)


def attend(bias, qkv, first, count):
    length = qkv.shape[2]
    return pl.pallas_call(
        attend_kernel,
        grid=(count,),
        in_specs=[
            pl.BlockSpec(bias.shape, lambda h: (0, 0, 0)),
            pl.BlockSpec((3, HEAD, length), lambda h: (0, h + first, 0)),
        ],
        out_specs=[
            pl.BlockSpec((HEAD, length), lambda h: (h, 0)),
            pl.BlockSpec((1, 1, length), lambda h: (h, 0, 0)),
        ],
        scratch_shapes=[pltpu.VMEM((length, HEAD), BF16)],
        out_shape=[
            jax.ShapeDtypeStruct((count * HEAD, length), BF16),
            jax.ShapeDtypeStruct((count, 1, length), F32),
        ],
        compiler_params=params(),
        cost_estimate=cost(4e9 * count, count * length * HEAD * 8),
        name="attend",
    )(bias, qkv)


def attend_back_kernel(
    shared, rank_ref, bias, x_ref, mine_ref, got_ref, l_ref, old_ref, g_ref,
    key_rows, value_rows, query_rows, grad_rows, grad, key_sum, value_sum,
):
    length = x_ref.shape[2]
    share = length // 2
    scale = jnp.asarray(HEAD**-0.5, BF16)
    first = rank_ref[0] == 0
    mine, got = mine_ref[...], got_ref[...]
    grad[:, :share] = jnp.where(first, mine, got)
    grad[:, share:] = jnp.where(first, got, mine)
    key_rows[...] = x_ref[1].T
    value_rows[...] = x_ref[2].T
    grad_rows[...] = grad[...].T
    query_rows[...] = (x_ref[0] * scale).T
    tiles = length // TILE
    for i in reversed(range(tiles)):
        here = pl.ds(i * TILE, TILE)
        parts = score_parts(key_rows, x_ref[0, :, here] * scale, bias, i, length)
        lse = l_ref[0, :, here]
        at, centre, pairs = 0, 0.0, []
        for s in parts:
            p = jnp.exp(s - lse)
            gp = dot(value_rows[at : at + s.shape[0]], grad[:, here], 1, 0)
            centre = centre + jnp.sum(p * gp, axis=0, keepdims=True)
            pairs.append((p, gp))
            at += s.shape[0]
        at, dq = 0, 0.0
        for p, gp in pairs:
            span = slice(at, at + p.shape[0])
            gs = (p * (gp - centre)).astype(BF16)
            dq = dq + dot(x_ref[1, :, span], gs, 1, 0)
            dk = dot(gs, query_rows[here], 1, 0)
            dv = dot(p.astype(BF16), grad_rows[here], 1, 0)
            if i == tiles - 1:
                key_sum[span], value_sum[span] = dk, dv
            else:
                key_sum[span] += dk
                value_sum[span] += dv
            at += p.shape[0]
        g_ref[0, :, here] = (dq * HEAD**-0.5).astype(BF16)
    g_ref[1] = key_sum[...].T.astype(BF16)
    g_ref[2] = value_sum[...].T.astype(BF16)
    if shared:
        @pl.when(pl.program_id(0) == pl.num_programs(0) - 1)
        def _():
            g_ref[:, HEAD // 2 :, :] = jnp.zeros((3, HEAD // 2, length), BF16)


def attend_back(bias, rank, qkv, mine, got, lse, first, count, shared, old=None):
    length = qkv.shape[2]
    rows = pltpu.VMEM((length, HEAD), BF16)
    sums = pltpu.VMEM((length, HEAD), F32)
    heads = pl.BlockSpec((3, HEAD, length), lambda h, r: (0, h + first, 0))
    half = pl.BlockSpec((HEAD, length // 2), lambda h, r: (h + first, 0))
    alias = {}
    if old is not None:
        alias = {6: 0}
    else:
        old = jnp.zeros((8, 128), BF16)
    return pl.pallas_call(
        functools.partial(attend_back_kernel, shared),
        grid_spec=pltpu.PrefetchScalarGridSpec(
            num_scalar_prefetch=1,
            grid=(count,),
            in_specs=[
                pl.BlockSpec(bias.shape, lambda h, r: (0, 0, 0)),
                heads,
                half,
                half,
                pl.BlockSpec((1, 1, length), lambda h, r: (h + first, 0, 0)),
                pl.BlockSpec(memory_space=pl.ANY),
            ],
            out_specs=[heads],
            scratch_shapes=[rows] * 4
            + [pltpu.VMEM((HEAD, length), BF16)]
            + [sums] * 2,
        ),
        out_shape=[jax.ShapeDtypeStruct(qkv.shape, BF16)],
        input_output_aliases=alias,
        compiler_params=params(),
        cost_estimate=cost(6.8e9 * count, count * length * HEAD * 14),
        name="attend_back",
    )(rank, bias, qkv, mine, got, lse, old)[0]


def norm_rows(x):
    x = x - jnp.mean(x, axis=0, keepdims=True)
    inv = lax.rsqrt(jnp.mean(x * x, axis=0, keepdims=True) + EPSILON)
    return x * inv, inv


def own_first(rank, a):
    half = a.shape[0] // 2
    return jnp.where(rank == 0, a, jnp.concatenate((a[half:], a[:half]), 0))


def turn_weights(core, mine, got, turned):
    a, b = unit(core, mine, got)
    count = a.shape[1]
    turned[:count] = a.T
    turned[count:] = b.T[2 * count - turned.shape[0] :]


def norm_qkv_kernel(core_ref, xo_ref, xt_ref, m_ref, g_ref, v_ref, b_ref, h_ref, q_ref, turned):
    @pl.when(first_step())
    def _():
        turn_weights(core_ref[0], m_ref[...], g_ref[...], turned)

    x = jnp.concatenate((xo_ref[...], xt_ref[...]), 0).astype(F32)
    h = (norm_rows(x)[0] * v_ref[:, 0:1] + v_ref[:, 1:2]).astype(BF16)
    h_ref[...] = h
    q_ref[...] = (dot(turned[...], h, 1, 0) + b_ref[...]).astype(BF16)


def norm_qkv(core, x_own, x_other, mine, got, vectors, bias):
    own, length = x_own.shape
    depth = 2 * own
    rows = bias.shape[0]
    column = lambda n: pl.BlockSpec((n, TILE), lambda i, s: (0, i))
    whole = lambda a: pl.BlockSpec(a.shape, lambda i, s: (0, 0))
    return pl.pallas_call(
        norm_qkv_kernel,
        grid_spec=pltpu.PrefetchScalarGridSpec(
            num_scalar_prefetch=1,
            grid=(length // TILE,),
            in_specs=[column(own)] * 2 + [whole(a) for a in (mine, got, vectors, bias)],
            out_specs=[column(depth), column(rows)],
            scratch_shapes=[pltpu.VMEM((rows, depth), BF16)],
        ),
        out_shape=[jax.ShapeDtypeStruct((n, length), BF16) for n in (depth, rows)],
        compiler_params=params(),
        cost_estimate=cost(2 * depth * rows * length, depth * length * 6),
        name="norm_qkv",
    )(core, x_own, x_other, mine, got, vectors, bias)


def qkv_kernel(core_ref, h_ref, m_ref, g_ref, b_ref, q_ref, turned):
    @pl.when(first_step())
    def _():
        turn_weights(core_ref[0], m_ref[...], g_ref[...], turned)

    q_ref[...] = (dot(turned[...], h_ref[...], 1, 0) + b_ref[...]).astype(BF16)


def qkv_of(core, h_one, mine, got, bias):
    depth, length = h_one.shape
    rows = bias.shape[0]
    column = lambda n: pl.BlockSpec((n, TILE), lambda i, s: (0, i))
    whole = lambda a: pl.BlockSpec(a.shape, lambda i, s: (0, 0))
    return pl.pallas_call(
        qkv_kernel,
        grid_spec=pltpu.PrefetchScalarGridSpec(
            num_scalar_prefetch=1,
            grid=(length // TILE,),
            in_specs=[column(depth)] + [whole(a) for a in (mine, got, bias)],
            out_specs=column(rows),
            scratch_shapes=[pltpu.VMEM((rows, depth), BF16)],
        ),
        out_shape=jax.ShapeDtypeStruct((rows, length), BF16),
        compiler_params=params(),
        cost_estimate=cost(2 * depth * rows * length, depth * length * 4),
        name="qkv",
    )(core, h_one, mine, got, bias)


def project_kernel(
    spot_ref, xo_ref, xt_ref, a_ref, b_ref, ga_ref, gb_ref, c_ref, m_ref, g_ref, v_ref,
    p_ref, h_ref, c_out, turned,
):
    @pl.when(first_step())
    def _():
        own = xo_ref.shape[0]
        parts = [own_first(spot_ref[0], w[:, :own]) for w in (m_ref, g_ref)]
        turn_weights(spot_ref[1], *parts, turned)

    rank = spot_ref[0]
    own = xo_ref.shape[0]
    a, b, half = a_ref.shape[0], b_ref.shape[0], HEAD // 2
    c_out[rows_at(half * rank, a)] = a_ref[...]
    c_out[rows_at(half * rank + a, b)] = b_ref[...]
    c_out[rows_at((a + b) * (1 - rank), half)] = c_ref[:half]
    c_out[rows_at(own + (a + b) * rank, half)] = c_ref[half:]
    c_out[rows_at(own + half * (1 - rank), a)] = ga_ref[...]
    c_out[rows_at(own + half * (1 - rank) + a, b)] = gb_ref[...]
    low = (dot(turned[...], c_out[...], 1, 0) + v_ref[:, 0:1]).astype(BF16)
    p_ref[...] = low
    mid = jnp.concatenate((xo_ref[...], xt_ref[...]), 0).astype(F32) + low.astype(F32)
    h_ref[...] = (norm_rows(mid)[0] * v_ref[:, 1:2] + v_ref[:, 2:3]).astype(BF16)


def out_columns(depth):
    return pl.BlockSpec((depth, -(-depth // (2 * LANES)) * LANES), lambda i, s: (0, 0))


def project(spot, x_own, x_other, pieces, mine, got, vectors):
    own, length = x_own.shape
    depth = 2 * own
    column = lambda rows: pl.BlockSpec((rows, TILE), lambda i, s: (0, i))
    whole = lambda a: pl.BlockSpec(a.shape, lambda i, s: (0, 0))
    return pl.pallas_call(
        project_kernel,
        grid_spec=pltpu.PrefetchScalarGridSpec(
            num_scalar_prefetch=1,
            grid=(length // TILE,),
            in_specs=[column(own)] * 2
            + [column(p.shape[0]) for p in pieces]
            + [out_columns(depth)] * 2
            + [whole(vectors)],
            out_specs=[column(depth)] * 3,
            scratch_shapes=[pltpu.VMEM((depth, depth), BF16)],
        ),
        out_shape=[jax.ShapeDtypeStruct((depth, length), BF16)] * 3,
        compiler_params=params(),
        cost_estimate=cost(2 * depth * depth * length, depth * length * 10),
        name="project",
    )(spot, x_own, x_other, *pieces, mine, got, vectors)


def feed_kernel(
    spot_ref, h_ref, go_ref, gt_ref, pm_ref, pg_ref, qm_ref, qg_ref, bias_ref, *rest
):
    mid_ref, out_ref, gh_ref, gb_ref, gs_ref, up, down, sums, sems = rest[-9:]
    split = up.shape[1] - qm_ref.shape[1]
    lead = pm_ref.shape[1] - split
    hidden = up.shape[1]

    @pl.when(pl.program_id(0) == 0)
    def _():
        half = up.shape[0] // 2

        def copies(up_p, up_q, down_p, down_q):
            made = []
            for i, (first, second, whole) in enumerate(((up_p, up_q, up), (down_p, down_q, down))):
                for j in range(2):
                    rows = pl.ds(half * j, half)
                    to = rows_at(half * (j ^ spot_ref[2]), half)
                    at = 4 * i + 2 * j
                    made += [
                        pltpu.make_async_copy(
                            first.at[rows, lead:], whole.at[to, :split], sems.at[at]
                        ),
                        pltpu.make_async_copy(
                            second.at[rows, :], whole.at[to, split:], sems.at[at + 1]
                        ),
                    ]
            return made

        def bring(these):
            for c in these:
                c.start()
            for c in these:
                c.wait()

        @pl.when(spot_ref[1] == 0)
        def _():
            bring(copies(pm_ref, qm_ref, pg_ref, qg_ref))

        @pl.when(spot_ref[1] == 1)
        def _():
            bring(copies(pg_ref, qg_ref, pm_ref, qm_ref))

        gb_ref[...] = jnp.zeros_like(gb_ref)
        sums[...] = jnp.zeros_like(sums)

    sums[...] += lane_sums(go_ref[...].astype(F32))

    @pl.when(last_step())
    def _():
        gs_ref[...] = row_sums(sums[...])

    root = (2 / jnp.pi) ** 0.5
    h = h_ref[...]
    g = jnp.concatenate((go_ref[...], gt_ref[...]), 0)
    for span in (slice(0, split), slice(split, hidden)):
        u = dot(h, up[:, span], 0, 0) + bias_ref[:, span]
        grad_act = dot(g, down[:, span], 0, 0)
        square = u * u
        t = jnp.tanh(u * (root + (root * 0.044715) * square))
        half = 0.5 + 0.5 * t
        mid_ref[0, :, span] = (u * half).astype(BF16)
        slope = half + (0.5 * u) * (1 - t * t) * (root + (3 * root * 0.044715) * square)
        gup = (grad_act * slope).astype(BF16)
        mid_ref[1, :, span] = gup
        gb_ref[:, span] += jnp.sum(gup.astype(F32), axis=0, keepdims=True)
    gh_ref[...] = dot(up[...], mid_ref[1], 1, 1).astype(BF16)
    out_ref[...] = dot(down[...], mid_ref[0], 1, 1).astype(BF16)


def feed(spot, count, h_two, g_own, g_other, weights, bias_up, tile, old):
    depth, length = h_two.shape
    own = g_own.shape[0]
    hidden = bias_up.shape[1]
    column = lambda rows: pl.BlockSpec((rows, tile), lambda i, s: (0, s[0] + i))
    anywhere = pl.BlockSpec(memory_space=pl.ANY)
    vector = pl.BlockSpec((1, hidden), lambda i, s: (0, 0))
    aliases = {} if old is None else {9: 0, 10: 1}
    return pl.pallas_call(
        feed_kernel,
        grid_spec=pltpu.PrefetchScalarGridSpec(
            num_scalar_prefetch=1,
            grid=(count,),
            in_specs=[column(depth), column(own), column(own)]
            + [anywhere] * 4
            + [vector]
            + [anywhere] * len(aliases),
            out_specs=[
                pl.BlockSpec((2, tile, hidden), lambda i, s: (0, s[0] + i, 0)),
                column(depth),
                pl.BlockSpec((depth, tile), lambda i, s: (0, i)),
                vector,
                pl.BlockSpec((1, own), lambda i, s: (0, 0)),
            ],
            scratch_shapes=[
                pltpu.VMEM((depth, hidden), BF16),
                pltpu.VMEM((depth, hidden), BF16),
                pltpu.VMEM((own, LANES), F32),
                pltpu.SemaphoreType.DMA((8,)),
            ],
        ),
        out_shape=[
            jax.ShapeDtypeStruct((2, length, hidden), BF16),
            jax.ShapeDtypeStruct((depth, length), BF16),
            jax.ShapeDtypeStruct((depth, count * tile), BF16),
            jax.ShapeDtypeStruct((1, hidden), F32),
            jax.ShapeDtypeStruct((1, own), F32),
        ],
        input_output_aliases=aliases,
        compiler_params=params(),
        cost_estimate=cost(8 * depth * count * tile * hidden, 12 * depth * hidden),
        name="feed",
    )(spot, h_two, g_own, g_other, *weights, bias_up, *(old or ()))


def weight_grad_kernel(which_ref, h_ref, go_ref, gt_ref, m_ref, p_ref, q_ref):
    half = pl.program_id(0) < pl.num_programs(0) // 2
    g = jnp.where(half, go_ref[...], gt_ref[...])
    rows = jnp.where(which_ref[0] == 0, g, h_ref[...])
    split = p_ref.shape[1]
    p_ref[...] = dot(rows, m_ref[0, :, :split], 1, 0).astype(BF16)
    q_ref[...] = dot(rows, m_ref[0, :, split:], 1, 0).astype(BF16)


def weight_grad(which, h_two, g_own, g_other, middle, split):
    depth, length = h_two.shape
    hidden = middle.shape[2]
    steps = 2
    rows = depth // steps
    return pl.pallas_call(
        weight_grad_kernel,
        grid_spec=pltpu.PrefetchScalarGridSpec(
            num_scalar_prefetch=1,
            grid=(steps,),
            in_specs=[
                pl.BlockSpec((rows, length), lambda i, s: (i, 0)),
                pl.BlockSpec((rows, length), lambda i, s: (0, 0)),
                pl.BlockSpec((rows, length), lambda i, s: (0, 0)),
                pl.BlockSpec((1, length, hidden), lambda i, s: (s[0], 0, 0)),
            ],
            out_specs=[pl.BlockSpec((rows, n), lambda i, s: (i, 0)) for n in (split, hidden - split)],
        ),
        out_shape=[jax.ShapeDtypeStruct((depth, n), BF16) for n in (split, hidden - split)],
        compiler_params=params(),
        cost_estimate=cost(2 * depth * length * hidden, 2 * (2 * depth + hidden) * length),
        name="weight_grad",
    )(which, h_two, g_own, g_other, middle)


def mid_back_kernel(
    spot_ref, xo_ref, xt_ref, p_ref, go_ref, gt_ref, keep_ref, got_ref, m_ref, g_ref, v_ref,
    gp_ref, ma_ref, mb_ref, sa_ref, sb_ref, n_ref, w_own, w_other, gc, sums,
):
    @pl.when(first_step())
    def _():
        n = w_own.shape[1]
        parts = [own_first(spot_ref[2], w[:, :n]) for w in (m_ref, g_ref)]
        w_own[...], w_other[...] = unit(spot_ref[1], *parts)
        sums[...] = jnp.zeros_like(sums)

    own = xo_ref.shape[0]
    rank = spot_ref[2]
    keep, got = keep_ref[...].astype(F32), got_ref[...].astype(F32)
    gh = keep + jnp.concatenate((got[own:], got[:own]), 0)
    mid = jnp.concatenate((xo_ref[...], xt_ref[...]), 0).astype(F32) + p_ref[...].astype(F32)
    hat, inv = norm_rows(mid)
    e = gh * v_ref[:, 1:2]
    grad = jnp.concatenate((go_ref[...], gt_ref[...]), 0).astype(F32) + inv * (
        e - jnp.mean(e, axis=0, keepdims=True) - hat * jnp.mean(e * hat, axis=0, keepdims=True)
    )
    gp = grad.astype(BF16)
    gp_ref[...] = gp
    gc[...] = (dot(w_own[...], gp[:own], 1, 0) + dot(w_other[...], gp[own:], 1, 0)).astype(BF16)
    half = HEAD // 2
    a, b = ma_ref.shape[0], mb_ref.shape[0] - HEAD
    near, away = half * rank, own + half * (1 - rank)
    own_half = gc[rows_at((a + b) * (1 - rank), half)]
    other_half = gc[rows_at(own + (a + b) * rank, half)]
    ma_ref[...] = gc[rows_at(near, a)]
    mb_ref[:b] = gc[rows_at(near + a, b)]
    mb_ref[b : b + half] = own_half
    mb_ref[b + half :] = other_half
    sa_ref[...] = gc[rows_at(away, a)]
    sb_ref[:b] = gc[rows_at(away + a, b)]
    sb_ref[b : b + half] = other_half
    sb_ref[b + half :] = own_half
    sums[...] += jnp.concatenate(
        (lane_sums(gh * hat), lane_sums(gh), lane_sums(gp.astype(F32))), 1
    )

    @pl.when(last_step())
    def _():
        n_ref[...] = row_sums(sums[...])


def mid_back(spot, x_own, x_other, projected, g_own, g_other, keep, got, mine, got_w, vectors, rows_a, rows_b):
    own, length = x_own.shape
    depth = 2 * own
    share = length // 2
    column = lambda rows: pl.BlockSpec((rows, TILE), lambda i, s: (0, s[0] + i))
    local = lambda rows: pl.BlockSpec((rows, TILE), lambda i, s: (0, i))
    whole = lambda a: pl.BlockSpec(a.shape, lambda i, s: (0, 0))
    out = lambda rows: jax.ShapeDtypeStruct((rows, share), BF16)
    sizes = (depth, rows_a, rows_b, rows_a, rows_b)
    return pl.pallas_call(
        mid_back_kernel,
        grid_spec=pltpu.PrefetchScalarGridSpec(
            num_scalar_prefetch=1,
            grid=(share // TILE,),
            in_specs=[column(own), column(own), column(depth), column(own), column(own)]
            + [local(depth)] * 2
            + [out_columns(depth)] * 2
            + [whole(vectors)],
            out_specs=[local(r) for r in sizes] + [pl.BlockSpec((3, depth), lambda i, s: (0, 0))],
            scratch_shapes=[pltpu.VMEM((depth, own), BF16)] * 2
            + [pltpu.VMEM((depth, TILE), BF16), pltpu.VMEM((depth, 3 * LANES), F32)],
        ),
        out_shape=[out(r) for r in sizes] + [jax.ShapeDtypeStruct((3, depth), F32)],
        compiler_params=params(),
        cost_estimate=cost(2 * depth * depth * share, depth * share * 16),
        name="mid_back",
    )(spot, x_own, x_other, projected, g_own, g_other, keep, got, mine, got_w, vectors)


def half_lanes(columns):
    return -(-columns // (2 * LANES)) * LANES


def grads_a_kernel(which_ref, h_ref, g_ref, w_ref):
    w_ref[...] = dot(h_ref[...], g_ref[...], 1, 1).astype(BF16)


def grads_b_kernel(which_ref, h_ref, c_ref, g_ref, p_ref, w_ref):
    which = which_ref[0]
    out = half_lanes(p_ref.shape[0])
    cols = w_ref.shape[1] - out
    skip = g_ref.shape[0] - cols
    skip_out = p_ref.shape[0] - out
    w_ref[:, :cols] = dot(h_ref[...], g_ref[rows_at(skip * which, cols)], 1, 1).astype(BF16)
    half = pl.ds(pl.multiple_of(skip_out * which, HEAD // 2), out)
    w_ref[:, cols:] = dot(c_ref[...], p_ref[half], 1, 1).astype(BF16)


def grads_a(which, h_one, grad):
    depth, length = h_one.shape
    cols = grad.shape[0] // 2
    return pl.pallas_call(
        grads_a_kernel,
        grid_spec=pltpu.PrefetchScalarGridSpec(
            num_scalar_prefetch=1,
            grid=(2,),
            in_specs=[
                pl.BlockSpec((depth // 2, length), lambda i, s: (i, 0)),
                pl.BlockSpec((cols, length), lambda i, s: (s[0], 0)),
            ],
            out_specs=pl.BlockSpec((depth // 2, cols), lambda i, s: (i, 0)),
        ),
        out_shape=jax.ShapeDtypeStruct((depth, cols), BF16),
        compiler_params=params(),
        cost_estimate=cost(2 * depth * cols * length, 2 * depth * length),
        name="grads_a",
    )(which, h_one, grad)


def grads_b(which, h_one, context, grad, gp_own, cols):
    depth, length = h_one.shape
    total = cols + half_lanes(gp_own.shape[0])
    whole = lambda a: pl.BlockSpec(a.shape, lambda i, s: (0, 0))
    part = pl.BlockSpec((depth // 2, length), lambda i, s: (i, 0))
    return pl.pallas_call(
        grads_b_kernel,
        grid_spec=pltpu.PrefetchScalarGridSpec(
            num_scalar_prefetch=1,
            grid=(2,),
            in_specs=[part, part, whole(grad), whole(gp_own)],
            out_specs=pl.BlockSpec((depth // 2, total), lambda i, s: (i, 0)),
        ),
        out_shape=jax.ShapeDtypeStruct((depth, total), BF16),
        compiler_params=params(),
        cost_estimate=cost(2 * depth * total * length, 6 * depth * length),
        name="grads_b",
    )(which, h_one, context, grad, gp_own)


def qkv_back_kernel(
    core_ref, xo_ref, xt_ref, gb_ref, ga_ref, bm_ref, bg_ref, am_ref, ag_ref, v_ref,
    keep_ref, send_ref, s_ref, n_ref, db_ref, da_ref, b_low, b_high, a_low, a_high, n_sum, b_sum, a_sum,
):
    @pl.when(first_step())
    def _():
        b_low[...], b_high[...] = unit(core_ref[0], bm_ref[...], bg_ref[...])
        a_low[...], a_high[...] = unit(core_ref[0], am_ref[...], ag_ref[...])
        for r in (n_sum, b_sum, a_sum):
            r[...] = jnp.zeros_like(r)

    own = xo_ref.shape[0]
    gb, ga = gb_ref[...], ga_ref[...]
    cols_b, cols_a = b_low.shape[1], a_low.shape[1]
    twice = 2 * cols_b - gb.shape[0]
    rest = jnp.concatenate((jnp.zeros((twice, gb.shape[1]), BF16), gb[cols_b:]), 0)
    gh = (dot(b_low[...], gb[:cols_b], 1, 0) + dot(b_high[...], rest, 1, 0)) + (
        dot(a_low[...], ga[:cols_a], 1, 0) + dot(a_high[...], ga[cols_a:], 1, 0)
    )
    keep_ref[...] = gh[:own].astype(BF16)
    send_ref[...] = gh[own:].astype(BF16)
    x = jnp.concatenate((xo_ref[...], xt_ref[...]), 0).astype(F32)
    hat, inv = norm_rows(x)
    both = gh * hat
    gain = v_ref[:, 0:1]
    s_ref[...] = jnp.concatenate(
        (
            jnp.sum(gh * gain, axis=0, keepdims=True),
            jnp.sum(both * gain, axis=0, keepdims=True),
            jnp.mean(x, axis=0, keepdims=True),
            inv,
        ),
        0,
    )
    n_sum[...] += jnp.concatenate((lane_sums(both), lane_sums(gh)), 1)
    b_sum[...] += lane_sums(gb.astype(F32))
    a_sum[...] += lane_sums(ga.astype(F32))

    @pl.when(last_step())
    def _():
        n_ref[...] = row_sums(n_sum[...])
        db_ref[...] = row_sums(b_sum[...])
        da_ref[...] = row_sums(a_sum[...])


def qkv_back(core, x_own, x_other, grad_b, grad_a, w_b, w_a, vectors, first, count):
    own = x_own.shape[0]
    depth = 2 * own
    column = lambda rows: pl.BlockSpec((rows, TILE), lambda i, s: (0, first + i))
    local = lambda rows: pl.BlockSpec((rows, TILE), lambda i, s: (0, i))
    whole = lambda a: pl.BlockSpec(a.shape, lambda i, s: (0, 0))
    span = count * TILE
    out = jax.ShapeDtypeStruct
    rows = (depth, grad_b.shape[0], grad_a.shape[0])
    flat = [out((n, r), F32) for n, r in zip((2, 1, 1), rows)]
    return pl.pallas_call(
        qkv_back_kernel,
        grid_spec=pltpu.PrefetchScalarGridSpec(
            num_scalar_prefetch=1,
            grid=(count,),
            in_specs=[column(own)] * 2
            + [column(grad_b.shape[0]), column(grad_a.shape[0])]
            + [whole(a) for a in (*w_b, *w_a, vectors)],
            out_specs=[local(own), local(own), local(4)] + [whole(t) for t in flat],
            scratch_shapes=[pltpu.VMEM(w.shape, BF16) for w in (*w_b, *w_a)]
            + [pltpu.VMEM((r, n * LANES), F32) for n, r in zip((2, 1, 1), rows)],
        ),
        out_shape=[out((own, span), BF16), out((own, span), BF16), out((4, span), F32)] + flat,
        compiler_params=params(),
        cost_estimate=cost(2 * depth * span * (rows[1] + rows[2]), depth * span * 12),
        name="qkv_back",
    )(core, x_own, x_other, grad_b, grad_a, *w_b, *w_a, vectors)


def by_bit(bit, a, b):
    return jnp.where(lax.axis_index("wide") & bit == 0, a, b)


def flip(a, bit):
    size = lax.axis_size("wide")
    return lax.ppermute(a, "wide", [(i, i ^ bit) for i in range(size)])


class Gather:
    def __init__(self, a, b, order):
        self.kept = by_bit(1, a, b)
        self.got = flip(by_bit(1, b, a), 1)
        self.order = list(order)
        self.bits = []
        self.last = None

    def merge(self):
        kept, got = self.kept, self.got
        if self.last is None:
            axis, low = 0, lax.axis_index("wide") & 1 == 0
        else:
            axis = sum(1 for b in self.bits if b > self.last)
            low = lax.axis_index("wide") & self.last == 0
            if self.last == max(self.order_all):
                low = low == (lax.axis_index("narrow") == 0)
            shape = kept.shape[:axis] + (1,) + kept.shape[axis:]
            kept, got = kept.reshape(shape), got.reshape(shape)
            self.bits.append(self.last)
        self.cur = jnp.where(
            low, jnp.concatenate((kept, got), axis), jnp.concatenate((got, kept), axis)
        )

    def held(self):
        return self.cur

    def hold(self, value):
        self.cur = value

    @property
    def order_all(self):
        return self.order + self.bits + ([self.last] if self.last else [])

    def send(self):
        self.last = self.order.pop(0) if self.order else 1
        if self.last == 1:
            self.cur = self.cur.reshape(-1, self.cur.shape[-1])
        self.kept, self.got = self.cur, flip(self.cur, self.last)

    def step(self, *gates):
        self.merge()
        if gates:
            self.cur = after(self.cur, *gates)
        self.send()


class Whole:
    def __init__(self, a, b):
        self.kept = by_bit(1, a, b)
        self.got = flip(by_bit(1, b, a), 1)
        self.stage = 0

    def merge(self):
        if self.stage == 0:
            low = lax.axis_index("wide") & 1 == 0
            kept, got = self.kept, self.got
            self.cur = jnp.where(
                low, jnp.concatenate((kept, got), 0), jnp.concatenate((got, kept), 0)
            )

    def held(self):
        return self.cur

    def hold(self, value):
        self.cur = value

    def send(self):
        if self.stage == 0:
            size = lax.axis_size("wide")
            groups = [list(range(c, size, 2)) for c in range(2)]
            self.cur = lax.all_gather(
                self.cur, "wide", axis=0, tiled=True, axis_index_groups=groups
            )
        else:
            self.got = flip(self.cur, 1)
        self.stage += 1


class Scatter:
    def __init__(self, send, order):
        self.got = flip(send, 1)
        self.order = list(order)
        self.axes = sorted(order, reverse=True)
        self.top = self.axes[0]

    def merge(self):
        self.cur = self.kept.astype(F32) + self.got.astype(F32)
        if self.order:
            cur = self.cur.astype(BF16)
            if cur.ndim == 2:
                cur = cur.reshape((2,) * len(self.axes) + (-1, cur.shape[-1]))
            bit = self.order.pop(0)
            axis = self.axes.index(bit)
            self.axes.remove(bit)
            index = (lax.axis_index("wide") & bit != 0).astype(jnp.int32)
            if bit == self.top:
                index = index ^ lax.axis_index("narrow")
        else:
            bit, axis = 1, 0
            cur = self.cur.reshape(2, -1, self.cur.shape[-1])
            index = lax.axis_index("wide") & 1
        self.bit = bit
        self.keep = lax.dynamic_index_in_dim(cur, index, axis, keepdims=False)
        self.away = lax.dynamic_index_in_dim(cur, 1 - index, axis, keepdims=False)

    def send(self):
        self.kept, self.got = self.keep, flip(self.away, self.bit)

    def step(self, *gates):
        self.merge()
        if gates:
            self.away = after(self.away, *gates)
        self.send()

    def held(self):
        return self.keep, self.away

    def hold(self, value):
        self.keep, self.away = value

    def result(self):
        return by_bit(1, self.kept, self.got), by_bit(1, self.got, self.kept)


def meet(values, *moves):
    for m in moves:
        m.merge()
    values, held = lax.optimization_barrier((values, [m.held() for m in moves]))
    for m, h in zip(moves, held):
        m.hold(h)
        m.send()
    return values


def pair_plan(
    tokens,
    piece_starts,
    ln1_gain,
    ln1_bias,
    w_qkv,
    bias_qv,
    w_out,
    bias_out,
    ln2_gain,
    ln2_bias,
    w_up,
    bias_up,
    w_down,
    bias_down,
    cotangent,
):
    rank = lax.axis_index("narrow")
    first = rank == 0
    core = lax.axis_index("wide") & 1
    own, length = tokens.shape
    depth = 2 * own
    whole = own // HEAD * HEAD
    rest = own - whole
    rows_a = whole // 2
    rows_b = whole - rows_a + 2 * rest
    heads_a, heads_b = rows_a // HEAD, rows_b // HEAD
    block = w_out.shape[0]
    hidden = w_up.shape[1]
    tile = length // 4
    part = -(-(hidden + own) // 256) * LANES
    split = hidden - part
    split_back = hidden // 256 * LANES + LANES
    rank_arg = rank.astype(jnp.int32)[None]

    def swap(a):
        return lax.ppermute(a, "narrow", [(0, 1), (1, 0)])

    def mine_first(a, b, axis):
        return jnp.where(first, jnp.concatenate((a, b), axis), jnp.concatenate((b, a), axis))

    def heads_first(a):
        return jnp.where(first, a, jnp.concatenate((a[..., rest:], a[..., :rest]), -1))

    def heads_back(a):
        return jnp.where(first, a, jnp.concatenate((a[..., whole:], a[..., :whole]), -1))

    def at_rows(bias):
        return jnp.stack((bias[0], jnp.zeros_like(bias[0]), bias[1])).reshape(-1, 1)

    far, near, side = 8, 4, 2
    inward, outward = (far, near, side), (side, far, near)
    w_heads = heads_first(w_qkv)
    shard_a = w_heads[:, :, :rows_a].reshape(block, -1)
    cols_a = shard_a.shape[1] // 2
    get_a = Gather(shard_a[:, :cols_a], shard_a[:, cols_a:], inward)
    bias_local = heads_first(bias_qv)
    own_vectors = jnp.concatenate(
        (jnp.stack((ln1_gain, ln1_bias, ln2_gain, ln2_bias, bias_out)), bias_local), 0
    )
    half_rows = w_heads[:, :, whole:].reshape(-1, own)
    count = own_vectors.shape[0]
    small_swap = swap(jnp.concatenate((own_vectors, half_rows, w_out), 0))
    small_swap, x_own, w_heads, w_out_in, w_up_in, w_down_in, g_own = meet(
        (small_swap, tokens, w_heads, w_out, w_up, w_down, cotangent), get_a
    )
    x_other = swap(x_own)
    other_vectors = small_swap[:count]
    other_half = small_swap[count:-block].reshape(block, 3, rest)
    w_out_other = small_swap[-block:]
    vectors = jnp.concatenate((own_vectors[:5], other_vectors[:5]), 1).astype(F32).T
    gain_one, shift_one = vectors[:, 0:1], vectors[:, 1:2]
    project_vectors = jnp.stack((vectors[:, 4], vectors[:, 2], vectors[:, 3]), 1)
    w_down_t = w_down_in.T
    get_q = Whole(w_up_in[:, split:], w_down_t[:, split:])
    shard_b = jnp.concatenate((w_heads[:, :, rows_a:], other_half), 2).reshape(block, -1)
    cols_b = -(-shard_b.shape[1] // 256) * 128
    skip = shard_b.shape[1] - cols_b
    get_b = Gather(shard_b[:, :cols_b], shard_b[:, skip:], inward)
    pad = jnp.zeros((block, part - split - own), BF16)
    get_p = Whole(
        jnp.concatenate((w_out_in, pad, w_up_in[:, :split]), 1),
        jnp.concatenate((w_out_other, pad, w_down_t[:, :split]), 1),
    )
    meet((), get_a, get_q, get_p)
    starts = meet(piece_starts[0], get_a, get_b)
    seen = mask_bias(starts, length)
    seen = meet(seen, get_a, get_b)
    x_other, get_a.got = meet((x_other, get_a.got), get_b)

    early = 2 * length // 3
    g_other = [swap(after(g_own[:, :early], x_other))]
    bias_f = bias_local.astype(F32)
    bias_a = bias_f[:, :rows_a]
    bias_b = jnp.concatenate((bias_f[:, rows_a:], other_vectors[5:, whole:].astype(F32)), 1)
    core_arg = core[None]
    w_a = (get_a.cur, get_a.got)
    h_one, qkv_a = norm_qkv(core_arg, tokens, x_other, *w_a, vectors, at_rows(bias_a))
    qkv_a = qkv_a.reshape(3, rows_a, length)
    qkv_a, h_one = meet((qkv_a, h_one), get_b)

    context_a, lse_a = attend(seen, qkv_a, 0, heads_a)
    context_a, g_other[0], h_b, get_b.got = meet(
        (context_a, g_other[0], h_one, get_b.got), get_p
    )

    context_a_other = swap(context_a)
    w_b = (get_b.cur, get_b.got)
    qkv_b = qkv_of(core_arg, h_b, *w_b, at_rows(bias_b)).reshape(3, rows_b, length)
    whole_b = heads_b - 1
    context_b, lse_b = attend(seen, qkv_b, 0, whole_b)
    context_b, context_a_other, qkv_c = meet((context_b, context_a_other, qkv_b))

    context_b_other = swap(context_b)
    context_c, lse_c = attend(seen, qkv_c, whole_b, 1)
    lse_b = jnp.concatenate((lse_b, lse_c), 0)
    context_b_other, context_c, get_p.got = meet((context_b_other, context_c, get_p.got), get_q)

    g_other.append(swap(after(g_own[:, early:], context_b_other)))
    pieces = (context_a, context_b, context_a_other, context_b_other, context_c)
    w_o = (get_p.cur, get_p.got)
    places = jnp.stack((rank, core)).astype(jnp.int32)
    projected, h_two, context = project(places, tokens, x_other, pieces, *w_o, project_vectors)
    projected, h_two, context, g_other, get_q.got = meet(
        (projected, h_two, context, g_other, get_q.got)
    )
    g_other = jnp.concatenate(g_other, 1)

    weights = (get_p.cur, get_p.got, get_q.cur, get_q.got)
    bias_up_f = bias_up.astype(F32)[None]
    steps = length // 2 // TILE

    def spot(at):
        return jnp.stack((at, core, rank)).astype(jnp.int32)

    *old, gh_send, gb_send, gs_send = feed(
        spot(steps * (1 - rank)), steps, h_two, cotangent, g_other, weights, bias_up_f, TILE, None
    )
    old, gh_send, gb_send = meet((old, gh_send, gb_send))
    gh_got = swap(gh_send)
    middle, down_part, gh_keep, gb_keep, gs_keep = feed(
        spot(steps * rank), steps, h_two, cotangent, g_other, weights, bias_up_f, TILE, old
    )
    grad_bias_up = gb_send[0] + gb_keep[0]
    send_p, send_q = weight_grad(core[None], h_two, cotangent, g_other, middle, split_back)
    gh_got, gh_keep, send_p, send_q, middle, down_part = meet(
        (gh_got, gh_keep, send_p, send_q, middle, down_part)
    )

    put_p = Scatter(send_p, (side, near, far))
    put_q = Scatter(send_q, (near, far, side))
    gp, mine_a, mine_b, send_a, send_b, grad_two = mid_back(
        spot(steps * rank), tokens, x_other, projected, cotangent, g_other, gh_keep,
        gh_got, *w_o, project_vectors, rows_a, rows_b,
    )
    gp, mine_a, mine_b, send_a, send_b, middle = meet((gp, mine_a, mine_b, send_a, send_b, middle))

    got_b = swap(send_b)
    put_p.kept, put_q.kept = weight_grad(1 - core[None], h_two, cotangent, g_other, middle, split_back)
    got_b, mine_b, send_a, gp = meet((got_b, mine_b, send_a, gp), put_p, put_q)

    got_a = swap(send_a)
    gp_other = swap(gp[own:])
    back_b = attend_back(seen, rank_arg, qkv_b, mine_b, got_b, lse_b, 0, heads_b, True)
    back_b, got_a, gp_other, down_part = meet((back_b, got_a, gp_other, down_part), put_p, put_q)

    down_other = swap(down_part[own:])
    gp_own = mine_first(gp[:own], gp_other, 1)
    grad_b = back_b.reshape(3 * rows_b, length)

    put_b = Scatter(grads_b(1 - core_arg, h_one, context, grad_b, gp_own, cols_b), (side, near, far))
    put_b.kept, mine_a, qkv_a = meet(
        (grads_b(core_arg, h_one, context, grad_b, gp_own, cols_b), mine_a, qkv_a)
    )

    back_a = attend_back(seen, rank_arg, qkv_a, mine_a, got_a, lse_a, 0, heads_a, False)
    back_a, down_other = meet((back_a, down_other), put_p, put_q, put_b)
    grad_a = back_a.reshape(3 * rows_a, length)

    put_a = Scatter(grads_a(1 - core_arg, h_one, grad_a), (near, far, side))
    put_a.kept = grads_a(core_arg, h_one, grad_a)
    grad_a = meet(grad_a, put_a)
    halves = []
    for i in range(2):
        out = qkv_back(
            core_arg, tokens, x_other, grad_b, grad_a, w_b, w_a, vectors, steps * i, steps
        )
        if i == 0:
            out, grad_a = meet((out, grad_a), put_a, put_b, put_p, put_q)
        else:
            out = meet(out, put_a, put_b)
        halves.append([out[0], swap(out[1])] + list(out[2:]))
    halves[0][1] = meet(halves[0][1], put_a, put_b)
    sum_up_p, sum_down_p = put_p.result()
    sum_up_q, sum_down_q = put_q.result()
    low_b, high_b = put_b.result()
    sum_a = jnp.concatenate(put_a.result(), 1).reshape(block, 3, rows_a)
    out_cols = half_lanes(own)
    sum_out = jnp.concatenate((low_b[:, cols_b:], high_b[:, cols_b + 2 * out_cols - own :]), 1)
    sum_b = jnp.concatenate((low_b[:, :cols_b], high_b[:, cols_b - skip : cols_b]), 1)
    sum_b = sum_b.reshape(block, 3, rows_b)[:, :, : rows_b - rest]
    sum_w_qkv = heads_back(jnp.concatenate((sum_a, sum_b), 2))

    vec_b = (halves[0][4] + halves[1][4]).reshape(3, rows_b)
    vec_a = (halves[0][5] + halves[1][5]).reshape(3, rows_a)
    shared = jnp.concatenate((halves[0][3] + halves[1][3], grad_two), 0)
    vec = jnp.concatenate((vec_a, vec_b[:, : rows_b - rest]), 1)
    parts = [
        shared[:, :own].reshape(-1),
        vec[0],
        vec[2],
        (gs_send + gs_keep)[0],
        grad_bias_up,
        shared[:, own:].reshape(-1),
    ]
    total = jnp.concatenate(parts)
    total = jnp.concatenate((total, jnp.zeros((-total.shape[0] % 1024,), F32))).reshape(-1, LANES)
    for bit in (1, side, near, far):
        total = total + flip(total, bit)
    total = total.reshape(-1)
    tail = 8 * own + hidden
    added = swap(total[tail : tail + 5 * own])
    total = jnp.concatenate((total[: 5 * own] + added, total[5 * own : tail]))
    small = [total[i * own : (i + 1) * own] for i in range(8)]

    down_sum = down_part[:own].astype(F32) + down_other.astype(F32)
    output = (
        tokens.astype(F32)
        + projected[:own].astype(F32)
        + (down_sum + bias_down.astype(F32)[:, None])
    ).astype(BF16)

    stats = jnp.concatenate((halves[0][2], halves[1][2]), 1)
    row_stats, stats = stats[2:], stats[:2]
    stats = (stats + swap(stats)) / depth
    keep = jnp.concatenate((halves[0][0], halves[1][0]), 1).astype(F32)
    got = jnp.concatenate((halves[0][1], halves[1][1]), 1)
    mean_one, inv_one = row_stats[:1], row_stats[1:]
    hat = (tokens.astype(F32) - mean_one) * inv_one
    e = (keep + got.astype(F32)) * gain_one[:own]
    grad_tokens = gp_own.astype(F32) + inv_one * (e - stats[:1] - hat * stats[1:])
    return (
        output,
        grad_tokens,
        small[0],
        small[1],
        sum_w_qkv,
        heads_back(jnp.stack((small[5], small[6]))),
        sum_out,
        small[4],
        small[2],
        small[3],
        jnp.concatenate((sum_up_p, sum_up_q), 1),
        total[8 * own :],
        jnp.concatenate((sum_down_p, sum_down_q), 1).T,
        small[7],
    )


def solution(mesh):
    in_specs = (
        P("narrow", "wide"),
        P("wide", None),
        P("narrow"),
        P("narrow"),
        P("wide", None, "narrow"),
        P(None, "narrow"),
        P("wide", "narrow"),
        P("narrow"),
        P("narrow"),
        P("narrow"),
        P("wide", "narrow"),
        P("narrow"),
        P("narrow", "wide"),
        P("narrow"),
        P("narrow", "wide"),
    )
    out_specs = (
        P("narrow", "wide"),
        P("narrow", "wide"),
        P("narrow"),
        P("narrow"),
        P("wide", None, "narrow"),
        P(None, "narrow"),
        P("wide", "narrow"),
        P("narrow"),
        P("narrow"),
        P("narrow"),
        P("wide", "narrow"),
        P("narrow"),
        P("narrow", "wide"),
        P("narrow"),
    )
    paired = mesh.shape["narrow"] == 2 and mesh.shape["wide"] == 16
    return jax.shard_map(
        pair_plan if paired else any_mesh, mesh=mesh, in_specs=in_specs, out_specs=out_specs, check_vma=False
    )
```

```python
import functools
import math
from functools import partial

import jax
import jax.numpy as jnp
from jax import lax
from jax.experimental import pallas as pl
from jax.experimental.pallas import tpu as pltpu
from jax.sharding import PartitionSpec as P

HEADS = 17
PIECE = 256


EPSILON = 1e-05


def normalize(row_data, gain_vec, shift_vec):
    centre = jnp.mean(row_data, axis=-1, keepdims=True)
    centred = row_data - centre
    spread = jnp.mean(centred * centred, axis=-1, keepdims=True)
    return centred * lax.rsqrt(spread + EPSILON) * gain_vec + shift_vec


def norm_back(row_data, gain_vec, shift_vec, grad_rows):
    unused, pull_back = jax.vjp(normalize, row_data, gain_vec, shift_vec)
    return pull_back(grad_rows)


def full_rows(partial_rows):
    return lax.psum(partial_rows, "narrow")


def visible_mask(starts, query_pos, key_pos):
    query_in = (query_pos[:, None] >= starts[None, :]) & (
        query_pos[:, None] < starts[None, :] + PIECE
    )
    key_in = (key_pos[:, None] >= starts[None, :]) & (key_pos[:, None] < starts[None, :] + PIECE)
    shared = jnp.any(query_in[:, None, :] & key_in[None, :, :], axis=-1)
    return (key_pos[None, :] <= query_pos[:, None]) | shared


def to_heads(matrix):
    return matrix.reshape(matrix.shape[0], HEADS, matrix.shape[1] // HEADS)


def attention_scores(query_rows, key_full, visible, score_scale):
    raw = (
        jnp.einsum(
            "qhd,khd->hqk",
            to_heads(query_rows),
            to_heads(key_full),
            preferred_element_type=jnp.float32,
        )
        * score_scale
    )
    return jnp.where(visible[None], raw, -1e30)


def any_mesh(
    tokens,
    piece_starts,
    ln1_gain,
    ln1_bias,
    w_qkv,
    bias_qv,
    w_out,
    bias_out,
    ln2_gain,
    ln2_bias,
    w_up,
    bias_up,
    w_down,
    bias_down,
    cotangent,
):
    narrow_size = lax.axis_size("narrow")
    narrow_rank = lax.axis_index("narrow")
    col_width, length = tokens.shape
    full_width = col_width * narrow_size
    queries = length // narrow_size
    score_scale = (full_width // HEADS) ** (-0.5)
    col_start = narrow_rank * col_width
    row_start = narrow_rank * queries

    def own_cols(matrix):
        return lax.dynamic_slice_in_dim(matrix, col_start, col_width, matrix.ndim - 1)

    x_cols, dy_cols, gain_one, shift_one, gain_two, shift_two = (
        lax.all_gather(tokens, "narrow", axis=0, tiled=True),
        lax.all_gather(cotangent, "narrow", axis=0, tiled=True),
        lax.all_gather(ln1_gain, "narrow", axis=0, tiled=True),
        lax.all_gather(ln1_bias, "narrow", axis=0, tiled=True),
        lax.all_gather(ln2_gain, "narrow", axis=0, tiled=True),
        lax.all_gather(ln2_bias, "narrow", axis=0, tiled=True),
    )
    x_rows = x_cols.T
    dy_rows = dy_cols.T
    qkv_cols, out_cols, up_cols, down_rows = (
        lax.all_gather(w_qkv, "wide", axis=0, tiled=True),
        lax.all_gather(w_out, "wide", axis=0, tiled=True),
        lax.all_gather(w_up, "wide", axis=0, tiled=True),
        lax.all_gather(w_down, "wide", axis=1, tiled=True),
    )
    gain_one = gain_one.astype(jnp.float32)
    shift_one = shift_one.astype(jnp.float32)
    gain_two = gain_two.astype(jnp.float32)
    shift_two = shift_two.astype(jnp.float32)
    x_full = x_rows.astype(jnp.float32)
    h_one = normalize(x_full, gain_one, shift_one).astype(jnp.bfloat16)
    mixed = jnp.einsum("td,dcf->tcf", h_one, qkv_cols, preferred_element_type=jnp.float32)
    bias_cols = bias_qv.astype(jnp.float32)
    query_cols = (mixed[:, 0] + bias_cols[0]).astype(jnp.bfloat16)
    key_cols = mixed[:, 1].astype(jnp.bfloat16)
    value_cols = (mixed[:, 2] + bias_cols[1]).astype(jnp.bfloat16)
    query_full, key_full, value_full = (
        lax.all_gather(query_cols, "narrow", axis=1, tiled=True),
        lax.all_gather(key_cols, "narrow", axis=1, tiled=True),
        lax.all_gather(value_cols, "narrow", axis=1, tiled=True),
    )
    query_rows = lax.dynamic_slice_in_dim(query_full, row_start, queries, 0)
    query_pos = row_start + jnp.arange(queries, dtype=jnp.int32)
    key_pos = jnp.arange(length, dtype=jnp.int32)
    visible = visible_mask(piece_starts[0], query_pos, key_pos)
    masked = attention_scores(query_rows, key_full, visible, score_scale)
    row_top = jnp.max(masked, axis=-1, keepdims=True)
    weights = jnp.exp(masked - row_top)
    row_total = jnp.sum(weights, axis=-1, keepdims=True)
    log_total = row_top + jnp.log(row_total)
    probs_low = (weights / row_total).astype(jnp.bfloat16)
    context = jnp.einsum(
        "hqk,khd->qhd", probs_low, to_heads(value_full), preferred_element_type=jnp.float32
    )
    context = context.reshape(queries, full_width).astype(jnp.bfloat16)
    context_full = lax.all_gather(context, "narrow", axis=0, tiled=True)
    projected = jnp.dot(
        context_full, out_cols, preferred_element_type=jnp.float32
    ) + bias_out.astype(jnp.float32)
    projected_low = projected.astype(jnp.bfloat16)
    projected_full = lax.all_gather(projected_low, "narrow", axis=1, tiled=True)
    mid_full = x_full + projected_full.astype(jnp.float32)
    mid_rows = tokens.T.astype(jnp.float32) + projected_low.astype(jnp.float32)
    h_two = normalize(mid_full, gain_two, shift_two).astype(jnp.bfloat16)
    up_pre = jnp.dot(h_two, up_cols, preferred_element_type=jnp.float32) + bias_up.astype(
        jnp.float32
    )
    act_value, gelu_pull = jax.vjp(partial(jax.nn.gelu, approximate=True), up_pre)
    act_low = act_value.astype(jnp.bfloat16)
    partial_down = jnp.dot(act_low, down_rows, preferred_element_type=jnp.float32)
    down_sum = lax.psum_scatter(
        partial_down.astype(jnp.bfloat16), "narrow", scatter_dimension=1, tiled=True
    ).astype(jnp.float32)
    output = (mid_rows + (down_sum + bias_down.astype(jnp.float32))).astype(jnp.bfloat16)
    grad_out = cotangent.T.astype(jnp.float32)
    grad_bias_down = jnp.sum(grad_out, axis=0)
    grad_w_down = jnp.einsum("tf,td->fd", act_low, dy_rows, preferred_element_type=jnp.float32)
    grad_act = jnp.einsum("td,fd->tf", dy_rows, down_rows, preferred_element_type=jnp.float32)
    grad_up = gelu_pull(grad_act)[0].astype(jnp.bfloat16)
    grad_bias_up = jnp.sum(grad_up.astype(jnp.float32), axis=0)
    grad_w_up = jnp.einsum("td,tf->df", h_two, grad_up, preferred_element_type=jnp.float32)
    grad_h_two = full_rows(
        jnp.einsum("tf,df->td", grad_up, up_cols, preferred_element_type=jnp.float32)
    )
    grad_mid_full, grad_gain_two, grad_shift_two = norm_back(
        mid_full, gain_two, shift_two, grad_h_two
    )
    grad_mid = grad_out + own_cols(grad_mid_full)
    grad_projected = grad_mid.astype(jnp.bfloat16)
    grad_bias_out = jnp.sum(grad_projected.astype(jnp.float32), axis=0)
    grad_w_out = jnp.einsum(
        "td,tc->dc", context_full, grad_projected, preferred_element_type=jnp.float32
    )
    grad_context = lax.psum_scatter(
        jnp.einsum("tc,dc->td", grad_projected, out_cols, preferred_element_type=jnp.float32),
        "narrow",
        scatter_dimension=0,
        tiled=True,
    ).astype(jnp.bfloat16)
    weights_back = jnp.exp(masked - log_total)
    context_heads = to_heads(grad_context)
    grad_probs = jnp.einsum(
        "qhd,khd->hqk", context_heads, to_heads(value_full), preferred_element_type=jnp.float32
    )
    centre = jnp.sum(weights_back * grad_probs, axis=-1, keepdims=True)
    grad_scores = (weights_back * (grad_probs - centre)).astype(jnp.bfloat16)
    grad_query = jnp.einsum(
        "hqk,khd->qhd", grad_scores, to_heads(key_full), preferred_element_type=jnp.float32
    )
    grad_query = grad_query.reshape(queries, full_width) * score_scale
    probs_back = weights_back.astype(jnp.bfloat16)
    grad_key = jnp.einsum(
        "hqk,qhd->khd", grad_scores, to_heads(query_rows), preferred_element_type=jnp.float32
    )
    grad_key = grad_key.reshape(length, full_width) * score_scale
    grad_value = jnp.einsum(
        "hqk,qhd->khd", probs_back, context_heads, preferred_element_type=jnp.float32
    )
    grad_value = grad_value.reshape(length, full_width)
    placed = jnp.zeros((length, full_width), jnp.float32)
    placed = lax.dynamic_update_slice_in_dim(placed, grad_query, row_start, 0)
    stacked = jnp.stack((placed, grad_key, grad_value), axis=1)
    grad_mixed = lax.psum_scatter(stacked, "narrow", scatter_dimension=2, tiled=True).astype(
        jnp.bfloat16
    )
    grad_mixed_f = grad_mixed.astype(jnp.float32)
    grad_bias_qv = jnp.stack(
        (jnp.sum(grad_mixed_f[:, 0], axis=0), jnp.sum(grad_mixed_f[:, 2], axis=0))
    )
    grad_w_qkv = jnp.einsum("td,tcf->dcf", h_one, grad_mixed, preferred_element_type=jnp.float32)
    grad_h_one = full_rows(
        jnp.einsum("tcf,dcf->td", grad_mixed, qkv_cols, preferred_element_type=jnp.float32)
    )
    grad_x_full, grad_gain_one, grad_shift_one = norm_back(x_full, gain_one, shift_one, grad_h_one)
    grad_tokens = grad_mid + own_cols(grad_x_full)
    sum_w_qkv, sum_w_out, sum_w_up, sum_w_down = (
        lax.psum_scatter(grad_w_qkv, "wide", scatter_dimension=0, tiled=True),
        lax.psum_scatter(grad_w_out, "wide", scatter_dimension=0, tiled=True),
        lax.psum_scatter(grad_w_up, "wide", scatter_dimension=0, tiled=True),
        lax.psum_scatter(grad_w_down, "wide", scatter_dimension=1, tiled=True),
    )
    (
        sum_gain_one,
        sum_shift_one,
        sum_bias_qv,
        sum_bias_out,
        sum_gain_two,
        sum_shift_two,
        sum_bias_up,
        sum_bias_down,
    ) = lax.psum(
        (
            own_cols(grad_gain_one),
            own_cols(grad_shift_one),
            grad_bias_qv,
            grad_bias_out,
            own_cols(grad_gain_two),
            own_cols(grad_shift_two),
            grad_bias_up,
            grad_bias_down,
        ),
        "wide",
    )
    return (
        output.T,
        grad_tokens.T,
        sum_gain_one,
        sum_shift_one,
        sum_w_qkv,
        sum_bias_qv,
        sum_w_out,
        sum_bias_out,
        sum_gain_two,
        sum_shift_two,
        sum_w_up,
        sum_bias_up,
        sum_w_down,
        sum_bias_down,
    )


F32 = jnp.float32
BF16 = jnp.bfloat16
HEAD = 64
TILE = 256
MIB = 1 << 20
LANES = 128
SPARE = 16
PACE = 1e-6


def dot(a, b, dim_a, dim_b):
    return lax.dot_general(a, b, (((dim_a,), (dim_b,)), ((), ())), preferred_element_type=F32)


def after(value, *others):
    return lax.optimization_barrier((value,) + others)[0]


def cost(flops, moved):
    return pl.CostEstimate(flops=1 + int(PACE * flops), bytes_accessed=1 + int(PACE * moved), transcendentals=0)


def params(mib):
    return pltpu.CompilerParams(vmem_limit_bytes=mib * MIB)


def in_turns(stages, items):
    states = [None] * len(items)
    for tick in range(len(items) + len(stages) - 1):
        for j, stage in enumerate(stages):
            i = tick - j
            if 0 <= i < len(items):
                states[i] = stage(items[i], states[i])


def lane_sums(a):
    return functools.reduce(
        jnp.add, [a[:, i : i + LANES] for i in range(0, a.shape[1], LANES)]
    )


def row_sums(acc):
    return jnp.concatenate(
        [
            jnp.sum(acc[:, i : i + LANES].T, axis=0, keepdims=True)
            for i in range(0, acc.shape[1], LANES)
        ],
        0,
    )


def rows_at(start, size):
    return pl.ds(pl.multiple_of(start, HEAD // 2), size)


def first_step():
    return pl.program_id(0) == 0


def last_step():
    return pl.program_id(0) == pl.num_programs(0) - 1


def unit(rows, a, b):
    mine = rows == 0
    return jnp.where(mine, a, b), jnp.where(mine, b, a)


def bias_kernel(starts_ref, bias_ref):
    length = bias_ref.shape[0] * TILE
    for i in range(length // TILE):
        low = i * TILE
        rows = min(2 * TILE, length - low)
        key = low + lax.broadcasted_iota(jnp.int32, (rows, TILE), 0)
        query = low + lax.broadcasted_iota(jnp.int32, (rows, TILE), 1)
        seen = key <= query
        for p in range(starts_ref.shape[0]):
            s = starts_ref[p]
            seen = seen | (
                (key >= s) & (key < s + PIECE) & (query >= s) & (query < s + PIECE)
            )
        bias_ref[i, :rows, :] = jnp.where(seen, 0.0, -1e30)


def mask_bias(starts, length):
    shape = (length // TILE, 2 * TILE, TILE)
    return pl.pallas_call(
        bias_kernel,
        in_specs=[pl.BlockSpec(memory_space=pltpu.SMEM)],
        out_specs=pl.BlockSpec(memory_space=pltpu.VMEM),
        out_shape=jax.ShapeDtypeStruct(shape, F32),
        compiler_params=params(16),
        name="mask_bias",
    )(starts)


def spans(i, length):
    low = i * TILE
    high = min(low + 2 * TILE, length)
    return ((0, low), (low, high)) if low > 0 else ((low, high),)


def scores(key_rows, query, bias, i, span):
    s = dot(key_rows[span[0] : span[1]], query, 1, 0)
    return s if span[0] < i * TILE else s + bias[i, : span[1] - span[0], :]


def attend_kernel(bias, x_ref, c_ref, l_ref, key_rows):
    length = x_ref.shape[2]
    key_rows[...] = x_ref[1].T

    def score(i, _):
        query = x_ref[0, :, pl.ds(i * TILE, TILE)] * jnp.asarray(HEAD**-0.5, BF16)
        return [(span, scores(key_rows, query, bias, i, span)) for span in spans(i, length)]

    def weigh(i, parts):
        here = pl.ds(i * TILE, TILE)
        top = functools.reduce(
            jnp.maximum, [jnp.max(s, axis=0, keepdims=True) for _, s in parts]
        )
        total, acc = 0.0, 0.0
        for span, s in parts:
            p = jnp.exp(s - top)
            total = total + jnp.sum(p, axis=0, keepdims=True)
            acc = acc + dot(x_ref[2, :, span[0] : span[1]], p.astype(BF16), 1, 0)
        c_ref[:, here] = (acc / total).astype(BF16)
        l_ref[0, :, here] = top + jnp.log(total)

    in_turns((score, weigh), range(length // TILE))


def attend(bias, qkv, first, count):
    length = qkv.shape[2]
    return pl.pallas_call(
        attend_kernel,
        grid=(count,),
        in_specs=[
            pl.BlockSpec(bias.shape, lambda h: (0, 0, 0)),
            pl.BlockSpec((3, HEAD, length), lambda h: (0, h + first, 0)),
        ],
        out_specs=[
            pl.BlockSpec((HEAD, length), lambda h: (h, 0)),
            pl.BlockSpec((1, 1, length), lambda h: (h, 0, 0)),
        ],
        scratch_shapes=[pltpu.VMEM((length, HEAD), BF16)],
        out_shape=[
            jax.ShapeDtypeStruct((count * HEAD, length), BF16),
            jax.ShapeDtypeStruct((count, 1, length), F32),
        ],
        compiler_params=params(24),
        cost_estimate=cost(4e9 * count, count * length * HEAD * 8),
        name="attend",
    )(bias, qkv)


def attend_back_kernel(
    shared, rank_ref, bias, x_ref, mine_ref, got_ref, l_ref, old_ref, g_ref,
    key_rows, value_rows, query_rows, grad_rows, grad, key_sum, value_sum,
):
    length = x_ref.shape[2]
    share = length // 2
    scale = jnp.asarray(HEAD**-0.5, BF16)
    first = rank_ref[0] == 0
    mine, got = mine_ref[...], got_ref[...]
    grad[:, :share] = jnp.where(first, mine, got)
    grad[:, share:] = jnp.where(first, got, mine)
    key_rows[...] = x_ref[1].T
    value_rows[...] = x_ref[2].T
    grad_rows[...] = grad[...].T
    query_rows[...] = (x_ref[0] * scale).T
    tiles = length // TILE

    def score(i, _):
        here = pl.ds(i * TILE, TILE)
        query, out = x_ref[0, :, here] * scale, grad[:, here]
        return [
            (span, scores(key_rows, query, bias, i, span), dot(value_rows[span[0] : span[1]], out, 1, 0))
            for span in spans(i, length)
        ]

    def weigh(i, parts):
        lse = l_ref[0, :, pl.ds(i * TILE, TILE)]
        weights = [jnp.exp(s - lse) for _, s, _ in parts]
        centre = functools.reduce(
            jnp.add, [jnp.sum(p * g, axis=0, keepdims=True) for p, (_, _, g) in zip(weights, parts)]
        )
        return [
            (span, p.astype(BF16), (p * (g - centre)).astype(BF16))
            for p, (span, _, g) in zip(weights, parts)
        ]

    def gather(i, parts):
        here = pl.ds(i * TILE, TILE)
        dq = 0.0
        for (low, high), p, gs in parts:
            dq = dq + dot(x_ref[1, :, low:high], gs, 1, 0)
            dk, dv = dot(gs, query_rows[here], 1, 0), dot(p, grad_rows[here], 1, 0)
            if i == tiles - 1:
                key_sum[low:high], value_sum[low:high] = dk, dv
            else:
                key_sum[low:high] += dk
                value_sum[low:high] += dv
        g_ref[0, :, here] = (dq * HEAD**-0.5).astype(BF16)

    in_turns((score, weigh, gather), list(reversed(range(tiles))))
    g_ref[1] = key_sum[...].T.astype(BF16)
    g_ref[2] = value_sum[...].T.astype(BF16)
    if shared:
        @pl.when(pl.program_id(0) == pl.num_programs(0) - 1)
        def _():
            g_ref[:, HEAD // 2 :, :] = jnp.zeros((3, HEAD // 2, length), BF16)


def attend_back(bias, rank, qkv, mine, got, lse, first, count, shared, old=None):
    length = qkv.shape[2]
    rows = pltpu.VMEM((length, HEAD), BF16)
    sums = pltpu.VMEM((length, HEAD), F32)
    heads = pl.BlockSpec((3, HEAD, length), lambda h, r: (0, h + first, 0))
    half = pl.BlockSpec((HEAD, length // 2), lambda h, r: (h + first, 0))
    alias = {}
    if old is not None:
        alias = {6: 0}
    else:
        old = jnp.zeros((8, 128), BF16)
    return pl.pallas_call(
        functools.partial(attend_back_kernel, shared),
        grid_spec=pltpu.PrefetchScalarGridSpec(
            num_scalar_prefetch=1,
            grid=(count,),
            in_specs=[
                pl.BlockSpec(bias.shape, lambda h, r: (0, 0, 0)),
                heads,
                half,
                half,
                pl.BlockSpec((1, 1, length), lambda h, r: (h + first, 0, 0)),
                pl.BlockSpec(memory_space=pl.ANY),
            ],
            out_specs=[heads],
            scratch_shapes=[rows] * 4
            + [pltpu.VMEM((HEAD, length), BF16)]
            + [sums] * 2,
        ),
        out_shape=[jax.ShapeDtypeStruct(qkv.shape, BF16)],
        input_output_aliases=alias,
        compiler_params=params(34),
        cost_estimate=cost(6.8e9 * count, count * length * HEAD * 14),
        name="attend_back",
    )(rank, bias, qkv, mine, got, lse, old)[0]


def norm_rows(x):
    x = x - jnp.mean(x, axis=0, keepdims=True)
    inv = lax.rsqrt(jnp.mean(x * x, axis=0, keepdims=True) + EPSILON)
    return x * inv, inv


def own_first(rank, a):
    half = a.shape[0] // 2
    return jnp.where(rank == 0, a, jnp.concatenate((a[half:], a[:half]), 0))


def half_lanes(columns):
    return -(-columns // (2 * LANES)) * LANES


def turn_weights(core, mine, got, turned):
    a, b = unit(core, mine, got)
    count = a.shape[1]
    turned[:count] = a.T
    turned[count:] = b.T[2 * count - turned.shape[0] :]


def norm_qkv_kernel(core_ref, xo_ref, xt_ref, m_ref, g_ref, v_ref, b_ref, h_ref, q_ref, turned):
    @pl.when(first_step())
    def _():
        turn_weights(core_ref[0], m_ref[...], g_ref[...], turned)

    x = jnp.concatenate((xo_ref[...], xt_ref[...]), 0).astype(F32)
    h = (norm_rows(x)[0] * v_ref[:, 0:1] + v_ref[:, 1:2]).astype(BF16)
    h_ref[...] = h
    q_ref[...] = (dot(turned[...], h, 1, 0) + b_ref[...]).astype(BF16)


def norm_qkv(core, x_own, x_other, mine, got, vectors, bias):
    own, length = x_own.shape
    depth = 2 * own
    rows = bias.shape[0]
    column = lambda n: pl.BlockSpec((n, TILE), lambda i, s: (0, i))
    whole = lambda a: pl.BlockSpec(a.shape, lambda i, s: (0, 0))
    return pl.pallas_call(
        norm_qkv_kernel,
        grid_spec=pltpu.PrefetchScalarGridSpec(
            num_scalar_prefetch=1,
            grid=(length // TILE,),
            in_specs=[column(own)] * 2 + [whole(a) for a in (mine, got, vectors, bias)],
            out_specs=[column(depth), column(rows)],
            scratch_shapes=[pltpu.VMEM((rows, depth), BF16)],
        ),
        out_shape=[jax.ShapeDtypeStruct((n, length), BF16) for n in (depth, rows)],
        compiler_params=params(24),
        cost_estimate=cost(2 * depth * rows * length, depth * length * 6),
        name="norm_qkv",
    )(core, x_own, x_other, mine, got, vectors, bias)


def qkv_kernel(core_ref, h_ref, m_ref, g_ref, b_ref, q_ref, turned):
    @pl.when(first_step())
    def _():
        turn_weights(core_ref[0], m_ref[...], g_ref[...], turned)

    q_ref[...] = (dot(turned[...], h_ref[...], 1, 0) + b_ref[...]).astype(BF16)


def qkv_of(core, h_one, mine, got, bias):
    depth, length = h_one.shape
    rows = bias.shape[0]
    column = lambda n: pl.BlockSpec((n, TILE), lambda i, s: (0, i))
    whole = lambda a: pl.BlockSpec(a.shape, lambda i, s: (0, 0))
    return pl.pallas_call(
        qkv_kernel,
        grid_spec=pltpu.PrefetchScalarGridSpec(
            num_scalar_prefetch=1,
            grid=(length // TILE,),
            in_specs=[column(depth)] + [whole(a) for a in (mine, got, bias)],
            out_specs=column(rows),
            scratch_shapes=[pltpu.VMEM((rows, depth), BF16)],
        ),
        out_shape=jax.ShapeDtypeStruct((rows, length), BF16),
        compiler_params=params(24),
        cost_estimate=cost(2 * depth * rows * length, depth * length * 4),
        name="qkv",
    )(core, h_one, mine, got, bias)


def project_kernel(
    spot_ref, xo_ref, xt_ref, a_ref, b_ref, ga_ref, gb_ref, c_ref, m_ref, g_ref, v_ref,
    p_ref, h_ref, c_out, turned,
):
    @pl.when(first_step())
    def _():
        own = xo_ref.shape[0]
        parts = [own_first(spot_ref[0], w[:, :own]) for w in (m_ref, g_ref)]
        turn_weights(spot_ref[1], *parts, turned)

    rank = spot_ref[0]
    own = xo_ref.shape[0]
    a, b, half = a_ref.shape[0], b_ref.shape[0], HEAD // 2
    c_out[rows_at(half * rank, a)] = a_ref[...]
    c_out[rows_at(half * rank + a, b)] = b_ref[...]
    c_out[rows_at((a + b) * (1 - rank), half)] = c_ref[:half]
    c_out[rows_at(own + (a + b) * rank, half)] = c_ref[half:]
    c_out[rows_at(own + half * (1 - rank), a)] = ga_ref[...]
    c_out[rows_at(own + half * (1 - rank) + a, b)] = gb_ref[...]
    low = (dot(turned[...], c_out[...], 1, 0) + v_ref[:, 0:1]).astype(BF16)
    p_ref[...] = low
    mid = jnp.concatenate((xo_ref[...], xt_ref[...]), 0).astype(F32) + low.astype(F32)
    h_ref[...] = (norm_rows(mid)[0] * v_ref[:, 1:2] + v_ref[:, 2:3]).astype(BF16)


def out_columns(depth):
    return pl.BlockSpec((depth, -(-depth // (2 * LANES)) * LANES), lambda i, s: (0, 0))


def project(spot, x_own, x_other, pieces, mine, got, vectors):
    own, length = x_own.shape
    depth = 2 * own
    column = lambda rows: pl.BlockSpec((rows, TILE), lambda i, s: (0, i))
    whole = lambda a: pl.BlockSpec(a.shape, lambda i, s: (0, 0))
    return pl.pallas_call(
        project_kernel,
        grid_spec=pltpu.PrefetchScalarGridSpec(
            num_scalar_prefetch=1,
            grid=(length // TILE,),
            in_specs=[column(own)] * 2
            + [column(p.shape[0]) for p in pieces]
            + [out_columns(depth)] * 2
            + [whole(vectors)],
            out_specs=[column(depth)] * 3,
            scratch_shapes=[pltpu.VMEM((depth, depth), BF16)],
        ),
        out_shape=[jax.ShapeDtypeStruct((depth, length), BF16)] * 3,
        compiler_params=params(28),
        cost_estimate=cost(2 * depth * depth * length, depth * length * 10),
        name="project",
    )(spot, x_own, x_other, *pieces, mine, got, vectors)


def feed_kernel(
    spot_ref, h_ref, go_ref, gt_ref, pm_ref, pg_ref, qm_ref, qg_ref, bias_ref, *rest
):
    mid_ref, own_ref, other_ref, gh_ref, gb_ref, gs_ref, up, down, sums, sems = rest[-10:]
    split = up.shape[1] - qm_ref.shape[1]
    lead = pm_ref.shape[1] - split
    hidden = up.shape[1]

    @pl.when(pl.program_id(0) == 0)
    def _():
        half = up.shape[0] // 2

        def copies(up_p, up_q, down_p, down_q):
            made = []
            for i, (first, second, whole) in enumerate(((up_p, up_q, up), (down_p, down_q, down))):
                for j in range(2):
                    rows = pl.ds(half * j, half)
                    to = rows_at(half * (j ^ spot_ref[2]), half)
                    at = 4 * i + 2 * j
                    made += [
                        pltpu.make_async_copy(
                            first.at[rows, lead:], whole.at[to, :split], sems.at[at]
                        ),
                        pltpu.make_async_copy(
                            second.at[rows, :], whole.at[to, split:], sems.at[at + 1]
                        ),
                    ]
            return made

        def bring(these):
            for c in these:
                c.start()
            for c in these:
                c.wait()

        @pl.when(spot_ref[1] == 0)
        def _():
            bring(copies(pm_ref, qm_ref, pg_ref, qg_ref))

        @pl.when(spot_ref[1] == 1)
        def _():
            bring(copies(pg_ref, qg_ref, pm_ref, qm_ref))

        gb_ref[...] = jnp.zeros_like(gb_ref)
        sums[...] = jnp.zeros_like(sums)

    sums[...] += lane_sums(go_ref[...].astype(F32))

    @pl.when(last_step())
    def _():
        gs_ref[...] = row_sums(sums[...])

    root = (2 / jnp.pi) ** 0.5
    h = h_ref[...]
    g = jnp.concatenate((go_ref[...], gt_ref[...]), 0)
    for span in (slice(0, split), slice(split, hidden)):
        u = dot(h, up[:, span], 0, 0) + bias_ref[:, span]
        grad_act = dot(g, down[:, span], 0, 0)
        square = u * u
        t = jnp.tanh(u * (root + (root * 0.044715) * square))
        half = 0.5 + 0.5 * t
        mid_ref[0, :, span] = (u * half).astype(BF16)
        slope = half + (0.5 * u) * (1 - t * t) * (root + (3 * root * 0.044715) * square)
        gup = (grad_act * slope).astype(BF16)
        mid_ref[1, :, span] = gup
        gb_ref[:, span] += jnp.sum(gup.astype(F32), axis=0, keepdims=True)
    gh_ref[...] = dot(up[...], mid_ref[1], 1, 1).astype(BF16)
    out = dot(down[...], mid_ref[0], 1, 1).astype(BF16)
    n = own_ref.shape[0]
    own_ref[...], other_ref[...] = out[:n], out[n:]


def feed(spot, count, h_two, g_own, g_other, weights, bias_up, tile, old):
    depth, length = h_two.shape
    own = g_own.shape[0]
    hidden = bias_up.shape[1]
    column = lambda rows: pl.BlockSpec((rows, tile), lambda i, s: (0, s[0] + i))
    anywhere = pl.BlockSpec(memory_space=pl.ANY)
    vector = pl.BlockSpec((1, hidden), lambda i, s: (0, 0))
    local = lambda rows: pl.BlockSpec((rows, tile), lambda i, s: (0, i))
    aliases = {} if old is None else {9: 0}
    return pl.pallas_call(
        feed_kernel,
        grid_spec=pltpu.PrefetchScalarGridSpec(
            num_scalar_prefetch=1,
            grid=(count,),
            in_specs=[column(depth), column(own), column(own)]
            + [anywhere] * 4
            + [vector]
            + [anywhere] * len(aliases),
            out_specs=[
                pl.BlockSpec((2, tile, hidden), lambda i, s: (0, s[0] + i, 0)),
                local(own),
                local(own),
                local(depth),
                vector,
                pl.BlockSpec((1, own), lambda i, s: (0, 0)),
            ],
            scratch_shapes=[
                pltpu.VMEM((depth, hidden), BF16),
                pltpu.VMEM((depth, hidden), BF16),
                pltpu.VMEM((own, LANES), F32),
                pltpu.SemaphoreType.DMA((8,)),
            ],
        ),
        out_shape=[
            jax.ShapeDtypeStruct((2, length, hidden), BF16),
            *(jax.ShapeDtypeStruct((n, count * tile), BF16) for n in (own, own, depth)),
            jax.ShapeDtypeStruct((1, hidden), F32),
            jax.ShapeDtypeStruct((1, own), F32),
        ],
        input_output_aliases=aliases,
        compiler_params=params(50),
        cost_estimate=cost(8 * depth * count * tile * hidden, 12 * depth * hidden),
        name="feed",
    )(spot, h_two, g_own, g_other, *weights, bias_up, *([] if old is None else [old]))


def weight_grad_kernel(which_ref, h_ref, go_ref, gt_ref, m_ref, *rest):
    half = pl.program_id(0) < pl.num_programs(0) // 2
    g = jnp.where(half, go_ref[...], gt_ref[...])
    rows = jnp.where(which_ref[0] == 0, g, h_ref[...])
    if len(rest) == 2:
        p_ref, q_ref = rest
        split = p_ref.shape[1]
        p_ref[...] = dot(rows, m_ref[0, :, :split], 1, 0).astype(BF16)
        q_ref[...] = dot(rows, m_ref[0, :, split:], 1, 0).astype(BF16)
        return
    pg_ref, qg_ref, pk_ref, pa_ref, qk_ref, qa_ref = rest
    split = pg_ref.shape[1]
    p = (dot(rows, m_ref[0, :, :split], 1, 0) + pg_ref[...].astype(F32)).astype(BF16)
    q = (dot(rows, m_ref[0, :, split:], 1, 0) + qg_ref[...].astype(F32)).astype(BF16)
    n = p.shape[0] // 4
    low = jnp.concatenate((p[:n], p[2 * n : 3 * n]), 0)
    high = jnp.concatenate((p[n : 2 * n], p[3 * n :]), 0)
    pk_ref[...], pa_ref[...] = unit(which_ref[1], low, high)
    qk_ref[...], qa_ref[...] = unit(which_ref[2], q[: 2 * n], q[2 * n :])


def weight_grad(which, h_two, g_own, g_other, middle, split, got=None):
    depth, length = h_two.shape
    hidden = middle.shape[2]
    steps = 2
    rows = depth // steps
    parts = (split, hidden - split)
    blocks = [pl.BlockSpec((rows, n), lambda i, s: (i, 0)) for n in parts]
    in_specs = [
        pl.BlockSpec((rows, length), lambda i, s: (i, 0)),
        pl.BlockSpec((rows, length), lambda i, s: (0, 0)),
        pl.BlockSpec((rows, length), lambda i, s: (0, 0)),
        pl.BlockSpec((1, length, hidden), lambda i, s: (s[0], 0, 0)),
    ]
    out_specs, shapes = blocks, [jax.ShapeDtypeStruct((depth, n), BF16) for n in parts]
    if got is not None:
        in_specs += blocks
        out_specs = [pl.BlockSpec((rows // 2, n), lambda i, s: (i, 0)) for n in parts for _ in range(2)]
        shapes = [jax.ShapeDtypeStruct((depth // 2, n), BF16) for n in parts for _ in range(2)]
    return pl.pallas_call(
        weight_grad_kernel,
        grid_spec=pltpu.PrefetchScalarGridSpec(
            num_scalar_prefetch=1, grid=(steps,), in_specs=in_specs, out_specs=out_specs
        ),
        out_shape=shapes,
        compiler_params=params(44),
        cost_estimate=cost(2 * depth * length * hidden, 2 * (2 * depth + hidden) * length),
        name="weight_grad",
    )(which, h_two, g_own, g_other, middle, *(got or ()))


def mid_back_kernel(
    spot_ref, xo_ref, xt_ref, p_ref, go_ref, gt_ref, keep_ref, got_ref, m_ref, g_ref, v_ref,
    gp_ref, gq_ref, ma_ref, mb_ref, sa_ref, sb_ref, n_ref, w_own, w_other, gc, sums,
):
    @pl.when(first_step())
    def _():
        n = w_own.shape[1]
        parts = [own_first(spot_ref[2], w[:, :n]) for w in (m_ref, g_ref)]
        w_own[...], w_other[...] = unit(spot_ref[1], *parts)
        sums[...] = jnp.zeros_like(sums)

    own = xo_ref.shape[0]
    rank = spot_ref[2]
    keep, got = keep_ref[...].astype(F32), got_ref[...].astype(F32)
    gh = keep + jnp.concatenate((got[own:], got[:own]), 0)
    mid = jnp.concatenate((xo_ref[...], xt_ref[...]), 0).astype(F32) + p_ref[...].astype(F32)
    hat, inv = norm_rows(mid)
    e = gh * v_ref[:, 1:2]
    grad = jnp.concatenate((go_ref[...], gt_ref[...]), 0).astype(F32) + inv * (
        e - jnp.mean(e, axis=0, keepdims=True) - hat * jnp.mean(e * hat, axis=0, keepdims=True)
    )
    gp = grad.astype(BF16)
    gp_ref[...], gq_ref[...] = gp[:own], gp[own:]
    gc[...] = (dot(w_own[...], gp[:own], 1, 0) + dot(w_other[...], gp[own:], 1, 0)).astype(BF16)
    half = HEAD // 2
    a, b = ma_ref.shape[0], mb_ref.shape[0] - HEAD
    near, away = half * rank, own + half * (1 - rank)
    own_half = gc[rows_at((a + b) * (1 - rank), half)]
    other_half = gc[rows_at(own + (a + b) * rank, half)]
    ma_ref[...] = gc[rows_at(near, a)]
    mb_ref[:b] = gc[rows_at(near + a, b)]
    mb_ref[b : b + half] = own_half
    mb_ref[b + half :] = other_half
    sa_ref[...] = gc[rows_at(away, a)]
    sb_ref[:b] = gc[rows_at(away + a, b)]
    sb_ref[b : b + half] = other_half
    sb_ref[b + half :] = own_half
    sums[...] += jnp.concatenate(
        (lane_sums(gh * hat), lane_sums(gh), lane_sums(gp.astype(F32))), 1
    )

    @pl.when(last_step())
    def _():
        n_ref[...] = row_sums(sums[...])


def mid_back(spot, x_own, x_other, projected, g_own, g_other, keep, got, mine, got_w, vectors, rows_a, rows_b):
    own, length = x_own.shape
    depth = 2 * own
    share = length // 2
    column = lambda rows: pl.BlockSpec((rows, TILE), lambda i, s: (0, s[0] + i))
    local = lambda rows: pl.BlockSpec((rows, TILE), lambda i, s: (0, i))
    whole = lambda a: pl.BlockSpec(a.shape, lambda i, s: (0, 0))
    out = lambda rows: jax.ShapeDtypeStruct((rows, share), BF16)
    sizes = (own, own, rows_a, rows_b, rows_a, rows_b)
    return pl.pallas_call(
        mid_back_kernel,
        grid_spec=pltpu.PrefetchScalarGridSpec(
            num_scalar_prefetch=1,
            grid=(share // TILE,),
            in_specs=[column(own), column(own), column(depth), column(own), column(own)]
            + [local(depth)] * 2
            + [out_columns(depth)] * 2
            + [whole(vectors)],
            out_specs=[local(r) for r in sizes] + [pl.BlockSpec((3, depth), lambda i, s: (0, 0))],
            scratch_shapes=[pltpu.VMEM((depth, own), BF16)] * 2
            + [pltpu.VMEM((depth, TILE), BF16), pltpu.VMEM((depth, 3 * LANES), F32)],
        ),
        out_shape=[out(r) for r in sizes] + [jax.ShapeDtypeStruct((3, depth), F32)],
        compiler_params=params(60),
        cost_estimate=cost(2 * depth * depth * share, depth * share * 16),
        name="mid_back",
    )(spot, x_own, x_other, projected, g_own, g_other, keep, got, mine, got_w, vectors)


def half_lanes(columns):
    return -(-columns // (2 * LANES)) * LANES


def grads_kernel(place_ref, h_ref, g_ref, send_ref, keep_ref):
    cols = send_ref.shape[1]
    low = dot(h_ref[...], g_ref[:cols], 1, 1).astype(BF16)
    high = dot(h_ref[...], g_ref[g_ref.shape[0] - cols :], 1, 1).astype(BF16)
    keep_ref[...], send_ref[...] = unit(place_ref[1], low, high)


def grads_out_kernel(place_ref, h_ref, c_ref, g_ref, pm_ref, pg_ref, send_ref, keep_ref, gp):
    @pl.when(first_step())
    def _():
        share = pm_ref.shape[1]
        gp[:, :share], gp[:, share:] = unit(place_ref[0], pm_ref[...], pg_ref[...])

    out = half_lanes(gp.shape[0])
    cols = send_ref.shape[1] - out
    for lhs, rhs, n, to in (
        (h_ref, g_ref, cols, slice(0, cols)),
        (c_ref, gp, out, slice(cols, cols + out)),
    ):
        low = dot(lhs[...], rhs[:n], 1, 1).astype(BF16)
        high = dot(lhs[...], rhs[rhs.shape[0] - n :], 1, 1).astype(BF16)
        keep_ref[:, to], send_ref[:, to] = unit(place_ref[1], low, high)


def column_grads(places, cols, h_one, grad, context=None, gp=None, gp_got=None):
    depth, length = h_one.shape
    kernel, total, scratch = grads_kernel, cols, []
    part = pl.BlockSpec((depth // 2, length), lambda i, s: (i, 0))
    whole = lambda a: pl.BlockSpec(a.shape, lambda i, s: (0, 0))
    args, specs = [h_one, grad], [part, whole(grad)]
    if context is not None:
        kernel, total = grads_out_kernel, cols + half_lanes(gp.shape[0])
        args = [h_one, context, grad, gp, gp_got]
        specs = [part, part] + [whole(a) for a in args[2:]]
        scratch = [pltpu.VMEM((gp.shape[0], length), BF16)]
    return pl.pallas_call(
        kernel,
        grid_spec=pltpu.PrefetchScalarGridSpec(
            num_scalar_prefetch=1,
            grid=(2,),
            in_specs=specs,
            out_specs=[pl.BlockSpec((depth // 2, total), lambda i, s: (i, 0))] * 2,
            scratch_shapes=scratch,
        ),
        out_shape=[jax.ShapeDtypeStruct((depth, total), BF16)] * 2,
        compiler_params=params(32),
        cost_estimate=cost(4 * depth * total * length, 6 * depth * length),
        name="column_grads",
    )(places, *args)


def output_kernel(
    place_ref, x_ref, p_ref, b_ref, low_ref, high_ref, low_got_ref, high_got_ref, o_ref
):
    mine = pl.program_id(0) // (pl.num_programs(0) // 2) == place_ref[0]
    pick = lambda a, b: jnp.where(mine, a[...], b[...]).astype(F32)
    down = pick(high_ref, low_ref) + pick(low_got_ref, high_got_ref)
    o_ref[...] = (
        x_ref[...].astype(F32) + p_ref[...].astype(F32) + (down + b_ref[...])
    ).astype(BF16)


def close_output(places, x_own, projected, bias, low, high, low_got, high_got):
    own, length = x_own.shape
    column = pl.BlockSpec((own, TILE), lambda i, s: (0, i))
    steps = length // 2 // TILE
    half = pl.BlockSpec((own, TILE), lambda i, s: (0, lax.rem(i, steps)))
    return pl.pallas_call(
        output_kernel,
        grid_spec=pltpu.PrefetchScalarGridSpec(
            num_scalar_prefetch=1,
            grid=(2 * steps,),
            in_specs=[column] * 2 + [pl.BlockSpec((own, 1), lambda i, s: (0, 0))] + [half] * 4,
            out_specs=column,
        ),
        out_shape=jax.ShapeDtypeStruct((own, length), BF16),
        compiler_params=params(24),
        cost_estimate=cost(0, 0),
        name="close_output",
    )(places, x_own, projected, bias, low, high, low_got, high_got)


def tokens_kernel(half, place_ref, x_ref, gp_ref, gq_ref, keep_ref, got_ref, s_ref, v_ref, old_ref, o_ref):
    own = x_ref.shape[0]
    gp = jnp.where(place_ref[0] == half, gp_ref[...], gq_ref[...]).astype(F32)
    e = (keep_ref[...].astype(F32) + got_ref[:own].astype(F32)) * v_ref[:own, 0:1]
    others = got_ref[own:].astype(F32)
    mean, inv = s_ref[2:3], s_ref[3:4]
    total = (s_ref[:2] + (others[:2] + others[2:4])) * (0.5 / own)
    hat = (x_ref[...].astype(F32) - mean) * inv
    o_ref[...] = gp + inv * (e - total[:1] - hat * total[1:])


def close_tokens(places, half, x_own, gp, gp_got, keep, got, stats, vectors, old):
    own, length = x_own.shape
    steps = length // 2 // TILE
    column = pl.BlockSpec((own, TILE), lambda i, s: (0, steps * half + i))
    local = lambda rows: pl.BlockSpec((rows, TILE), lambda i, s: (0, i))
    alias = {8: 0} if half else {}
    return pl.pallas_call(
        functools.partial(tokens_kernel, half),
        grid_spec=pltpu.PrefetchScalarGridSpec(
            num_scalar_prefetch=1,
            grid=(steps,),
            in_specs=[column]
            + [local(own)] * 3
            + [local(own + SPARE), local(4), pl.BlockSpec(vectors.shape, lambda i, s: (0, 0))]
            + [pl.BlockSpec(memory_space=pl.ANY)],
            out_specs=column,
        ),
        out_shape=jax.ShapeDtypeStruct((own, length), F32),
        input_output_aliases=alias,
        compiler_params=params(24),
        cost_estimate=cost(0, 0),
        name="close_tokens",
    )(places, x_own, gp, gp_got, keep, got, stats, vectors, old)


def qkv_back_kernel(
    core_ref, xo_ref, xt_ref, gb_ref, ga_ref, bm_ref, bg_ref, am_ref, ag_ref, v_ref,
    keep_ref, send_ref, s_ref, n_ref, db_ref, da_ref, b_low, b_high, a_low, a_high, n_sum, b_sum, a_sum,
):
    @pl.when(first_step())
    def _():
        b_low[...], b_high[...] = unit(core_ref[0], bm_ref[...], bg_ref[...])
        a_low[...], a_high[...] = unit(core_ref[0], am_ref[...], ag_ref[...])
        for r in (n_sum, b_sum, a_sum):
            r[...] = jnp.zeros_like(r)

    own = xo_ref.shape[0]
    gb, ga = gb_ref[...], ga_ref[...]
    cols_b, cols_a = b_low.shape[1], a_low.shape[1]
    twice = 2 * cols_b - gb.shape[0]
    rest = jnp.concatenate((jnp.zeros((twice, gb.shape[1]), BF16), gb[cols_b:]), 0)
    gh = (dot(b_low[...], gb[:cols_b], 1, 0) + dot(b_high[...], rest, 1, 0)) + (
        dot(a_low[...], ga[:cols_a], 1, 0) + dot(a_high[...], ga[cols_a:], 1, 0)
    )
    keep_ref[...] = gh[:own].astype(BF16)
    send_ref[:own] = gh[own:].astype(BF16)
    x = jnp.concatenate((xo_ref[...], xt_ref[...]), 0).astype(F32)
    hat, inv = norm_rows(x)
    both = gh * hat
    gain = v_ref[:, 0:1]
    mine = jnp.concatenate(
        (jnp.sum(gh * gain, axis=0, keepdims=True), jnp.sum(both * gain, axis=0, keepdims=True)), 0
    )
    s_ref[...] = jnp.concatenate((mine, jnp.mean(x, axis=0, keepdims=True), inv), 0)
    high = mine.astype(BF16).astype(F32)
    parts = jnp.concatenate((high, mine - high, jnp.zeros((SPARE - 4, mine.shape[1]), F32)), 0)
    send_ref[own:] = parts.astype(BF16)
    n_sum[...] += jnp.concatenate((lane_sums(both), lane_sums(gh)), 1)
    b_sum[...] += lane_sums(gb.astype(F32))
    a_sum[...] += lane_sums(ga.astype(F32))

    @pl.when(last_step())
    def _():
        n_ref[...] = row_sums(n_sum[...])
        db_ref[...] = row_sums(b_sum[...])
        da_ref[...] = row_sums(a_sum[...])


def qkv_back(core, x_own, x_other, grad_b, grad_a, w_b, w_a, vectors, first, count):
    own = x_own.shape[0]
    depth = 2 * own
    column = lambda rows: pl.BlockSpec((rows, TILE), lambda i, s: (0, first + i))
    local = lambda rows: pl.BlockSpec((rows, TILE), lambda i, s: (0, i))
    whole = lambda a: pl.BlockSpec(a.shape, lambda i, s: (0, 0))
    span = count * TILE
    out = jax.ShapeDtypeStruct
    rows = (depth, grad_b.shape[0], grad_a.shape[0])
    flat = [out((n, r), F32) for n, r in zip((2, 1, 1), rows)]
    return pl.pallas_call(
        qkv_back_kernel,
        grid_spec=pltpu.PrefetchScalarGridSpec(
            num_scalar_prefetch=1,
            grid=(count,),
            in_specs=[column(own)] * 2
            + [column(grad_b.shape[0]), column(grad_a.shape[0])]
            + [whole(a) for a in (*w_b, *w_a, vectors)],
            out_specs=[local(own), local(own + SPARE), local(4)] + [whole(t) for t in flat],
            scratch_shapes=[pltpu.VMEM(w.shape, BF16) for w in (*w_b, *w_a)]
            + [pltpu.VMEM((r, n * LANES), F32) for n, r in zip((2, 1, 1), rows)],
        ),
        out_shape=[out((own, span), BF16), out((own + SPARE, span), BF16), out((4, span), F32)]
        + flat,
        compiler_params=params(36),
        cost_estimate=cost(2 * depth * span * (rows[1] + rows[2]), depth * span * 12),
        name="qkv_back",
    )(core, x_own, x_other, grad_b, grad_a, *w_b, *w_a, vectors)


def by_bit(bit, a, b):
    return jnp.where(lax.axis_index("wide") & bit == 0, a, b)


def flip(a, bit):
    size = lax.axis_size("wide")
    return lax.ppermute(a, "wide", [(i, i ^ bit) for i in range(size)])


def join_kernel(place_ref, kept_ref, got_ref, out_ref):
    first = place_ref[0] == 0
    if out_ref.ndim == 2:
        half = kept_ref.shape[0]
        out_ref[:half] = jnp.where(first, kept_ref[...], got_ref[...])
        out_ref[half:] = jnp.where(first, got_ref[...], kept_ref[...])
    else:
        here = pl.program_id(1) == place_ref[0]
        out_ref[...] = jnp.where(here, kept_ref[...], got_ref[...])


def join(kept, got, place, axis):
    rows, cols = kept.shape[-2:]
    call = dict(compiler_params=params(16), cost_estimate=cost(0, 0), name="join")
    place = place.astype(jnp.int32)[None]
    if axis is None:
        spec = lambda n: pl.BlockSpec((n, cols), lambda i, s: (0, 0))
        grid_spec = pltpu.PrefetchScalarGridSpec(
            num_scalar_prefetch=1, grid=(1,), in_specs=[spec(rows)] * 2, out_specs=spec(2 * rows)
        )
        shape = jax.ShapeDtypeStruct((2 * rows, cols), kept.dtype)
        return pl.pallas_call(join_kernel, grid_spec=grid_spec, out_shape=shape, **call)(place, kept, got)
    outer, inner = math.prod(kept.shape[:axis]), math.prod(kept.shape[axis:-1])
    spec = pl.BlockSpec((1, 1, inner, cols), lambda a, j, s: (a, 0, 0, 0))
    grid_spec = pltpu.PrefetchScalarGridSpec(
        num_scalar_prefetch=1,
        grid=(outer, 2),
        in_specs=[spec] * 2,
        out_specs=pl.BlockSpec((1, 1, inner, cols), lambda a, j, s: (a, j, 0, 0)),
    )
    shape = jax.ShapeDtypeStruct((outer, 2, inner, cols), kept.dtype)
    args = [a.reshape(outer, 1, inner, cols) for a in (kept, got)]
    out = pl.pallas_call(join_kernel, grid_spec=grid_spec, out_shape=shape, **call)(place, *args)
    return out.reshape(kept.shape[:axis] + (2,) + kept.shape[axis:])


def fold_kernel(index_ref, kept_ref, got_ref, keep_ref, away_ref):
    total = kept_ref[...].astype(F32) + got_ref[...].astype(F32)
    if kept_ref.ndim == 2:
        half = keep_ref.shape[0]
        low, high = total[:half], total[half:]
        first = index_ref[0] == 0
        keep_ref[...], away_ref[...] = jnp.where(first, low, high), jnp.where(first, high, low)
        return
    total = total.astype(BF16).reshape(keep_ref.shape)

    @pl.when(pl.program_id(1) == 0)
    def _():
        keep_ref[...] = total

    @pl.when(pl.program_id(1) == 1)
    def _():
        away_ref[...] = total


def fold(kept, got, index, axis):
    rows, cols = kept.shape[-2:]
    call = dict(compiler_params=params(16), cost_estimate=cost(0, 0), name="fold")
    index = index.astype(jnp.int32)[None]
    if axis is None:
        spec = lambda n: pl.BlockSpec((n, cols), lambda i, s: (0, 0))
        grid_spec = pltpu.PrefetchScalarGridSpec(
            num_scalar_prefetch=1, grid=(1,), in_specs=[spec(rows)] * 2, out_specs=[spec(rows // 2)] * 2
        )
        shape = [jax.ShapeDtypeStruct((rows // 2, cols), F32)] * 2
        return pl.pallas_call(fold_kernel, grid_spec=grid_spec, out_shape=shape, **call)(index, kept, got)
    outer, inner = math.prod(kept.shape[:axis]), math.prod(kept.shape[axis + 1 : -1])
    grid_spec = pltpu.PrefetchScalarGridSpec(
        num_scalar_prefetch=1,
        grid=(outer, 2),
        in_specs=[pl.BlockSpec((1, 1, inner, cols), lambda a, j, s: (a, j ^ s[0], 0, 0))] * 2,
        out_specs=[pl.BlockSpec((1, inner, cols), lambda a, j, s: (a, 0, 0))] * 2,
    )
    shape = [jax.ShapeDtypeStruct((outer, inner, cols), BF16)] * 2
    args = [a.reshape(outer, 2, inner, cols) for a in (kept, got)]
    out = pl.pallas_call(fold_kernel, grid_spec=grid_spec, out_shape=shape, **call)(index, *args)
    return [o.reshape(kept.shape[:axis] + kept.shape[axis + 1 :]) for o in out]


class Gather:
    def __init__(self, a, b, order):
        self.kept = by_bit(1, a, b)
        self.got = flip(by_bit(1, b, a), 1)
        self.order = list(order)
        self.bits = []
        self.last = None

    def merge(self):
        if self.last is None:
            axis, place = None, lax.axis_index("wide") & 1
        else:
            axis = sum(1 for b in self.bits if b > self.last)
            place = (lax.axis_index("wide") & self.last != 0).astype(jnp.int32)
            if self.last == max(self.order + self.bits + [self.last]):
                place = place ^ lax.axis_index("narrow")
            self.bits.append(self.last)
        self.cur = join(self.kept, self.got, place, axis)

    def came(self):
        return self.got

    def come(self, value):
        self.got = value

    def held(self):
        return self.cur

    def hold(self, value):
        self.cur = value

    def send(self):
        self.last = self.order.pop(0) if self.order else 1
        if self.last == 1:
            self.cur = self.cur.reshape(-1, self.cur.shape[-1])
        self.kept, self.got = self.cur, flip(self.cur, self.last)


class Whole:
    def __init__(self, a, b):
        self.kept = by_bit(1, a, b)
        self.got = flip(by_bit(1, b, a), 1)
        self.stage = 0

    def merge(self):
        if self.stage == 0:
            low = lax.axis_index("wide") & 1 == 0
            kept, got = self.kept, self.got
            self.cur = jnp.where(
                low, jnp.concatenate((kept, got), 0), jnp.concatenate((got, kept), 0)
            )

    def came(self):
        return self.got if self.stage == 0 else self.cur

    def come(self, value):
        if self.stage == 0:
            self.got = value
        else:
            self.cur = value

    def held(self):
        return self.cur

    def hold(self, value):
        self.cur = value

    def send(self):
        if self.stage == 0:
            size = lax.axis_size("wide")
            groups = [list(range(c, size, 2)) for c in range(2)]
            self.cur = lax.all_gather(
                self.cur, "wide", axis=0, tiled=True, axis_index_groups=groups
            )
        else:
            self.got = flip(self.cur, 1)
        self.stage += 1


class Scatter:
    def __init__(self, send, order):
        self.got = flip(send, 1)
        self.order = list(order)
        self.axes = sorted(order, reverse=True)
        self.top = self.axes[0]

    def merge(self):
        kept, got = self.kept, self.got
        if self.order:
            if kept.ndim == 2:
                shape = (2,) * len(self.axes) + (-1, kept.shape[-1])
                kept, got = kept.reshape(shape), got.reshape(shape)
            bit = self.order.pop(0)
            axis = self.axes.index(bit)
            self.axes.remove(bit)
            index = (lax.axis_index("wide") & bit != 0).astype(jnp.int32)
            if bit == self.top:
                index = index ^ lax.axis_index("narrow")
        else:
            bit, axis, index = 1, None, lax.axis_index("wide") & 1
        self.bit = bit
        self.keep, self.away = fold(kept, got, index, axis)

    def next_index(self):
        index = (lax.axis_index("wide") & self.order[0] != 0).astype(jnp.int32)
        return index ^ lax.axis_index("narrow") if self.order[0] == self.top else index

    def start(self, other, *halves):
        for m, keep, away in ((self, *halves[:2]), (other, *halves[2:])):
            m.bit = m.order.pop(0)
            m.axes.remove(m.bit)
            shape = (2,) * len(m.axes) + (-1, keep.shape[-1])
            m.keep, m.away = keep.reshape(shape), away.reshape(shape)

    def came(self):
        return self.got

    def come(self, value):
        self.got = value

    def held(self):
        return self.keep, self.away

    def hold(self, value):
        self.keep, self.away = value

    def send(self):
        self.kept, self.got = self.keep, flip(self.away, self.bit)

    def result(self):
        return by_bit(1, self.kept, self.got), by_bit(1, self.got, self.kept)


def meet(values, *moves, wait=()):
    moves = list(moves) + list(wait)
    values, came = lax.optimization_barrier((values, [m.came() for m in moves]))
    for m, c in zip(moves, came):
        m.come(c)
        m.merge()
    values, held = lax.optimization_barrier((values, [m.held() for m in moves]))
    for m, h in zip(moves, held):
        m.hold(h)
        if m not in wait:
            m.send()
    return values


def send_now(values, *moves):
    values, held = lax.optimization_barrier((values, [m.held() for m in moves]))
    for m, h in zip(moves, held):
        m.hold(h)
        m.send()
    return values


def pair_plan(
    tokens,
    piece_starts,
    ln1_gain,
    ln1_bias,
    w_qkv,
    bias_qv,
    w_out,
    bias_out,
    ln2_gain,
    ln2_bias,
    w_up,
    bias_up,
    w_down,
    bias_down,
    cotangent,
):
    rank = lax.axis_index("narrow")
    first = rank == 0
    core = lax.axis_index("wide") & 1
    own, length = tokens.shape
    depth = 2 * own
    whole = own // HEAD * HEAD
    rest = own - whole
    rows_a = whole // 2
    rows_b = whole - rows_a + 2 * rest
    heads_a, heads_b = rows_a // HEAD, rows_b // HEAD
    block = w_out.shape[0]
    hidden = w_up.shape[1]
    tile = length // 4
    part = -(-(hidden + own) // 256) * LANES
    split = hidden - part
    split_back = hidden // 256 * LANES + LANES
    rank_arg = rank.astype(jnp.int32)[None]

    def swap(a):
        return lax.ppermute(a, "narrow", [(0, 1), (1, 0)])

    def heads_first(a):
        return jnp.where(first, a, jnp.concatenate((a[..., rest:], a[..., :rest]), -1))

    def heads_back(a):
        return jnp.where(first, a, jnp.concatenate((a[..., whole:], a[..., :whole]), -1))

    def at_rows(bias):
        return jnp.stack((bias[0], jnp.zeros_like(bias[0]), bias[1])).reshape(-1, 1)

    far, near, side = 8, 4, 2
    inward, outward = (far, near, side), (side, far, near)
    w_heads = heads_first(w_qkv)
    shard_a = w_heads[:, :, :rows_a].reshape(block, -1)
    cols_a = shard_a.shape[1] // 2
    get_a = Gather(shard_a[:, :cols_a], shard_a[:, cols_a:], inward)
    bias_local = heads_first(bias_qv)
    own_vectors = jnp.concatenate(
        (jnp.stack((ln1_gain, ln1_bias, ln2_gain, ln2_bias, bias_out)), bias_local), 0
    )
    half_rows = w_heads[:, :, whole:].reshape(-1, own)
    count = own_vectors.shape[0]
    small_swap = swap(jnp.concatenate((own_vectors, half_rows, w_out), 0))
    other_half = small_swap[count:-block].reshape(block, 3, rest)
    shard_b = jnp.concatenate((w_heads[:, :, rows_a:], other_half), 2).reshape(block, -1)
    cols_b = -(-shard_b.shape[1] // 256) * 128
    skip = shard_b.shape[1] - cols_b
    get_b = Gather(shard_b[:, :cols_b], shard_b[:, skip:], inward)
    pad = jnp.zeros((block, part - split - own), BF16)
    get_p = Whole(
        jnp.concatenate((w_out, pad, w_up[:, :split]), 1),
        jnp.concatenate((small_swap[-block:], pad, w_down.T[:, :split]), 1),
    )
    get_p.merge()
    get_p.send()
    small_swap, x_own, w_heads, w_up_in, w_down_in, g_own = meet(
        (small_swap, tokens, w_heads, w_up, w_down, cotangent), get_a
    )
    x_other = swap(x_own)
    other_vectors = small_swap[:count]
    vectors = jnp.concatenate((own_vectors[:5], other_vectors[:5]), 1).astype(F32).T
    gain_one, shift_one = vectors[:, 0:1], vectors[:, 1:2]
    project_vectors = jnp.stack((vectors[:, 4], vectors[:, 2], vectors[:, 3]), 1)
    w_down_t = w_down_in.T
    get_q = Whole(w_up_in[:, split:], w_down_t[:, split:])
    meet((), get_a, get_b, get_q)
    starts = meet(piece_starts[0], get_a, get_b)
    seen = mask_bias(starts, length)
    seen = meet(seen, get_a, get_b)
    x_other, get_a.got = meet((x_other, get_a.got))

    g_other = swap(after(g_own, x_other))
    bias_f = bias_local.astype(F32)
    bias_a = bias_f[:, :rows_a]
    bias_b = jnp.concatenate((bias_f[:, rows_a:], other_vectors[5:, whole:].astype(F32)), 1)
    core_arg = core[None]
    w_a = (get_a.cur, get_a.got)
    h_one, qkv_a = norm_qkv(core_arg, tokens, x_other, *w_a, vectors, at_rows(bias_a))
    qkv_a = qkv_a.reshape(3, rows_a, length)
    qkv_a, h_one = meet((qkv_a, h_one), get_b)

    context_a, lse_a = attend(seen, qkv_a, 0, heads_a)
    context_a, g_other, h_b, get_b.got = meet((context_a, g_other, h_one, get_b.got), get_p)

    context_a_other = swap(context_a)
    w_b = (get_b.cur, get_b.got)
    qkv_b = qkv_of(core_arg, h_b, *w_b, at_rows(bias_b)).reshape(3, rows_b, length)
    whole_b = heads_b - 1
    context_b, lse_b = attend(seen, qkv_b, 0, whole_b)
    context_b, context_a_other, qkv_c = meet((context_b, context_a_other, qkv_b))

    context_b_other = swap(context_b)
    context_c, lse_c = attend(seen, qkv_c, whole_b, 1)
    lse_b = jnp.concatenate((lse_b, lse_c), 0)
    context_b_other, context_c, get_p.got = meet((context_b_other, context_c, get_p.got), get_q)

    pieces = (context_a, context_b, context_a_other, context_b_other, context_c)
    w_o = (get_p.cur, get_p.got)
    places = jnp.stack((rank, core)).astype(jnp.int32)
    projected, h_two, context = project(places, tokens, x_other, pieces, *w_o, project_vectors)
    projected, h_two, context, get_q.got = meet((projected, h_two, context, get_q.got))

    weights = (get_p.cur, get_p.got, get_q.cur, get_q.got)
    bias_up_f = bias_up.astype(F32)[None]
    steps = length // 2 // TILE

    def spot(at):
        return jnp.stack((at, core, rank)).astype(jnp.int32)

    old, low_own, low_other, gh_send, gb_send, gs_send = feed(
        spot(steps * (1 - rank)), steps, h_two, cotangent, g_other, weights, bias_up_f, TILE, None
    )
    old, gh_send = meet((old, gh_send))
    gh_got = swap(gh_send)
    middle, high_own, high_other, gh_keep, gb_keep, gs_keep = feed(
        spot(steps * rank), steps, h_two, cotangent, g_other, weights, bias_up_f, TILE, old
    )
    grad_bias_up = gb_send + gb_keep
    send_p, send_q = weight_grad(core[None], h_two, cotangent, g_other, middle, split_back)
    gh_got, gh_keep, send_p, send_q, middle, low_other = meet(
        (gh_got, gh_keep, send_p, send_q, middle, low_other)
    )

    put_p = Scatter(send_p, (side, near, far))
    put_q = Scatter(send_q, (near, far, side))
    low_got = swap(low_other)
    gp, gp_away, mine_a, mine_b, send_a, send_b, grad_two = mid_back(
        spot(steps * rank), tokens, x_other, projected, cotangent, g_other, gh_keep,
        gh_got, *w_o, project_vectors, rows_a, rows_b,
    )
    gp, gp_away, mine_a, mine_b, send_a, send_b, middle, put_p.got, put_q.got = meet(
        (gp, gp_away, mine_a, mine_b, send_a, send_b, middle, put_p.got, put_q.got)
    )

    got_b = swap(send_b)
    put_p.start(put_q, *weight_grad(
        jnp.stack((1 - core, put_p.next_index(), put_q.next_index())).astype(jnp.int32),
        h_two, cotangent, g_other, middle, split_back, (put_p.got, put_q.got),
    ))
    got_b, mine_b, send_a, gp_away, low_got = send_now(
        meet((got_b, mine_b, send_a, gp_away, low_got)), put_p, put_q
    )

    got_a = swap(send_a)
    gp_got = swap(gp_away)
    back_b = attend_back(seen, rank_arg, qkv_b, mine_b, got_b, lse_b, 0, heads_b, True)
    back_b, got_a, gp_got, high_other = meet((back_b, got_a, gp_got, high_other), put_p, put_q)

    high_got = swap(high_other)
    grad_b = back_b.reshape(3 * rows_b, length)

    send_b, keep_b = column_grads(places, cols_b, h_one, grad_b, context, gp, gp_got)
    put_b = Scatter(send_b, (side, near, far))
    put_b.kept, mine_a, qkv_a = meet((keep_b, mine_a, qkv_a))

    back_a = attend_back(seen, rank_arg, qkv_a, mine_a, got_a, lse_a, 0, heads_a // 2, False)
    back_a = meet(back_a, put_b)
    back_a = attend_back(
        seen, rank_arg, qkv_a, mine_a, got_a, lse_a, heads_a // 2, heads_a - heads_a // 2, False, back_a
    )
    back_a, high_got = meet((back_a, high_got), put_p, put_q)
    grad_a = back_a.reshape(3 * rows_a, length)

    def back(i):
        return qkv_back(
            core_arg, tokens, x_other, grad_b, grad_a, w_b, w_a, vectors, steps * i, steps
        )

    def vector_parts(sums_0, sums_1):
        def row(a):
            return jnp.pad(a, ((0, 0), (0, depth - a.shape[1])))

        sums = [a + b for a, b in zip(sums_0, sums_1)]
        low = [grad_bias_up[:, :depth], grad_bias_up[:, depth:]]
        return jnp.concatenate(
            (sums[0], grad_two, row(sums[1]), row(sums[2]), row(gs_send + gs_keep), *map(row, low))
        )

    def quad_sum(total):
        return total + flip(total, 1) + flip(total, side) + flip(total, 1 + side)

    send_a, keep_a = column_grads(places, cols_a, h_one, grad_a)
    keep, send, stats, *sums_0 = back(0)
    send_a, keep_a, keep, send, stats, sums_0, grad_a, low_got = meet(
        (send_a, keep_a, keep, send, stats, sums_0, grad_a, low_got), put_b, put_p, put_q
    )
    put_a = Scatter(send_a, (side, near, far))
    put_a.kept = keep_a
    got = swap(send)
    output = close_output(
        places, tokens, projected, bias_down.astype(F32)[:, None], low_own, high_own, low_got, high_got
    )
    output, grad_a = meet((output, grad_a), put_a)
    keep_1, send_1, stats_1, *sums = back(1)
    keep_1, send_1, stats_1, sums, got, sums_0 = meet(
        (keep_1, send_1, stats_1, sums, got, sums_0), put_a, put_b
    )
    got_1 = swap(send_1)
    grad_tokens = close_tokens(
        places, 0, tokens, gp, gp_got, keep, got, stats, vectors, jnp.zeros((8, LANES), F32)
    )
    grad_tokens, sums = meet((grad_tokens, sums), put_a, wait=(put_b,))
    grad_tokens, got_1, total = meet((grad_tokens, got_1, quad_sum(vector_parts(sums_0, sums))), put_a)
    grad_tokens = close_tokens(
        places, 1, tokens, gp, gp_got, keep_1, got_1, stats_1, vectors, grad_tokens
    )
    total = send_now(total, put_b)
    total = total + flip(total, near) + flip(total, far) + flip(total, near + far)
    sum_up_p, sum_down_p = put_p.result()
    sum_up_q, sum_down_q = put_q.result()
    low_b, high_b = put_b.result()
    sum_a = jnp.concatenate(put_a.result(), 1).reshape(block, 3, rows_a)
    out_cols = half_lanes(own)
    sum_out = jnp.concatenate((low_b[:, cols_b:], high_b[:, cols_b + 2 * out_cols - own :]), 1)
    sum_b = jnp.concatenate((low_b[:, :cols_b], high_b[:, cols_b - skip : cols_b]), 1)
    sum_b = sum_b.reshape(block, 3, rows_b)[:, :, : rows_b - rest]
    sum_w_qkv = heads_back(jnp.concatenate((sum_a, sum_b), 2))

    two = total[:5, :own] + swap(total[:5, own:])
    vec = [
        jnp.concatenate(
            (total[6, i * rows_a : (i + 1) * rows_a], total[5, i * rows_b : (i + 1) * rows_b - rest])
        )
        for i in (0, 2)
    ]
    return (
        output,
        grad_tokens,
        two[0],
        two[1],
        sum_w_qkv,
        heads_back(jnp.stack(vec)),
        sum_out,
        two[4],
        two[2],
        two[3],
        jnp.concatenate((sum_up_p, sum_up_q), 1),
        jnp.concatenate((total[8], total[9]))[:hidden],
        jnp.concatenate((sum_down_p, sum_down_q), 1).T,
        total[7, :own],
    )


def solution(mesh):
    in_specs = (
        P("narrow", "wide"),
        P("wide", None),
        P("narrow"),
        P("narrow"),
        P("wide", None, "narrow"),
        P(None, "narrow"),
        P("wide", "narrow"),
        P("narrow"),
        P("narrow"),
        P("narrow"),
        P("wide", "narrow"),
        P("narrow"),
        P("narrow", "wide"),
        P("narrow"),
        P("narrow", "wide"),
    )
    out_specs = (
        P("narrow", "wide"),
        P("narrow", "wide"),
        P("narrow"),
        P("narrow"),
        P("wide", None, "narrow"),
        P(None, "narrow"),
        P("wide", "narrow"),
        P("narrow"),
        P("narrow"),
        P("narrow"),
        P("wide", "narrow"),
        P("narrow"),
        P("narrow", "wide"),
        P("narrow"),
    )
    paired = mesh.shape["narrow"] == 2 and mesh.shape["wide"] == 16
    return jax.shard_map(
        pair_plan if paired else any_mesh, mesh=mesh, in_specs=in_specs, out_specs=out_specs, check_vma=False
    )
```

```python
import functools
import math
from functools import partial

import jax
import jax.numpy as jnp
from jax import lax
from jax.experimental import pallas as pl
from jax.experimental.pallas import tpu as pltpu
from jax.sharding import PartitionSpec as P

HEADS = 17
PIECE = 256


EPSILON = 1e-05


def normalize(row_data, gain_vec, shift_vec):
    centre = jnp.mean(row_data, axis=-1, keepdims=True)
    centred = row_data - centre
    spread = jnp.mean(centred * centred, axis=-1, keepdims=True)
    return centred * lax.rsqrt(spread + EPSILON) * gain_vec + shift_vec


def norm_back(row_data, gain_vec, shift_vec, grad_rows):
    unused, pull_back = jax.vjp(normalize, row_data, gain_vec, shift_vec)
    return pull_back(grad_rows)


def full_rows(partial_rows):
    return lax.psum(partial_rows, "narrow")


def visible_mask(starts, query_pos, key_pos):
    query_in = (query_pos[:, None] >= starts[None, :]) & (
        query_pos[:, None] < starts[None, :] + PIECE
    )
    key_in = (key_pos[:, None] >= starts[None, :]) & (key_pos[:, None] < starts[None, :] + PIECE)
    shared = jnp.any(query_in[:, None, :] & key_in[None, :, :], axis=-1)
    return (key_pos[None, :] <= query_pos[:, None]) | shared


def to_heads(matrix):
    return matrix.reshape(matrix.shape[0], HEADS, matrix.shape[1] // HEADS)


def attention_scores(query_rows, key_full, visible, score_scale):
    raw = (
        jnp.einsum(
            "qhd,khd->hqk",
            to_heads(query_rows),
            to_heads(key_full),
            preferred_element_type=jnp.float32,
        )
        * score_scale
    )
    return jnp.where(visible[None], raw, -1e30)


def any_mesh(
    tokens,
    piece_starts,
    ln1_gain,
    ln1_bias,
    w_qkv,
    bias_qv,
    w_out,
    bias_out,
    ln2_gain,
    ln2_bias,
    w_up,
    bias_up,
    w_down,
    bias_down,
    cotangent,
):
    narrow_size = lax.axis_size("narrow")
    narrow_rank = lax.axis_index("narrow")
    col_width, length = tokens.shape
    full_width = col_width * narrow_size
    queries = length // narrow_size
    score_scale = (full_width // HEADS) ** (-0.5)
    col_start = narrow_rank * col_width
    row_start = narrow_rank * queries

    def own_cols(matrix):
        return lax.dynamic_slice_in_dim(matrix, col_start, col_width, matrix.ndim - 1)

    x_cols, dy_cols, gain_one, shift_one, gain_two, shift_two = (
        lax.all_gather(tokens, "narrow", axis=0, tiled=True),
        lax.all_gather(cotangent, "narrow", axis=0, tiled=True),
        lax.all_gather(ln1_gain, "narrow", axis=0, tiled=True),
        lax.all_gather(ln1_bias, "narrow", axis=0, tiled=True),
        lax.all_gather(ln2_gain, "narrow", axis=0, tiled=True),
        lax.all_gather(ln2_bias, "narrow", axis=0, tiled=True),
    )
    x_rows = x_cols.T
    dy_rows = dy_cols.T
    qkv_cols, out_cols, up_cols, down_rows = (
        lax.all_gather(w_qkv, "wide", axis=0, tiled=True),
        lax.all_gather(w_out, "wide", axis=0, tiled=True),
        lax.all_gather(w_up, "wide", axis=0, tiled=True),
        lax.all_gather(w_down, "wide", axis=1, tiled=True),
    )
    gain_one = gain_one.astype(jnp.float32)
    shift_one = shift_one.astype(jnp.float32)
    gain_two = gain_two.astype(jnp.float32)
    shift_two = shift_two.astype(jnp.float32)
    x_full = x_rows.astype(jnp.float32)
    h_one = normalize(x_full, gain_one, shift_one).astype(jnp.bfloat16)
    mixed = jnp.einsum("td,dcf->tcf", h_one, qkv_cols, preferred_element_type=jnp.float32)
    bias_cols = bias_qv.astype(jnp.float32)
    query_cols = (mixed[:, 0] + bias_cols[0]).astype(jnp.bfloat16)
    key_cols = mixed[:, 1].astype(jnp.bfloat16)
    value_cols = (mixed[:, 2] + bias_cols[1]).astype(jnp.bfloat16)
    query_full, key_full, value_full = (
        lax.all_gather(query_cols, "narrow", axis=1, tiled=True),
        lax.all_gather(key_cols, "narrow", axis=1, tiled=True),
        lax.all_gather(value_cols, "narrow", axis=1, tiled=True),
    )
    query_rows = lax.dynamic_slice_in_dim(query_full, row_start, queries, 0)
    query_pos = row_start + jnp.arange(queries, dtype=jnp.int32)
    key_pos = jnp.arange(length, dtype=jnp.int32)
    visible = visible_mask(piece_starts[0], query_pos, key_pos)
    masked = attention_scores(query_rows, key_full, visible, score_scale)
    row_top = jnp.max(masked, axis=-1, keepdims=True)
    weights = jnp.exp(masked - row_top)
    row_total = jnp.sum(weights, axis=-1, keepdims=True)
    log_total = row_top + jnp.log(row_total)
    probs_low = (weights / row_total).astype(jnp.bfloat16)
    context = jnp.einsum(
        "hqk,khd->qhd", probs_low, to_heads(value_full), preferred_element_type=jnp.float32
    )
    context = context.reshape(queries, full_width).astype(jnp.bfloat16)
    context_full = lax.all_gather(context, "narrow", axis=0, tiled=True)
    projected = jnp.dot(
        context_full, out_cols, preferred_element_type=jnp.float32
    ) + bias_out.astype(jnp.float32)
    projected_low = projected.astype(jnp.bfloat16)
    projected_full = lax.all_gather(projected_low, "narrow", axis=1, tiled=True)
    mid_full = x_full + projected_full.astype(jnp.float32)
    mid_rows = tokens.T.astype(jnp.float32) + projected_low.astype(jnp.float32)
    h_two = normalize(mid_full, gain_two, shift_two).astype(jnp.bfloat16)
    up_pre = jnp.dot(h_two, up_cols, preferred_element_type=jnp.float32) + bias_up.astype(
        jnp.float32
    )
    act_value, gelu_pull = jax.vjp(partial(jax.nn.gelu, approximate=True), up_pre)
    act_low = act_value.astype(jnp.bfloat16)
    partial_down = jnp.dot(act_low, down_rows, preferred_element_type=jnp.float32)
    down_sum = lax.psum_scatter(
        partial_down.astype(jnp.bfloat16), "narrow", scatter_dimension=1, tiled=True
    ).astype(jnp.float32)
    output = (mid_rows + (down_sum + bias_down.astype(jnp.float32))).astype(jnp.bfloat16)
    grad_out = cotangent.T.astype(jnp.float32)
    grad_bias_down = jnp.sum(grad_out, axis=0)
    grad_w_down = jnp.einsum("tf,td->fd", act_low, dy_rows, preferred_element_type=jnp.float32)
    grad_act = jnp.einsum("td,fd->tf", dy_rows, down_rows, preferred_element_type=jnp.float32)
    grad_up = gelu_pull(grad_act)[0].astype(jnp.bfloat16)
    grad_bias_up = jnp.sum(grad_up.astype(jnp.float32), axis=0)
    grad_w_up = jnp.einsum("td,tf->df", h_two, grad_up, preferred_element_type=jnp.float32)
    grad_h_two = full_rows(
        jnp.einsum("tf,df->td", grad_up, up_cols, preferred_element_type=jnp.float32)
    )
    grad_mid_full, grad_gain_two, grad_shift_two = norm_back(
        mid_full, gain_two, shift_two, grad_h_two
    )
    grad_mid = grad_out + own_cols(grad_mid_full)
    grad_projected = grad_mid.astype(jnp.bfloat16)
    grad_bias_out = jnp.sum(grad_projected.astype(jnp.float32), axis=0)
    grad_w_out = jnp.einsum(
        "td,tc->dc", context_full, grad_projected, preferred_element_type=jnp.float32
    )
    grad_context = lax.psum_scatter(
        jnp.einsum("tc,dc->td", grad_projected, out_cols, preferred_element_type=jnp.float32),
        "narrow",
        scatter_dimension=0,
        tiled=True,
    ).astype(jnp.bfloat16)
    weights_back = jnp.exp(masked - log_total)
    context_heads = to_heads(grad_context)
    grad_probs = jnp.einsum(
        "qhd,khd->hqk", context_heads, to_heads(value_full), preferred_element_type=jnp.float32
    )
    centre = jnp.sum(weights_back * grad_probs, axis=-1, keepdims=True)
    grad_scores = (weights_back * (grad_probs - centre)).astype(jnp.bfloat16)
    grad_query = jnp.einsum(
        "hqk,khd->qhd", grad_scores, to_heads(key_full), preferred_element_type=jnp.float32
    )
    grad_query = grad_query.reshape(queries, full_width) * score_scale
    probs_back = weights_back.astype(jnp.bfloat16)
    grad_key = jnp.einsum(
        "hqk,qhd->khd", grad_scores, to_heads(query_rows), preferred_element_type=jnp.float32
    )
    grad_key = grad_key.reshape(length, full_width) * score_scale
    grad_value = jnp.einsum(
        "hqk,qhd->khd", probs_back, context_heads, preferred_element_type=jnp.float32
    )
    grad_value = grad_value.reshape(length, full_width)
    placed = jnp.zeros((length, full_width), jnp.float32)
    placed = lax.dynamic_update_slice_in_dim(placed, grad_query, row_start, 0)
    stacked = jnp.stack((placed, grad_key, grad_value), axis=1)
    grad_mixed = lax.psum_scatter(stacked, "narrow", scatter_dimension=2, tiled=True).astype(
        jnp.bfloat16
    )
    grad_mixed_f = grad_mixed.astype(jnp.float32)
    grad_bias_qv = jnp.stack(
        (jnp.sum(grad_mixed_f[:, 0], axis=0), jnp.sum(grad_mixed_f[:, 2], axis=0))
    )
    grad_w_qkv = jnp.einsum("td,tcf->dcf", h_one, grad_mixed, preferred_element_type=jnp.float32)
    grad_h_one = full_rows(
        jnp.einsum("tcf,dcf->td", grad_mixed, qkv_cols, preferred_element_type=jnp.float32)
    )
    grad_x_full, grad_gain_one, grad_shift_one = norm_back(x_full, gain_one, shift_one, grad_h_one)
    grad_tokens = grad_mid + own_cols(grad_x_full)
    sum_w_qkv, sum_w_out, sum_w_up, sum_w_down = (
        lax.psum_scatter(grad_w_qkv, "wide", scatter_dimension=0, tiled=True),
        lax.psum_scatter(grad_w_out, "wide", scatter_dimension=0, tiled=True),
        lax.psum_scatter(grad_w_up, "wide", scatter_dimension=0, tiled=True),
        lax.psum_scatter(grad_w_down, "wide", scatter_dimension=1, tiled=True),
    )
    (
        sum_gain_one,
        sum_shift_one,
        sum_bias_qv,
        sum_bias_out,
        sum_gain_two,
        sum_shift_two,
        sum_bias_up,
        sum_bias_down,
    ) = lax.psum(
        (
            own_cols(grad_gain_one),
            own_cols(grad_shift_one),
            grad_bias_qv,
            grad_bias_out,
            own_cols(grad_gain_two),
            own_cols(grad_shift_two),
            grad_bias_up,
            grad_bias_down,
        ),
        "wide",
    )
    return (
        output.T,
        grad_tokens.T,
        sum_gain_one,
        sum_shift_one,
        sum_w_qkv,
        sum_bias_qv,
        sum_w_out,
        sum_bias_out,
        sum_gain_two,
        sum_shift_two,
        sum_w_up,
        sum_bias_up,
        sum_w_down,
        sum_bias_down,
    )


F32 = jnp.float32
BF16 = jnp.bfloat16
HEAD = 64
TILE = 256
MIB = 1 << 20
LANES = 128
SPARE = 16
PACE = 1e-6


def dot(a, b, dim_a, dim_b):
    return lax.dot_general(a, b, (((dim_a,), (dim_b,)), ((), ())), preferred_element_type=F32)


def after(value, *others):
    return lax.optimization_barrier((value,) + others)[0]


def cost(flops, moved):
    return pl.CostEstimate(flops=1 + int(PACE * flops), bytes_accessed=1 + int(PACE * moved), transcendentals=0)


def params(mib):
    return pltpu.CompilerParams(vmem_limit_bytes=mib * MIB)


def in_turns(stages, items):
    states = [None] * len(items)
    for tick in range(len(items) + len(stages) - 1):
        for j, stage in enumerate(stages):
            i = tick - j
            if 0 <= i < len(items):
                states[i] = stage(items[i], states[i])


def lane_sums(a):
    return functools.reduce(
        jnp.add, [a[:, i : i + LANES] for i in range(0, a.shape[1], LANES)]
    )


def row_sums(acc):
    return jnp.concatenate(
        [
            jnp.sum(acc[:, i : i + LANES].T, axis=0, keepdims=True)
            for i in range(0, acc.shape[1], LANES)
        ],
        0,
    )


def rows_at(start, size):
    return pl.ds(pl.multiple_of(start, HEAD // 2), size)


def first_step():
    return pl.program_id(0) == 0


def last_step():
    return pl.program_id(0) == pl.num_programs(0) - 1


def unit(rows, a, b):
    mine = rows == 0
    return jnp.where(mine, a, b), jnp.where(mine, b, a)


def bias_kernel(starts_ref, bias_ref):
    length = bias_ref.shape[0] * TILE
    for i in range(length // TILE):
        low = i * TILE
        rows = min(2 * TILE, length - low)
        key = low + lax.broadcasted_iota(jnp.int32, (rows, TILE), 0)
        query = low + lax.broadcasted_iota(jnp.int32, (rows, TILE), 1)
        seen = key <= query
        for p in range(starts_ref.shape[0]):
            s = starts_ref[p]
            seen = seen | (
                (key >= s) & (key < s + PIECE) & (query >= s) & (query < s + PIECE)
            )
        bias_ref[i, :rows, :] = jnp.where(seen, 0.0, -1e30)


def mask_bias(starts, length):
    shape = (length // TILE, 2 * TILE, TILE)
    return pl.pallas_call(
        bias_kernel,
        in_specs=[pl.BlockSpec(memory_space=pltpu.SMEM)],
        out_specs=pl.BlockSpec(memory_space=pltpu.VMEM),
        out_shape=jax.ShapeDtypeStruct(shape, F32),
        compiler_params=params(16),
        name="mask_bias",
    )(starts)


def spans(i, length):
    low = i * TILE
    high = min(low + 2 * TILE, length)
    return ((0, low), (low, high)) if low > 0 else ((low, high),)


def scores(key_rows, query, bias, i, span):
    s = dot(key_rows[span[0] : span[1]], query, 1, 0)
    return s if span[0] < i * TILE else s + bias[i, : span[1] - span[0], :]


def attend_kernel(bias, x_ref, c_ref, l_ref, key_rows):
    length = x_ref.shape[2]
    key_rows[...] = x_ref[1].T

    def score(i, _):
        query = x_ref[0, :, pl.ds(i * TILE, TILE)] * jnp.asarray(HEAD**-0.5, BF16)
        return [(span, scores(key_rows, query, bias, i, span)) for span in spans(i, length)]

    def weigh(i, parts):
        here = pl.ds(i * TILE, TILE)
        top = functools.reduce(
            jnp.maximum, [jnp.max(s, axis=0, keepdims=True) for _, s in parts]
        )
        total, acc = 0.0, 0.0
        for span, s in parts:
            p = jnp.exp(s - top)
            total = total + jnp.sum(p, axis=0, keepdims=True)
            acc = acc + dot(x_ref[2, :, span[0] : span[1]], p.astype(BF16), 1, 0)
        c_ref[:, here] = (acc / total).astype(BF16)
        l_ref[0, :, here] = top + jnp.log(total)

    in_turns((score, weigh), range(length // TILE))


def attend(bias, qkv, first, count):
    length = qkv.shape[2]
    return pl.pallas_call(
        attend_kernel,
        grid=(count,),
        in_specs=[
            pl.BlockSpec(bias.shape, lambda h: (0, 0, 0)),
            pl.BlockSpec((3, HEAD, length), lambda h: (0, h + first, 0)),
        ],
        out_specs=[
            pl.BlockSpec((HEAD, length), lambda h: (h, 0)),
            pl.BlockSpec((1, 1, length), lambda h: (h, 0, 0)),
        ],
        scratch_shapes=[pltpu.VMEM((length, HEAD), BF16)],
        out_shape=[
            jax.ShapeDtypeStruct((count * HEAD, length), BF16),
            jax.ShapeDtypeStruct((count, 1, length), F32),
        ],
        compiler_params=params(24),
        cost_estimate=cost(4e9 * count, count * length * HEAD * 8),
        name="attend",
    )(bias, qkv)


def attend_back_kernel(
    shared, rank_ref, bias, x_ref, mine_ref, got_ref, l_ref, old_ref, g_ref,
    key_rows, value_rows, query_rows, grad_rows, grad, key_sum, value_sum,
):
    length = x_ref.shape[2]
    share = length // 2
    scale = jnp.asarray(HEAD**-0.5, BF16)
    first = rank_ref[0] == 0
    mine, got = mine_ref[...], got_ref[...]
    grad[:, :share] = jnp.where(first, mine, got)
    grad[:, share:] = jnp.where(first, got, mine)
    key_rows[...] = x_ref[1].T
    value_rows[...] = x_ref[2].T
    grad_rows[...] = grad[...].T
    query_rows[...] = (x_ref[0] * scale).T
    tiles = length // TILE

    def score(i, _):
        here = pl.ds(i * TILE, TILE)
        query, out = x_ref[0, :, here] * scale, grad[:, here]
        return [
            (span, scores(key_rows, query, bias, i, span), dot(value_rows[span[0] : span[1]], out, 1, 0))
            for span in spans(i, length)
        ]

    def weigh(i, parts):
        lse = l_ref[0, :, pl.ds(i * TILE, TILE)]
        weights = [jnp.exp(s - lse) for _, s, _ in parts]
        centre = functools.reduce(
            jnp.add, [jnp.sum(p * g, axis=0, keepdims=True) for p, (_, _, g) in zip(weights, parts)]
        )
        return [
            (span, p.astype(BF16), (p * (g - centre)).astype(BF16))
            for p, (span, _, g) in zip(weights, parts)
        ]

    def gather(i, parts):
        here = pl.ds(i * TILE, TILE)
        dq = 0.0
        for (low, high), p, gs in parts:
            dq = dq + dot(x_ref[1, :, low:high], gs, 1, 0)
            dk, dv = dot(gs, query_rows[here], 1, 0), dot(p, grad_rows[here], 1, 0)
            if i == tiles - 1:
                key_sum[low:high], value_sum[low:high] = dk, dv
            else:
                key_sum[low:high] += dk
                value_sum[low:high] += dv
        g_ref[0, :, here] = (dq * HEAD**-0.5).astype(BF16)

    in_turns((score, weigh, gather), list(reversed(range(tiles))))
    g_ref[1] = key_sum[...].T.astype(BF16)
    g_ref[2] = value_sum[...].T.astype(BF16)
    if shared:
        @pl.when(pl.program_id(0) == pl.num_programs(0) - 1)
        def _():
            g_ref[:, HEAD // 2 :, :] = jnp.zeros((3, HEAD // 2, length), BF16)


def attend_back(bias, rank, qkv, mine, got, lse, first, count, shared, old=None):
    length = qkv.shape[2]
    rows = pltpu.VMEM((length, HEAD), BF16)
    sums = pltpu.VMEM((length, HEAD), F32)
    heads = pl.BlockSpec((3, HEAD, length), lambda h, r: (0, h + first, 0))
    half = pl.BlockSpec((HEAD, length // 2), lambda h, r: (h + first, 0))
    alias = {}
    if old is not None:
        alias = {6: 0}
    else:
        old = jnp.zeros((8, 128), BF16)
    return pl.pallas_call(
        functools.partial(attend_back_kernel, shared),
        grid_spec=pltpu.PrefetchScalarGridSpec(
            num_scalar_prefetch=1,
            grid=(count,),
            in_specs=[
                pl.BlockSpec(bias.shape, lambda h, r: (0, 0, 0)),
                heads,
                half,
                half,
                pl.BlockSpec((1, 1, length), lambda h, r: (h + first, 0, 0)),
                pl.BlockSpec(memory_space=pl.ANY),
            ],
            out_specs=[heads],
            scratch_shapes=[rows] * 4
            + [pltpu.VMEM((HEAD, length), BF16)]
            + [sums] * 2,
        ),
        out_shape=[jax.ShapeDtypeStruct(qkv.shape, BF16)],
        input_output_aliases=alias,
        compiler_params=params(34),
        cost_estimate=cost(6.8e9 * count, count * length * HEAD * 14),
        name="attend_back",
    )(rank, bias, qkv, mine, got, lse, old)[0]


def norm_rows(x):
    x = x - jnp.mean(x, axis=0, keepdims=True)
    inv = lax.rsqrt(jnp.mean(x * x, axis=0, keepdims=True) + EPSILON)
    return x * inv, inv


def own_first(rank, a):
    half = a.shape[0] // 2
    return jnp.where(rank == 0, a, jnp.concatenate((a[half:], a[:half]), 0))


def half_lanes(columns):
    return -(-columns // (2 * LANES)) * LANES


def turn_weights(core, mine, got, turned):
    a, b = unit(core, mine, got)
    count = a.shape[1]
    turned[:count] = a.T
    turned[count:] = b.T[2 * count - turned.shape[0] :]


def norm_qkv_kernel(core_ref, xo_ref, xt_ref, m_ref, g_ref, v_ref, b_ref, h_ref, q_ref, turned):
    @pl.when(first_step())
    def _():
        turn_weights(core_ref[0], m_ref[...], g_ref[...], turned)

    x = jnp.concatenate((xo_ref[...], xt_ref[...]), 0).astype(F32)
    h = (norm_rows(x)[0] * v_ref[:, 0:1] + v_ref[:, 1:2]).astype(BF16)
    h_ref[...] = h
    q_ref[...] = (dot(turned[...], h, 1, 0) + b_ref[...]).astype(BF16)


def norm_qkv(core, x_own, x_other, mine, got, vectors, bias):
    own, length = x_own.shape
    depth = 2 * own
    rows = bias.shape[0]
    column = lambda n: pl.BlockSpec((n, TILE), lambda i, s: (0, i))
    whole = lambda a: pl.BlockSpec(a.shape, lambda i, s: (0, 0))
    return pl.pallas_call(
        norm_qkv_kernel,
        grid_spec=pltpu.PrefetchScalarGridSpec(
            num_scalar_prefetch=1,
            grid=(length // TILE,),
            in_specs=[column(own)] * 2 + [whole(a) for a in (mine, got, vectors, bias)],
            out_specs=[column(depth), column(rows)],
            scratch_shapes=[pltpu.VMEM((rows, depth), BF16)],
        ),
        out_shape=[jax.ShapeDtypeStruct((n, length), BF16) for n in (depth, rows)],
        compiler_params=params(60),
        cost_estimate=cost(2 * depth * rows * length, depth * length * 6),
        name="norm_qkv",
    )(core, x_own, x_other, mine, got, vectors, bias)


def qkv_kernel(core_ref, h_ref, m_ref, g_ref, b_ref, q_ref, turned):
    @pl.when(first_step())
    def _():
        turn_weights(core_ref[0], m_ref[...], g_ref[...], turned)

    q_ref[...] = (dot(turned[...], h_ref[...], 1, 0) + b_ref[...]).astype(BF16)


def qkv_of(core, h_one, mine, got, bias):
    depth, length = h_one.shape
    rows = bias.shape[0]
    column = lambda n: pl.BlockSpec((n, TILE), lambda i, s: (0, i))
    whole = lambda a: pl.BlockSpec(a.shape, lambda i, s: (0, 0))
    return pl.pallas_call(
        qkv_kernel,
        grid_spec=pltpu.PrefetchScalarGridSpec(
            num_scalar_prefetch=1,
            grid=(length // TILE,),
            in_specs=[column(depth)] + [whole(a) for a in (mine, got, bias)],
            out_specs=column(rows),
            scratch_shapes=[pltpu.VMEM((rows, depth), BF16)],
        ),
        out_shape=jax.ShapeDtypeStruct((rows, length), BF16),
        compiler_params=params(24),
        cost_estimate=cost(2 * depth * rows * length, depth * length * 4),
        name="qkv",
    )(core, h_one, mine, got, bias)


def project_kernel(
    spot_ref, xo_ref, xt_ref, a_ref, b_ref, d_ref, ga_ref, gb_ref, gd_ref, c_ref, m_ref, g_ref, v_ref,
    p_ref, h_ref, c_out, turned,
):
    @pl.when(first_step())
    def _():
        own = xo_ref.shape[0]
        parts = [own_first(spot_ref[0], w[:, :own]) for w in (m_ref, g_ref)]
        turn_weights(spot_ref[1], *parts, turned)

    rank = spot_ref[0]
    own = xo_ref.shape[0]
    half, whole = HEAD // 2, own - HEAD // 2
    for refs, at in (((a_ref, b_ref, d_ref), half * rank), ((ga_ref, gb_ref, gd_ref), own + half * (1 - rank))):
        for ref in refs:
            c_out[rows_at(at, ref.shape[0])] = ref[...]
            at = at + ref.shape[0]
    c_out[rows_at(whole * (1 - rank), half)] = c_ref[:half]
    c_out[rows_at(own + whole * rank, half)] = c_ref[half:]
    low = (dot(turned[...], c_out[...], 1, 0) + v_ref[:, 0:1]).astype(BF16)
    p_ref[...] = low
    mid = jnp.concatenate((xo_ref[...], xt_ref[...]), 0).astype(F32) + low.astype(F32)
    h_ref[...] = (norm_rows(mid)[0] * v_ref[:, 1:2] + v_ref[:, 2:3]).astype(BF16)


def out_columns(depth):
    return pl.BlockSpec((depth, -(-depth // (2 * LANES)) * LANES), lambda i, s: (0, 0))


def project(spot, x_own, x_other, pieces, mine, got, vectors):
    own, length = x_own.shape
    depth = 2 * own
    column = lambda rows: pl.BlockSpec((rows, TILE), lambda i, s: (0, i))
    whole = lambda a: pl.BlockSpec(a.shape, lambda i, s: (0, 0))
    return pl.pallas_call(
        project_kernel,
        grid_spec=pltpu.PrefetchScalarGridSpec(
            num_scalar_prefetch=1,
            grid=(length // TILE,),
            in_specs=[column(own)] * 2
            + [column(p.shape[0]) for p in pieces]
            + [out_columns(depth)] * 2
            + [whole(vectors)],
            out_specs=[column(depth)] * 3,
            scratch_shapes=[pltpu.VMEM((depth, depth), BF16)],
        ),
        out_shape=[jax.ShapeDtypeStruct((depth, length), BF16)] * 3,
        compiler_params=params(60),
        cost_estimate=cost(2 * depth * depth * length, depth * length * 10),
        name="project",
    )(spot, x_own, x_other, *pieces, mine, got, vectors)


def feed_kernel(
    spot_ref, h_ref, go_ref, gt_ref, pm_ref, pg_ref, qm_ref, qg_ref, bias_ref, *rest
):
    mid_ref, own_ref, other_ref, gh_ref, gb_ref, gs_ref, up, down, sums, sems = rest[-10:]
    split = up.shape[1] - qm_ref.shape[1]
    lead = pm_ref.shape[1] - split
    hidden = up.shape[1]

    @pl.when(pl.program_id(0) == 0)
    def _():
        half = up.shape[0] // 2

        def copies(up_p, up_q, down_p, down_q):
            made = []
            for i, (first, second, whole) in enumerate(((up_p, up_q, up), (down_p, down_q, down))):
                for j in range(2):
                    rows = pl.ds(half * j, half)
                    to = rows_at(half * (j ^ spot_ref[2]), half)
                    at = 4 * i + 2 * j
                    made += [
                        pltpu.make_async_copy(
                            first.at[rows, lead:], whole.at[to, :split], sems.at[at]
                        ),
                        pltpu.make_async_copy(
                            second.at[rows, :], whole.at[to, split:], sems.at[at + 1]
                        ),
                    ]
            return made

        def bring(these):
            for c in these:
                c.start()
            for c in these:
                c.wait()

        @pl.when(spot_ref[1] == 0)
        def _():
            bring(copies(pm_ref, qm_ref, pg_ref, qg_ref))

        @pl.when(spot_ref[1] == 1)
        def _():
            bring(copies(pg_ref, qg_ref, pm_ref, qm_ref))

        gb_ref[...] = jnp.zeros_like(gb_ref)
        sums[...] = jnp.zeros_like(sums)

    sums[...] += lane_sums(go_ref[...].astype(F32))

    @pl.when(last_step())
    def _():
        gs_ref[...] = row_sums(sums[...])

    root = (2 / jnp.pi) ** 0.5
    h = h_ref[...]
    g = jnp.concatenate((go_ref[...], gt_ref[...]), 0)
    for span in (slice(0, split), slice(split, hidden)):
        u = dot(h, up[:, span], 0, 0) + bias_ref[:, span]
        grad_act = dot(g, down[:, span], 0, 0)
        square = u * u
        t = jnp.tanh(u * (root + (root * 0.044715) * square))
        half = 0.5 + 0.5 * t
        mid_ref[0, :, span] = (u * half).astype(BF16)
        slope = half + (0.5 * u) * (1 - t * t) * (root + (3 * root * 0.044715) * square)
        gup = (grad_act * slope).astype(BF16)
        mid_ref[1, :, span] = gup
        gb_ref[:, span] += jnp.sum(gup.astype(F32), axis=0, keepdims=True)
    gh_ref[...] = dot(up[...], mid_ref[1], 1, 1).astype(BF16)
    out = dot(down[...], mid_ref[0], 1, 1).astype(BF16)
    n = own_ref.shape[0]
    own_ref[...], other_ref[...] = out[:n], out[n:]


def feed(spot, count, h_two, g_own, g_other, weights, bias_up, tile, old):
    depth, length = h_two.shape
    own = g_own.shape[0]
    hidden = bias_up.shape[1]
    column = lambda rows: pl.BlockSpec((rows, tile), lambda i, s: (0, s[0] + i))
    anywhere = pl.BlockSpec(memory_space=pl.ANY)
    vector = pl.BlockSpec((1, hidden), lambda i, s: (0, 0))
    local = lambda rows: pl.BlockSpec((rows, tile), lambda i, s: (0, i))
    aliases = {} if old is None else {9: 0}
    return pl.pallas_call(
        feed_kernel,
        grid_spec=pltpu.PrefetchScalarGridSpec(
            num_scalar_prefetch=1,
            grid=(count,),
            in_specs=[column(depth), column(own), column(own)]
            + [anywhere] * 4
            + [vector]
            + [anywhere] * len(aliases),
            out_specs=[
                pl.BlockSpec((2, tile, hidden), lambda i, s: (0, s[0] + i, 0)),
                local(own),
                local(own),
                local(depth),
                vector,
                pl.BlockSpec((1, own), lambda i, s: (0, 0)),
            ],
            scratch_shapes=[
                pltpu.VMEM((depth, hidden), BF16),
                pltpu.VMEM((depth, hidden), BF16),
                pltpu.VMEM((own, LANES), F32),
                pltpu.SemaphoreType.DMA((8,)),
            ],
        ),
        out_shape=[
            jax.ShapeDtypeStruct((2, length, hidden), BF16),
            *(jax.ShapeDtypeStruct((n, count * tile), BF16) for n in (own, own, depth)),
            jax.ShapeDtypeStruct((1, hidden), F32),
            jax.ShapeDtypeStruct((1, own), F32),
        ],
        input_output_aliases=aliases,
        compiler_params=params(50),
        cost_estimate=cost(8 * depth * count * tile * hidden, 12 * depth * hidden),
        name="feed",
    )(spot, h_two, g_own, g_other, *weights, bias_up, *([] if old is None else [old]))


def weight_grad_kernel(which_ref, h_ref, go_ref, gt_ref, m_ref, *rest):
    half = pl.program_id(0) < pl.num_programs(0) // 2
    g = jnp.where(half, go_ref[...], gt_ref[...])
    rows = jnp.where(which_ref[0] == 0, g, h_ref[...])
    if len(rest) == 2:
        p_ref, q_ref = rest
        split = p_ref.shape[1]
        p_ref[...] = dot(rows, m_ref[0, :, :split], 1, 0).astype(BF16)
        q_ref[...] = dot(rows, m_ref[0, :, split:], 1, 0).astype(BF16)
        return
    pg_ref, qg_ref, pk_ref, pa_ref, qk_ref, qa_ref = rest
    split = pg_ref.shape[1]
    p = (dot(rows, m_ref[0, :, :split], 1, 0) + pg_ref[...].astype(F32)).astype(BF16)
    q = (dot(rows, m_ref[0, :, split:], 1, 0) + qg_ref[...].astype(F32)).astype(BF16)
    n = p.shape[0] // 4
    low = jnp.concatenate((p[:n], p[2 * n : 3 * n]), 0)
    high = jnp.concatenate((p[n : 2 * n], p[3 * n :]), 0)
    pk_ref[...], pa_ref[...] = unit(which_ref[1], low, high)
    qk_ref[...], qa_ref[...] = unit(which_ref[2], q[: 2 * n], q[2 * n :])


def weight_grad(which, h_two, g_own, g_other, middle, split, got=None):
    depth, length = h_two.shape
    hidden = middle.shape[2]
    steps = 2
    rows = depth // steps
    parts = (split, hidden - split)
    blocks = [pl.BlockSpec((rows, n), lambda i, s: (i, 0)) for n in parts]
    in_specs = [
        pl.BlockSpec((rows, length), lambda i, s: (i, 0)),
        pl.BlockSpec((rows, length), lambda i, s: (0, 0)),
        pl.BlockSpec((rows, length), lambda i, s: (0, 0)),
        pl.BlockSpec((1, length, hidden), lambda i, s: (s[0], 0, 0)),
    ]
    out_specs, shapes = blocks, [jax.ShapeDtypeStruct((depth, n), BF16) for n in parts]
    if got is not None:
        in_specs += blocks
        out_specs = [pl.BlockSpec((rows // 2, n), lambda i, s: (i, 0)) for n in parts for _ in range(2)]
        shapes = [jax.ShapeDtypeStruct((depth // 2, n), BF16) for n in parts for _ in range(2)]
    return pl.pallas_call(
        weight_grad_kernel,
        grid_spec=pltpu.PrefetchScalarGridSpec(
            num_scalar_prefetch=1, grid=(steps,), in_specs=in_specs, out_specs=out_specs
        ),
        out_shape=shapes,
        compiler_params=params(44),
        cost_estimate=cost(2 * depth * length * hidden, 2 * (2 * depth + hidden) * length),
        name="weight_grad",
    )(which, h_two, g_own, g_other, middle, *(got or ()))


def mid_back_kernel(
    spot_ref, xo_ref, xt_ref, p_ref, go_ref, gt_ref, keep_ref, got_ref, m_ref, g_ref, v_ref,
    gp_ref, gq_ref, ma_ref, mb_ref, sa_ref, sb_ref, n_ref, w_own, w_other, gc, sums,
):
    @pl.when(first_step())
    def _():
        n = w_own.shape[1]
        parts = [own_first(spot_ref[2], w[:, :n]) for w in (m_ref, g_ref)]
        w_own[...], w_other[...] = unit(spot_ref[1], *parts)
        sums[...] = jnp.zeros_like(sums)

    own = xo_ref.shape[0]
    rank = spot_ref[2]
    keep, got = keep_ref[...].astype(F32), got_ref[...].astype(F32)
    gh = keep + jnp.concatenate((got[own:], got[:own]), 0)
    mid = jnp.concatenate((xo_ref[...], xt_ref[...]), 0).astype(F32) + p_ref[...].astype(F32)
    hat, inv = norm_rows(mid)
    e = gh * v_ref[:, 1:2]
    grad = jnp.concatenate((go_ref[...], gt_ref[...]), 0).astype(F32) + inv * (
        e - jnp.mean(e, axis=0, keepdims=True) - hat * jnp.mean(e * hat, axis=0, keepdims=True)
    )
    gp = grad.astype(BF16)
    gp_ref[...], gq_ref[...] = gp[:own], gp[own:]
    gc[...] = (dot(w_own[...], gp[:own], 1, 0) + dot(w_other[...], gp[own:], 1, 0)).astype(BF16)
    half = HEAD // 2
    a, b = ma_ref.shape[0], mb_ref.shape[0] - HEAD
    near, away = half * rank, own + half * (1 - rank)
    own_half = gc[rows_at((a + b) * (1 - rank), half)]
    other_half = gc[rows_at(own + (a + b) * rank, half)]
    ma_ref[...] = gc[rows_at(near, a)]
    mb_ref[:b] = gc[rows_at(near + a, b)]
    mb_ref[b : b + half] = own_half
    mb_ref[b + half :] = other_half
    sa_ref[...] = gc[rows_at(away, a)]
    sb_ref[:b] = gc[rows_at(away + a, b)]
    sb_ref[b : b + half] = other_half
    sb_ref[b + half :] = own_half
    sums[...] += jnp.concatenate(
        (lane_sums(gh * hat), lane_sums(gh), lane_sums(gp.astype(F32))), 1
    )

    @pl.when(last_step())
    def _():
        n_ref[...] = row_sums(sums[...])


def mid_back(spot, x_own, x_other, projected, g_own, g_other, keep, got, mine, got_w, vectors, rows_a, rows_b):
    own, length = x_own.shape
    depth = 2 * own
    share = length // 2
    column = lambda rows: pl.BlockSpec((rows, TILE), lambda i, s: (0, s[0] + i))
    local = lambda rows: pl.BlockSpec((rows, TILE), lambda i, s: (0, i))
    whole = lambda a: pl.BlockSpec(a.shape, lambda i, s: (0, 0))
    out = lambda rows: jax.ShapeDtypeStruct((rows, share), BF16)
    sizes = (own, own, rows_a, rows_b, rows_a, rows_b)
    return pl.pallas_call(
        mid_back_kernel,
        grid_spec=pltpu.PrefetchScalarGridSpec(
            num_scalar_prefetch=1,
            grid=(share // TILE,),
            in_specs=[column(own), column(own), column(depth), column(own), column(own)]
            + [local(depth)] * 2
            + [out_columns(depth)] * 2
            + [whole(vectors)],
            out_specs=[local(r) for r in sizes] + [pl.BlockSpec((3, depth), lambda i, s: (0, 0))],
            scratch_shapes=[pltpu.VMEM((depth, own), BF16)] * 2
            + [pltpu.VMEM((depth, TILE), BF16), pltpu.VMEM((depth, 3 * LANES), F32)],
        ),
        out_shape=[out(r) for r in sizes] + [jax.ShapeDtypeStruct((3, depth), F32)],
        compiler_params=params(60),
        cost_estimate=cost(2 * depth * depth * share, depth * share * 16),
        name="mid_back",
    )(spot, x_own, x_other, projected, g_own, g_other, keep, got, mine, got_w, vectors)


def half_lanes(columns):
    return -(-columns // (2 * LANES)) * LANES


def grads_kernel(place_ref, h_ref, g_ref, send_ref, keep_ref):
    cols = send_ref.shape[1]
    low = dot(h_ref[...], g_ref[:cols], 1, 1).astype(BF16)
    high = dot(h_ref[...], g_ref[g_ref.shape[0] - cols :], 1, 1).astype(BF16)
    keep_ref[...], send_ref[...] = unit(place_ref[1], low, high)


def grads_out_kernel(place_ref, h_ref, c_ref, g_ref, pm_ref, pg_ref, send_ref, keep_ref, gp):
    @pl.when(first_step())
    def _():
        share = pm_ref.shape[1]
        gp[:, :share], gp[:, share:] = unit(place_ref[0], pm_ref[...], pg_ref[...])

    out = half_lanes(gp.shape[0])
    cols = send_ref.shape[1] - out
    for lhs, rhs, n, to in (
        (h_ref, g_ref, cols, slice(0, cols)),
        (c_ref, gp, out, slice(cols, cols + out)),
    ):
        low = dot(lhs[...], rhs[:n], 1, 1).astype(BF16)
        high = dot(lhs[...], rhs[rhs.shape[0] - n :], 1, 1).astype(BF16)
        keep_ref[:, to], send_ref[:, to] = unit(place_ref[1], low, high)


def column_grads(places, cols, h_one, grad, context=None, gp=None, gp_got=None):
    depth, length = h_one.shape
    kernel, total, scratch = grads_kernel, cols, []
    part = pl.BlockSpec((depth // 2, length), lambda i, s: (i, 0))
    whole = lambda a: pl.BlockSpec(a.shape, lambda i, s: (0, 0))
    args, specs = [h_one, grad], [part, whole(grad)]
    if context is not None:
        kernel, total = grads_out_kernel, cols + half_lanes(gp.shape[0])
        args = [h_one, context, grad, gp, gp_got]
        specs = [part, part] + [whole(a) for a in args[2:]]
        scratch = [pltpu.VMEM((gp.shape[0], length), BF16)]
    return pl.pallas_call(
        kernel,
        grid_spec=pltpu.PrefetchScalarGridSpec(
            num_scalar_prefetch=1,
            grid=(2,),
            in_specs=specs,
            out_specs=[pl.BlockSpec((depth // 2, total), lambda i, s: (i, 0))] * 2,
            scratch_shapes=scratch,
        ),
        out_shape=[jax.ShapeDtypeStruct((depth, total), BF16)] * 2,
        compiler_params=params(32),
        cost_estimate=cost(4 * depth * total * length, 6 * depth * length),
        name="column_grads",
    )(places, *args)


def output_kernel(
    place_ref, x_ref, p_ref, b_ref, low_ref, high_ref, low_got_ref, high_got_ref, o_ref
):
    mine = pl.program_id(0) // (pl.num_programs(0) // 2) == place_ref[0]
    pick = lambda a, b: jnp.where(mine, a[...], b[...]).astype(F32)
    down = pick(high_ref, low_ref) + pick(low_got_ref, high_got_ref)
    o_ref[...] = (
        x_ref[...].astype(F32) + p_ref[...].astype(F32) + (down + b_ref[...])
    ).astype(BF16)


def close_output(places, x_own, projected, bias, low, high, low_got, high_got):
    own, length = x_own.shape
    column = pl.BlockSpec((own, TILE), lambda i, s: (0, i))
    steps = length // 2 // TILE
    half = pl.BlockSpec((own, TILE), lambda i, s: (0, lax.rem(i, steps)))
    return pl.pallas_call(
        output_kernel,
        grid_spec=pltpu.PrefetchScalarGridSpec(
            num_scalar_prefetch=1,
            grid=(2 * steps,),
            in_specs=[column] * 2 + [pl.BlockSpec((own, 1), lambda i, s: (0, 0))] + [half] * 4,
            out_specs=column,
        ),
        out_shape=jax.ShapeDtypeStruct((own, length), BF16),
        compiler_params=params(24),
        cost_estimate=cost(0, 0),
        name="close_output",
    )(places, x_own, projected, bias, low, high, low_got, high_got)


def tokens_kernel(place_ref, x_ref, gp_ref, gq_ref, keep_ref, got_ref, s_ref, v_ref, o_ref):
    own = x_ref.shape[0]
    mine = pl.program_id(0) // (pl.num_programs(0) // 2) == place_ref[0]
    gp = jnp.where(mine, gp_ref[...], gq_ref[...]).astype(F32)
    e = (keep_ref[...].astype(F32) + got_ref[:own].astype(F32)) * v_ref[:own, 0:1]
    others = got_ref[own:].astype(F32)
    mean, inv = s_ref[2:3], s_ref[3:4]
    total = (s_ref[:2] + (others[:2] + others[2:4])) * (0.5 / own)
    hat = (x_ref[...].astype(F32) - mean) * inv
    o_ref[...] = gp + inv * (e - total[:1] - hat * total[1:])


def close_tokens(places, x_own, gp, gp_got, keep, got, stats, vectors):
    own, length = x_own.shape
    steps = length // 2 // TILE
    column = lambda rows: pl.BlockSpec((rows, TILE), lambda i, s: (0, i))
    half = pl.BlockSpec((own, TILE), lambda i, s: (0, lax.rem(i, steps)))
    return pl.pallas_call(
        tokens_kernel,
        grid_spec=pltpu.PrefetchScalarGridSpec(
            num_scalar_prefetch=1,
            grid=(2 * steps,),
            in_specs=[column(own), half, half, column(own), column(own + SPARE), column(4)]
            + [pl.BlockSpec(vectors.shape, lambda i, s: (0, 0))],
            out_specs=column(own),
        ),
        out_shape=jax.ShapeDtypeStruct((own, length), F32),
        compiler_params=params(24),
        cost_estimate=cost(0, 0),
        name="close_tokens",
    )(places, x_own, gp, gp_got, keep, got, stats, vectors)


def qkv_back_kernel(
    core_ref, xo_ref, xt_ref, gb_ref, ga_ref, bm_ref, bg_ref, am_ref, ag_ref, v_ref,
    keep_ref, send_ref, s_ref, n_ref, db_ref, da_ref, b_low, b_high, a_low, a_high, n_sum, b_sum, a_sum,
):
    @pl.when(first_step())
    def _():
        b_low[...], b_high[...] = unit(core_ref[0], bm_ref[...], bg_ref[...])
        a_low[...], a_high[...] = unit(core_ref[0], am_ref[...], ag_ref[...])
        for r in (n_sum, b_sum, a_sum):
            r[...] = jnp.zeros_like(r)

    own = xo_ref.shape[0]
    gb, ga = gb_ref[...], ga_ref[...]
    cols_b, cols_a = b_low.shape[1], a_low.shape[1]
    twice = 2 * cols_b - gb.shape[0]
    rest = jnp.concatenate((jnp.zeros((twice, gb.shape[1]), BF16), gb[cols_b:]), 0)
    gh = (dot(b_low[...], gb[:cols_b], 1, 0) + dot(b_high[...], rest, 1, 0)) + (
        dot(a_low[...], ga[:cols_a], 1, 0) + dot(a_high[...], ga[cols_a:], 1, 0)
    )
    keep_ref[...] = gh[:own].astype(BF16)
    send_ref[:own] = gh[own:].astype(BF16)
    x = jnp.concatenate((xo_ref[...], xt_ref[...]), 0).astype(F32)
    hat, inv = norm_rows(x)
    both = gh * hat
    gain = v_ref[:, 0:1]
    mine = jnp.concatenate(
        (jnp.sum(gh * gain, axis=0, keepdims=True), jnp.sum(both * gain, axis=0, keepdims=True)), 0
    )
    s_ref[...] = jnp.concatenate((mine, jnp.mean(x, axis=0, keepdims=True), inv), 0)
    high = mine.astype(BF16).astype(F32)
    parts = jnp.concatenate((high, mine - high, jnp.zeros((SPARE - 4, mine.shape[1]), F32)), 0)
    send_ref[own:] = parts.astype(BF16)
    n_sum[...] += jnp.concatenate((lane_sums(both), lane_sums(gh)), 1)
    b_sum[...] += lane_sums(gb.astype(F32))
    a_sum[...] += lane_sums(ga.astype(F32))

    @pl.when(last_step())
    def _():
        n_ref[...] = row_sums(n_sum[...])
        db_ref[...] = row_sums(b_sum[...])
        da_ref[...] = row_sums(a_sum[...])


def qkv_back(core, x_own, x_other, grad_b, grad_a, w_b, w_a, vectors):
    own = x_own.shape[0]
    depth = 2 * own
    column = lambda rows: pl.BlockSpec((rows, TILE), lambda i, s: (0, i))
    whole = lambda a: pl.BlockSpec(a.shape, lambda i, s: (0, 0))
    span = x_own.shape[1]
    out = jax.ShapeDtypeStruct
    rows = (depth, grad_b.shape[0], grad_a.shape[0])
    flat = [out((n, r), F32) for n, r in zip((2, 1, 1), rows)]
    return pl.pallas_call(
        qkv_back_kernel,
        grid_spec=pltpu.PrefetchScalarGridSpec(
            num_scalar_prefetch=1,
            grid=(span // TILE,),
            in_specs=[column(own)] * 2
            + [column(grad_b.shape[0]), column(grad_a.shape[0])]
            + [whole(a) for a in (*w_b, *w_a, vectors)],
            out_specs=[column(own), column(own + SPARE), column(4)] + [whole(t) for t in flat],
            scratch_shapes=[pltpu.VMEM(w.shape, BF16) for w in (*w_b, *w_a)]
            + [pltpu.VMEM((r, n * LANES), F32) for n, r in zip((2, 1, 1), rows)],
        ),
        out_shape=[out((own, span), BF16), out((own + SPARE, span), BF16), out((4, span), F32)]
        + flat,
        compiler_params=params(36),
        cost_estimate=cost(2 * depth * span * (rows[1] + rows[2]), depth * span * 12),
        name="qkv_back",
    )(core, x_own, x_other, grad_b, grad_a, *w_b, *w_a, vectors)


def by_bit(bit, a, b):
    return jnp.where(lax.axis_index("wide") & bit == 0, a, b)


def flip(a, bit):
    size = lax.axis_size("wide")
    return lax.ppermute(a, "wide", [(i, i ^ bit) for i in range(size)])


def join_kernel(place_ref, kept_ref, got_ref, out_ref):
    first = place_ref[0] == 0
    if out_ref.ndim == 2:
        half = kept_ref.shape[0]
        out_ref[:half] = jnp.where(first, kept_ref[...], got_ref[...])
        out_ref[half:] = jnp.where(first, got_ref[...], kept_ref[...])
    else:
        here = pl.program_id(1) == place_ref[0]
        out_ref[...] = jnp.where(here, kept_ref[...], got_ref[...])


def join(kept, got, place, axis):
    rows, cols = kept.shape[-2:]
    call = dict(compiler_params=params(16), cost_estimate=cost(0, 0), name="join")
    place = place.astype(jnp.int32)[None]
    if axis is None:
        spec = lambda n: pl.BlockSpec((n, cols), lambda i, s: (0, 0))
        grid_spec = pltpu.PrefetchScalarGridSpec(
            num_scalar_prefetch=1, grid=(1,), in_specs=[spec(rows)] * 2, out_specs=spec(2 * rows)
        )
        shape = jax.ShapeDtypeStruct((2 * rows, cols), kept.dtype)
        return pl.pallas_call(join_kernel, grid_spec=grid_spec, out_shape=shape, **call)(place, kept, got)
    outer, inner = math.prod(kept.shape[:axis]), math.prod(kept.shape[axis:-1])
    spec = pl.BlockSpec((1, 1, inner, cols), lambda a, j, s: (a, 0, 0, 0))
    grid_spec = pltpu.PrefetchScalarGridSpec(
        num_scalar_prefetch=1,
        grid=(outer, 2),
        in_specs=[spec] * 2,
        out_specs=pl.BlockSpec((1, 1, inner, cols), lambda a, j, s: (a, j, 0, 0)),
    )
    shape = jax.ShapeDtypeStruct((outer, 2, inner, cols), kept.dtype)
    args = [a.reshape(outer, 1, inner, cols) for a in (kept, got)]
    out = pl.pallas_call(join_kernel, grid_spec=grid_spec, out_shape=shape, **call)(place, *args)
    return out.reshape(kept.shape[:axis] + (2,) + kept.shape[axis:])


def fold_kernel(index_ref, kept_ref, got_ref, keep_ref, away_ref):
    total = kept_ref[...].astype(F32) + got_ref[...].astype(F32)
    if kept_ref.ndim == 2:
        half = keep_ref.shape[0]
        low, high = total[:half], total[half:]
        first = index_ref[0] == 0
        keep_ref[...], away_ref[...] = jnp.where(first, low, high), jnp.where(first, high, low)
        return
    total = total.astype(BF16).reshape(keep_ref.shape)

    @pl.when(pl.program_id(1) == 0)
    def _():
        keep_ref[...] = total

    @pl.when(pl.program_id(1) == 1)
    def _():
        away_ref[...] = total


def fold(kept, got, index, axis):
    rows, cols = kept.shape[-2:]
    call = dict(compiler_params=params(16), cost_estimate=cost(0, 0), name="fold")
    index = index.astype(jnp.int32)[None]
    if axis is None:
        spec = lambda n: pl.BlockSpec((n, cols), lambda i, s: (0, 0))
        grid_spec = pltpu.PrefetchScalarGridSpec(
            num_scalar_prefetch=1, grid=(1,), in_specs=[spec(rows)] * 2, out_specs=[spec(rows // 2)] * 2
        )
        shape = [jax.ShapeDtypeStruct((rows // 2, cols), F32)] * 2
        return pl.pallas_call(fold_kernel, grid_spec=grid_spec, out_shape=shape, **call)(index, kept, got)
    outer, inner = math.prod(kept.shape[:axis]), math.prod(kept.shape[axis + 1 : -1])
    grid_spec = pltpu.PrefetchScalarGridSpec(
        num_scalar_prefetch=1,
        grid=(outer, 2),
        in_specs=[pl.BlockSpec((1, 1, inner, cols), lambda a, j, s: (a, j ^ s[0], 0, 0))] * 2,
        out_specs=[pl.BlockSpec((1, inner, cols), lambda a, j, s: (a, 0, 0))] * 2,
    )
    shape = [jax.ShapeDtypeStruct((outer, inner, cols), BF16)] * 2
    args = [a.reshape(outer, 2, inner, cols) for a in (kept, got)]
    out = pl.pallas_call(fold_kernel, grid_spec=grid_spec, out_shape=shape, **call)(index, *args)
    return [o.reshape(kept.shape[:axis] + kept.shape[axis + 1 :]) for o in out]


class Gather:
    def __init__(self, a, b, order):
        self.kept = by_bit(1, a, b)
        self.got = flip(by_bit(1, b, a), 1)
        self.order = list(order)
        self.bits = []
        self.last = None

    def merge(self):
        if self.last is None:
            axis, place = None, lax.axis_index("wide") & 1
        else:
            axis = sum(1 for b in self.bits if b > self.last)
            place = (lax.axis_index("wide") & self.last != 0).astype(jnp.int32)
            if self.last == max(self.order + self.bits + [self.last]):
                place = place ^ lax.axis_index("narrow")
            self.bits.append(self.last)
        self.cur = join(self.kept, self.got, place, axis)

    def came(self):
        return self.got

    def come(self, value):
        self.got = value

    def held(self):
        return self.cur

    def hold(self, value):
        self.cur = value

    def send(self):
        self.last = self.order.pop(0) if self.order else 1
        if self.last == 1:
            self.cur = self.cur.reshape(-1, self.cur.shape[-1])
        self.kept, self.got = self.cur, flip(self.cur, self.last)


class Whole:
    def __init__(self, a, b):
        self.kept = by_bit(1, a, b)
        self.got = flip(by_bit(1, b, a), 1)
        self.stage = 0

    def merge(self):
        if self.stage == 0:
            low = lax.axis_index("wide") & 1 == 0
            kept, got = self.kept, self.got
            self.cur = jnp.where(
                low, jnp.concatenate((kept, got), 0), jnp.concatenate((got, kept), 0)
            )

    def came(self):
        return self.got if self.stage == 0 else self.cur

    def come(self, value):
        if self.stage == 0:
            self.got = value
        else:
            self.cur = value

    def held(self):
        return self.cur

    def hold(self, value):
        self.cur = value

    def send(self):
        if self.stage == 0:
            size = lax.axis_size("wide")
            groups = [list(range(c, size, 2)) for c in range(2)]
            self.cur = lax.all_gather(
                self.cur, "wide", axis=0, tiled=True, axis_index_groups=groups
            )
        else:
            self.got = flip(self.cur, 1)
        self.stage += 1


class Scatter:
    def __init__(self, send, order):
        self.got = flip(send, 1)
        self.order = list(order)
        self.axes = sorted(order, reverse=True)
        self.top = self.axes[0]

    def merge(self):
        kept, got = self.kept, self.got
        if self.order:
            if kept.ndim == 2:
                shape = (2,) * len(self.axes) + (-1, kept.shape[-1])
                kept, got = kept.reshape(shape), got.reshape(shape)
            bit = self.order.pop(0)
            axis = self.axes.index(bit)
            self.axes.remove(bit)
            index = (lax.axis_index("wide") & bit != 0).astype(jnp.int32)
            if bit == self.top:
                index = index ^ lax.axis_index("narrow")
        else:
            bit, axis, index = 1, None, lax.axis_index("wide") & 1
        self.bit = bit
        self.keep, self.away = fold(kept, got, index, axis)

    def next_index(self):
        index = (lax.axis_index("wide") & self.order[0] != 0).astype(jnp.int32)
        return index ^ lax.axis_index("narrow") if self.order[0] == self.top else index

    def start(self, other, *halves):
        for m, keep, away in ((self, *halves[:2]), (other, *halves[2:])):
            m.bit = m.order.pop(0)
            m.axes.remove(m.bit)
            shape = (2,) * len(m.axes) + (-1, keep.shape[-1])
            m.keep, m.away = keep.reshape(shape), away.reshape(shape)

    def came(self):
        return self.got

    def come(self, value):
        self.got = value

    def held(self):
        return self.keep, self.away

    def hold(self, value):
        self.keep, self.away = value

    def send(self):
        self.kept, self.got = self.keep, flip(self.away, self.bit)

    def result(self):
        return by_bit(1, self.kept, self.got), by_bit(1, self.got, self.kept)


def meet(values, *moves, wait=()):
    moves = list(moves) + list(wait)
    values, came = lax.optimization_barrier((values, [m.came() for m in moves]))
    for m, c in zip(moves, came):
        m.come(c)
        m.merge()
    values, held = lax.optimization_barrier((values, [m.held() for m in moves]))
    for m, h in zip(moves, held):
        m.hold(h)
        if m not in wait:
            m.send()
    return values


def send_now(values, *moves):
    values, held = lax.optimization_barrier((values, [m.held() for m in moves]))
    for m, h in zip(moves, held):
        m.hold(h)
        m.send()
    return values


def pair_plan(
    tokens,
    piece_starts,
    ln1_gain,
    ln1_bias,
    w_qkv,
    bias_qv,
    w_out,
    bias_out,
    ln2_gain,
    ln2_bias,
    w_up,
    bias_up,
    w_down,
    bias_down,
    cotangent,
):
    rank = lax.axis_index("narrow")
    first = rank == 0
    core = lax.axis_index("wide") & 1
    own, length = tokens.shape
    depth = 2 * own
    whole = own // HEAD * HEAD
    rest = own - whole
    rows_a = whole // 2
    rows_b = whole - rows_a + 2 * rest
    heads_a, heads_b = rows_a // HEAD, rows_b // HEAD
    block = w_out.shape[0]
    hidden = w_up.shape[1]
    tile = length // 4
    part = -(-(hidden + own) // 256) * LANES
    split = hidden - part
    split_back = hidden // 256 * LANES + 2 * LANES
    rank_arg = rank.astype(jnp.int32)[None]

    def swap(a):
        return lax.ppermute(a, "narrow", [(0, 1), (1, 0)])

    def heads_first(a):
        return jnp.where(first, a, jnp.concatenate((a[..., rest:], a[..., :rest]), -1))

    def heads_back(a):
        return jnp.where(first, a, jnp.concatenate((a[..., whole:], a[..., :whole]), -1))

    def at_rows(bias):
        return jnp.stack((bias[0], jnp.zeros_like(bias[0]), bias[1])).reshape(-1, 1)

    far, near, side = 8, 4, 2
    inward, outward = (far, near, side), (side, far, near)
    w_heads = heads_first(w_qkv)
    shard_a = w_heads[:, :, :rows_a].reshape(block, -1)
    cols_a = shard_a.shape[1] // 2
    get_a = Gather(shard_a[:, :cols_a], shard_a[:, cols_a:], inward)
    bias_local = heads_first(bias_qv)
    own_vectors = jnp.concatenate(
        (jnp.stack((ln1_gain, ln1_bias, ln2_gain, ln2_bias, bias_out)), bias_local), 0
    )
    half_rows = w_heads[:, :, whole:].reshape(-1, own)
    count = own_vectors.shape[0]
    small_swap = swap(jnp.concatenate((own_vectors, half_rows, w_out), 0))
    x_own, w_up_in, w_down_in, g_own = meet((tokens, w_up, w_down, cotangent), get_a)
    small_swap, x_own = lax.optimization_barrier((small_swap, x_own))
    x_other = swap(x_own)
    other_half = small_swap[count:-block].reshape(block, 3, rest)
    shard_b = jnp.concatenate((w_heads[:, :, rows_a:], other_half), 2).reshape(block, -1)
    cols_b = -(-shard_b.shape[1] // 256) * 128
    skip = shard_b.shape[1] - cols_b
    get_b = Gather(shard_b[:, :cols_b], shard_b[:, skip:], inward)
    pad = jnp.zeros((block, part - split - own), BF16)
    get_p = Whole(
        jnp.concatenate((w_out, pad, w_up[:, :split]), 1),
        jnp.concatenate((small_swap[-block:], pad, w_down.T[:, :split]), 1),
    )
    get_p.merge()
    get_p.send()
    other_vectors = small_swap[:count]
    vectors = jnp.concatenate((own_vectors[:5], other_vectors[:5]), 1).astype(F32).T
    gain_one, shift_one = vectors[:, 0:1], vectors[:, 1:2]
    project_vectors = jnp.stack((vectors[:, 4], vectors[:, 2], vectors[:, 3]), 1)
    w_down_t = w_down_in.T
    get_q = Whole(w_up_in[:, split:], w_down_t[:, split:])
    meet((), get_a, get_b, get_q)
    starts = meet(piece_starts[0], get_a, get_b)
    seen = mask_bias(starts, length)
    seen, x_other = meet((seen, x_other), get_a, get_b)
    g_other = swap(after(g_own, x_other))
    x_other, get_a.got = meet((x_other, get_a.got))

    bias_f = bias_local.astype(F32)
    bias_a = bias_f[:, :rows_a]
    bias_b = jnp.concatenate((bias_f[:, rows_a:], other_vectors[5:, whole:].astype(F32)), 1)
    core_arg = core[None]
    w_a = (get_a.cur, get_a.got)
    h_one, qkv_a = norm_qkv(core_arg, tokens, x_other, *w_a, vectors, at_rows(bias_a))
    qkv_a = qkv_a.reshape(3, rows_a, length)

    context_a, lse_a = attend(seen, qkv_a, 0, heads_a)
    context_a, h_one = meet((context_a, h_one), get_b, get_p)
    h_b, get_b.got = meet((h_one, get_b.got))

    context_a_other = swap(after(context_a, g_other))
    w_b = (get_b.cur, get_b.got)
    qkv_b = qkv_of(core_arg, h_b, *w_b, at_rows(bias_b)).reshape(3, rows_b, length)
    whole_b = heads_b - 1
    half_b = whole_b // 2
    context_b, lse_b = attend(seen, qkv_b, 0, half_b)
    context_b, qkv_d = meet((context_b, qkv_b))
    context_b_other = swap(after(context_b, context_a_other))
    context_d, lse_d = attend(seen, qkv_d, half_b, whole_b - half_b)
    context_d, qkv_c = meet((context_d, qkv_d))

    context_d_other = swap(after(context_d, context_b_other))
    context_c, lse_c = attend(seen, qkv_c, whole_b, 1)
    lse_b = jnp.concatenate((lse_b, lse_d, lse_c), 0)
    context_a_other, context_b_other, context_d_other, context_c, get_p.got = meet(
        (context_a_other, context_b_other, context_d_other, context_c, get_p.got)
    )

    pieces = (
        context_a, context_b, context_d, context_a_other, context_b_other, context_d_other, context_c
    )
    w_o = (get_p.cur, get_p.got)
    places = jnp.stack((rank, core)).astype(jnp.int32)
    projected, h_two, context = project(places, tokens, x_other, pieces, *w_o, project_vectors)
    projected, h_two, context = meet((projected, h_two, context), get_q)
    get_q.got, h_two = meet((get_q.got, h_two))

    weights = (get_p.cur, get_p.got, get_q.cur, get_q.got)
    bias_up_f = bias_up.astype(F32)[None]
    steps = length // 2 // TILE

    def spot(at):
        return jnp.stack((at, core, rank)).astype(jnp.int32)

    old, low_own, low_other, gh_send, gb_send, gs_send = feed(
        spot(steps * (1 - rank)), steps, h_two, cotangent, g_other, weights, bias_up_f, TILE, None
    )
    old, gh_send = meet((old, gh_send))
    gh_got = swap(gh_send)
    middle, high_own, high_other, gh_keep, gb_keep, gs_keep = feed(
        spot(steps * rank), steps, h_two, cotangent, g_other, weights, bias_up_f, TILE, old
    )
    grad_bias_up = gb_send + gb_keep
    send_p, send_q = weight_grad(core[None], h_two, cotangent, g_other, middle, split_back)
    gh_got, gh_keep, send_p, send_q, middle, low_other = meet(
        (gh_got, gh_keep, send_p, send_q, middle, low_other)
    )

    put_p = Scatter(send_p, (side, near, far))
    put_q = Scatter(send_q, (near, far, side))
    low_got = swap(low_other)
    gp, gp_away, mine_a, mine_b, send_a, send_b, grad_two = mid_back(
        spot(steps * rank), tokens, x_other, projected, cotangent, g_other, gh_keep,
        gh_got, *w_o, project_vectors, rows_a, rows_b,
    )
    gp, gp_away, mine_a, mine_b, send_a, send_b, middle, put_p.got, put_q.got = meet(
        (gp, gp_away, mine_a, mine_b, send_a, send_b, middle, put_p.got, put_q.got)
    )

    got_b = swap(send_b)
    put_p.start(put_q, *weight_grad(
        jnp.stack((1 - core, put_p.next_index(), put_q.next_index())).astype(jnp.int32),
        h_two, cotangent, g_other, middle, split_back, (put_p.got, put_q.got),
    ))
    got_b, mine_b, send_a, gp_away, low_got = send_now(
        meet((got_b, mine_b, send_a, gp_away, low_got)), put_p, put_q
    )

    got_a = swap(send_a)
    gp_got = swap(gp_away)
    back_b = attend_back(seen, rank_arg, qkv_b, mine_b, got_b, lse_b, 0, heads_b, True)
    back_b, got_a, gp_got, high_other = meet((back_b, got_a, gp_got, high_other), put_p, put_q)

    high_got = swap(high_other)
    grad_b = back_b.reshape(3 * rows_b, length)

    half_a = heads_a // 2
    back_a = attend_back(seen, rank_arg, qkv_a, mine_a, got_a, lse_a, 0, half_a, False)
    send_b, keep_b = column_grads(places, cols_b, h_one, grad_b, context, gp, gp_got)
    back_a, send_b, keep_b, high_got = meet(
        (back_a, send_b, keep_b, high_got), wait=(put_p, put_q)
    )
    put_b = Scatter(send_b, (side, near, far))
    put_b.kept = keep_b
    back_a = attend_back(
        seen, rank_arg, qkv_a, mine_a, got_a, lse_a, half_a, heads_a - half_a, False, back_a
    )
    back_a = send_now(meet(back_a, put_b), put_p, put_q)
    grad_a = back_a.reshape(3 * rows_a, length)

    def vector_parts(sums):
        def row(a):
            return jnp.pad(a, ((0, 0), (0, depth - a.shape[1])))

        low = [grad_bias_up[:, :depth], grad_bias_up[:, depth:]]
        return jnp.concatenate(
            (sums[0], grad_two, row(sums[1]), row(sums[2]), row(gs_send + gs_keep), *map(row, low))
        )

    send_a, keep_a = column_grads(places, cols_a, h_one, grad_a)
    keep, send, stats, *sums = qkv_back(
        core_arg, tokens, x_other, grad_b, grad_a, w_b, w_a, vectors
    )
    output = close_output(
        places, tokens, projected, bias_down.astype(F32)[:, None], low_own, high_own, low_got, high_got
    )
    send_a, keep_a, keep, send, stats, sums, output = meet(
        (send_a, keep_a, keep, send, stats, sums, output), put_b, put_p, put_q
    )
    put_a = Scatter(send_a, (side, near, far))
    put_a.kept = keep_a
    got = swap(send)
    total = meet(vector_parts(sums), put_a)
    total = total + flip(total, 1)
    total = meet(total, put_a, put_b)
    total = total + flip(total, side)
    total = meet(total, put_a)
    total = total + flip(total, near)
    total = meet(total, put_a, put_b)
    total = total + flip(total, far)
    got, total = meet((got, total))
    grad_tokens = close_tokens(places, tokens, gp, gp_got, keep, got, stats, vectors)
    sum_up_p, sum_down_p = put_p.result()
    sum_up_q, sum_down_q = put_q.result()
    low_b, high_b = put_b.result()
    sum_a = jnp.concatenate(put_a.result(), 1).reshape(block, 3, rows_a)
    out_cols = half_lanes(own)
    sum_out = jnp.concatenate((low_b[:, cols_b:], high_b[:, cols_b + 2 * out_cols - own :]), 1)
    sum_b = jnp.concatenate((low_b[:, :cols_b], high_b[:, cols_b - skip : cols_b]), 1)
    sum_b = sum_b.reshape(block, 3, rows_b)[:, :, : rows_b - rest]
    sum_w_qkv = heads_back(jnp.concatenate((sum_a, sum_b), 2))

    two = total[:5, :own] + swap(total[:5, own:])
    vec = [
        jnp.concatenate(
            (total[6, i * rows_a : (i + 1) * rows_a], total[5, i * rows_b : (i + 1) * rows_b - rest])
        )
        for i in (0, 2)
    ]
    return (
        output,
        grad_tokens,
        two[0],
        two[1],
        sum_w_qkv,
        heads_back(jnp.stack(vec)),
        sum_out,
        two[4],
        two[2],
        two[3],
        jnp.concatenate((sum_up_p, sum_up_q), 1),
        jnp.concatenate((total[8], total[9]))[:hidden],
        jnp.concatenate((sum_down_p, sum_down_q), 1).T,
        total[7, :own],
    )


def solution(mesh):
    in_specs = (
        P("narrow", "wide"),
        P("wide", None),
        P("narrow"),
        P("narrow"),
        P("wide", None, "narrow"),
        P(None, "narrow"),
        P("wide", "narrow"),
        P("narrow"),
        P("narrow"),
        P("narrow"),
        P("wide", "narrow"),
        P("narrow"),
        P("narrow", "wide"),
        P("narrow"),
        P("narrow", "wide"),
    )
    out_specs = (
        P("narrow", "wide"),
        P("narrow", "wide"),
        P("narrow"),
        P("narrow"),
        P("wide", None, "narrow"),
        P(None, "narrow"),
        P("wide", "narrow"),
        P("narrow"),
        P("narrow"),
        P("narrow"),
        P("wide", "narrow"),
        P("narrow"),
        P("narrow", "wide"),
        P("narrow"),
    )
    paired = mesh.shape["narrow"] == 2 and mesh.shape["wide"] == 16
    return jax.shard_map(
        pair_plan if paired else any_mesh, mesh=mesh, in_specs=in_specs, out_specs=out_specs, check_vma=False
    )
```

```python
import functools
import math
from functools import partial

import jax
import jax.numpy as jnp
from jax import lax
from jax.experimental import pallas as pl
from jax.experimental.pallas import tpu as pltpu
from jax.sharding import PartitionSpec as P

HEADS = 17
PIECE = 256


EPSILON = 1e-05


def normalize(row_data, gain_vec, shift_vec):
    centre = jnp.mean(row_data, axis=-1, keepdims=True)
    centred = row_data - centre
    spread = jnp.mean(centred * centred, axis=-1, keepdims=True)
    return centred * lax.rsqrt(spread + EPSILON) * gain_vec + shift_vec


def norm_back(row_data, gain_vec, shift_vec, grad_rows):
    unused, pull_back = jax.vjp(normalize, row_data, gain_vec, shift_vec)
    return pull_back(grad_rows)


def full_rows(partial_rows):
    return lax.psum(partial_rows, "narrow")


def visible_mask(starts, query_pos, key_pos):
    query_in = (query_pos[:, None] >= starts[None, :]) & (
        query_pos[:, None] < starts[None, :] + PIECE
    )
    key_in = (key_pos[:, None] >= starts[None, :]) & (key_pos[:, None] < starts[None, :] + PIECE)
    shared = jnp.any(query_in[:, None, :] & key_in[None, :, :], axis=-1)
    return (key_pos[None, :] <= query_pos[:, None]) | shared


def to_heads(matrix):
    return matrix.reshape(matrix.shape[0], HEADS, matrix.shape[1] // HEADS)


def attention_scores(query_rows, key_full, visible, score_scale):
    raw = (
        jnp.einsum(
            "qhd,khd->hqk",
            to_heads(query_rows),
            to_heads(key_full),
            preferred_element_type=jnp.float32,
        )
        * score_scale
    )
    return jnp.where(visible[None], raw, -1e30)


def any_mesh(
    tokens,
    piece_starts,
    ln1_gain,
    ln1_bias,
    w_qkv,
    bias_qv,
    w_out,
    bias_out,
    ln2_gain,
    ln2_bias,
    w_up,
    bias_up,
    w_down,
    bias_down,
    cotangent,
):
    narrow_size = lax.axis_size("narrow")
    narrow_rank = lax.axis_index("narrow")
    col_width, length = tokens.shape
    full_width = col_width * narrow_size
    queries = length // narrow_size
    score_scale = (full_width // HEADS) ** (-0.5)
    col_start = narrow_rank * col_width
    row_start = narrow_rank * queries

    def own_cols(matrix):
        return lax.dynamic_slice_in_dim(matrix, col_start, col_width, matrix.ndim - 1)

    x_cols, dy_cols, gain_one, shift_one, gain_two, shift_two = (
        lax.all_gather(tokens, "narrow", axis=0, tiled=True),
        lax.all_gather(cotangent, "narrow", axis=0, tiled=True),
        lax.all_gather(ln1_gain, "narrow", axis=0, tiled=True),
        lax.all_gather(ln1_bias, "narrow", axis=0, tiled=True),
        lax.all_gather(ln2_gain, "narrow", axis=0, tiled=True),
        lax.all_gather(ln2_bias, "narrow", axis=0, tiled=True),
    )
    x_rows = x_cols.T
    dy_rows = dy_cols.T
    qkv_cols, out_cols, up_cols, down_rows = (
        lax.all_gather(w_qkv, "wide", axis=0, tiled=True),
        lax.all_gather(w_out, "wide", axis=0, tiled=True),
        lax.all_gather(w_up, "wide", axis=0, tiled=True),
        lax.all_gather(w_down, "wide", axis=1, tiled=True),
    )
    gain_one = gain_one.astype(jnp.float32)
    shift_one = shift_one.astype(jnp.float32)
    gain_two = gain_two.astype(jnp.float32)
    shift_two = shift_two.astype(jnp.float32)
    x_full = x_rows.astype(jnp.float32)
    h_one = normalize(x_full, gain_one, shift_one).astype(jnp.bfloat16)
    mixed = jnp.einsum("td,dcf->tcf", h_one, qkv_cols, preferred_element_type=jnp.float32)
    bias_cols = bias_qv.astype(jnp.float32)
    query_cols = (mixed[:, 0] + bias_cols[0]).astype(jnp.bfloat16)
    key_cols = mixed[:, 1].astype(jnp.bfloat16)
    value_cols = (mixed[:, 2] + bias_cols[1]).astype(jnp.bfloat16)
    query_full, key_full, value_full = (
        lax.all_gather(query_cols, "narrow", axis=1, tiled=True),
        lax.all_gather(key_cols, "narrow", axis=1, tiled=True),
        lax.all_gather(value_cols, "narrow", axis=1, tiled=True),
    )
    query_rows = lax.dynamic_slice_in_dim(query_full, row_start, queries, 0)
    query_pos = row_start + jnp.arange(queries, dtype=jnp.int32)
    key_pos = jnp.arange(length, dtype=jnp.int32)
    visible = visible_mask(piece_starts[0], query_pos, key_pos)
    masked = attention_scores(query_rows, key_full, visible, score_scale)
    row_top = jnp.max(masked, axis=-1, keepdims=True)
    weights = jnp.exp(masked - row_top)
    row_total = jnp.sum(weights, axis=-1, keepdims=True)
    log_total = row_top + jnp.log(row_total)
    probs_low = (weights / row_total).astype(jnp.bfloat16)
    context = jnp.einsum(
        "hqk,khd->qhd", probs_low, to_heads(value_full), preferred_element_type=jnp.float32
    )
    context = context.reshape(queries, full_width).astype(jnp.bfloat16)
    context_full = lax.all_gather(context, "narrow", axis=0, tiled=True)
    projected = jnp.dot(
        context_full, out_cols, preferred_element_type=jnp.float32
    ) + bias_out.astype(jnp.float32)
    projected_low = projected.astype(jnp.bfloat16)
    projected_full = lax.all_gather(projected_low, "narrow", axis=1, tiled=True)
    mid_full = x_full + projected_full.astype(jnp.float32)
    mid_rows = tokens.T.astype(jnp.float32) + projected_low.astype(jnp.float32)
    h_two = normalize(mid_full, gain_two, shift_two).astype(jnp.bfloat16)
    up_pre = jnp.dot(h_two, up_cols, preferred_element_type=jnp.float32) + bias_up.astype(
        jnp.float32
    )
    act_value, gelu_pull = jax.vjp(partial(jax.nn.gelu, approximate=True), up_pre)
    act_low = act_value.astype(jnp.bfloat16)
    partial_down = jnp.dot(act_low, down_rows, preferred_element_type=jnp.float32)
    down_sum = lax.psum_scatter(
        partial_down.astype(jnp.bfloat16), "narrow", scatter_dimension=1, tiled=True
    ).astype(jnp.float32)
    output = (mid_rows + (down_sum + bias_down.astype(jnp.float32))).astype(jnp.bfloat16)
    grad_out = cotangent.T.astype(jnp.float32)
    grad_bias_down = jnp.sum(grad_out, axis=0)
    grad_w_down = jnp.einsum("tf,td->fd", act_low, dy_rows, preferred_element_type=jnp.float32)
    grad_act = jnp.einsum("td,fd->tf", dy_rows, down_rows, preferred_element_type=jnp.float32)
    grad_up = gelu_pull(grad_act)[0].astype(jnp.bfloat16)
    grad_bias_up = jnp.sum(grad_up.astype(jnp.float32), axis=0)
    grad_w_up = jnp.einsum("td,tf->df", h_two, grad_up, preferred_element_type=jnp.float32)
    grad_h_two = full_rows(
        jnp.einsum("tf,df->td", grad_up, up_cols, preferred_element_type=jnp.float32)
    )
    grad_mid_full, grad_gain_two, grad_shift_two = norm_back(
        mid_full, gain_two, shift_two, grad_h_two
    )
    grad_mid = grad_out + own_cols(grad_mid_full)
    grad_projected = grad_mid.astype(jnp.bfloat16)
    grad_bias_out = jnp.sum(grad_projected.astype(jnp.float32), axis=0)
    grad_w_out = jnp.einsum(
        "td,tc->dc", context_full, grad_projected, preferred_element_type=jnp.float32
    )
    grad_context = lax.psum_scatter(
        jnp.einsum("tc,dc->td", grad_projected, out_cols, preferred_element_type=jnp.float32),
        "narrow",
        scatter_dimension=0,
        tiled=True,
    ).astype(jnp.bfloat16)
    weights_back = jnp.exp(masked - log_total)
    context_heads = to_heads(grad_context)
    grad_probs = jnp.einsum(
        "qhd,khd->hqk", context_heads, to_heads(value_full), preferred_element_type=jnp.float32
    )
    centre = jnp.sum(weights_back * grad_probs, axis=-1, keepdims=True)
    grad_scores = (weights_back * (grad_probs - centre)).astype(jnp.bfloat16)
    grad_query = jnp.einsum(
        "hqk,khd->qhd", grad_scores, to_heads(key_full), preferred_element_type=jnp.float32
    )
    grad_query = grad_query.reshape(queries, full_width) * score_scale
    probs_back = weights_back.astype(jnp.bfloat16)
    grad_key = jnp.einsum(
        "hqk,qhd->khd", grad_scores, to_heads(query_rows), preferred_element_type=jnp.float32
    )
    grad_key = grad_key.reshape(length, full_width) * score_scale
    grad_value = jnp.einsum(
        "hqk,qhd->khd", probs_back, context_heads, preferred_element_type=jnp.float32
    )
    grad_value = grad_value.reshape(length, full_width)
    placed = jnp.zeros((length, full_width), jnp.float32)
    placed = lax.dynamic_update_slice_in_dim(placed, grad_query, row_start, 0)
    stacked = jnp.stack((placed, grad_key, grad_value), axis=1)
    grad_mixed = lax.psum_scatter(stacked, "narrow", scatter_dimension=2, tiled=True).astype(
        jnp.bfloat16
    )
    grad_mixed_f = grad_mixed.astype(jnp.float32)
    grad_bias_qv = jnp.stack(
        (jnp.sum(grad_mixed_f[:, 0], axis=0), jnp.sum(grad_mixed_f[:, 2], axis=0))
    )
    grad_w_qkv = jnp.einsum("td,tcf->dcf", h_one, grad_mixed, preferred_element_type=jnp.float32)
    grad_h_one = full_rows(
        jnp.einsum("tcf,dcf->td", grad_mixed, qkv_cols, preferred_element_type=jnp.float32)
    )
    grad_x_full, grad_gain_one, grad_shift_one = norm_back(x_full, gain_one, shift_one, grad_h_one)
    grad_tokens = grad_mid + own_cols(grad_x_full)
    sum_w_qkv, sum_w_out, sum_w_up, sum_w_down = (
        lax.psum_scatter(grad_w_qkv, "wide", scatter_dimension=0, tiled=True),
        lax.psum_scatter(grad_w_out, "wide", scatter_dimension=0, tiled=True),
        lax.psum_scatter(grad_w_up, "wide", scatter_dimension=0, tiled=True),
        lax.psum_scatter(grad_w_down, "wide", scatter_dimension=1, tiled=True),
    )
    (
        sum_gain_one,
        sum_shift_one,
        sum_bias_qv,
        sum_bias_out,
        sum_gain_two,
        sum_shift_two,
        sum_bias_up,
        sum_bias_down,
    ) = lax.psum(
        (
            own_cols(grad_gain_one),
            own_cols(grad_shift_one),
            grad_bias_qv,
            grad_bias_out,
            own_cols(grad_gain_two),
            own_cols(grad_shift_two),
            grad_bias_up,
            grad_bias_down,
        ),
        "wide",
    )
    return (
        output.T,
        grad_tokens.T,
        sum_gain_one,
        sum_shift_one,
        sum_w_qkv,
        sum_bias_qv,
        sum_w_out,
        sum_bias_out,
        sum_gain_two,
        sum_shift_two,
        sum_w_up,
        sum_bias_up,
        sum_w_down,
        sum_bias_down,
    )


F32 = jnp.float32
BF16 = jnp.bfloat16
HEAD = 64
TILE = 256
MIB = 1 << 20
LANES = 128
SPARE = 16
PACE = 1e-6


def dot(a, b, dim_a, dim_b):
    return lax.dot_general(a, b, (((dim_a,), (dim_b,)), ((), ())), preferred_element_type=F32)


def after(value, *others):
    return lax.optimization_barrier((value,) + others)[0]


def cost(flops, moved):
    return pl.CostEstimate(flops=1 + int(PACE * flops), bytes_accessed=1 + int(PACE * moved), transcendentals=0)


def params(mib):
    return pltpu.CompilerParams(vmem_limit_bytes=mib * MIB)


def in_turns(stages, items):
    states = [None] * len(items)
    for tick in range(len(items) + len(stages) - 1):
        for j, stage in enumerate(stages):
            i = tick - j
            if 0 <= i < len(items):
                states[i] = stage(items[i], states[i])


def lane_sums(a):
    return functools.reduce(
        jnp.add, [a[:, i : i + LANES] for i in range(0, a.shape[1], LANES)]
    )


def row_sums(acc):
    return jnp.concatenate(
        [
            jnp.sum(acc[:, i : i + LANES].T, axis=0, keepdims=True)
            for i in range(0, acc.shape[1], LANES)
        ],
        0,
    )


def rows_at(start, size):
    return pl.ds(pl.multiple_of(start, HEAD // 2), size)


def first_step():
    return pl.program_id(0) == 0


def last_step():
    return pl.program_id(0) == pl.num_programs(0) - 1


def unit(rows, a, b):
    mine = rows == 0
    return jnp.where(mine, a, b), jnp.where(mine, b, a)


def bias_kernel(starts_ref, bias_ref):
    length = bias_ref.shape[0] * TILE
    for i in range(length // TILE):
        low = i * TILE
        rows = min(2 * TILE, length - low)
        key = low + lax.broadcasted_iota(jnp.int32, (rows, TILE), 0)
        query = low + lax.broadcasted_iota(jnp.int32, (rows, TILE), 1)
        seen = key <= query
        for p in range(starts_ref.shape[0]):
            s = starts_ref[p]
            seen = seen | (
                (key >= s) & (key < s + PIECE) & (query >= s) & (query < s + PIECE)
            )
        bias_ref[i, :rows, :] = jnp.where(seen, 0.0, -1e30)


def mask_bias(starts, length):
    shape = (length // TILE, 2 * TILE, TILE)
    return pl.pallas_call(
        bias_kernel,
        in_specs=[pl.BlockSpec(memory_space=pltpu.SMEM)],
        out_specs=pl.BlockSpec(memory_space=pltpu.VMEM),
        out_shape=jax.ShapeDtypeStruct(shape, F32),
        compiler_params=params(16),
        name="mask_bias",
    )(starts)


def spans(i, length):
    low = i * TILE
    high = min(low + 2 * TILE, length)
    return ((0, low), (low, high)) if low > 0 else ((low, high),)


def scores(key_rows, query, bias, i, span):
    s = dot(key_rows[span[0] : span[1]], query, 1, 0)
    return s if span[0] < i * TILE else s + bias[i, : span[1] - span[0], :]


def attend_kernel(bias, x_ref, c_ref, l_ref, key_rows):
    length = x_ref.shape[2]
    key_rows[...] = x_ref[1].T

    def score(i, _):
        query = x_ref[0, :, pl.ds(i * TILE, TILE)] * jnp.asarray(HEAD**-0.5, BF16)
        return [(span, scores(key_rows, query, bias, i, span)) for span in spans(i, length)]

    def weigh(i, parts):
        here = pl.ds(i * TILE, TILE)
        top = functools.reduce(
            jnp.maximum, [jnp.max(s, axis=0, keepdims=True) for _, s in parts]
        )
        total, acc = 0.0, 0.0
        for span, s in parts:
            p = jnp.exp(s - top)
            total = total + jnp.sum(p, axis=0, keepdims=True)
            acc = acc + dot(x_ref[2, :, span[0] : span[1]], p.astype(BF16), 1, 0)
        c_ref[:, here] = (acc / total).astype(BF16)
        l_ref[0, :, here] = top + jnp.log(total)

    in_turns((score, weigh), range(length // TILE))


def attend(bias, qkv, first, count):
    length = qkv.shape[2]
    return pl.pallas_call(
        attend_kernel,
        grid=(count,),
        in_specs=[
            pl.BlockSpec(bias.shape, lambda h: (0, 0, 0)),
            pl.BlockSpec((3, HEAD, length), lambda h: (0, h + first, 0)),
        ],
        out_specs=[
            pl.BlockSpec((HEAD, length), lambda h: (h, 0)),
            pl.BlockSpec((1, 1, length), lambda h: (h, 0, 0)),
        ],
        scratch_shapes=[pltpu.VMEM((length, HEAD), BF16)],
        out_shape=[
            jax.ShapeDtypeStruct((count * HEAD, length), BF16),
            jax.ShapeDtypeStruct((count, 1, length), F32),
        ],
        compiler_params=params(24),
        cost_estimate=cost(4e9 * count, count * length * HEAD * 8),
        name="attend",
    )(bias, qkv)


def attend_back_kernel(
    shared, rank_ref, bias, x_ref, mine_ref, got_ref, l_ref, old_ref, g_ref,
    key_rows, value_rows, query_rows, grad_rows, grad, key_sum, value_sum,
):
    length = x_ref.shape[2]
    share = length // 2
    scale = jnp.asarray(HEAD**-0.5, BF16)
    first = rank_ref[0] == 0
    mine, got = mine_ref[...], got_ref[...]
    grad[:, :share] = jnp.where(first, mine, got)
    grad[:, share:] = jnp.where(first, got, mine)
    key_rows[...] = x_ref[1].T
    value_rows[...] = x_ref[2].T
    grad_rows[...] = grad[...].T
    query_rows[...] = (x_ref[0] * scale).T
    tiles = length // TILE

    def score(i, _):
        here = pl.ds(i * TILE, TILE)
        query, out = x_ref[0, :, here] * scale, grad[:, here]
        return [
            (span, scores(key_rows, query, bias, i, span), dot(value_rows[span[0] : span[1]], out, 1, 0))
            for span in spans(i, length)
        ]

    def weigh(i, parts):
        lse = l_ref[0, :, pl.ds(i * TILE, TILE)]
        weights = [jnp.exp(s - lse) for _, s, _ in parts]
        centre = functools.reduce(
            jnp.add, [jnp.sum(p * g, axis=0, keepdims=True) for p, (_, _, g) in zip(weights, parts)]
        )
        return [
            (span, p.astype(BF16), (p * (g - centre)).astype(BF16))
            for p, (span, _, g) in zip(weights, parts)
        ]

    def gather(i, parts):
        here = pl.ds(i * TILE, TILE)
        dq = 0.0
        for (low, high), p, gs in parts:
            dq = dq + dot(x_ref[1, :, low:high], gs, 1, 0)
            dk, dv = dot(gs, query_rows[here], 1, 0), dot(p, grad_rows[here], 1, 0)
            if i == tiles - 1:
                key_sum[low:high], value_sum[low:high] = dk, dv
            else:
                key_sum[low:high] += dk
                value_sum[low:high] += dv
        g_ref[0, :, here] = (dq * HEAD**-0.5).astype(BF16)

    in_turns((score, weigh, gather), list(reversed(range(tiles))))
    g_ref[1] = key_sum[...].T.astype(BF16)
    g_ref[2] = value_sum[...].T.astype(BF16)
    if shared:
        @pl.when(pl.program_id(0) == pl.num_programs(0) - 1)
        def _():
            g_ref[:, HEAD // 2 :, :] = jnp.zeros((3, HEAD // 2, length), BF16)


def attend_back(bias, rank, qkv, mine, got, lse, first, count, shared, old=None):
    length = qkv.shape[2]
    rows = pltpu.VMEM((length, HEAD), BF16)
    sums = pltpu.VMEM((length, HEAD), F32)
    heads = pl.BlockSpec((3, HEAD, length), lambda h, r: (0, h + first, 0))
    half = pl.BlockSpec((HEAD, length // 2), lambda h, r: (h + first, 0))
    alias = {}
    if old is not None:
        alias = {6: 0}
    else:
        old = jnp.zeros((8, 128), BF16)
    return pl.pallas_call(
        functools.partial(attend_back_kernel, shared),
        grid_spec=pltpu.PrefetchScalarGridSpec(
            num_scalar_prefetch=1,
            grid=(count,),
            in_specs=[
                pl.BlockSpec(bias.shape, lambda h, r: (0, 0, 0)),
                heads,
                half,
                half,
                pl.BlockSpec((1, 1, length), lambda h, r: (h + first, 0, 0)),
                pl.BlockSpec(memory_space=pl.ANY),
            ],
            out_specs=[heads],
            scratch_shapes=[rows] * 4
            + [pltpu.VMEM((HEAD, length), BF16)]
            + [sums] * 2,
        ),
        out_shape=[jax.ShapeDtypeStruct(qkv.shape, BF16)],
        input_output_aliases=alias,
        compiler_params=params(34),
        cost_estimate=cost(6.8e9 * count, count * length * HEAD * 14),
        name="attend_back",
    )(rank, bias, qkv, mine, got, lse, old)[0]


def norm_rows(x):
    x = x - jnp.mean(x, axis=0, keepdims=True)
    inv = lax.rsqrt(jnp.mean(x * x, axis=0, keepdims=True) + EPSILON)
    return x * inv, inv


def own_first(rank, a):
    half = a.shape[0] // 2
    return jnp.where(rank == 0, a, jnp.concatenate((a[half:], a[:half]), 0))


def half_lanes(columns):
    return -(-columns // (2 * LANES)) * LANES


def turn_weights(core, mine, got, turned):
    a, b = unit(core, mine, got)
    count = a.shape[1]
    turned[:count] = a.T
    turned[count:] = b.T[2 * count - turned.shape[0] :]


def norm_qkv_kernel(core_ref, xo_ref, xt_ref, m_ref, g_ref, v_ref, b_ref, h_ref, q_ref, turned):
    @pl.when(first_step())
    def _():
        turn_weights(core_ref[0], m_ref[...], g_ref[...], turned)

    x = jnp.concatenate((xo_ref[...], xt_ref[...]), 0).astype(F32)
    h = (norm_rows(x)[0] * v_ref[:, 0:1] + v_ref[:, 1:2]).astype(BF16)
    h_ref[...] = h
    q_ref[...] = (dot(turned[...], h, 1, 0) + b_ref[...]).astype(BF16)


def norm_qkv(core, x_own, x_other, mine, got, vectors, bias):
    own, length = x_own.shape
    depth = 2 * own
    rows = bias.shape[0]
    column = lambda n: pl.BlockSpec((n, TILE), lambda i, s: (0, i))
    whole = lambda a: pl.BlockSpec(a.shape, lambda i, s: (0, 0))
    return pl.pallas_call(
        norm_qkv_kernel,
        grid_spec=pltpu.PrefetchScalarGridSpec(
            num_scalar_prefetch=1,
            grid=(length // TILE,),
            in_specs=[column(own)] * 2 + [whole(a) for a in (mine, got, vectors, bias)],
            out_specs=[column(depth), column(rows)],
            scratch_shapes=[pltpu.VMEM((rows, depth), BF16)],
        ),
        out_shape=[jax.ShapeDtypeStruct((n, length), BF16) for n in (depth, rows)],
        compiler_params=params(60),
        cost_estimate=cost(2 * depth * rows * length, depth * length * 6),
        name="norm_qkv",
    )(core, x_own, x_other, mine, got, vectors, bias)


def qkv_kernel(core_ref, h_ref, m_ref, g_ref, b_ref, q_ref, turned):
    @pl.when(first_step())
    def _():
        turn_weights(core_ref[0], m_ref[...], g_ref[...], turned)

    q_ref[...] = (dot(turned[...], h_ref[...], 1, 0) + b_ref[...]).astype(BF16)


def qkv_of(core, h_one, mine, got, bias):
    depth, length = h_one.shape
    rows = bias.shape[0]
    column = lambda n: pl.BlockSpec((n, TILE), lambda i, s: (0, i))
    whole = lambda a: pl.BlockSpec(a.shape, lambda i, s: (0, 0))
    return pl.pallas_call(
        qkv_kernel,
        grid_spec=pltpu.PrefetchScalarGridSpec(
            num_scalar_prefetch=1,
            grid=(length // TILE,),
            in_specs=[column(depth)] + [whole(a) for a in (mine, got, bias)],
            out_specs=column(rows),
            scratch_shapes=[pltpu.VMEM((rows, depth), BF16)],
        ),
        out_shape=jax.ShapeDtypeStruct((rows, length), BF16),
        compiler_params=params(24),
        cost_estimate=cost(2 * depth * rows * length, depth * length * 4),
        name="qkv",
    )(core, h_one, mine, got, bias)


def project_kernel(
    spot_ref, xo_ref, xt_ref, a_ref, b_ref, d_ref, ga_ref, gb_ref, gd_ref, c_ref, m_ref, g_ref, v_ref,
    p_ref, h_ref, c_out, turned,
):
    @pl.when(first_step())
    def _():
        own = xo_ref.shape[0]
        parts = [own_first(spot_ref[0], w[:, :own]) for w in (m_ref, g_ref)]
        turn_weights(spot_ref[1], *parts, turned)

    rank = spot_ref[0]
    own = xo_ref.shape[0]
    half, whole = HEAD // 2, own - HEAD // 2
    for refs, at in (((a_ref, b_ref, d_ref), half * rank), ((ga_ref, gb_ref, gd_ref), own + half * (1 - rank))):
        for ref in refs:
            c_out[rows_at(at, ref.shape[0])] = ref[...]
            at = at + ref.shape[0]
    c_out[rows_at(whole * (1 - rank), half)] = c_ref[:half]
    c_out[rows_at(own + whole * rank, half)] = c_ref[half:]
    low = (dot(turned[...], c_out[...], 1, 0) + v_ref[:, 4:5]).astype(BF16)
    p_ref[...] = low
    mid = jnp.concatenate((xo_ref[...], xt_ref[...]), 0).astype(F32) + low.astype(F32)
    h_ref[...] = (norm_rows(mid)[0] * v_ref[:, 2:3] + v_ref[:, 3:4]).astype(BF16)


def out_columns(depth):
    return pl.BlockSpec((depth, -(-depth // (2 * LANES)) * LANES), lambda i, s: (0, 0))


def project(spot, x_own, x_other, pieces, mine, got, vectors):
    own, length = x_own.shape
    depth = 2 * own
    column = lambda rows: pl.BlockSpec((rows, TILE), lambda i, s: (0, i))
    whole = lambda a: pl.BlockSpec(a.shape, lambda i, s: (0, 0))
    return pl.pallas_call(
        project_kernel,
        grid_spec=pltpu.PrefetchScalarGridSpec(
            num_scalar_prefetch=1,
            grid=(length // TILE,),
            in_specs=[column(own)] * 2
            + [column(p.shape[0]) for p in pieces]
            + [out_columns(depth)] * 2
            + [whole(vectors)],
            out_specs=[column(depth)] * 3,
            scratch_shapes=[pltpu.VMEM((depth, depth), BF16)],
        ),
        out_shape=[jax.ShapeDtypeStruct((depth, length), BF16)] * 3,
        compiler_params=params(60),
        cost_estimate=cost(2 * depth * depth * length, depth * length * 10),
        name="project",
    )(spot, x_own, x_other, *pieces, mine, got, vectors)


def feed_kernel(
    spot_ref, h_ref, go_ref, gt_ref, pm_ref, pg_ref, qm_ref, qg_ref, bias_ref, *rest
):
    mid_ref, own_ref, other_ref, gh_ref, gb_ref, gs_ref, up, down, sums, sems = rest[-10:]
    split = up.shape[1] - qm_ref.shape[1]
    lead = pm_ref.shape[1] - split
    hidden = up.shape[1]

    @pl.when(pl.program_id(0) == 0)
    def _():
        half = up.shape[0] // 2

        def copies(up_p, up_q, down_p, down_q):
            made = []
            for i, (first, second, whole) in enumerate(((up_p, up_q, up), (down_p, down_q, down))):
                for j in range(2):
                    rows = pl.ds(half * j, half)
                    to = rows_at(half * (j ^ spot_ref[2]), half)
                    at = 4 * i + 2 * j
                    made += [
                        pltpu.make_async_copy(
                            first.at[rows, lead:], whole.at[to, :split], sems.at[at]
                        ),
                        pltpu.make_async_copy(
                            second.at[rows, :], whole.at[to, split:], sems.at[at + 1]
                        ),
                    ]
            return made

        def bring(these):
            for c in these:
                c.start()
            for c in these:
                c.wait()

        @pl.when(spot_ref[1] == 0)
        def _():
            bring(copies(pm_ref, qm_ref, pg_ref, qg_ref))

        @pl.when(spot_ref[1] == 1)
        def _():
            bring(copies(pg_ref, qg_ref, pm_ref, qm_ref))

        gb_ref[...] = jnp.zeros_like(gb_ref)
        sums[...] = jnp.zeros_like(sums)

    sums[...] += lane_sums(go_ref[...].astype(F32))

    @pl.when(last_step())
    def _():
        gs_ref[...] = row_sums(sums[...])

    root = (2 / jnp.pi) ** 0.5
    h = h_ref[...]
    g = jnp.concatenate((go_ref[...], gt_ref[...]), 0)
    for span in (slice(0, split), slice(split, hidden)):
        u = dot(h, up[:, span], 0, 0) + bias_ref[:, span]
        grad_act = dot(g, down[:, span], 0, 0)
        square = u * u
        t = jnp.tanh(u * (root + (root * 0.044715) * square))
        half = 0.5 + 0.5 * t
        mid_ref[0, :, span] = (u * half).astype(BF16)
        slope = half + (0.5 * u) * (1 - t * t) * (root + (3 * root * 0.044715) * square)
        gup = (grad_act * slope).astype(BF16)
        mid_ref[1, :, span] = gup
        gb_ref[:, span] += jnp.sum(gup.astype(F32), axis=0, keepdims=True)
    gh_ref[...] = dot(up[...], mid_ref[1], 1, 1).astype(BF16)
    out = dot(down[...], mid_ref[0], 1, 1).astype(BF16)
    n = own_ref.shape[0]
    own_ref[...], other_ref[...] = out[:n], out[n:]


def feed(spot, count, h_two, g_own, g_other, weights, bias_up, tile, old):
    depth, length = h_two.shape
    own = g_own.shape[0]
    hidden = bias_up.shape[1]
    column = lambda rows: pl.BlockSpec((rows, tile), lambda i, s: (0, s[0] + i))
    anywhere = pl.BlockSpec(memory_space=pl.ANY)
    vector = pl.BlockSpec((1, hidden), lambda i, s: (0, 0))
    local = lambda rows: pl.BlockSpec((rows, tile), lambda i, s: (0, i))
    aliases = {} if old is None else {9: 0}
    return pl.pallas_call(
        feed_kernel,
        grid_spec=pltpu.PrefetchScalarGridSpec(
            num_scalar_prefetch=1,
            grid=(count,),
            in_specs=[column(depth), column(own), column(own)]
            + [anywhere] * 4
            + [vector]
            + [anywhere] * len(aliases),
            out_specs=[
                pl.BlockSpec((2, tile, hidden), lambda i, s: (0, s[0] + i, 0)),
                local(own),
                local(own),
                local(depth),
                vector,
                pl.BlockSpec((1, own), lambda i, s: (0, 0)),
            ],
            scratch_shapes=[
                pltpu.VMEM((depth, hidden), BF16),
                pltpu.VMEM((depth, hidden), BF16),
                pltpu.VMEM((own, LANES), F32),
                pltpu.SemaphoreType.DMA((8,)),
            ],
        ),
        out_shape=[
            jax.ShapeDtypeStruct((2, length, hidden), BF16),
            *(jax.ShapeDtypeStruct((n, count * tile), BF16) for n in (own, own, depth)),
            jax.ShapeDtypeStruct((1, hidden), F32),
            jax.ShapeDtypeStruct((1, own), F32),
        ],
        input_output_aliases=aliases,
        compiler_params=params(50),
        cost_estimate=cost(8 * depth * count * tile * hidden, 12 * depth * hidden),
        name="feed",
    )(spot, h_two, g_own, g_other, *weights, bias_up, *([] if old is None else [old]))


def weight_grad_kernel(which_ref, h_ref, go_ref, gt_ref, m_ref, *rest):
    rest, (lhs, rhs, sems) = rest[:-3], rest[-3:]
    half = lhs.shape[1]
    step = pl.program_id(0)
    split = rest[0].shape[1]
    columns = (slice(0, split), slice(split, rhs.shape[1]))
    which = which_ref[0]

    def part(i):
        return pltpu.make_async_copy(h_ref.at[pl.ds(half * i, half)], lhs.at[i], sems.at[i])

    def column(i):
        return pltpu.make_async_copy(m_ref.at[which, :, columns[i]], rhs.at[:, columns[i]], sems.at[2 + i])

    @pl.when(first_step())
    def _():
        @pl.when(which == 0)
        def _():
            for i, g in enumerate((go_ref, gt_ref)):
                pltpu.make_async_copy(g, lhs.at[i], sems.at[i]).start()

        @pl.when(which == 1)
        def _():
            for i in range(2):
                part(i).start()

        column(0).start()
        column(1).start()
        part(0).wait()
        column(0).wait()

    @pl.when(last_step())
    def _():
        part(1).wait()

    rows = lhs[step]
    p = dot(rows, rhs[:, columns[0]], 1, 0)

    @pl.when(first_step())
    def _():
        column(1).wait()

    q = dot(rows, rhs[:, columns[1]], 1, 0)
    if len(rest) == 2:
        rest[0][...], rest[1][...] = p.astype(BF16), q.astype(BF16)
        return
    pg_ref, qg_ref, pk_ref, pa_ref, qk_ref, qa_ref = rest
    p = (p + pg_ref[...].astype(F32)).astype(BF16)
    q = (q + qg_ref[...].astype(F32)).astype(BF16)
    n = p.shape[0] // 4
    low = jnp.concatenate((p[:n], p[2 * n : 3 * n]), 0)
    high = jnp.concatenate((p[n : 2 * n], p[3 * n :]), 0)
    pk_ref[...], pa_ref[...] = unit(which_ref[1], low, high)
    qk_ref[...], qa_ref[...] = unit(which_ref[2], q[: 2 * n], q[2 * n :])


def weight_grad(which, h_two, g_own, g_other, middle, split, got=None):
    depth, length = h_two.shape
    hidden = middle.shape[2]
    steps = 2
    rows = depth // steps
    parts = (split, hidden - split)
    blocks = [pl.BlockSpec((rows, n), lambda i, s: (i, 0)) for n in parts]
    in_specs = [pl.BlockSpec(memory_space=pl.ANY)] * 4
    out_specs, shapes = blocks, [jax.ShapeDtypeStruct((depth, n), BF16) for n in parts]
    if got is not None:
        in_specs += blocks
        out_specs = [pl.BlockSpec((rows // 2, n), lambda i, s: (i, 0)) for n in parts for _ in range(2)]
        shapes = [jax.ShapeDtypeStruct((depth // 2, n), BF16) for n in parts for _ in range(2)]
    return pl.pallas_call(
        weight_grad_kernel,
        grid_spec=pltpu.PrefetchScalarGridSpec(
            num_scalar_prefetch=1,
            grid=(steps,),
            in_specs=in_specs,
            out_specs=out_specs,
            scratch_shapes=[
                pltpu.VMEM((steps, rows, length), BF16),
                pltpu.VMEM((length, hidden), BF16),
                pltpu.SemaphoreType.DMA((4,)),
            ],
        ),
        out_shape=shapes,
        compiler_params=params(60),
        cost_estimate=cost(2 * depth * length * hidden, 2 * (2 * depth + hidden) * length),
        name="weight_grad",
    )(which, h_two, g_own, g_other, middle, *(got or ()))


def mid_back_kernel(
    spot_ref, xo_ref, xt_ref, p_ref, go_ref, gt_ref, keep_ref, got_ref, m_ref, g_ref, v_ref,
    gp_ref, gq_ref, ma_ref, mb_ref, sa_ref, sb_ref, n_ref, w_own, w_other, gc, sums,
):
    @pl.when(first_step())
    def _():
        n = w_own.shape[1]
        parts = [own_first(spot_ref[2], w[:, :n]) for w in (m_ref, g_ref)]
        w_own[...], w_other[...] = unit(spot_ref[1], *parts)
        sums[...] = jnp.zeros_like(sums)

    own = xo_ref.shape[0]
    rank = spot_ref[2]
    keep, got = keep_ref[...].astype(F32), got_ref[...].astype(F32)
    gh = keep + jnp.concatenate((got[own:], got[:own]), 0)
    mid = jnp.concatenate((xo_ref[...], xt_ref[...]), 0).astype(F32) + p_ref[...].astype(F32)
    hat, inv = norm_rows(mid)
    e = gh * v_ref[:, 2:3]
    grad = jnp.concatenate((go_ref[...], gt_ref[...]), 0).astype(F32) + inv * (
        e - jnp.mean(e, axis=0, keepdims=True) - hat * jnp.mean(e * hat, axis=0, keepdims=True)
    )
    gp = grad.astype(BF16)
    gp_ref[...], gq_ref[...] = gp[:own], gp[own:]
    gc[...] = (dot(w_own[...], gp[:own], 1, 0) + dot(w_other[...], gp[own:], 1, 0)).astype(BF16)
    half = HEAD // 2
    a, b = ma_ref.shape[0], mb_ref.shape[0] - HEAD
    near, away = half * rank, own + half * (1 - rank)
    own_half = gc[rows_at((a + b) * (1 - rank), half)]
    other_half = gc[rows_at(own + (a + b) * rank, half)]
    ma_ref[...] = gc[rows_at(near, a)]
    mb_ref[:b] = gc[rows_at(near + a, b)]
    mb_ref[b : b + half] = own_half
    mb_ref[b + half :] = other_half
    sa_ref[...] = gc[rows_at(away, a)]
    sb_ref[:b] = gc[rows_at(away + a, b)]
    sb_ref[b : b + half] = other_half
    sb_ref[b + half :] = own_half
    sums[...] += jnp.concatenate(
        (lane_sums(gh * hat), lane_sums(gh), lane_sums(gp.astype(F32))), 1
    )

    @pl.when(last_step())
    def _():
        n_ref[...] = row_sums(sums[...])


def mid_back(spot, x_own, x_other, projected, g_own, g_other, keep, got, mine, got_w, vectors, rows_a, rows_b):
    own, length = x_own.shape
    depth = 2 * own
    share = length // 2
    column = lambda rows: pl.BlockSpec((rows, TILE), lambda i, s: (0, s[0] + i))
    local = lambda rows: pl.BlockSpec((rows, TILE), lambda i, s: (0, i))
    whole = lambda a: pl.BlockSpec(a.shape, lambda i, s: (0, 0))
    out = lambda rows: jax.ShapeDtypeStruct((rows, share), BF16)
    sizes = (own, own, rows_a, rows_b, rows_a, rows_b)
    return pl.pallas_call(
        mid_back_kernel,
        grid_spec=pltpu.PrefetchScalarGridSpec(
            num_scalar_prefetch=1,
            grid=(share // TILE,),
            in_specs=[column(own), column(own), column(depth), column(own), column(own)]
            + [local(depth)] * 2
            + [out_columns(depth)] * 2
            + [whole(vectors)],
            out_specs=[local(r) for r in sizes] + [pl.BlockSpec((3, depth), lambda i, s: (0, 0))],
            scratch_shapes=[pltpu.VMEM((depth, own), BF16)] * 2
            + [pltpu.VMEM((depth, TILE), BF16), pltpu.VMEM((depth, 3 * LANES), F32)],
        ),
        out_shape=[out(r) for r in sizes] + [jax.ShapeDtypeStruct((3, depth), F32)],
        compiler_params=params(60),
        cost_estimate=cost(2 * depth * depth * share, depth * share * 16),
        name="mid_back",
    )(spot, x_own, x_other, projected, g_own, g_other, keep, got, mine, got_w, vectors)


def half_lanes(columns):
    return -(-columns // (2 * LANES)) * LANES


def grads_kernel(place_ref, h_ref, g_ref, send_ref, keep_ref):
    cols = send_ref.shape[1]
    low = dot(h_ref[...], g_ref[:cols], 1, 1).astype(BF16)
    high = dot(h_ref[...], g_ref[g_ref.shape[0] - cols :], 1, 1).astype(BF16)
    keep_ref[...], send_ref[...] = unit(place_ref[1], low, high)


def grads_out_kernel(place_ref, h_ref, c_ref, g_ref, pm_ref, pg_ref, send_ref, keep_ref, gp):
    @pl.when(first_step())
    def _():
        share = pm_ref.shape[1]
        gp[:, :share], gp[:, share:] = unit(place_ref[0], pm_ref[...], pg_ref[...])

    out = half_lanes(gp.shape[0])
    cols = send_ref.shape[1] - out
    for lhs, rhs, n, to in (
        (h_ref, g_ref, cols, slice(0, cols)),
        (c_ref, gp, out, slice(cols, cols + out)),
    ):
        low = dot(lhs[...], rhs[:n], 1, 1).astype(BF16)
        high = dot(lhs[...], rhs[rhs.shape[0] - n :], 1, 1).astype(BF16)
        keep_ref[:, to], send_ref[:, to] = unit(place_ref[1], low, high)


def column_grads(places, cols, h_one, grad, context=None, gp=None, gp_got=None):
    depth, length = h_one.shape
    kernel, total, scratch = grads_kernel, cols, []
    part = pl.BlockSpec((depth // 2, length), lambda i, s: (i, 0))
    whole = lambda a: pl.BlockSpec(a.shape, lambda i, s: (0, 0))
    args, specs = [h_one, grad], [part, whole(grad)]
    if context is not None:
        kernel, total = grads_out_kernel, cols + half_lanes(gp.shape[0])
        args = [h_one, context, grad, gp, gp_got]
        specs = [part, part] + [whole(a) for a in args[2:]]
        scratch = [pltpu.VMEM((gp.shape[0], length), BF16)]
    return pl.pallas_call(
        kernel,
        grid_spec=pltpu.PrefetchScalarGridSpec(
            num_scalar_prefetch=1,
            grid=(2,),
            in_specs=specs,
            out_specs=[pl.BlockSpec((depth // 2, total), lambda i, s: (i, 0))] * 2,
            scratch_shapes=scratch,
        ),
        out_shape=[jax.ShapeDtypeStruct((depth, total), BF16)] * 2,
        compiler_params=params(32),
        cost_estimate=cost(4 * depth * total * length, 6 * depth * length),
        name="column_grads",
    )(places, *args)


def output_kernel(
    place_ref, x_ref, p_ref, b_ref, low_ref, high_ref, low_got_ref, high_got_ref, o_ref
):
    mine = pl.program_id(0) // (pl.num_programs(0) // 2) == place_ref[0]
    pick = lambda a, b: jnp.where(mine, a[...], b[...]).astype(F32)
    down = pick(high_ref, low_ref) + pick(low_got_ref, high_got_ref)
    o_ref[...] = (
        x_ref[...].astype(F32) + p_ref[...].astype(F32) + (down + b_ref[...])
    ).astype(BF16)


def close_output(places, x_own, projected, bias, low, high, low_got, high_got):
    own, length = x_own.shape
    column = pl.BlockSpec((own, TILE), lambda i, s: (0, i))
    steps = length // 2 // TILE
    half = pl.BlockSpec((own, TILE), lambda i, s: (0, lax.rem(i, steps)))
    return pl.pallas_call(
        output_kernel,
        grid_spec=pltpu.PrefetchScalarGridSpec(
            num_scalar_prefetch=1,
            grid=(2 * steps,),
            in_specs=[column] * 2 + [pl.BlockSpec((own, 1), lambda i, s: (0, 0))] + [half] * 4,
            out_specs=column,
        ),
        out_shape=jax.ShapeDtypeStruct((own, length), BF16),
        compiler_params=params(60),
        cost_estimate=cost(0, 0),
        name="close_output",
    )(places, x_own, projected, bias, low, high, low_got, high_got)


def tokens_kernel(place_ref, x_ref, gp_ref, gq_ref, keep_ref, got_ref, s_ref, v_ref, o_ref):
    own = x_ref.shape[0]
    mine = pl.program_id(0) // (pl.num_programs(0) // 2) == place_ref[0]
    gp = jnp.where(mine, gp_ref[...], gq_ref[...]).astype(F32)
    e = (keep_ref[...].astype(F32) + got_ref[:own].astype(F32)) * v_ref[:own, 0:1]
    others = got_ref[own:].astype(F32)
    mean, inv = s_ref[2:3], s_ref[3:4]
    total = (s_ref[:2] + (others[:2] + others[2:4])) * (0.5 / own)
    hat = (x_ref[...].astype(F32) - mean) * inv
    o_ref[...] = gp + inv * (e - total[:1] - hat * total[1:])


def close_tokens(places, x_own, gp, gp_got, keep, got, stats, vectors):
    own, length = x_own.shape
    steps = length // 2 // TILE
    column = lambda rows: pl.BlockSpec((rows, TILE), lambda i, s: (0, i))
    half = pl.BlockSpec((own, TILE), lambda i, s: (0, lax.rem(i, steps)))
    return pl.pallas_call(
        tokens_kernel,
        grid_spec=pltpu.PrefetchScalarGridSpec(
            num_scalar_prefetch=1,
            grid=(2 * steps,),
            in_specs=[column(own), half, half, column(own), column(own + SPARE), column(4)]
            + [pl.BlockSpec(vectors.shape, lambda i, s: (0, 0))],
            out_specs=column(own),
        ),
        out_shape=jax.ShapeDtypeStruct((own, length), F32),
        compiler_params=params(60),
        cost_estimate=cost(0, 0),
        name="close_tokens",
    )(places, x_own, gp, gp_got, keep, got, stats, vectors)


def qkv_back_kernel(
    core_ref, xo_ref, xt_ref, gb_ref, ga_ref, bm_ref, bg_ref, am_ref, ag_ref, v_ref,
    keep_ref, send_ref, s_ref, n_ref, db_ref, da_ref, b_low, b_high, a_low, a_high, n_sum, b_sum, a_sum,
):
    @pl.when(first_step())
    def _():
        b_low[...], b_high[...] = unit(core_ref[0], bm_ref[...], bg_ref[...])
        a_low[...], a_high[...] = unit(core_ref[0], am_ref[...], ag_ref[...])
        for r in (n_sum, b_sum, a_sum):
            r[...] = jnp.zeros_like(r)

    own = xo_ref.shape[0]
    gb, ga = gb_ref[...], ga_ref[...]
    cols_b, cols_a = b_low.shape[1], a_low.shape[1]
    twice = 2 * cols_b - gb.shape[0]
    rest = jnp.concatenate((jnp.zeros((twice, gb.shape[1]), BF16), gb[cols_b:]), 0)
    gh = (dot(b_low[...], gb[:cols_b], 1, 0) + dot(b_high[...], rest, 1, 0)) + (
        dot(a_low[...], ga[:cols_a], 1, 0) + dot(a_high[...], ga[cols_a:], 1, 0)
    )
    keep_ref[...] = gh[:own].astype(BF16)
    send_ref[:own] = gh[own:].astype(BF16)
    x = jnp.concatenate((xo_ref[...], xt_ref[...]), 0).astype(F32)
    hat, inv = norm_rows(x)
    both = gh * hat
    gain = v_ref[:, 0:1]
    mine = jnp.concatenate(
        (jnp.sum(gh * gain, axis=0, keepdims=True), jnp.sum(both * gain, axis=0, keepdims=True)), 0
    )
    s_ref[...] = jnp.concatenate((mine, jnp.mean(x, axis=0, keepdims=True), inv), 0)
    high = mine.astype(BF16).astype(F32)
    parts = jnp.concatenate((high, mine - high, jnp.zeros((SPARE - 4, mine.shape[1]), F32)), 0)
    send_ref[own:] = parts.astype(BF16)
    n_sum[...] += jnp.concatenate((lane_sums(both), lane_sums(gh)), 1)
    b_sum[...] += lane_sums(gb.astype(F32))
    a_sum[...] += lane_sums(ga.astype(F32))

    @pl.when(last_step())
    def _():
        n_ref[...] = row_sums(n_sum[...])
        db_ref[...] = row_sums(b_sum[...])
        da_ref[...] = row_sums(a_sum[...])


def qkv_back(core, x_own, x_other, grad_b, grad_a, w_b, w_a, vectors):
    own = x_own.shape[0]
    depth = 2 * own
    column = lambda rows: pl.BlockSpec((rows, TILE), lambda i, s: (0, i))
    whole = lambda a: pl.BlockSpec(a.shape, lambda i, s: (0, 0))
    span = x_own.shape[1]
    out = jax.ShapeDtypeStruct
    rows = (depth, grad_b.shape[0], grad_a.shape[0])
    flat = [out((n, r), F32) for n, r in zip((2, 1, 1), rows)]
    return pl.pallas_call(
        qkv_back_kernel,
        grid_spec=pltpu.PrefetchScalarGridSpec(
            num_scalar_prefetch=1,
            grid=(span // TILE,),
            in_specs=[column(own)] * 2
            + [column(grad_b.shape[0]), column(grad_a.shape[0])]
            + [whole(a) for a in (*w_b, *w_a, vectors)],
            out_specs=[column(own), column(own + SPARE), column(4)] + [whole(t) for t in flat],
            scratch_shapes=[pltpu.VMEM(w.shape, BF16) for w in (*w_b, *w_a)]
            + [pltpu.VMEM((r, n * LANES), F32) for n, r in zip((2, 1, 1), rows)],
        ),
        out_shape=[out((own, span), BF16), out((own + SPARE, span), BF16), out((4, span), F32)]
        + flat,
        compiler_params=params(36),
        cost_estimate=cost(2 * depth * span * (rows[1] + rows[2]), depth * span * 12),
        name="qkv_back",
    )(core, x_own, x_other, grad_b, grad_a, *w_b, *w_a, vectors)


def by_bit(bit, a, b):
    return jnp.where(lax.axis_index("wide") & bit == 0, a, b)


def flip(a, bit):
    size = lax.axis_size("wide")
    return lax.ppermute(a, "wide", [(i, i ^ bit) for i in range(size)])


def join_kernel(place_ref, kept_ref, got_ref, out_ref):
    first = place_ref[0] == 0
    if out_ref.ndim == 2:
        half = kept_ref.shape[0]
        out_ref[:half] = jnp.where(first, kept_ref[...], got_ref[...])
        out_ref[half:] = jnp.where(first, got_ref[...], kept_ref[...])
    else:
        out_ref[:, 0:1] = jnp.where(first, kept_ref[...], got_ref[...])
        out_ref[:, 1:2] = jnp.where(first, got_ref[...], kept_ref[...])


def join(kept, got, place, axis):
    rows, cols = kept.shape[-2:]
    call = dict(compiler_params=params(16), cost_estimate=cost(0, 0), name="join")
    place = place.astype(jnp.int32)[None]
    if axis is None:
        spec = lambda n: pl.BlockSpec((n, cols), lambda i, s: (0, 0))
        grid_spec = pltpu.PrefetchScalarGridSpec(
            num_scalar_prefetch=1, grid=(1,), in_specs=[spec(rows)] * 2, out_specs=spec(2 * rows)
        )
        shape = jax.ShapeDtypeStruct((2 * rows, cols), kept.dtype)
        return pl.pallas_call(join_kernel, grid_spec=grid_spec, out_shape=shape, **call)(place, kept, got)
    outer, inner = math.prod(kept.shape[:axis]), math.prod(kept.shape[axis:-1])
    spec = lambda n: pl.BlockSpec((outer, n, inner, cols), lambda i, s: (0, 0, 0, 0))
    grid_spec = pltpu.PrefetchScalarGridSpec(
        num_scalar_prefetch=1, grid=(1,), in_specs=[spec(1)] * 2, out_specs=spec(2)
    )
    shape = jax.ShapeDtypeStruct((outer, 2, inner, cols), kept.dtype)
    args = [a.reshape(outer, 1, inner, cols) for a in (kept, got)]
    out = pl.pallas_call(join_kernel, grid_spec=grid_spec, out_shape=shape, **call)(place, *args)
    return out.reshape(kept.shape[:axis] + (2,) + kept.shape[axis:])


def fold_kernel(index_ref, kept_ref, got_ref, keep_ref, away_ref):
    total = kept_ref[...].astype(F32) + got_ref[...].astype(F32)
    if kept_ref.ndim == 2:
        half = keep_ref.shape[0]
        low, high = total[:half], total[half:]
        first = index_ref[0] == 0
        keep_ref[...], away_ref[...] = jnp.where(first, low, high), jnp.where(first, high, low)
        return
    total = total.astype(BF16).reshape(keep_ref.shape)

    @pl.when(pl.program_id(1) == 0)
    def _():
        keep_ref[...] = total

    @pl.when(pl.program_id(1) == 1)
    def _():
        away_ref[...] = total


def fold(kept, got, index, axis):
    rows, cols = kept.shape[-2:]
    call = dict(compiler_params=params(16), cost_estimate=cost(0, 0), name="fold")
    index = index.astype(jnp.int32)[None]
    if axis is None:
        spec = lambda n: pl.BlockSpec((n, cols), lambda i, s: (0, 0))
        grid_spec = pltpu.PrefetchScalarGridSpec(
            num_scalar_prefetch=1, grid=(1,), in_specs=[spec(rows)] * 2, out_specs=[spec(rows // 2)] * 2
        )
        shape = [jax.ShapeDtypeStruct((rows // 2, cols), F32)] * 2
        return pl.pallas_call(fold_kernel, grid_spec=grid_spec, out_shape=shape, **call)(index, kept, got)
    outer, inner = math.prod(kept.shape[:axis]), math.prod(kept.shape[axis + 1 : -1])
    grid_spec = pltpu.PrefetchScalarGridSpec(
        num_scalar_prefetch=1,
        grid=(outer, 2),
        in_specs=[pl.BlockSpec((1, 1, inner, cols), lambda a, j, s: (a, j ^ s[0], 0, 0))] * 2,
        out_specs=[pl.BlockSpec((1, inner, cols), lambda a, j, s: (a, 0, 0))] * 2,
    )
    shape = [jax.ShapeDtypeStruct((outer, inner, cols), BF16)] * 2
    args = [a.reshape(outer, 2, inner, cols) for a in (kept, got)]
    out = pl.pallas_call(fold_kernel, grid_spec=grid_spec, out_shape=shape, **call)(index, *args)
    return [o.reshape(kept.shape[:axis] + kept.shape[axis + 1 :]) for o in out]


class Gather:
    def __init__(self, a, b, order):
        self.kept = by_bit(1, a, b)
        self.got = flip(by_bit(1, b, a), 1)
        self.order = list(order)
        self.bits = []
        self.last = None

    def merge(self):
        if self.last is None:
            axis, place = None, lax.axis_index("wide") & 1
        else:
            axis = sum(1 for b in self.bits if b > self.last)
            place = (lax.axis_index("wide") & self.last != 0).astype(jnp.int32)
            if self.last == max(self.order + self.bits + [self.last]):
                place = place ^ lax.axis_index("narrow")
            self.bits.append(self.last)
        self.cur = join(self.kept, self.got, place, axis)

    def came(self):
        return self.got

    def come(self, value):
        self.got = value

    def held(self):
        return self.cur

    def hold(self, value):
        self.cur = value

    def send(self):
        self.last = self.order.pop(0) if self.order else 1
        if self.last == 1:
            self.cur = self.cur.reshape(-1, self.cur.shape[-1])
        self.kept, self.got = self.cur, flip(self.cur, self.last)


class Whole:
    def __init__(self, a, b):
        self.kept = by_bit(1, a, b)
        self.got = flip(by_bit(1, b, a), 1)
        self.stage = 0

    def merge(self):
        if self.stage == 0:
            low = lax.axis_index("wide") & 1 == 0
            kept, got = self.kept, self.got
            self.cur = jnp.where(
                low, jnp.concatenate((kept, got), 0), jnp.concatenate((got, kept), 0)
            )

    def came(self):
        return self.got if self.stage == 0 else self.cur

    def come(self, value):
        if self.stage == 0:
            self.got = value
        else:
            self.cur = value

    def held(self):
        return self.cur

    def hold(self, value):
        self.cur = value

    def send(self):
        if self.stage == 0:
            size = lax.axis_size("wide")
            groups = [list(range(c, size, 2)) for c in range(2)]
            self.cur = lax.all_gather(
                self.cur, "wide", axis=0, tiled=True, axis_index_groups=groups
            )
        else:
            self.got = flip(self.cur, 1)
        self.stage += 1


class Scatter:
    def __init__(self, send, order):
        self.got = flip(send, 1)
        self.order = list(order)
        self.axes = sorted(order, reverse=True)
        self.top = self.axes[0]

    def merge(self):
        kept, got = self.kept, self.got
        if self.order:
            if kept.ndim == 2:
                shape = (2,) * len(self.axes) + (-1, kept.shape[-1])
                kept, got = kept.reshape(shape), got.reshape(shape)
            bit = self.order.pop(0)
            axis = self.axes.index(bit)
            self.axes.remove(bit)
            index = (lax.axis_index("wide") & bit != 0).astype(jnp.int32)
            if bit == self.top:
                index = index ^ lax.axis_index("narrow")
        else:
            bit, axis, index = 1, None, lax.axis_index("wide") & 1
        self.bit = bit
        self.keep, self.away = fold(kept, got, index, axis)

    def next_index(self):
        index = (lax.axis_index("wide") & self.order[0] != 0).astype(jnp.int32)
        return index ^ lax.axis_index("narrow") if self.order[0] == self.top else index

    def start(self, other, *halves):
        for m, keep, away in ((self, *halves[:2]), (other, *halves[2:])):
            m.bit = m.order.pop(0)
            m.axes.remove(m.bit)
            shape = (2,) * len(m.axes) + (-1, keep.shape[-1])
            m.keep, m.away = keep.reshape(shape), away.reshape(shape)

    def came(self):
        return self.got

    def come(self, value):
        self.got = value

    def held(self):
        return self.keep, self.away

    def hold(self, value):
        self.keep, self.away = value

    def send(self):
        self.kept, self.got = self.keep, flip(self.away, self.bit)

    def result(self):
        return by_bit(1, self.kept, self.got), by_bit(1, self.got, self.kept)


def meet(values, *moves, wait=()):
    moves = list(moves) + list(wait)
    values, came = lax.optimization_barrier((values, [m.came() for m in moves]))
    for m, c in zip(moves, came):
        m.come(c)
        m.merge()
    values, held = lax.optimization_barrier((values, [m.held() for m in moves]))
    for m, h in zip(moves, held):
        m.hold(h)
        if m not in wait:
            m.send()
    return values


def send_now(values, *moves):
    values, held = lax.optimization_barrier((values, [m.held() for m in moves]))
    for m, h in zip(moves, held):
        m.hold(h)
        m.send()
    return values


def pair_plan(
    tokens,
    piece_starts,
    ln1_gain,
    ln1_bias,
    w_qkv,
    bias_qv,
    w_out,
    bias_out,
    ln2_gain,
    ln2_bias,
    w_up,
    bias_up,
    w_down,
    bias_down,
    cotangent,
):
    rank = lax.axis_index("narrow")
    first = rank == 0
    core = lax.axis_index("wide") & 1
    own, length = tokens.shape
    depth = 2 * own
    whole = own // HEAD * HEAD
    rest = own - whole
    rows_a = whole // 2
    rows_b = whole - rows_a + 2 * rest
    heads_a, heads_b = rows_a // HEAD, rows_b // HEAD
    block = w_out.shape[0]
    hidden = w_up.shape[1]
    tile = length // 4
    part = -(-(hidden + own) // 256) * LANES
    split = hidden - part
    split_back = hidden // 256 * LANES + 2 * LANES
    rank_arg = rank.astype(jnp.int32)[None]

    def swap(a):
        return lax.ppermute(a, "narrow", [(0, 1), (1, 0)])

    def heads_first(a):
        return jnp.where(first, a, jnp.concatenate((a[..., rest:], a[..., :rest]), -1))

    def heads_back(a):
        return jnp.where(first, a, jnp.concatenate((a[..., whole:], a[..., :whole]), -1))

    def at_rows(bias):
        return jnp.stack((bias[0], jnp.zeros_like(bias[0]), bias[1])).reshape(-1, 1)

    far, near, side = 8, 4, 2
    inward, outward = (far, near, side), (side, far, near)
    w_out_other = swap(w_out)
    w_heads = heads_first(w_qkv)
    shard_a = w_heads[:, :, :rows_a].reshape(block, -1)
    cols_a = shard_a.shape[1] // 2
    get_a = Gather(shard_a[:, :cols_a], shard_a[:, cols_a:], inward)
    pad = jnp.zeros((block, part - split - own), BF16)
    get_p = Whole(
        jnp.concatenate((w_out, pad, w_up[:, :split]), 1),
        jnp.concatenate((w_out_other, pad, w_down.T[:, :split]), 1),
    )
    get_p.merge()
    get_p.send()
    bias_local = heads_first(bias_qv)
    own_vectors = jnp.concatenate(
        (jnp.stack((ln1_gain, ln1_bias, ln2_gain, ln2_bias, bias_out)), bias_local), 0
    )
    half_rows = w_heads[:, :, whole:].reshape(-1, own)
    count = own_vectors.shape[0]
    small_swap = swap(jnp.concatenate((own_vectors, half_rows), 0))
    w_up_in, w_down_in, g_own = meet((w_up, w_down, cotangent), get_a)
    small_swap, x_own = lax.optimization_barrier((small_swap, tokens))
    x_other = swap(x_own)
    other_half = small_swap[count:].reshape(block, 3, rest)
    shard_b = jnp.concatenate((w_heads[:, :, rows_a:], other_half), 2).reshape(block, -1)
    cols_b = -(-shard_b.shape[1] // 256) * 128
    skip = shard_b.shape[1] - cols_b
    get_b = Gather(shard_b[:, :cols_b], shard_b[:, skip:], inward)
    other_vectors = small_swap[:count]
    vectors = jnp.concatenate((own_vectors[:5], other_vectors[:5]), 1).astype(F32).T
    gain_one, shift_one = vectors[:, 0:1], vectors[:, 1:2]
    bias_f = bias_local.astype(F32)
    bias_a = bias_f[:, :rows_a]
    bias_b = jnp.concatenate((bias_f[:, rows_a:], other_vectors[5:, whole:].astype(F32)), 1)
    bias_a, bias_b = at_rows(bias_a), at_rows(bias_b)
    w_down_t = w_down_in.T
    get_q = Whole(w_up_in[:, split:], w_down_t[:, split:])
    meet((), get_a, get_b, get_q)
    starts, g_own = meet((piece_starts[0], g_own), get_a, get_b)
    g_other = swap(g_own)
    seen = mask_bias(starts, length)
    seen, x_other, bias_a, bias_b, vectors = meet((seen, x_other, bias_a, bias_b, vectors), get_a, get_b)
    x_other, get_a.got = meet((x_other, get_a.got))

    core_arg = core[None]
    w_a = (get_a.cur, get_a.got)
    h_one, qkv_a = norm_qkv(core_arg, tokens, x_other, *w_a, vectors, bias_a)
    qkv_a = qkv_a.reshape(3, rows_a, length)

    context_a, lse_a = attend(seen, qkv_a, 0, heads_a)
    context_a, h_one = meet((context_a, h_one), get_b, get_p)
    h_b, get_b.got = meet((h_one, get_b.got))

    context_a_other = swap(after(context_a, g_other))
    w_b = (get_b.cur, get_b.got)
    qkv_b = qkv_of(core_arg, h_b, *w_b, bias_b).reshape(3, rows_b, length)
    whole_b = heads_b - 1
    half_b = whole_b // 2
    context_b, lse_b = attend(seen, qkv_b, 0, half_b)
    context_b, qkv_d = meet((context_b, qkv_b))
    context_b_other = swap(after(context_b, context_a_other))
    context_d, lse_d = attend(seen, qkv_d, half_b, whole_b - half_b)
    context_d, qkv_c = meet((context_d, qkv_d))

    context_d_other = swap(after(context_d, context_b_other))
    context_c, lse_c = attend(seen, qkv_c, whole_b, 1)
    lse_b = jnp.concatenate((lse_b, lse_d, lse_c), 0)
    context_a_other, context_b_other, context_d_other, context_c, get_p.got = meet(
        (context_a_other, context_b_other, context_d_other, context_c, get_p.got), get_q
    )

    pieces = (
        context_a, context_b, context_d, context_a_other, context_b_other, context_d_other, context_c
    )
    w_o = (get_p.cur, get_p.got)
    places = jnp.stack((rank, core)).astype(jnp.int32)
    projected, h_two, context = project(places, tokens, x_other, pieces, *w_o, vectors)
    projected, h_two, context, get_q.got = meet((projected, h_two, context, get_q.got))

    weights = (get_p.cur, get_p.got, get_q.cur, get_q.got)
    bias_up_f = bias_up.astype(F32)[None]
    steps = length // 2 // TILE

    def spot(at):
        return jnp.stack((at, core, rank)).astype(jnp.int32)

    old, low_own, low_other, gh_send, gb_send, gs_send = feed(
        spot(steps * (1 - rank)), steps, h_two, cotangent, g_other, weights, bias_up_f, TILE, None
    )
    old, gh_send = meet((old, gh_send))
    gh_got = swap(gh_send)
    middle, high_own, high_other, gh_keep, gb_keep, gs_keep = feed(
        spot(steps * rank), steps, h_two, cotangent, g_other, weights, bias_up_f, TILE, old
    )
    grad_bias_up = gb_send + gb_keep
    send_p, send_q = weight_grad(core[None], h_two, cotangent, g_other, middle, split_back)
    gh_got, gh_keep, send_p, send_q, middle, low_other = meet(
        (gh_got, gh_keep, send_p, send_q, middle, low_other)
    )

    put_p = Scatter(send_p, (side, near, far))
    put_q = Scatter(send_q, (near, far, side))
    low_got = swap(low_other)
    gp, gp_away, mine_a, mine_b, send_a, send_b, grad_two = mid_back(
        spot(steps * rank), tokens, x_other, projected, cotangent, g_other, gh_keep,
        gh_got, *w_o, vectors, rows_a, rows_b,
    )
    gp, gp_away, mine_a, mine_b, send_a, send_b, middle, put_p.got, put_q.got = meet(
        (gp, gp_away, mine_a, mine_b, send_a, send_b, middle, put_p.got, put_q.got)
    )

    got_b = swap(send_b)
    put_p.start(put_q, *weight_grad(
        jnp.stack((1 - core, put_p.next_index(), put_q.next_index())).astype(jnp.int32),
        h_two, cotangent, g_other, middle, split_back, (put_p.got, put_q.got),
    ))
    got_b, mine_b, send_a, gp_away, low_got = send_now(
        meet((got_b, mine_b, send_a, gp_away, low_got)), put_p, put_q
    )

    got_a = swap(send_a)
    gp_got = swap(gp_away)
    back_b = attend_back(seen, rank_arg, qkv_b, mine_b, got_b, lse_b, 0, heads_b, True)
    back_b, got_a, gp_got, high_other = meet((back_b, got_a, gp_got, high_other), put_p, put_q)

    high_got = swap(high_other)
    grad_b = back_b.reshape(3 * rows_b, length)

    half_a = heads_a // 2
    back_a = attend_back(seen, rank_arg, qkv_a, mine_a, got_a, lse_a, 0, half_a, False)
    send_b, keep_b = column_grads(places, cols_b, h_one, grad_b, context, gp, gp_got)
    back_a, send_b, keep_b, high_got = meet(
        (back_a, send_b, keep_b, high_got), wait=(put_p, put_q)
    )
    put_b = Scatter(send_b, (side, near, far))
    put_b.kept = keep_b
    back_a = attend_back(
        seen, rank_arg, qkv_a, mine_a, got_a, lse_a, half_a, heads_a - half_a, False, back_a
    )
    back_a = send_now(meet(back_a, put_b), put_p, put_q)
    grad_a = back_a.reshape(3 * rows_a, length)

    def vector_parts(sums):
        def row(a):
            return jnp.pad(a, ((0, 0), (0, depth - a.shape[1])))

        low = [grad_bias_up[:, :depth], grad_bias_up[:, depth:]]
        return jnp.concatenate(
            (sums[0], grad_two, row(sums[1]), row(sums[2]), row(gs_send + gs_keep), *map(row, low))
        )

    send_a, keep_a = column_grads(places, cols_a, h_one, grad_a)
    put_a = Scatter(send_a, (side, near, far))
    put_a.kept = keep_a
    keep, send, stats, *sums = qkv_back(
        core_arg, tokens, x_other, grad_b, grad_a, w_b, w_a, vectors
    )
    got = swap(send)
    keep, stats, sums, low_got = meet((keep, stats, sums, low_got), put_a, put_b, put_p, put_q)
    total = vector_parts(sums)
    total = total + flip(total, 1)
    output = close_output(
        places, tokens, projected, bias_down.astype(F32)[:, None], low_own, high_own, low_got, high_got
    )
    total, output = meet((total, output), put_a, put_b)
    total = total + flip(total, side)
    total = meet(total, put_a)
    total = total + flip(total, near)
    total = meet(total, put_a, put_b)
    total = total + flip(total, far)
    got, total = meet((got, total))
    grad_tokens = close_tokens(places, tokens, gp, gp_got, keep, got, stats, vectors)
    sum_up_p, sum_down_p = put_p.result()
    sum_up_q, sum_down_q = put_q.result()
    low_b, high_b = put_b.result()
    sum_a = jnp.concatenate(put_a.result(), 1).reshape(block, 3, rows_a)
    out_cols = half_lanes(own)
    sum_out = jnp.concatenate((low_b[:, cols_b:], high_b[:, cols_b + 2 * out_cols - own :]), 1)
    sum_b = jnp.concatenate((low_b[:, :cols_b], high_b[:, cols_b - skip : cols_b]), 1)
    sum_b = sum_b.reshape(block, 3, rows_b)[:, :, : rows_b - rest]
    sum_w_qkv = heads_back(jnp.concatenate((sum_a, sum_b), 2))

    two = total[:5, :own] + swap(total[:5, own:])
    vec = [
        jnp.concatenate(
            (total[6, i * rows_a : (i + 1) * rows_a], total[5, i * rows_b : (i + 1) * rows_b - rest])
        )
        for i in (0, 2)
    ]
    return (
        output,
        grad_tokens,
        two[0],
        two[1],
        sum_w_qkv,
        heads_back(jnp.stack(vec)),
        sum_out,
        two[4],
        two[2],
        two[3],
        jnp.concatenate((sum_up_p, sum_up_q), 1),
        jnp.concatenate((total[8], total[9]))[:hidden],
        jnp.concatenate((sum_down_p, sum_down_q), 1).T,
        total[7, :own],
    )


def solution(mesh):
    in_specs = (
        P("narrow", "wide"),
        P("wide", None),
        P("narrow"),
        P("narrow"),
        P("wide", None, "narrow"),
        P(None, "narrow"),
        P("wide", "narrow"),
        P("narrow"),
        P("narrow"),
        P("narrow"),
        P("wide", "narrow"),
        P("narrow"),
        P("narrow", "wide"),
        P("narrow"),
        P("narrow", "wide"),
    )
    out_specs = (
        P("narrow", "wide"),
        P("narrow", "wide"),
        P("narrow"),
        P("narrow"),
        P("wide", None, "narrow"),
        P(None, "narrow"),
        P("wide", "narrow"),
        P("narrow"),
        P("narrow"),
        P("narrow"),
        P("wide", "narrow"),
        P("narrow"),
        P("narrow", "wide"),
        P("narrow"),
    )
    paired = mesh.shape["narrow"] == 2 and mesh.shape["wide"] == 16
    return jax.shard_map(
        pair_plan if paired else any_mesh, mesh=mesh, in_specs=in_specs, out_specs=out_specs, check_vma=False
    )
```

```python
import functools
import math
from functools import partial

import jax
import jax.numpy as jnp
from jax import lax
from jax.experimental import pallas as pl
from jax.experimental.pallas import tpu as pltpu
from jax.sharding import PartitionSpec as P

HEADS = 17
PIECE = 256


EPSILON = 1e-05


def normalize(row_data, gain_vec, shift_vec):
    centre = jnp.mean(row_data, axis=-1, keepdims=True)
    centred = row_data - centre
    spread = jnp.mean(centred * centred, axis=-1, keepdims=True)
    return centred * lax.rsqrt(spread + EPSILON) * gain_vec + shift_vec


def norm_back(row_data, gain_vec, shift_vec, grad_rows):
    unused, pull_back = jax.vjp(normalize, row_data, gain_vec, shift_vec)
    return pull_back(grad_rows)


def full_rows(partial_rows):
    return lax.psum(partial_rows, "narrow")


def visible_mask(starts, query_pos, key_pos):
    query_in = (query_pos[:, None] >= starts[None, :]) & (
        query_pos[:, None] < starts[None, :] + PIECE
    )
    key_in = (key_pos[:, None] >= starts[None, :]) & (key_pos[:, None] < starts[None, :] + PIECE)
    shared = jnp.any(query_in[:, None, :] & key_in[None, :, :], axis=-1)
    return (key_pos[None, :] <= query_pos[:, None]) | shared


def to_heads(matrix):
    return matrix.reshape(matrix.shape[0], HEADS, matrix.shape[1] // HEADS)


def attention_scores(query_rows, key_full, visible, score_scale):
    raw = (
        jnp.einsum(
            "qhd,khd->hqk",
            to_heads(query_rows),
            to_heads(key_full),
            preferred_element_type=jnp.float32,
        )
        * score_scale
    )
    return jnp.where(visible[None], raw, -1e30)


def any_mesh(
    tokens,
    piece_starts,
    ln1_gain,
    ln1_bias,
    w_qkv,
    bias_qv,
    w_out,
    bias_out,
    ln2_gain,
    ln2_bias,
    w_up,
    bias_up,
    w_down,
    bias_down,
    cotangent,
):
    narrow_size = lax.axis_size("narrow")
    narrow_rank = lax.axis_index("narrow")
    col_width, length = tokens.shape
    full_width = col_width * narrow_size
    queries = length // narrow_size
    score_scale = (full_width // HEADS) ** (-0.5)
    col_start = narrow_rank * col_width
    row_start = narrow_rank * queries

    def own_cols(matrix):
        return lax.dynamic_slice_in_dim(matrix, col_start, col_width, matrix.ndim - 1)

    x_cols, dy_cols, gain_one, shift_one, gain_two, shift_two = (
        lax.all_gather(tokens, "narrow", axis=0, tiled=True),
        lax.all_gather(cotangent, "narrow", axis=0, tiled=True),
        lax.all_gather(ln1_gain, "narrow", axis=0, tiled=True),
        lax.all_gather(ln1_bias, "narrow", axis=0, tiled=True),
        lax.all_gather(ln2_gain, "narrow", axis=0, tiled=True),
        lax.all_gather(ln2_bias, "narrow", axis=0, tiled=True),
    )
    x_rows = x_cols.T
    dy_rows = dy_cols.T
    qkv_cols, out_cols, up_cols, down_rows = (
        lax.all_gather(w_qkv, "wide", axis=0, tiled=True),
        lax.all_gather(w_out, "wide", axis=0, tiled=True),
        lax.all_gather(w_up, "wide", axis=0, tiled=True),
        lax.all_gather(w_down, "wide", axis=1, tiled=True),
    )
    gain_one = gain_one.astype(jnp.float32)
    shift_one = shift_one.astype(jnp.float32)
    gain_two = gain_two.astype(jnp.float32)
    shift_two = shift_two.astype(jnp.float32)
    x_full = x_rows.astype(jnp.float32)
    h_one = normalize(x_full, gain_one, shift_one).astype(jnp.bfloat16)
    mixed = jnp.einsum("td,dcf->tcf", h_one, qkv_cols, preferred_element_type=jnp.float32)
    bias_cols = bias_qv.astype(jnp.float32)
    query_cols = (mixed[:, 0] + bias_cols[0]).astype(jnp.bfloat16)
    key_cols = mixed[:, 1].astype(jnp.bfloat16)
    value_cols = (mixed[:, 2] + bias_cols[1]).astype(jnp.bfloat16)
    query_full, key_full, value_full = (
        lax.all_gather(query_cols, "narrow", axis=1, tiled=True),
        lax.all_gather(key_cols, "narrow", axis=1, tiled=True),
        lax.all_gather(value_cols, "narrow", axis=1, tiled=True),
    )
    query_rows = lax.dynamic_slice_in_dim(query_full, row_start, queries, 0)
    query_pos = row_start + jnp.arange(queries, dtype=jnp.int32)
    key_pos = jnp.arange(length, dtype=jnp.int32)
    visible = visible_mask(piece_starts[0], query_pos, key_pos)
    masked = attention_scores(query_rows, key_full, visible, score_scale)
    row_top = jnp.max(masked, axis=-1, keepdims=True)
    weights = jnp.exp(masked - row_top)
    row_total = jnp.sum(weights, axis=-1, keepdims=True)
    log_total = row_top + jnp.log(row_total)
    probs_low = (weights / row_total).astype(jnp.bfloat16)
    context = jnp.einsum(
        "hqk,khd->qhd", probs_low, to_heads(value_full), preferred_element_type=jnp.float32
    )
    context = context.reshape(queries, full_width).astype(jnp.bfloat16)
    context_full = lax.all_gather(context, "narrow", axis=0, tiled=True)
    projected = jnp.dot(
        context_full, out_cols, preferred_element_type=jnp.float32
    ) + bias_out.astype(jnp.float32)
    projected_low = projected.astype(jnp.bfloat16)
    projected_full = lax.all_gather(projected_low, "narrow", axis=1, tiled=True)
    mid_full = x_full + projected_full.astype(jnp.float32)
    mid_rows = tokens.T.astype(jnp.float32) + projected_low.astype(jnp.float32)
    h_two = normalize(mid_full, gain_two, shift_two).astype(jnp.bfloat16)
    up_pre = jnp.dot(h_two, up_cols, preferred_element_type=jnp.float32) + bias_up.astype(
        jnp.float32
    )
    act_value, gelu_pull = jax.vjp(partial(jax.nn.gelu, approximate=True), up_pre)
    act_low = act_value.astype(jnp.bfloat16)
    partial_down = jnp.dot(act_low, down_rows, preferred_element_type=jnp.float32)
    down_sum = lax.psum_scatter(
        partial_down.astype(jnp.bfloat16), "narrow", scatter_dimension=1, tiled=True
    ).astype(jnp.float32)
    output = (mid_rows + (down_sum + bias_down.astype(jnp.float32))).astype(jnp.bfloat16)
    grad_out = cotangent.T.astype(jnp.float32)
    grad_bias_down = jnp.sum(grad_out, axis=0)
    grad_w_down = jnp.einsum("tf,td->fd", act_low, dy_rows, preferred_element_type=jnp.float32)
    grad_act = jnp.einsum("td,fd->tf", dy_rows, down_rows, preferred_element_type=jnp.float32)
    grad_up = gelu_pull(grad_act)[0].astype(jnp.bfloat16)
    grad_bias_up = jnp.sum(grad_up.astype(jnp.float32), axis=0)
    grad_w_up = jnp.einsum("td,tf->df", h_two, grad_up, preferred_element_type=jnp.float32)
    grad_h_two = full_rows(
        jnp.einsum("tf,df->td", grad_up, up_cols, preferred_element_type=jnp.float32)
    )
    grad_mid_full, grad_gain_two, grad_shift_two = norm_back(
        mid_full, gain_two, shift_two, grad_h_two
    )
    grad_mid = grad_out + own_cols(grad_mid_full)
    grad_projected = grad_mid.astype(jnp.bfloat16)
    grad_bias_out = jnp.sum(grad_projected.astype(jnp.float32), axis=0)
    grad_w_out = jnp.einsum(
        "td,tc->dc", context_full, grad_projected, preferred_element_type=jnp.float32
    )
    grad_context = lax.psum_scatter(
        jnp.einsum("tc,dc->td", grad_projected, out_cols, preferred_element_type=jnp.float32),
        "narrow",
        scatter_dimension=0,
        tiled=True,
    ).astype(jnp.bfloat16)
    weights_back = jnp.exp(masked - log_total)
    context_heads = to_heads(grad_context)
    grad_probs = jnp.einsum(
        "qhd,khd->hqk", context_heads, to_heads(value_full), preferred_element_type=jnp.float32
    )
    centre = jnp.sum(weights_back * grad_probs, axis=-1, keepdims=True)
    grad_scores = (weights_back * (grad_probs - centre)).astype(jnp.bfloat16)
    grad_query = jnp.einsum(
        "hqk,khd->qhd", grad_scores, to_heads(key_full), preferred_element_type=jnp.float32
    )
    grad_query = grad_query.reshape(queries, full_width) * score_scale
    probs_back = weights_back.astype(jnp.bfloat16)
    grad_key = jnp.einsum(
        "hqk,qhd->khd", grad_scores, to_heads(query_rows), preferred_element_type=jnp.float32
    )
    grad_key = grad_key.reshape(length, full_width) * score_scale
    grad_value = jnp.einsum(
        "hqk,qhd->khd", probs_back, context_heads, preferred_element_type=jnp.float32
    )
    grad_value = grad_value.reshape(length, full_width)
    placed = jnp.zeros((length, full_width), jnp.float32)
    placed = lax.dynamic_update_slice_in_dim(placed, grad_query, row_start, 0)
    stacked = jnp.stack((placed, grad_key, grad_value), axis=1)
    grad_mixed = lax.psum_scatter(stacked, "narrow", scatter_dimension=2, tiled=True).astype(
        jnp.bfloat16
    )
    grad_mixed_f = grad_mixed.astype(jnp.float32)
    grad_bias_qv = jnp.stack(
        (jnp.sum(grad_mixed_f[:, 0], axis=0), jnp.sum(grad_mixed_f[:, 2], axis=0))
    )
    grad_w_qkv = jnp.einsum("td,tcf->dcf", h_one, grad_mixed, preferred_element_type=jnp.float32)
    grad_h_one = full_rows(
        jnp.einsum("tcf,dcf->td", grad_mixed, qkv_cols, preferred_element_type=jnp.float32)
    )
    grad_x_full, grad_gain_one, grad_shift_one = norm_back(x_full, gain_one, shift_one, grad_h_one)
    grad_tokens = grad_mid + own_cols(grad_x_full)
    sum_w_qkv, sum_w_out, sum_w_up, sum_w_down = (
        lax.psum_scatter(grad_w_qkv, "wide", scatter_dimension=0, tiled=True),
        lax.psum_scatter(grad_w_out, "wide", scatter_dimension=0, tiled=True),
        lax.psum_scatter(grad_w_up, "wide", scatter_dimension=0, tiled=True),
        lax.psum_scatter(grad_w_down, "wide", scatter_dimension=1, tiled=True),
    )
    (
        sum_gain_one,
        sum_shift_one,
        sum_bias_qv,
        sum_bias_out,
        sum_gain_two,
        sum_shift_two,
        sum_bias_up,
        sum_bias_down,
    ) = lax.psum(
        (
            own_cols(grad_gain_one),
            own_cols(grad_shift_one),
            grad_bias_qv,
            grad_bias_out,
            own_cols(grad_gain_two),
            own_cols(grad_shift_two),
            grad_bias_up,
            grad_bias_down,
        ),
        "wide",
    )
    return (
        output.T,
        grad_tokens.T,
        sum_gain_one,
        sum_shift_one,
        sum_w_qkv,
        sum_bias_qv,
        sum_w_out,
        sum_bias_out,
        sum_gain_two,
        sum_shift_two,
        sum_w_up,
        sum_bias_up,
        sum_w_down,
        sum_bias_down,
    )


F32 = jnp.float32
BF16 = jnp.bfloat16
HEAD = 64
TILE = 256
MIB = 1 << 20
LANES = 128
SPARE = 16
PACE = 1e-6


def dot(a, b, dim_a, dim_b):
    return lax.dot_general(a, b, (((dim_a,), (dim_b,)), ((), ())), preferred_element_type=F32)


def after(value, *others):
    return lax.optimization_barrier((value,) + others)[0]


def cost(flops, moved):
    return pl.CostEstimate(flops=1 + int(PACE * flops), bytes_accessed=1 + int(PACE * moved), transcendentals=0)


def params(mib):
    return pltpu.CompilerParams(vmem_limit_bytes=mib * MIB)


def in_turns(stages, items):
    states = [None] * len(items)
    for tick in range(len(items) + len(stages) - 1):
        for j, stage in enumerate(stages):
            i = tick - j
            if 0 <= i < len(items):
                states[i] = stage(items[i], states[i])


def lane_sums(a):
    return functools.reduce(
        jnp.add, [a[:, i : i + LANES] for i in range(0, a.shape[1], LANES)]
    )


def row_sums(acc):
    return jnp.concatenate(
        [
            jnp.sum(acc[:, i : i + LANES].T, axis=0, keepdims=True)
            for i in range(0, acc.shape[1], LANES)
        ],
        0,
    )


def rows_at(start, size):
    return pl.ds(pl.multiple_of(start, HEAD // 2), size)


def first_step():
    return pl.program_id(0) == 0


def last_step():
    return pl.program_id(0) == pl.num_programs(0) - 1


def unit(rows, a, b):
    mine = rows == 0
    return jnp.where(mine, a, b), jnp.where(mine, b, a)


def bias_kernel(starts_ref, bias_ref):
    length = bias_ref.shape[0] * TILE
    for i in range(length // TILE):
        low = i * TILE
        rows = min(2 * TILE, length - low)
        key = low + lax.broadcasted_iota(jnp.int32, (rows, TILE), 0)
        query = low + lax.broadcasted_iota(jnp.int32, (rows, TILE), 1)
        seen = key <= query
        for p in range(starts_ref.shape[0]):
            s = starts_ref[p]
            seen = seen | (
                (key >= s) & (key < s + PIECE) & (query >= s) & (query < s + PIECE)
            )
        bias_ref[i, :rows, :] = jnp.where(seen, 0.0, -1e30)


def mask_bias(starts, length):
    shape = (length // TILE, 2 * TILE, TILE)
    return pl.pallas_call(
        bias_kernel,
        in_specs=[pl.BlockSpec(memory_space=pltpu.SMEM)],
        out_specs=pl.BlockSpec(memory_space=pltpu.VMEM),
        out_shape=jax.ShapeDtypeStruct(shape, F32),
        compiler_params=params(16),
        name="mask_bias",
    )(starts)


def spans(i, length):
    low = i * TILE
    high = min(low + 2 * TILE, length)
    return ((0, low), (low, high)) if low > 0 else ((low, high),)


def scores(key_rows, query, bias, i, span):
    s = dot(key_rows[span[0] : span[1]], query, 1, 0)
    return s if span[0] < i * TILE else s + bias[i, : span[1] - span[0], :]


def attend_kernel(bias, x_ref, c_ref, l_ref, key_rows):
    length = x_ref.shape[2]
    key_rows[...] = x_ref[1].T

    def score(i, _):
        query = x_ref[0, :, pl.ds(i * TILE, TILE)] * jnp.asarray(HEAD**-0.5, BF16)
        return [(span, scores(key_rows, query, bias, i, span)) for span in spans(i, length)]

    def weigh(i, parts):
        here = pl.ds(i * TILE, TILE)
        top = functools.reduce(
            jnp.maximum, [jnp.max(s, axis=0, keepdims=True) for _, s in parts]
        )
        total, acc = 0.0, 0.0
        for span, s in parts:
            p = jnp.exp(s - top)
            total = total + jnp.sum(p, axis=0, keepdims=True)
            acc = acc + dot(x_ref[2, :, span[0] : span[1]], p.astype(BF16), 1, 0)
        c_ref[:, here] = (acc / total).astype(BF16)
        l_ref[0, :, here] = top + jnp.log(total)

    in_turns((score, weigh), range(length // TILE))


def attend(bias, qkv, first, count):
    length = qkv.shape[2]
    return pl.pallas_call(
        attend_kernel,
        grid=(count,),
        in_specs=[
            pl.BlockSpec(bias.shape, lambda h: (0, 0, 0)),
            pl.BlockSpec((3, HEAD, length), lambda h: (0, h + first, 0)),
        ],
        out_specs=[
            pl.BlockSpec((HEAD, length), lambda h: (h, 0)),
            pl.BlockSpec((1, 1, length), lambda h: (h, 0, 0)),
        ],
        scratch_shapes=[pltpu.VMEM((length, HEAD), BF16)],
        out_shape=[
            jax.ShapeDtypeStruct((count * HEAD, length), BF16),
            jax.ShapeDtypeStruct((count, 1, length), F32),
        ],
        compiler_params=params(24),
        cost_estimate=cost(4e9 * count, count * length * HEAD * 8),
        name="attend",
    )(bias, qkv)


def attend_back_kernel(
    shared, rank_ref, bias, x_ref, mine_ref, got_ref, l_ref, old_ref, g_ref,
    key_rows, value_rows, query_rows, grad_rows, grad, key_sum, value_sum,
):
    length = x_ref.shape[2]
    share = length // 2
    scale = jnp.asarray(HEAD**-0.5, BF16)
    first = rank_ref[0] == 0
    mine, got = mine_ref[...], got_ref[...]
    grad[:, :share] = jnp.where(first, mine, got)
    grad[:, share:] = jnp.where(first, got, mine)
    key_rows[...] = x_ref[1].T
    value_rows[...] = x_ref[2].T
    grad_rows[...] = grad[...].T
    query_rows[...] = (x_ref[0] * scale).T
    tiles = length // TILE

    def score(i, _):
        here = pl.ds(i * TILE, TILE)
        query, out = x_ref[0, :, here] * scale, grad[:, here]
        return [
            (span, scores(key_rows, query, bias, i, span), dot(value_rows[span[0] : span[1]], out, 1, 0))
            for span in spans(i, length)
        ]

    def weigh(i, parts):
        lse = l_ref[0, :, pl.ds(i * TILE, TILE)]
        weights = [jnp.exp(s - lse) for _, s, _ in parts]
        centre = functools.reduce(
            jnp.add, [jnp.sum(p * g, axis=0, keepdims=True) for p, (_, _, g) in zip(weights, parts)]
        )
        return [
            (span, p.astype(BF16), (p * (g - centre)).astype(BF16))
            for p, (span, _, g) in zip(weights, parts)
        ]

    def gather(i, parts):
        here = pl.ds(i * TILE, TILE)
        dq = 0.0
        for (low, high), p, gs in parts:
            dq = dq + dot(x_ref[1, :, low:high], gs, 1, 0)
            dk, dv = dot(gs, query_rows[here], 1, 0), dot(p, grad_rows[here], 1, 0)
            if i == tiles - 1:
                key_sum[low:high], value_sum[low:high] = dk, dv
            else:
                key_sum[low:high] += dk
                value_sum[low:high] += dv
        g_ref[0, :, here] = (dq * HEAD**-0.5).astype(BF16)

    in_turns((score, weigh, gather), list(reversed(range(tiles))))
    g_ref[1] = key_sum[...].T.astype(BF16)
    g_ref[2] = value_sum[...].T.astype(BF16)
    if shared:
        @pl.when(pl.program_id(0) == pl.num_programs(0) - 1)
        def _():
            g_ref[:, HEAD // 2 :, :] = jnp.zeros((3, HEAD // 2, length), BF16)


def attend_back(bias, rank, qkv, mine, got, lse, first, count, shared, old=None):
    length = qkv.shape[2]
    rows = pltpu.VMEM((length, HEAD), BF16)
    sums = pltpu.VMEM((length, HEAD), F32)
    heads = pl.BlockSpec((3, HEAD, length), lambda h, r: (0, h + first, 0))
    half = pl.BlockSpec((HEAD, length // 2), lambda h, r: (h + first, 0))
    alias = {}
    if old is not None:
        alias = {6: 0}
    else:
        old = jnp.zeros((8, 128), BF16)
    return pl.pallas_call(
        functools.partial(attend_back_kernel, shared),
        grid_spec=pltpu.PrefetchScalarGridSpec(
            num_scalar_prefetch=1,
            grid=(count,),
            in_specs=[
                pl.BlockSpec(bias.shape, lambda h, r: (0, 0, 0)),
                heads,
                half,
                half,
                pl.BlockSpec((1, 1, length), lambda h, r: (h + first, 0, 0)),
                pl.BlockSpec(memory_space=pl.ANY),
            ],
            out_specs=[heads],
            scratch_shapes=[rows] * 4
            + [pltpu.VMEM((HEAD, length), BF16)]
            + [sums] * 2,
        ),
        out_shape=[jax.ShapeDtypeStruct(qkv.shape, BF16)],
        input_output_aliases=alias,
        compiler_params=params(34),
        cost_estimate=cost(6.8e9 * count, count * length * HEAD * 14),
        name="attend_back",
    )(rank, bias, qkv, mine, got, lse, old)[0]


def norm_rows(x):
    x = x - jnp.mean(x, axis=0, keepdims=True)
    inv = lax.rsqrt(jnp.mean(x * x, axis=0, keepdims=True) + EPSILON)
    return x * inv, inv


def own_first(rank, a):
    half = a.shape[0] // 2
    return jnp.where(rank == 0, a, jnp.concatenate((a[half:], a[:half]), 0))


def half_lanes(columns):
    return -(-columns // (2 * LANES)) * LANES


def turn_weights(core, mine, got, turned):
    a, b = unit(core, mine, got)
    count = a.shape[1]
    turned[:count] = a.T
    turned[count:] = b.T[2 * count - turned.shape[0] :]


def norm_qkv_kernel(core_ref, xo_ref, xt_ref, m_ref, g_ref, v_ref, b_ref, h_ref, q_ref, turned):
    @pl.when(first_step())
    def _():
        turn_weights(core_ref[0], m_ref[...], g_ref[...], turned)

    x = jnp.concatenate((xo_ref[...], xt_ref[...]), 0).astype(F32)
    h = (norm_rows(x)[0] * v_ref[:, 0:1] + v_ref[:, 1:2]).astype(BF16)
    h_ref[...] = h
    q_ref[...] = (dot(turned[...], h, 1, 0) + b_ref[...]).astype(BF16)


def norm_qkv(core, x_own, x_other, mine, got, vectors, bias):
    own, length = x_own.shape
    depth = 2 * own
    rows = bias.shape[0]
    column = lambda n: pl.BlockSpec((n, TILE), lambda i, s: (0, i))
    whole = lambda a: pl.BlockSpec(a.shape, lambda i, s: (0, 0))
    return pl.pallas_call(
        norm_qkv_kernel,
        grid_spec=pltpu.PrefetchScalarGridSpec(
            num_scalar_prefetch=1,
            grid=(length // TILE,),
            in_specs=[column(own)] * 2 + [whole(a) for a in (mine, got, vectors, bias)],
            out_specs=[column(depth), column(rows)],
            scratch_shapes=[pltpu.VMEM((rows, depth), BF16)],
        ),
        out_shape=[jax.ShapeDtypeStruct((n, length), BF16) for n in (depth, rows)],
        compiler_params=params(60),
        cost_estimate=cost(2 * depth * rows * length, depth * length * 6),
        name="norm_qkv",
    )(core, x_own, x_other, mine, got, vectors, bias)


def qkv_kernel(core_ref, h_ref, m_ref, g_ref, b_ref, q_ref, turned):
    @pl.when(first_step())
    def _():
        turn_weights(core_ref[0], m_ref[...], g_ref[...], turned)

    q_ref[...] = (dot(turned[...], h_ref[...], 1, 0) + b_ref[...]).astype(BF16)


def qkv_of(core, h_one, mine, got, bias):
    depth, length = h_one.shape
    rows = bias.shape[0]
    column = lambda n: pl.BlockSpec((n, TILE), lambda i, s: (0, i))
    whole = lambda a: pl.BlockSpec(a.shape, lambda i, s: (0, 0))
    return pl.pallas_call(
        qkv_kernel,
        grid_spec=pltpu.PrefetchScalarGridSpec(
            num_scalar_prefetch=1,
            grid=(length // TILE,),
            in_specs=[column(depth)] + [whole(a) for a in (mine, got, bias)],
            out_specs=column(rows),
            scratch_shapes=[pltpu.VMEM((rows, depth), BF16)],
        ),
        out_shape=jax.ShapeDtypeStruct((rows, length), BF16),
        compiler_params=params(24),
        cost_estimate=cost(2 * depth * rows * length, depth * length * 4),
        name="qkv",
    )(core, h_one, mine, got, bias)


def project_kernel(
    spot_ref, xo_ref, xt_ref, a_ref, b_ref, d_ref, ga_ref, gb_ref, gd_ref, c_ref, m_ref, g_ref, v_ref,
    p_ref, h_ref, c_out, turned,
):
    @pl.when(first_step())
    def _():
        own = xo_ref.shape[0]
        parts = [own_first(spot_ref[0], w[:, :own]) for w in (m_ref, g_ref)]
        turn_weights(spot_ref[1], *parts, turned)

    rank = spot_ref[0]
    own = xo_ref.shape[0]
    half, whole = HEAD // 2, own - HEAD // 2
    for refs, at in (((a_ref, b_ref, d_ref), half * rank), ((ga_ref, gb_ref, gd_ref), own + half * (1 - rank))):
        for ref in refs:
            c_out[rows_at(at, ref.shape[0])] = ref[...]
            at = at + ref.shape[0]
    c_out[rows_at(whole * (1 - rank), half)] = c_ref[:half]
    c_out[rows_at(own + whole * rank, half)] = c_ref[half:]
    low = (dot(turned[...], c_out[...], 1, 0) + v_ref[:, 4:5]).astype(BF16)
    p_ref[...] = low
    mid = jnp.concatenate((xo_ref[...], xt_ref[...]), 0).astype(F32) + low.astype(F32)
    h_ref[...] = (norm_rows(mid)[0] * v_ref[:, 2:3] + v_ref[:, 3:4]).astype(BF16)


def out_columns(depth):
    return pl.BlockSpec((depth, -(-depth // (2 * LANES)) * LANES), lambda i, s: (0, 0))


def project(spot, x_own, x_other, pieces, mine, got, vectors):
    own, length = x_own.shape
    depth = 2 * own
    column = lambda rows: pl.BlockSpec((rows, TILE), lambda i, s: (0, i))
    whole = lambda a: pl.BlockSpec(a.shape, lambda i, s: (0, 0))
    return pl.pallas_call(
        project_kernel,
        grid_spec=pltpu.PrefetchScalarGridSpec(
            num_scalar_prefetch=1,
            grid=(length // TILE,),
            in_specs=[column(own)] * 2
            + [column(p.shape[0]) for p in pieces]
            + [out_columns(depth)] * 2
            + [whole(vectors)],
            out_specs=[column(depth)] * 3,
            scratch_shapes=[pltpu.VMEM((depth, depth), BF16)],
        ),
        out_shape=[jax.ShapeDtypeStruct((depth, length), BF16)] * 3,
        compiler_params=params(60),
        cost_estimate=cost(2 * depth * depth * length, depth * length * 10),
        name="project",
    )(spot, x_own, x_other, *pieces, mine, got, vectors)


def feed_kernel(
    spot_ref, h_ref, go_ref, gt_ref, pm_ref, pg_ref, qm_ref, qg_ref, bias_ref, *rest
):
    mid_ref, own_ref, other_ref, gh_ref, gb_ref, gs_ref, up, down, sums, sems = rest[-10:]
    split = up.shape[1] - qm_ref.shape[1]
    lead = pm_ref.shape[1] - split
    hidden = up.shape[1]

    @pl.when(pl.program_id(0) == 0)
    def _():
        half = up.shape[0] // 2

        def copies(up_p, up_q, down_p, down_q):
            made = []
            for i, (first, second, whole) in enumerate(((up_p, up_q, up), (down_p, down_q, down))):
                for j in range(2):
                    rows = pl.ds(half * j, half)
                    to = rows_at(half * (j ^ spot_ref[2]), half)
                    at = 4 * i + 2 * j
                    made += [
                        pltpu.make_async_copy(
                            first.at[rows, lead:], whole.at[to, :split], sems.at[at]
                        ),
                        pltpu.make_async_copy(
                            second.at[rows, :], whole.at[to, split:], sems.at[at + 1]
                        ),
                    ]
            return made

        def bring(these):
            for c in these:
                c.start()
            for c in these:
                c.wait()

        @pl.when(spot_ref[1] == 0)
        def _():
            bring(copies(pm_ref, qm_ref, pg_ref, qg_ref))

        @pl.when(spot_ref[1] == 1)
        def _():
            bring(copies(pg_ref, qg_ref, pm_ref, qm_ref))

        gb_ref[...] = jnp.zeros_like(gb_ref)
        sums[...] = jnp.zeros_like(sums)

    sums[...] += lane_sums(go_ref[...].astype(F32))

    @pl.when(last_step())
    def _():
        gs_ref[...] = row_sums(sums[...])

    root = (2 / jnp.pi) ** 0.5
    h = h_ref[...]
    g = jnp.concatenate((go_ref[...], gt_ref[...]), 0)
    for span in (slice(0, split), slice(split, hidden)):
        u = dot(h, up[:, span], 0, 0) + bias_ref[:, span]
        grad_act = dot(g, down[:, span], 0, 0)
        square = u * u
        t = jnp.tanh(u * (root + (root * 0.044715) * square))
        half = 0.5 + 0.5 * t
        mid_ref[0, :, span] = (u * half).astype(BF16)
        slope = half + (0.5 * u) * (1 - t * t) * (root + (3 * root * 0.044715) * square)
        gup = (grad_act * slope).astype(BF16)
        mid_ref[1, :, span] = gup
        gb_ref[:, span] += jnp.sum(gup.astype(F32), axis=0, keepdims=True)
    gh_ref[...] = dot(up[...], mid_ref[1], 1, 1).astype(BF16)
    out = dot(down[...], mid_ref[0], 1, 1).astype(BF16)
    n = own_ref.shape[0]
    own_ref[...], other_ref[...] = out[:n], out[n:]


def feed(spot, count, h_two, g_own, g_other, weights, bias_up, tile, old):
    depth, length = h_two.shape
    own = g_own.shape[0]
    hidden = bias_up.shape[1]
    column = lambda rows: pl.BlockSpec((rows, tile), lambda i, s: (0, s[0] + i))
    anywhere = pl.BlockSpec(memory_space=pl.ANY)
    vector = pl.BlockSpec((1, hidden), lambda i, s: (0, 0))
    local = lambda rows: pl.BlockSpec((rows, tile), lambda i, s: (0, i))
    aliases = {} if old is None else {9: 0}
    return pl.pallas_call(
        feed_kernel,
        grid_spec=pltpu.PrefetchScalarGridSpec(
            num_scalar_prefetch=1,
            grid=(count,),
            in_specs=[column(depth), column(own), column(own)]
            + [anywhere] * 4
            + [vector]
            + [anywhere] * len(aliases),
            out_specs=[
                pl.BlockSpec((2, tile, hidden), lambda i, s: (0, s[0] + i, 0)),
                local(own),
                local(own),
                local(depth),
                vector,
                pl.BlockSpec((1, own), lambda i, s: (0, 0)),
            ],
            scratch_shapes=[
                pltpu.VMEM((depth, hidden), BF16),
                pltpu.VMEM((depth, hidden), BF16),
                pltpu.VMEM((own, LANES), F32),
                pltpu.SemaphoreType.DMA((8,)),
            ],
        ),
        out_shape=[
            jax.ShapeDtypeStruct((2, length, hidden), BF16),
            *(jax.ShapeDtypeStruct((n, count * tile), BF16) for n in (own, own, depth)),
            jax.ShapeDtypeStruct((1, hidden), F32),
            jax.ShapeDtypeStruct((1, own), F32),
        ],
        input_output_aliases=aliases,
        compiler_params=params(50),
        cost_estimate=cost(8 * depth * count * tile * hidden, 12 * depth * hidden),
        name="feed",
    )(spot, h_two, g_own, g_other, *weights, bias_up, *([] if old is None else [old]))


def weight_grad_kernel(which_ref, h_ref, go_ref, gt_ref, m_ref, *rest):
    rest, (lhs, rhs, sems) = rest[:-3], rest[-3:]
    half = lhs.shape[1]
    step = pl.program_id(0)
    split = rest[0].shape[1]
    columns = (slice(0, split), slice(split, rhs.shape[1]))
    which = which_ref[0]

    def part(i):
        return pltpu.make_async_copy(h_ref.at[pl.ds(half * i, half)], lhs.at[i], sems.at[i])

    def column(i):
        return pltpu.make_async_copy(m_ref.at[which, :, columns[i]], rhs.at[:, columns[i]], sems.at[2 + i])

    @pl.when(first_step())
    def _():
        @pl.when(which == 0)
        def _():
            for i, g in enumerate((go_ref, gt_ref)):
                pltpu.make_async_copy(g, lhs.at[i], sems.at[i]).start()

        @pl.when(which == 1)
        def _():
            for i in range(2):
                part(i).start()

        column(0).start()
        column(1).start()
        part(0).wait()
        column(0).wait()

    @pl.when(last_step())
    def _():
        part(1).wait()

    rows = lhs[step]
    p = dot(rows, rhs[:, columns[0]], 1, 0)

    @pl.when(first_step())
    def _():
        column(1).wait()

    q = dot(rows, rhs[:, columns[1]], 1, 0)
    if len(rest) == 2:
        rest[0][...], rest[1][...] = p.astype(BF16), q.astype(BF16)
        return
    pg_ref, qg_ref, pk_ref, pa_ref, qk_ref, qa_ref = rest
    p = (p + pg_ref[...].astype(F32)).astype(BF16)
    q = (q + qg_ref[...].astype(F32)).astype(BF16)
    n = p.shape[0] // 4
    low = jnp.concatenate((p[:n], p[2 * n : 3 * n]), 0)
    high = jnp.concatenate((p[n : 2 * n], p[3 * n :]), 0)
    pk_ref[...], pa_ref[...] = unit(which_ref[1], low, high)
    qk_ref[...], qa_ref[...] = unit(which_ref[2], q[: 2 * n], q[2 * n :])


def weight_grad(which, h_two, g_own, g_other, middle, split, got=None):
    depth, length = h_two.shape
    hidden = middle.shape[2]
    steps = 2
    rows = depth // steps
    parts = (split, hidden - split)
    blocks = [pl.BlockSpec((rows, n), lambda i, s: (i, 0)) for n in parts]
    in_specs = [pl.BlockSpec(memory_space=pl.ANY)] * 4
    out_specs, shapes = blocks, [jax.ShapeDtypeStruct((depth, n), BF16) for n in parts]
    if got is not None:
        in_specs += blocks
        out_specs = [pl.BlockSpec((rows // 2, n), lambda i, s: (i, 0)) for n in parts for _ in range(2)]
        shapes = [jax.ShapeDtypeStruct((depth // 2, n), BF16) for n in parts for _ in range(2)]
    return pl.pallas_call(
        weight_grad_kernel,
        grid_spec=pltpu.PrefetchScalarGridSpec(
            num_scalar_prefetch=1,
            grid=(steps,),
            in_specs=in_specs,
            out_specs=out_specs,
            scratch_shapes=[
                pltpu.VMEM((steps, rows, length), BF16),
                pltpu.VMEM((length, hidden), BF16),
                pltpu.SemaphoreType.DMA((4,)),
            ],
        ),
        out_shape=shapes,
        compiler_params=params(60),
        cost_estimate=cost(2 * depth * length * hidden, 2 * (2 * depth + hidden) * length),
        name="weight_grad",
    )(which, h_two, g_own, g_other, middle, *(got or ()))


def mid_back_kernel(
    spot_ref, xo_ref, xt_ref, p_ref, go_ref, gt_ref, keep_ref, got_ref, m_ref, g_ref, v_ref,
    gp_ref, gq_ref, ma_ref, mb_ref, sa_ref, sb_ref, n_ref, w_own, w_other, gc, sums,
):
    @pl.when(first_step())
    def _():
        n = w_own.shape[1]
        parts = [own_first(spot_ref[2], w[:, :n]) for w in (m_ref, g_ref)]
        w_own[...], w_other[...] = unit(spot_ref[1], *parts)
        sums[...] = jnp.zeros_like(sums)

    own = xo_ref.shape[0]
    rank = spot_ref[2]
    keep, got = keep_ref[...].astype(F32), got_ref[...].astype(F32)
    gh = keep + jnp.concatenate((got[own:], got[:own]), 0)
    mid = jnp.concatenate((xo_ref[...], xt_ref[...]), 0).astype(F32) + p_ref[...].astype(F32)
    hat, inv = norm_rows(mid)
    e = gh * v_ref[:, 2:3]
    grad = jnp.concatenate((go_ref[...], gt_ref[...]), 0).astype(F32) + inv * (
        e - jnp.mean(e, axis=0, keepdims=True) - hat * jnp.mean(e * hat, axis=0, keepdims=True)
    )
    gp = grad.astype(BF16)
    gp_ref[...], gq_ref[...] = gp[:own], gp[own:]
    gc[...] = (dot(w_own[...], gp[:own], 1, 0) + dot(w_other[...], gp[own:], 1, 0)).astype(BF16)
    half = HEAD // 2
    a, b = ma_ref.shape[0], mb_ref.shape[0] - HEAD
    near, away = half * rank, own + half * (1 - rank)
    own_half = gc[rows_at((a + b) * (1 - rank), half)]
    other_half = gc[rows_at(own + (a + b) * rank, half)]
    ma_ref[...] = gc[rows_at(near, a)]
    mb_ref[:b] = gc[rows_at(near + a, b)]
    mb_ref[b : b + half] = own_half
    mb_ref[b + half :] = other_half
    sa_ref[...] = gc[rows_at(away, a)]
    sb_ref[:b] = gc[rows_at(away + a, b)]
    sb_ref[b : b + half] = other_half
    sb_ref[b + half :] = own_half
    sums[...] += jnp.concatenate(
        (lane_sums(gh * hat), lane_sums(gh), lane_sums(gp.astype(F32))), 1
    )

    @pl.when(last_step())
    def _():
        n_ref[...] = row_sums(sums[...])


def mid_back(spot, x_own, x_other, projected, g_own, g_other, keep, got, mine, got_w, vectors, rows_a, rows_b):
    own, length = x_own.shape
    depth = 2 * own
    share = length // 2
    column = lambda rows: pl.BlockSpec((rows, TILE), lambda i, s: (0, s[0] + i))
    local = lambda rows: pl.BlockSpec((rows, TILE), lambda i, s: (0, i))
    whole = lambda a: pl.BlockSpec(a.shape, lambda i, s: (0, 0))
    out = lambda rows: jax.ShapeDtypeStruct((rows, share), BF16)
    sizes = (own, own, rows_a, rows_b, rows_a, rows_b)
    return pl.pallas_call(
        mid_back_kernel,
        grid_spec=pltpu.PrefetchScalarGridSpec(
            num_scalar_prefetch=1,
            grid=(share // TILE,),
            in_specs=[column(own), column(own), column(depth), column(own), column(own)]
            + [local(depth)] * 2
            + [out_columns(depth)] * 2
            + [whole(vectors)],
            out_specs=[local(r) for r in sizes] + [pl.BlockSpec((3, depth), lambda i, s: (0, 0))],
            scratch_shapes=[pltpu.VMEM((depth, own), BF16)] * 2
            + [pltpu.VMEM((depth, TILE), BF16), pltpu.VMEM((depth, 3 * LANES), F32)],
        ),
        out_shape=[out(r) for r in sizes] + [jax.ShapeDtypeStruct((3, depth), F32)],
        compiler_params=params(60),
        cost_estimate=cost(2 * depth * depth * share, depth * share * 16),
        name="mid_back",
    )(spot, x_own, x_other, projected, g_own, g_other, keep, got, mine, got_w, vectors)


def half_lanes(columns):
    return -(-columns // (2 * LANES)) * LANES


def grads_kernel(place_ref, h_ref, g_ref, send_ref, keep_ref):
    cols = send_ref.shape[1]
    low = dot(h_ref[...], g_ref[:cols], 1, 1).astype(BF16)
    high = dot(h_ref[...], g_ref[g_ref.shape[0] - cols :], 1, 1).astype(BF16)
    keep_ref[...], send_ref[...] = unit(place_ref[1], low, high)


def grads_out_kernel(place_ref, h_ref, c_ref, g_ref, pm_ref, pg_ref, send_ref, keep_ref, gp):
    @pl.when(first_step())
    def _():
        share = pm_ref.shape[1]
        gp[:, :share], gp[:, share:] = unit(place_ref[0], pm_ref[...], pg_ref[...])

    out = half_lanes(gp.shape[0])
    cols = send_ref.shape[1] - out
    for lhs, rhs, n, to in (
        (h_ref, g_ref, cols, slice(0, cols)),
        (c_ref, gp, out, slice(cols, cols + out)),
    ):
        low = dot(lhs[...], rhs[:n], 1, 1).astype(BF16)
        high = dot(lhs[...], rhs[rhs.shape[0] - n :], 1, 1).astype(BF16)
        keep_ref[:, to], send_ref[:, to] = unit(place_ref[1], low, high)


def column_grads(places, cols, h_one, grad, context=None, gp=None, gp_got=None):
    depth, length = h_one.shape
    kernel, total, scratch = grads_kernel, cols, []
    part = pl.BlockSpec((depth // 2, length), lambda i, s: (i, 0))
    whole = lambda a: pl.BlockSpec(a.shape, lambda i, s: (0, 0))
    args, specs = [h_one, grad], [part, whole(grad)]
    if context is not None:
        kernel, total = grads_out_kernel, cols + half_lanes(gp.shape[0])
        args = [h_one, context, grad, gp, gp_got]
        specs = [part, part] + [whole(a) for a in args[2:]]
        scratch = [pltpu.VMEM((gp.shape[0], length), BF16)]
    return pl.pallas_call(
        kernel,
        grid_spec=pltpu.PrefetchScalarGridSpec(
            num_scalar_prefetch=1,
            grid=(2,),
            in_specs=specs,
            out_specs=[pl.BlockSpec((depth // 2, total), lambda i, s: (i, 0))] * 2,
            scratch_shapes=scratch,
        ),
        out_shape=[jax.ShapeDtypeStruct((depth, total), BF16)] * 2,
        compiler_params=params(32),
        cost_estimate=cost(4 * depth * total * length, 6 * depth * length),
        name="column_grads",
    )(places, *args)


def output_kernel(
    place_ref, x_ref, p_ref, b_ref, low_ref, high_ref, low_got_ref, high_got_ref, o_ref
):
    mine = pl.program_id(0) // (pl.num_programs(0) // 2) == place_ref[0]
    pick = lambda a, b: jnp.where(mine, a[...], b[...]).astype(F32)
    down = pick(high_ref, low_ref) + pick(low_got_ref, high_got_ref)
    o_ref[...] = (
        x_ref[...].astype(F32) + p_ref[...].astype(F32) + (down + b_ref[...])
    ).astype(BF16)


def close_output(places, x_own, projected, bias, low, high, low_got, high_got):
    own, length = x_own.shape
    column = pl.BlockSpec((own, TILE), lambda i, s: (0, i))
    steps = length // 2 // TILE
    half = pl.BlockSpec((own, TILE), lambda i, s: (0, lax.rem(i, steps)))
    return pl.pallas_call(
        output_kernel,
        grid_spec=pltpu.PrefetchScalarGridSpec(
            num_scalar_prefetch=1,
            grid=(2 * steps,),
            in_specs=[column] * 2 + [pl.BlockSpec((own, 1), lambda i, s: (0, 0))] + [half] * 4,
            out_specs=column,
        ),
        out_shape=jax.ShapeDtypeStruct((own, length), BF16),
        compiler_params=params(60),
        cost_estimate=cost(0, 0),
        name="close_output",
    )(places, x_own, projected, bias, low, high, low_got, high_got)


def tokens_kernel(place_ref, x_ref, gp_ref, gq_ref, keep_ref, got_ref, s_ref, v_ref, o_ref):
    own = x_ref.shape[0]
    mine = pl.program_id(0) // (pl.num_programs(0) // 2) == place_ref[0]
    gp = jnp.where(mine, gp_ref[...], gq_ref[...]).astype(F32)
    e = (keep_ref[...].astype(F32) + got_ref[:own].astype(F32)) * v_ref[:own, 0:1]
    others = got_ref[own:].astype(F32)
    mean, inv = s_ref[2:3], s_ref[3:4]
    total = (s_ref[:2] + (others[:2] + others[2:4])) * (0.5 / own)
    hat = (x_ref[...].astype(F32) - mean) * inv
    o_ref[...] = gp + inv * (e - total[:1] - hat * total[1:])


def close_tokens(places, x_own, gp, gp_got, keep, got, stats, vectors):
    own, length = x_own.shape
    steps = length // 2 // TILE
    column = lambda rows: pl.BlockSpec((rows, TILE), lambda i, s: (0, i))
    half = pl.BlockSpec((own, TILE), lambda i, s: (0, lax.rem(i, steps)))
    return pl.pallas_call(
        tokens_kernel,
        grid_spec=pltpu.PrefetchScalarGridSpec(
            num_scalar_prefetch=1,
            grid=(2 * steps,),
            in_specs=[column(own), half, half, column(own), column(own + SPARE), column(4)]
            + [pl.BlockSpec(vectors.shape, lambda i, s: (0, 0))],
            out_specs=column(own),
        ),
        out_shape=jax.ShapeDtypeStruct((own, length), F32),
        compiler_params=params(60),
        cost_estimate=cost(0, 0),
        name="close_tokens",
    )(places, x_own, gp, gp_got, keep, got, stats, vectors)


def qkv_back_kernel(
    core_ref, xo_ref, xt_ref, gb_ref, ga_ref, bm_ref, bg_ref, am_ref, ag_ref, v_ref,
    keep_ref, send_ref, s_ref, n_ref, db_ref, da_ref, b_low, b_high, a_low, a_high, n_sum, b_sum, a_sum,
):
    @pl.when(first_step())
    def _():
        b_low[...], b_high[...] = unit(core_ref[0], bm_ref[...], bg_ref[...])
        a_low[...], a_high[...] = unit(core_ref[0], am_ref[...], ag_ref[...])
        for r in (n_sum, b_sum, a_sum):
            r[...] = jnp.zeros_like(r)

    own = xo_ref.shape[0]
    gb, ga = gb_ref[...], ga_ref[...]
    cols_b, cols_a = b_low.shape[1], a_low.shape[1]
    twice = 2 * cols_b - gb.shape[0]
    rest = jnp.concatenate((jnp.zeros((twice, gb.shape[1]), BF16), gb[cols_b:]), 0)
    gh = (dot(b_low[...], gb[:cols_b], 1, 0) + dot(b_high[...], rest, 1, 0)) + (
        dot(a_low[...], ga[:cols_a], 1, 0) + dot(a_high[...], ga[cols_a:], 1, 0)
    )
    keep_ref[...] = gh[:own].astype(BF16)
    send_ref[:own] = gh[own:].astype(BF16)
    x = jnp.concatenate((xo_ref[...], xt_ref[...]), 0).astype(F32)
    hat, inv = norm_rows(x)
    both = gh * hat
    gain = v_ref[:, 0:1]
    mine = jnp.concatenate(
        (jnp.sum(gh * gain, axis=0, keepdims=True), jnp.sum(both * gain, axis=0, keepdims=True)), 0
    )
    s_ref[...] = jnp.concatenate((mine, jnp.mean(x, axis=0, keepdims=True), inv), 0)
    high = mine.astype(BF16).astype(F32)
    parts = jnp.concatenate((high, mine - high, jnp.zeros((SPARE - 4, mine.shape[1]), F32)), 0)
    send_ref[own:] = parts.astype(BF16)
    n_sum[...] += jnp.concatenate((lane_sums(both), lane_sums(gh)), 1)
    b_sum[...] += lane_sums(gb.astype(F32))
    a_sum[...] += lane_sums(ga.astype(F32))

    @pl.when(last_step())
    def _():
        n_ref[...] = row_sums(n_sum[...])
        db_ref[...] = row_sums(b_sum[...])
        da_ref[...] = row_sums(a_sum[...])


def qkv_back(core, x_own, x_other, grad_b, grad_a, w_b, w_a, vectors):
    own = x_own.shape[0]
    depth = 2 * own
    column = lambda rows: pl.BlockSpec((rows, TILE), lambda i, s: (0, i))
    whole = lambda a: pl.BlockSpec(a.shape, lambda i, s: (0, 0))
    span = x_own.shape[1]
    out = jax.ShapeDtypeStruct
    rows = (depth, grad_b.shape[0], grad_a.shape[0])
    flat = [out((n, r), F32) for n, r in zip((2, 1, 1), rows)]
    return pl.pallas_call(
        qkv_back_kernel,
        grid_spec=pltpu.PrefetchScalarGridSpec(
            num_scalar_prefetch=1,
            grid=(span // TILE,),
            in_specs=[column(own)] * 2
            + [column(grad_b.shape[0]), column(grad_a.shape[0])]
            + [whole(a) for a in (*w_b, *w_a, vectors)],
            out_specs=[column(own), column(own + SPARE), column(4)] + [whole(t) for t in flat],
            scratch_shapes=[pltpu.VMEM(w.shape, BF16) for w in (*w_b, *w_a)]
            + [pltpu.VMEM((r, n * LANES), F32) for n, r in zip((2, 1, 1), rows)],
        ),
        out_shape=[out((own, span), BF16), out((own + SPARE, span), BF16), out((4, span), F32)]
        + flat,
        compiler_params=params(36),
        cost_estimate=cost(2 * depth * span * (rows[1] + rows[2]), depth * span * 12),
        name="qkv_back",
    )(core, x_own, x_other, grad_b, grad_a, *w_b, *w_a, vectors)


def by_bit(bit, a, b):
    return jnp.where(lax.axis_index("wide") & bit == 0, a, b)


def flip(a, bit):
    size = lax.axis_size("wide")
    return lax.ppermute(a, "wide", [(i, i ^ bit) for i in range(size)])


def join_kernel(place_ref, kept_ref, got_ref, out_ref):
    first = place_ref[0] == 0
    if out_ref.ndim == 2:
        half = kept_ref.shape[0]
        out_ref[:half] = jnp.where(first, kept_ref[...], got_ref[...])
        out_ref[half:] = jnp.where(first, got_ref[...], kept_ref[...])
    else:
        out_ref[:, 0:1] = jnp.where(first, kept_ref[...], got_ref[...])
        out_ref[:, 1:2] = jnp.where(first, got_ref[...], kept_ref[...])


def join(kept, got, place, axis):
    rows, cols = kept.shape[-2:]
    call = dict(compiler_params=params(16), cost_estimate=cost(0, 0), name="join")
    place = place.astype(jnp.int32)[None]
    if axis is None:
        spec = lambda n: pl.BlockSpec((n, cols), lambda i, s: (0, 0))
        grid_spec = pltpu.PrefetchScalarGridSpec(
            num_scalar_prefetch=1, grid=(1,), in_specs=[spec(rows)] * 2, out_specs=spec(2 * rows)
        )
        shape = jax.ShapeDtypeStruct((2 * rows, cols), kept.dtype)
        return pl.pallas_call(join_kernel, grid_spec=grid_spec, out_shape=shape, **call)(place, kept, got)
    outer, inner = math.prod(kept.shape[:axis]), math.prod(kept.shape[axis:-1])
    spec = lambda n: pl.BlockSpec((outer, n, inner, cols), lambda i, s: (0, 0, 0, 0))
    grid_spec = pltpu.PrefetchScalarGridSpec(
        num_scalar_prefetch=1, grid=(1,), in_specs=[spec(1)] * 2, out_specs=spec(2)
    )
    shape = jax.ShapeDtypeStruct((outer, 2, inner, cols), kept.dtype)
    args = [a.reshape(outer, 1, inner, cols) for a in (kept, got)]
    out = pl.pallas_call(join_kernel, grid_spec=grid_spec, out_shape=shape, **call)(place, *args)
    return out.reshape(kept.shape[:axis] + (2,) + kept.shape[axis:])


def fold_kernel(index_ref, kept_ref, got_ref, keep_ref, away_ref):
    total = kept_ref[...].astype(F32) + got_ref[...].astype(F32)
    if kept_ref.ndim == 2:
        half = keep_ref.shape[0]
        low, high = total[:half], total[half:]
        first = index_ref[0] == 0
        keep_ref[...], away_ref[...] = jnp.where(first, low, high), jnp.where(first, high, low)
        return
    total = total.astype(BF16).reshape(keep_ref.shape)

    @pl.when(pl.program_id(1) == 0)
    def _():
        keep_ref[...] = total

    @pl.when(pl.program_id(1) == 1)
    def _():
        away_ref[...] = total


def fold(kept, got, index, axis):
    rows, cols = kept.shape[-2:]
    call = dict(compiler_params=params(16), cost_estimate=cost(0, 0), name="fold")
    index = index.astype(jnp.int32)[None]
    if axis is None:
        spec = lambda n: pl.BlockSpec((n, cols), lambda i, s: (0, 0))
        grid_spec = pltpu.PrefetchScalarGridSpec(
            num_scalar_prefetch=1, grid=(1,), in_specs=[spec(rows)] * 2, out_specs=[spec(rows // 2)] * 2
        )
        shape = [jax.ShapeDtypeStruct((rows // 2, cols), F32)] * 2
        return pl.pallas_call(fold_kernel, grid_spec=grid_spec, out_shape=shape, **call)(index, kept, got)
    outer, inner = math.prod(kept.shape[:axis]), math.prod(kept.shape[axis + 1 : -1])
    grid_spec = pltpu.PrefetchScalarGridSpec(
        num_scalar_prefetch=1,
        grid=(outer, 2),
        in_specs=[pl.BlockSpec((1, 1, inner, cols), lambda a, j, s: (a, j ^ s[0], 0, 0))] * 2,
        out_specs=[pl.BlockSpec((1, inner, cols), lambda a, j, s: (a, 0, 0))] * 2,
    )
    shape = [jax.ShapeDtypeStruct((outer, inner, cols), BF16)] * 2
    args = [a.reshape(outer, 2, inner, cols) for a in (kept, got)]
    out = pl.pallas_call(fold_kernel, grid_spec=grid_spec, out_shape=shape, **call)(index, *args)
    return [o.reshape(kept.shape[:axis] + kept.shape[axis + 1 :]) for o in out]


class Gather:
    def __init__(self, a, b, order):
        self.kept = by_bit(1, a, b)
        self.got = flip(by_bit(1, b, a), 1)
        self.order = list(order)
        self.bits = []
        self.last = None

    def merge(self):
        if self.last is None:
            axis, place = None, lax.axis_index("wide") & 1
        else:
            axis = sum(1 for b in self.bits if b > self.last)
            place = (lax.axis_index("wide") & self.last != 0).astype(jnp.int32)
            if self.last == max(self.order + self.bits + [self.last]):
                place = place ^ lax.axis_index("narrow")
            self.bits.append(self.last)
        self.cur = join(self.kept, self.got, place, axis)

    def came(self):
        return self.got

    def come(self, value):
        self.got = value

    def held(self):
        return self.cur

    def hold(self, value):
        self.cur = value

    def send(self):
        self.last = self.order.pop(0) if self.order else 1
        if self.last == 1:
            self.cur = self.cur.reshape(-1, self.cur.shape[-1])
        self.kept, self.got = self.cur, flip(self.cur, self.last)


class Whole:
    def __init__(self, a, b):
        self.kept = by_bit(1, a, b)
        self.got = flip(by_bit(1, b, a), 1)
        self.stage = 0

    def merge(self):
        if self.stage == 0:
            low = lax.axis_index("wide") & 1 == 0
            kept, got = self.kept, self.got
            self.cur = jnp.where(
                low, jnp.concatenate((kept, got), 0), jnp.concatenate((got, kept), 0)
            )

    def came(self):
        return self.got if self.stage == 0 else self.cur

    def come(self, value):
        if self.stage == 0:
            self.got = value
        else:
            self.cur = value

    def held(self):
        return self.cur

    def hold(self, value):
        self.cur = value

    def send(self):
        if self.stage == 0:
            size = lax.axis_size("wide")
            groups = [list(range(c, size, 2)) for c in range(2)]
            self.cur = lax.all_gather(
                self.cur, "wide", axis=0, tiled=True, axis_index_groups=groups
            )
        else:
            self.got = flip(self.cur, 1)
        self.stage += 1


class Scatter:
    def __init__(self, send, order):
        self.got = flip(send, 1)
        self.order = list(order)
        self.axes = sorted(order, reverse=True)
        self.top = self.axes[0]

    def merge(self):
        kept, got = self.kept, self.got
        if self.order:
            if kept.ndim == 2:
                shape = (2,) * len(self.axes) + (-1, kept.shape[-1])
                kept, got = kept.reshape(shape), got.reshape(shape)
            bit = self.order.pop(0)
            axis = self.axes.index(bit)
            self.axes.remove(bit)
            index = (lax.axis_index("wide") & bit != 0).astype(jnp.int32)
            if bit == self.top:
                index = index ^ lax.axis_index("narrow")
        else:
            bit, axis, index = 1, None, lax.axis_index("wide") & 1
        self.bit = bit
        self.keep, self.away = fold(kept, got, index, axis)

    def next_index(self):
        index = (lax.axis_index("wide") & self.order[0] != 0).astype(jnp.int32)
        return index ^ lax.axis_index("narrow") if self.order[0] == self.top else index

    def start(self, other, *halves):
        for m, keep, away in ((self, *halves[:2]), (other, *halves[2:])):
            m.bit = m.order.pop(0)
            m.axes.remove(m.bit)
            shape = (2,) * len(m.axes) + (-1, keep.shape[-1])
            m.keep, m.away = keep.reshape(shape), away.reshape(shape)

    def came(self):
        return self.got

    def come(self, value):
        self.got = value

    def held(self):
        return self.keep, self.away

    def hold(self, value):
        self.keep, self.away = value

    def send(self):
        self.kept, self.got = self.keep, flip(self.away, self.bit)

    def result(self):
        return by_bit(1, self.kept, self.got), by_bit(1, self.got, self.kept)


def meet(values, *moves, wait=()):
    moves = list(moves) + list(wait)
    values, came = lax.optimization_barrier((values, [m.came() for m in moves]))
    for m, c in zip(moves, came):
        m.come(c)
        m.merge()
    values, held = lax.optimization_barrier((values, [m.held() for m in moves]))
    for m, h in zip(moves, held):
        m.hold(h)
        if m not in wait:
            m.send()
    return values


def send_now(values, *moves):
    values, held = lax.optimization_barrier((values, [m.held() for m in moves]))
    for m, h in zip(moves, held):
        m.hold(h)
        m.send()
    return values


def pair_plan(
    tokens,
    piece_starts,
    ln1_gain,
    ln1_bias,
    w_qkv,
    bias_qv,
    w_out,
    bias_out,
    ln2_gain,
    ln2_bias,
    w_up,
    bias_up,
    w_down,
    bias_down,
    cotangent,
):
    rank = lax.axis_index("narrow")
    first = rank == 0
    core = lax.axis_index("wide") & 1
    own, length = tokens.shape
    depth = 2 * own
    whole = own // HEAD * HEAD
    rest = own - whole
    rows_a = whole // 2
    rows_b = whole - rows_a + 2 * rest
    heads_a, heads_b = rows_a // HEAD, rows_b // HEAD
    block = w_out.shape[0]
    hidden = w_up.shape[1]
    tile = length // 4
    part = -(-(hidden + own) // 256) * LANES
    split = hidden - part
    split_back = hidden // 256 * LANES + 2 * LANES
    rank_arg = rank.astype(jnp.int32)[None]

    def swap(a):
        return lax.ppermute(a, "narrow", [(0, 1), (1, 0)])

    def heads_first(a):
        return jnp.where(first, a, jnp.concatenate((a[..., rest:], a[..., :rest]), -1))

    def heads_back(a):
        return jnp.where(first, a, jnp.concatenate((a[..., whole:], a[..., :whole]), -1))

    def at_rows(bias):
        return jnp.stack((bias[0], jnp.zeros_like(bias[0]), bias[1])).reshape(-1, 1)

    far, near, side = 8, 4, 2
    inward, outward = (far, near, side), (side, far, near)
    w_out_other = swap(w_out)
    w_heads = heads_first(w_qkv)
    shard_a = w_heads[:, :, :rows_a].reshape(block, -1)
    cols_a = shard_a.shape[1] // 2
    get_a = Gather(shard_a[:, :cols_a], shard_a[:, cols_a:], inward)
    pad = jnp.zeros((block, part - split - own), BF16)
    get_p = Whole(
        jnp.concatenate((w_out, pad, w_up[:, :split]), 1),
        jnp.concatenate((w_out_other, pad, w_down.T[:, :split]), 1),
    )
    get_p.merge()
    get_p.send()
    bias_local = heads_first(bias_qv)
    own_vectors = jnp.concatenate(
        (jnp.stack((ln1_gain, ln1_bias, ln2_gain, ln2_bias, bias_out)), bias_local), 0
    )
    half_rows = w_heads[:, :, whole:].reshape(-1, own)
    count = own_vectors.shape[0]
    small_swap = swap(jnp.concatenate((own_vectors, half_rows), 0))
    w_up_in, w_down_in, g_own = meet((w_up, w_down, cotangent), get_a)
    small_swap, x_own = lax.optimization_barrier((small_swap, tokens))
    x_other = swap(x_own)
    other_half = small_swap[count:].reshape(block, 3, rest)
    shard_b = jnp.concatenate((w_heads[:, :, rows_a:], other_half), 2).reshape(block, -1)
    cols_b = -(-shard_b.shape[1] // 256) * 128
    skip = shard_b.shape[1] - cols_b
    get_b = Gather(shard_b[:, :cols_b], shard_b[:, skip:], inward)
    other_vectors = small_swap[:count]
    vectors = jnp.concatenate((own_vectors[:5], other_vectors[:5]), 1).astype(F32).T
    gain_one, shift_one = vectors[:, 0:1], vectors[:, 1:2]
    bias_f = bias_local.astype(F32)
    bias_a = bias_f[:, :rows_a]
    bias_b = jnp.concatenate((bias_f[:, rows_a:], other_vectors[5:, whole:].astype(F32)), 1)
    bias_a, bias_b = at_rows(bias_a), at_rows(bias_b)
    w_down_t = w_down_in.T
    get_q = Whole(w_up_in[:, split:], w_down_t[:, split:])
    meet((), get_a, get_b, get_q)
    starts, g_own = meet((piece_starts[0], g_own), get_a, get_b)
    g_other = swap(g_own)
    seen = mask_bias(starts, length)
    seen, x_other, bias_a, bias_b, vectors = meet((seen, x_other, bias_a, bias_b, vectors), get_a, get_b)
    x_other, get_a.got = meet((x_other, get_a.got))

    core_arg = core[None]
    w_a = (get_a.cur, get_a.got)
    h_one, qkv_a = norm_qkv(core_arg, tokens, x_other, *w_a, vectors, bias_a)
    qkv_a = qkv_a.reshape(3, rows_a, length)

    context_a, lse_a = attend(seen, qkv_a, 0, heads_a)
    context_a, h_one = meet((context_a, h_one), get_b, get_p)
    h_b, get_b.got = meet((h_one, get_b.got))

    context_a_other = swap(after(context_a, g_other))
    w_b = (get_b.cur, get_b.got)
    qkv_b = qkv_of(core_arg, h_b, *w_b, bias_b).reshape(3, rows_b, length)
    whole_b = heads_b - 1
    half_b = whole_b // 2
    context_b, lse_b = attend(seen, qkv_b, 0, half_b)
    context_b, qkv_d = meet((context_b, qkv_b))
    context_b_other = swap(after(context_b, context_a_other))
    context_d, lse_d = attend(seen, qkv_d, half_b, whole_b - half_b)
    context_d, qkv_c = meet((context_d, qkv_d))

    context_d_other = swap(after(context_d, context_b_other))
    context_c, lse_c = attend(seen, qkv_c, whole_b, 1)
    lse_b = jnp.concatenate((lse_b, lse_d, lse_c), 0)
    context_a_other, context_b_other, context_d_other, context_c, get_p.got = meet(
        (context_a_other, context_b_other, context_d_other, context_c, get_p.got), get_q
    )

    pieces = (
        context_a, context_b, context_d, context_a_other, context_b_other, context_d_other, context_c
    )
    w_o = (get_p.cur, get_p.got)
    places = jnp.stack((rank, core)).astype(jnp.int32)
    projected, h_two, context = project(places, tokens, x_other, pieces, *w_o, vectors)
    projected, h_two, context, get_q.got = meet((projected, h_two, context, get_q.got))

    weights = (get_p.cur, get_p.got, get_q.cur, get_q.got)
    bias_up_f = bias_up.astype(F32)[None]
    steps = length // 2 // TILE

    def spot(at):
        return jnp.stack((at, core, rank)).astype(jnp.int32)

    old, low_own, low_other, gh_send, gb_send, gs_send = feed(
        spot(steps * (1 - rank)), steps, h_two, cotangent, g_other, weights, bias_up_f, TILE, None
    )
    old, gh_send = meet((old, gh_send))
    gh_got = swap(gh_send)
    middle, high_own, high_other, gh_keep, gb_keep, gs_keep = feed(
        spot(steps * rank), steps, h_two, cotangent, g_other, weights, bias_up_f, TILE, old
    )
    grad_bias_up = gb_send + gb_keep
    send_p, send_q = weight_grad(core[None], h_two, cotangent, g_other, middle, split_back)
    gh_got, gh_keep, send_p, send_q, middle, low_other = meet(
        (gh_got, gh_keep, send_p, send_q, middle, low_other)
    )

    put_p = Scatter(send_p, (side, near, far))
    put_q = Scatter(send_q, (near, far, side))
    low_got = swap(low_other)
    gp, gp_away, mine_a, mine_b, send_a, send_b, grad_two = mid_back(
        spot(steps * rank), tokens, x_other, projected, cotangent, g_other, gh_keep,
        gh_got, *w_o, vectors, rows_a, rows_b,
    )
    gp, gp_away, mine_a, mine_b, send_a, send_b, middle, put_p.got, put_q.got = meet(
        (gp, gp_away, mine_a, mine_b, send_a, send_b, middle, put_p.got, put_q.got)
    )

    got_b = swap(send_b)
    put_p.start(put_q, *weight_grad(
        jnp.stack((1 - core, put_p.next_index(), put_q.next_index())).astype(jnp.int32),
        h_two, cotangent, g_other, middle, split_back, (put_p.got, put_q.got),
    ))
    got_b, mine_b, send_a, gp_away, low_got = send_now(
        meet((got_b, mine_b, send_a, gp_away, low_got)), put_p, put_q
    )

    got_a = swap(send_a)
    gp_got = swap(gp_away)
    back_b = attend_back(seen, rank_arg, qkv_b, mine_b, got_b, lse_b, 0, heads_b, True)
    back_b, got_a, gp_got, high_other = meet((back_b, got_a, gp_got, high_other), put_p, put_q)

    high_got = swap(high_other)
    grad_b = back_b.reshape(3 * rows_b, length)

    half_a = heads_a // 2
    back_a = attend_back(seen, rank_arg, qkv_a, mine_a, got_a, lse_a, 0, half_a, False)
    send_b, keep_b = column_grads(places, cols_b, h_one, grad_b, context, gp, gp_got)
    back_a, send_b, keep_b, high_got = meet(
        (back_a, send_b, keep_b, high_got), wait=(put_p, put_q)
    )
    put_b = Scatter(send_b, (side, near, far))
    put_b.kept = keep_b
    back_a = attend_back(
        seen, rank_arg, qkv_a, mine_a, got_a, lse_a, half_a, heads_a - half_a, False, back_a
    )
    back_a = send_now(meet(back_a, put_b), put_p, put_q)
    grad_a = back_a.reshape(3 * rows_a, length)

    def vector_parts(sums):
        def row(a):
            return jnp.pad(a, ((0, 0), (0, depth - a.shape[1])))

        low = [grad_bias_up[:, :depth], grad_bias_up[:, depth:]]
        return jnp.concatenate(
            (sums[0], grad_two, row(sums[1]), row(sums[2]), row(gs_send + gs_keep), *map(row, low))
        )

    send_a, keep_a = column_grads(places, cols_a, h_one, grad_a)
    put_a = Scatter(send_a, (side, near, far))
    put_a.kept = keep_a
    keep, send, stats, *sums = qkv_back(
        core_arg, tokens, x_other, grad_b, grad_a, w_b, w_a, vectors
    )
    got = swap(send)
    keep, stats, sums, low_got = meet((keep, stats, sums, low_got), put_a, put_b, put_p, put_q)
    total = vector_parts(sums)
    total = total + flip(total, 1)
    output = close_output(
        places, tokens, projected, bias_down.astype(F32)[:, None], low_own, high_own, low_got, high_got
    )
    total, output = meet((total, output), put_a, put_b)
    total = total + flip(total, side)
    total = meet(total, put_a)
    total = total + flip(total, near)
    total, got = meet((total, got), put_a, put_b)
    total = total + flip(total, far)
    grad_tokens = close_tokens(places, tokens, gp, gp_got, keep, got, stats, vectors)
    sum_up_p, sum_down_p = put_p.result()
    sum_up_q, sum_down_q = put_q.result()
    low_b, high_b = put_b.result()
    sum_a = jnp.concatenate(put_a.result(), 1).reshape(block, 3, rows_a)
    out_cols = half_lanes(own)
    sum_out = jnp.concatenate((low_b[:, cols_b:], high_b[:, cols_b + 2 * out_cols - own :]), 1)
    sum_b = jnp.concatenate((low_b[:, :cols_b], high_b[:, cols_b - skip : cols_b]), 1)
    sum_b = sum_b.reshape(block, 3, rows_b)[:, :, : rows_b - rest]
    sum_w_qkv = heads_back(jnp.concatenate((sum_a, sum_b), 2))

    two = total[:5, :own] + swap(total[:5, own:])
    vec = [
        jnp.concatenate(
            (total[6, i * rows_a : (i + 1) * rows_a], total[5, i * rows_b : (i + 1) * rows_b - rest])
        )
        for i in (0, 2)
    ]
    return (
        output,
        grad_tokens,
        two[0],
        two[1],
        sum_w_qkv,
        heads_back(jnp.stack(vec)),
        sum_out,
        two[4],
        two[2],
        two[3],
        jnp.concatenate((sum_up_p, sum_up_q), 1),
        jnp.concatenate((total[8], total[9]))[:hidden],
        jnp.concatenate((sum_down_p, sum_down_q), 1).T,
        total[7, :own],
    )


def solution(mesh):
    in_specs = (
        P("narrow", "wide"),
        P("wide", None),
        P("narrow"),
        P("narrow"),
        P("wide", None, "narrow"),
        P(None, "narrow"),
        P("wide", "narrow"),
        P("narrow"),
        P("narrow"),
        P("narrow"),
        P("wide", "narrow"),
        P("narrow"),
        P("narrow", "wide"),
        P("narrow"),
        P("narrow", "wide"),
    )
    out_specs = (
        P("narrow", "wide"),
        P("narrow", "wide"),
        P("narrow"),
        P("narrow"),
        P("wide", None, "narrow"),
        P(None, "narrow"),
        P("wide", "narrow"),
        P("narrow"),
        P("narrow"),
        P("narrow"),
        P("wide", "narrow"),
        P("narrow"),
        P("narrow", "wide"),
        P("narrow"),
    )
    paired = mesh.shape["narrow"] == 2 and mesh.shape["wide"] == 16
    return jax.shard_map(
        pair_plan if paired else any_mesh, mesh=mesh, in_specs=in_specs, out_specs=out_specs, check_vma=False
    )
```

```python
import functools
import math
from functools import partial

import jax
import jax.numpy as jnp
from jax import lax
from jax.experimental import pallas as pl
from jax.experimental.pallas import tpu as pltpu
from jax.sharding import PartitionSpec as P

HEADS = 17
PIECE = 256


EPSILON = 1e-05


def normalize(row_data, gain_vec, shift_vec):
    centre = jnp.mean(row_data, axis=-1, keepdims=True)
    centred = row_data - centre
    spread = jnp.mean(centred * centred, axis=-1, keepdims=True)
    return centred * lax.rsqrt(spread + EPSILON) * gain_vec + shift_vec


def norm_back(row_data, gain_vec, shift_vec, grad_rows):
    unused, pull_back = jax.vjp(normalize, row_data, gain_vec, shift_vec)
    return pull_back(grad_rows)


def full_rows(partial_rows):
    return lax.psum(partial_rows, "narrow")


def visible_mask(starts, query_pos, key_pos):
    query_in = (query_pos[:, None] >= starts[None, :]) & (
        query_pos[:, None] < starts[None, :] + PIECE
    )
    key_in = (key_pos[:, None] >= starts[None, :]) & (key_pos[:, None] < starts[None, :] + PIECE)
    shared = jnp.any(query_in[:, None, :] & key_in[None, :, :], axis=-1)
    return (key_pos[None, :] <= query_pos[:, None]) | shared


def to_heads(matrix):
    return matrix.reshape(matrix.shape[0], HEADS, matrix.shape[1] // HEADS)


def attention_scores(query_rows, key_full, visible, score_scale):
    raw = (
        jnp.einsum(
            "qhd,khd->hqk",
            to_heads(query_rows),
            to_heads(key_full),
            preferred_element_type=jnp.float32,
        )
        * score_scale
    )
    return jnp.where(visible[None], raw, -1e30)


def any_mesh(
    tokens,
    piece_starts,
    ln1_gain,
    ln1_bias,
    w_qkv,
    bias_qv,
    w_out,
    bias_out,
    ln2_gain,
    ln2_bias,
    w_up,
    bias_up,
    w_down,
    bias_down,
    cotangent,
):
    narrow_size = lax.axis_size("narrow")
    narrow_rank = lax.axis_index("narrow")
    col_width, length = tokens.shape
    full_width = col_width * narrow_size
    queries = length // narrow_size
    score_scale = (full_width // HEADS) ** (-0.5)
    col_start = narrow_rank * col_width
    row_start = narrow_rank * queries

    def own_cols(matrix):
        return lax.dynamic_slice_in_dim(matrix, col_start, col_width, matrix.ndim - 1)

    x_cols, dy_cols, gain_one, shift_one, gain_two, shift_two = (
        lax.all_gather(tokens, "narrow", axis=0, tiled=True),
        lax.all_gather(cotangent, "narrow", axis=0, tiled=True),
        lax.all_gather(ln1_gain, "narrow", axis=0, tiled=True),
        lax.all_gather(ln1_bias, "narrow", axis=0, tiled=True),
        lax.all_gather(ln2_gain, "narrow", axis=0, tiled=True),
        lax.all_gather(ln2_bias, "narrow", axis=0, tiled=True),
    )
    x_rows = x_cols.T
    dy_rows = dy_cols.T
    qkv_cols, out_cols, up_cols, down_rows = (
        lax.all_gather(w_qkv, "wide", axis=0, tiled=True),
        lax.all_gather(w_out, "wide", axis=0, tiled=True),
        lax.all_gather(w_up, "wide", axis=0, tiled=True),
        lax.all_gather(w_down, "wide", axis=1, tiled=True),
    )
    gain_one = gain_one.astype(jnp.float32)
    shift_one = shift_one.astype(jnp.float32)
    gain_two = gain_two.astype(jnp.float32)
    shift_two = shift_two.astype(jnp.float32)
    x_full = x_rows.astype(jnp.float32)
    h_one = normalize(x_full, gain_one, shift_one).astype(jnp.bfloat16)
    mixed = jnp.einsum("td,dcf->tcf", h_one, qkv_cols, preferred_element_type=jnp.float32)
    bias_cols = bias_qv.astype(jnp.float32)
    query_cols = (mixed[:, 0] + bias_cols[0]).astype(jnp.bfloat16)
    key_cols = mixed[:, 1].astype(jnp.bfloat16)
    value_cols = (mixed[:, 2] + bias_cols[1]).astype(jnp.bfloat16)
    query_full, key_full, value_full = (
        lax.all_gather(query_cols, "narrow", axis=1, tiled=True),
        lax.all_gather(key_cols, "narrow", axis=1, tiled=True),
        lax.all_gather(value_cols, "narrow", axis=1, tiled=True),
    )
    query_rows = lax.dynamic_slice_in_dim(query_full, row_start, queries, 0)
    query_pos = row_start + jnp.arange(queries, dtype=jnp.int32)
    key_pos = jnp.arange(length, dtype=jnp.int32)
    visible = visible_mask(piece_starts[0], query_pos, key_pos)
    masked = attention_scores(query_rows, key_full, visible, score_scale)
    row_top = jnp.max(masked, axis=-1, keepdims=True)
    weights = jnp.exp(masked - row_top)
    row_total = jnp.sum(weights, axis=-1, keepdims=True)
    log_total = row_top + jnp.log(row_total)
    probs_low = (weights / row_total).astype(jnp.bfloat16)
    context = jnp.einsum(
        "hqk,khd->qhd", probs_low, to_heads(value_full), preferred_element_type=jnp.float32
    )
    context = context.reshape(queries, full_width).astype(jnp.bfloat16)
    context_full = lax.all_gather(context, "narrow", axis=0, tiled=True)
    projected = jnp.dot(
        context_full, out_cols, preferred_element_type=jnp.float32
    ) + bias_out.astype(jnp.float32)
    projected_low = projected.astype(jnp.bfloat16)
    projected_full = lax.all_gather(projected_low, "narrow", axis=1, tiled=True)
    mid_full = x_full + projected_full.astype(jnp.float32)
    mid_rows = tokens.T.astype(jnp.float32) + projected_low.astype(jnp.float32)
    h_two = normalize(mid_full, gain_two, shift_two).astype(jnp.bfloat16)
    up_pre = jnp.dot(h_two, up_cols, preferred_element_type=jnp.float32) + bias_up.astype(
        jnp.float32
    )
    act_value, gelu_pull = jax.vjp(partial(jax.nn.gelu, approximate=True), up_pre)
    act_low = act_value.astype(jnp.bfloat16)
    partial_down = jnp.dot(act_low, down_rows, preferred_element_type=jnp.float32)
    down_sum = lax.psum_scatter(
        partial_down.astype(jnp.bfloat16), "narrow", scatter_dimension=1, tiled=True
    ).astype(jnp.float32)
    output = (mid_rows + (down_sum + bias_down.astype(jnp.float32))).astype(jnp.bfloat16)
    grad_out = cotangent.T.astype(jnp.float32)
    grad_bias_down = jnp.sum(grad_out, axis=0)
    grad_w_down = jnp.einsum("tf,td->fd", act_low, dy_rows, preferred_element_type=jnp.float32)
    grad_act = jnp.einsum("td,fd->tf", dy_rows, down_rows, preferred_element_type=jnp.float32)
    grad_up = gelu_pull(grad_act)[0].astype(jnp.bfloat16)
    grad_bias_up = jnp.sum(grad_up.astype(jnp.float32), axis=0)
    grad_w_up = jnp.einsum("td,tf->df", h_two, grad_up, preferred_element_type=jnp.float32)
    grad_h_two = full_rows(
        jnp.einsum("tf,df->td", grad_up, up_cols, preferred_element_type=jnp.float32)
    )
    grad_mid_full, grad_gain_two, grad_shift_two = norm_back(
        mid_full, gain_two, shift_two, grad_h_two
    )
    grad_mid = grad_out + own_cols(grad_mid_full)
    grad_projected = grad_mid.astype(jnp.bfloat16)
    grad_bias_out = jnp.sum(grad_projected.astype(jnp.float32), axis=0)
    grad_w_out = jnp.einsum(
        "td,tc->dc", context_full, grad_projected, preferred_element_type=jnp.float32
    )
    grad_context = lax.psum_scatter(
        jnp.einsum("tc,dc->td", grad_projected, out_cols, preferred_element_type=jnp.float32),
        "narrow",
        scatter_dimension=0,
        tiled=True,
    ).astype(jnp.bfloat16)
    weights_back = jnp.exp(masked - log_total)
    context_heads = to_heads(grad_context)
    grad_probs = jnp.einsum(
        "qhd,khd->hqk", context_heads, to_heads(value_full), preferred_element_type=jnp.float32
    )
    centre = jnp.sum(weights_back * grad_probs, axis=-1, keepdims=True)
    grad_scores = (weights_back * (grad_probs - centre)).astype(jnp.bfloat16)
    grad_query = jnp.einsum(
        "hqk,khd->qhd", grad_scores, to_heads(key_full), preferred_element_type=jnp.float32
    )
    grad_query = grad_query.reshape(queries, full_width) * score_scale
    probs_back = weights_back.astype(jnp.bfloat16)
    grad_key = jnp.einsum(
        "hqk,qhd->khd", grad_scores, to_heads(query_rows), preferred_element_type=jnp.float32
    )
    grad_key = grad_key.reshape(length, full_width) * score_scale
    grad_value = jnp.einsum(
        "hqk,qhd->khd", probs_back, context_heads, preferred_element_type=jnp.float32
    )
    grad_value = grad_value.reshape(length, full_width)
    placed = jnp.zeros((length, full_width), jnp.float32)
    placed = lax.dynamic_update_slice_in_dim(placed, grad_query, row_start, 0)
    stacked = jnp.stack((placed, grad_key, grad_value), axis=1)
    grad_mixed = lax.psum_scatter(stacked, "narrow", scatter_dimension=2, tiled=True).astype(
        jnp.bfloat16
    )
    grad_mixed_f = grad_mixed.astype(jnp.float32)
    grad_bias_qv = jnp.stack(
        (jnp.sum(grad_mixed_f[:, 0], axis=0), jnp.sum(grad_mixed_f[:, 2], axis=0))
    )
    grad_w_qkv = jnp.einsum("td,tcf->dcf", h_one, grad_mixed, preferred_element_type=jnp.float32)
    grad_h_one = full_rows(
        jnp.einsum("tcf,dcf->td", grad_mixed, qkv_cols, preferred_element_type=jnp.float32)
    )
    grad_x_full, grad_gain_one, grad_shift_one = norm_back(x_full, gain_one, shift_one, grad_h_one)
    grad_tokens = grad_mid + own_cols(grad_x_full)
    sum_w_qkv, sum_w_out, sum_w_up, sum_w_down = (
        lax.psum_scatter(grad_w_qkv, "wide", scatter_dimension=0, tiled=True),
        lax.psum_scatter(grad_w_out, "wide", scatter_dimension=0, tiled=True),
        lax.psum_scatter(grad_w_up, "wide", scatter_dimension=0, tiled=True),
        lax.psum_scatter(grad_w_down, "wide", scatter_dimension=1, tiled=True),
    )
    (
        sum_gain_one,
        sum_shift_one,
        sum_bias_qv,
        sum_bias_out,
        sum_gain_two,
        sum_shift_two,
        sum_bias_up,
        sum_bias_down,
    ) = lax.psum(
        (
            own_cols(grad_gain_one),
            own_cols(grad_shift_one),
            grad_bias_qv,
            grad_bias_out,
            own_cols(grad_gain_two),
            own_cols(grad_shift_two),
            grad_bias_up,
            grad_bias_down,
        ),
        "wide",
    )
    return (
        output.T,
        grad_tokens.T,
        sum_gain_one,
        sum_shift_one,
        sum_w_qkv,
        sum_bias_qv,
        sum_w_out,
        sum_bias_out,
        sum_gain_two,
        sum_shift_two,
        sum_w_up,
        sum_bias_up,
        sum_w_down,
        sum_bias_down,
    )


F32 = jnp.float32
BF16 = jnp.bfloat16
HEAD = 64
TILE = 256
MIB = 1 << 20
LANES = 128
SPARE = 16
PACE = 1e-6


def dot(a, b, dim_a, dim_b):
    return lax.dot_general(a, b, (((dim_a,), (dim_b,)), ((), ())), preferred_element_type=F32)


def after(value, *others):
    return lax.optimization_barrier((value,) + others)[0]


def cost(flops, moved):
    return pl.CostEstimate(flops=1 + int(PACE * flops), bytes_accessed=1 + int(PACE * moved), transcendentals=0)


def params(mib):
    return pltpu.CompilerParams(vmem_limit_bytes=mib * MIB)


def in_turns(stages, items):
    states = [None] * len(items)
    for tick in range(len(items) + len(stages) - 1):
        for j, stage in enumerate(stages):
            i = tick - j
            if 0 <= i < len(items):
                states[i] = stage(items[i], states[i])


def lane_sums(a):
    return functools.reduce(
        jnp.add, [a[:, i : i + LANES] for i in range(0, a.shape[1], LANES)]
    )


def row_sums(acc):
    return jnp.concatenate(
        [
            jnp.sum(acc[:, i : i + LANES].T, axis=0, keepdims=True)
            for i in range(0, acc.shape[1], LANES)
        ],
        0,
    )


def rows_at(start, size):
    return pl.ds(pl.multiple_of(start, HEAD // 2), size)


def first_step():
    return pl.program_id(0) == 0


def last_step():
    return pl.program_id(0) == pl.num_programs(0) - 1


def unit(rows, a, b):
    mine = rows == 0
    return jnp.where(mine, a, b), jnp.where(mine, b, a)


def bias_kernel(starts_ref, bias_ref):
    length = bias_ref.shape[0] * TILE
    for i in range(length // TILE):
        low = i * TILE
        rows = min(2 * TILE, length - low)
        key = low + lax.broadcasted_iota(jnp.int32, (rows, TILE), 0)
        query = low + lax.broadcasted_iota(jnp.int32, (rows, TILE), 1)
        seen = key <= query
        for p in range(starts_ref.shape[0]):
            s = starts_ref[p]
            seen = seen | (
                (key >= s) & (key < s + PIECE) & (query >= s) & (query < s + PIECE)
            )
        bias_ref[i, :rows, :] = jnp.where(seen, 0.0, -1e30)


def mask_bias(starts, length):
    shape = (length // TILE, 2 * TILE, TILE)
    return pl.pallas_call(
        bias_kernel,
        in_specs=[pl.BlockSpec(memory_space=pltpu.SMEM)],
        out_specs=pl.BlockSpec(memory_space=pltpu.VMEM),
        out_shape=jax.ShapeDtypeStruct(shape, F32),
        compiler_params=params(16),
        name="mask_bias",
    )(starts)


def spans(i, length):
    low = i * TILE
    high = min(low + 2 * TILE, length)
    return ((0, low), (low, high)) if low > 0 else ((low, high),)


def scores(key_rows, query, bias, i, span):
    s = dot(key_rows[span[0] : span[1]], query, 1, 0)
    return s if span[0] < i * TILE else s + bias[i, : span[1] - span[0], :]


def attend_kernel(bias, x_ref, c_ref, l_ref, key_rows):
    length = x_ref.shape[2]
    key_rows[...] = x_ref[1].T

    def score(i, _):
        query = x_ref[0, :, pl.ds(i * TILE, TILE)] * jnp.asarray(HEAD**-0.5, BF16)
        return [(span, scores(key_rows, query, bias, i, span)) for span in spans(i, length)]

    def weigh(i, parts):
        here = pl.ds(i * TILE, TILE)
        top = functools.reduce(
            jnp.maximum, [jnp.max(s, axis=0, keepdims=True) for _, s in parts]
        )
        total, acc = 0.0, 0.0
        for span, s in parts:
            p = jnp.exp(s - top)
            total = total + jnp.sum(p, axis=0, keepdims=True)
            acc = acc + dot(x_ref[2, :, span[0] : span[1]], p.astype(BF16), 1, 0)
        c_ref[:, here] = (acc / total).astype(BF16)
        l_ref[0, :, here] = top + jnp.log(total)

    in_turns((score, weigh), range(length // TILE))


def attend(bias, qkv, first, count):
    length = qkv.shape[2]
    return pl.pallas_call(
        attend_kernel,
        grid=(count,),
        in_specs=[
            pl.BlockSpec(bias.shape, lambda h: (0, 0, 0)),
            pl.BlockSpec((3, HEAD, length), lambda h: (0, h + first, 0)),
        ],
        out_specs=[
            pl.BlockSpec((HEAD, length), lambda h: (h, 0)),
            pl.BlockSpec((1, 1, length), lambda h: (h, 0, 0)),
        ],
        scratch_shapes=[pltpu.VMEM((length, HEAD), BF16)],
        out_shape=[
            jax.ShapeDtypeStruct((count * HEAD, length), BF16),
            jax.ShapeDtypeStruct((count, 1, length), F32),
        ],
        compiler_params=params(24),
        cost_estimate=cost(4e9 * count, count * length * HEAD * 8),
        name="attend",
    )(bias, qkv)


def attend_back_kernel(
    shared, rank_ref, bias, x_ref, mine_ref, got_ref, l_ref, old_ref, g_ref,
    key_rows, value_rows, query_rows, grad_rows, grad, key_sum, value_sum,
):
    length = x_ref.shape[2]
    share = length // 2
    scale = jnp.asarray(HEAD**-0.5, BF16)
    first = rank_ref[0] == 0
    mine, got = mine_ref[...], got_ref[...]
    grad[:, :share] = jnp.where(first, mine, got)
    grad[:, share:] = jnp.where(first, got, mine)
    key_rows[...] = x_ref[1].T
    value_rows[...] = x_ref[2].T
    grad_rows[...] = grad[...].T
    query_rows[...] = (x_ref[0] * scale).T
    tiles = length // TILE

    def score(i, _):
        here = pl.ds(i * TILE, TILE)
        query, out = x_ref[0, :, here] * scale, grad[:, here]
        return [
            (span, scores(key_rows, query, bias, i, span), dot(value_rows[span[0] : span[1]], out, 1, 0))
            for span in spans(i, length)
        ]

    def weigh(i, parts):
        lse = l_ref[0, :, pl.ds(i * TILE, TILE)]
        weights = [jnp.exp(s - lse) for _, s, _ in parts]
        centre = functools.reduce(
            jnp.add, [jnp.sum(p * g, axis=0, keepdims=True) for p, (_, _, g) in zip(weights, parts)]
        )
        return [
            (span, p.astype(BF16), (p * (g - centre)).astype(BF16))
            for p, (span, _, g) in zip(weights, parts)
        ]

    def gather(i, parts):
        here = pl.ds(i * TILE, TILE)
        dq = 0.0
        for (low, high), p, gs in parts:
            dq = dq + dot(x_ref[1, :, low:high], gs, 1, 0)
            dk, dv = dot(gs, query_rows[here], 1, 0), dot(p, grad_rows[here], 1, 0)
            if i == tiles - 1:
                key_sum[low:high], value_sum[low:high] = dk, dv
            else:
                key_sum[low:high] += dk
                value_sum[low:high] += dv
        g_ref[0, :, here] = (dq * HEAD**-0.5).astype(BF16)

    in_turns((score, weigh, gather), list(reversed(range(tiles))))
    g_ref[1] = key_sum[...].T.astype(BF16)
    g_ref[2] = value_sum[...].T.astype(BF16)
    if shared:
        @pl.when(pl.program_id(0) == pl.num_programs(0) - 1)
        def _():
            g_ref[:, HEAD // 2 :, :] = jnp.zeros((3, HEAD // 2, length), BF16)


def attend_back(bias, rank, qkv, mine, got, lse, first, count, shared, old=None):
    length = qkv.shape[2]
    rows = pltpu.VMEM((length, HEAD), BF16)
    sums = pltpu.VMEM((length, HEAD), F32)
    heads = pl.BlockSpec((3, HEAD, length), lambda h, r: (0, h + first, 0))
    half = pl.BlockSpec((HEAD, length // 2), lambda h, r: (h + first, 0))
    alias = {}
    if old is not None:
        alias = {6: 0}
    else:
        old = jnp.zeros((8, 128), BF16)
    return pl.pallas_call(
        functools.partial(attend_back_kernel, shared),
        grid_spec=pltpu.PrefetchScalarGridSpec(
            num_scalar_prefetch=1,
            grid=(count,),
            in_specs=[
                pl.BlockSpec(bias.shape, lambda h, r: (0, 0, 0)),
                heads,
                half,
                half,
                pl.BlockSpec((1, 1, length), lambda h, r: (h + first, 0, 0)),
                pl.BlockSpec(memory_space=pl.ANY),
            ],
            out_specs=[heads],
            scratch_shapes=[rows] * 4
            + [pltpu.VMEM((HEAD, length), BF16)]
            + [sums] * 2,
        ),
        out_shape=[jax.ShapeDtypeStruct(qkv.shape, BF16)],
        input_output_aliases=alias,
        compiler_params=params(34),
        cost_estimate=cost(6.8e9 * count, count * length * HEAD * 14),
        name="attend_back",
    )(rank, bias, qkv, mine, got, lse, old)[0]


def norm_rows(x):
    x = x - jnp.mean(x, axis=0, keepdims=True)
    inv = lax.rsqrt(jnp.mean(x * x, axis=0, keepdims=True) + EPSILON)
    return x * inv, inv


def own_first(rank, a):
    half = a.shape[0] // 2
    return jnp.where(rank == 0, a, jnp.concatenate((a[half:], a[:half]), 0))


def half_lanes(columns):
    return -(-columns // (2 * LANES)) * LANES


def turn_weights(core, mine, got, turned):
    a, b = unit(core, mine, got)
    count = a.shape[1]
    turned[:count] = a.T
    turned[count:] = b.T[2 * count - turned.shape[0] :]


def norm_qkv_kernel(core_ref, xo_ref, xt_ref, m_ref, g_ref, v_ref, b_ref, h_ref, q_ref, turned):
    @pl.when(first_step())
    def _():
        turn_weights(core_ref[0], m_ref[...], g_ref[...], turned)

    x = jnp.concatenate((xo_ref[...], xt_ref[...]), 0).astype(F32)
    h = (norm_rows(x)[0] * v_ref[:, 0:1] + v_ref[:, 1:2]).astype(BF16)
    h_ref[...] = h
    q_ref[...] = (dot(turned[...], h, 1, 0) + b_ref[...]).astype(BF16)


def norm_qkv(core, x_own, x_other, mine, got, vectors, bias):
    own, length = x_own.shape
    depth = 2 * own
    rows = bias.shape[0]
    column = lambda n: pl.BlockSpec((n, TILE), lambda i, s: (0, i))
    whole = lambda a: pl.BlockSpec(a.shape, lambda i, s: (0, 0))
    return pl.pallas_call(
        norm_qkv_kernel,
        grid_spec=pltpu.PrefetchScalarGridSpec(
            num_scalar_prefetch=1,
            grid=(length // TILE,),
            in_specs=[column(own)] * 2 + [whole(a) for a in (mine, got, vectors, bias)],
            out_specs=[column(depth), column(rows)],
            scratch_shapes=[pltpu.VMEM((rows, depth), BF16)],
        ),
        out_shape=[jax.ShapeDtypeStruct((n, length), BF16) for n in (depth, rows)],
        compiler_params=params(60),
        cost_estimate=cost(2 * depth * rows * length, depth * length * 6),
        name="norm_qkv",
    )(core, x_own, x_other, mine, got, vectors, bias)


def qkv_kernel(core_ref, h_ref, m_ref, g_ref, b_ref, q_ref, turned):
    @pl.when(first_step())
    def _():
        turn_weights(core_ref[0], m_ref[...], g_ref[...], turned)

    q_ref[...] = (dot(turned[...], h_ref[...], 1, 0) + b_ref[...]).astype(BF16)


def qkv_of(core, h_one, mine, got, bias):
    depth, length = h_one.shape
    rows = bias.shape[0]
    column = lambda n: pl.BlockSpec((n, TILE), lambda i, s: (0, i))
    whole = lambda a: pl.BlockSpec(a.shape, lambda i, s: (0, 0))
    return pl.pallas_call(
        qkv_kernel,
        grid_spec=pltpu.PrefetchScalarGridSpec(
            num_scalar_prefetch=1,
            grid=(length // TILE,),
            in_specs=[column(depth)] + [whole(a) for a in (mine, got, bias)],
            out_specs=column(rows),
            scratch_shapes=[pltpu.VMEM((rows, depth), BF16)],
        ),
        out_shape=jax.ShapeDtypeStruct((rows, length), BF16),
        compiler_params=params(24),
        cost_estimate=cost(2 * depth * rows * length, depth * length * 4),
        name="qkv",
    )(core, h_one, mine, got, bias)


def project_kernel(
    spot_ref, xo_ref, xt_ref, a_ref, b_ref, d_ref, ga_ref, gb_ref, gd_ref, c_ref, m_ref, g_ref, v_ref,
    p_ref, h_ref, c_out, turned,
):
    @pl.when(first_step())
    def _():
        own = xo_ref.shape[0]
        parts = [own_first(spot_ref[0], w[:, :own]) for w in (m_ref, g_ref)]
        turn_weights(spot_ref[1], *parts, turned)

    rank = spot_ref[0]
    own = xo_ref.shape[0]
    half, whole = HEAD // 2, own - HEAD // 2
    for refs, at in (((a_ref, b_ref, d_ref), half * rank), ((ga_ref, gb_ref, gd_ref), own + half * (1 - rank))):
        for ref in refs:
            c_out[rows_at(at, ref.shape[0])] = ref[...]
            at = at + ref.shape[0]
    c_out[rows_at(whole * (1 - rank), half)] = c_ref[:half]
    c_out[rows_at(own + whole * rank, half)] = c_ref[half:]
    low = (dot(turned[...], c_out[...], 1, 0) + v_ref[:, 4:5]).astype(BF16)
    p_ref[...] = low
    mid = jnp.concatenate((xo_ref[...], xt_ref[...]), 0).astype(F32) + low.astype(F32)
    h_ref[...] = (norm_rows(mid)[0] * v_ref[:, 2:3] + v_ref[:, 3:4]).astype(BF16)


def out_columns(depth):
    return pl.BlockSpec((depth, -(-depth // (2 * LANES)) * LANES), lambda i, s: (0, 0))


def project(spot, x_own, x_other, pieces, mine, got, vectors):
    own, length = x_own.shape
    depth = 2 * own
    column = lambda rows: pl.BlockSpec((rows, TILE), lambda i, s: (0, i))
    whole = lambda a: pl.BlockSpec(a.shape, lambda i, s: (0, 0))
    return pl.pallas_call(
        project_kernel,
        grid_spec=pltpu.PrefetchScalarGridSpec(
            num_scalar_prefetch=1,
            grid=(length // TILE,),
            in_specs=[column(own)] * 2
            + [column(p.shape[0]) for p in pieces]
            + [out_columns(depth)] * 2
            + [whole(vectors)],
            out_specs=[column(depth)] * 3,
            scratch_shapes=[pltpu.VMEM((depth, depth), BF16)],
        ),
        out_shape=[jax.ShapeDtypeStruct((depth, length), BF16)] * 3,
        compiler_params=params(60),
        cost_estimate=cost(2 * depth * depth * length, depth * length * 10),
        name="project",
    )(spot, x_own, x_other, *pieces, mine, got, vectors)


def feed_kernel(
    spot_ref, h_ref, go_ref, gt_ref, pm_ref, pg_ref, qm_ref, qg_ref, bias_ref, *rest
):
    mid_ref, own_ref, other_ref, gh_ref, gb_ref, gs_ref, up, down, sums, sems = rest[-10:]
    split = up.shape[1] - qm_ref.shape[1]
    lead = pm_ref.shape[1] - split
    hidden = up.shape[1]

    @pl.when(pl.program_id(0) == 0)
    def _():
        half = up.shape[0] // 2

        def copies(up_p, up_q, down_p, down_q):
            made = []
            for i, (first, second, whole) in enumerate(((up_p, up_q, up), (down_p, down_q, down))):
                for j in range(2):
                    rows = pl.ds(half * j, half)
                    to = rows_at(half * (j ^ spot_ref[2]), half)
                    at = 4 * i + 2 * j
                    made += [
                        pltpu.make_async_copy(
                            first.at[rows, lead:], whole.at[to, :split], sems.at[at]
                        ),
                        pltpu.make_async_copy(
                            second.at[rows, :], whole.at[to, split:], sems.at[at + 1]
                        ),
                    ]
            return made

        def bring(these):
            for c in these:
                c.start()
            for c in these:
                c.wait()

        @pl.when(spot_ref[1] == 0)
        def _():
            bring(copies(pm_ref, qm_ref, pg_ref, qg_ref))

        @pl.when(spot_ref[1] == 1)
        def _():
            bring(copies(pg_ref, qg_ref, pm_ref, qm_ref))

        gb_ref[...] = jnp.zeros_like(gb_ref)
        sums[...] = jnp.zeros_like(sums)

    sums[...] += lane_sums(go_ref[...].astype(F32))

    @pl.when(last_step())
    def _():
        gs_ref[...] = row_sums(sums[...])

    root = (2 / jnp.pi) ** 0.5
    h = h_ref[...]
    g = jnp.concatenate((go_ref[...], gt_ref[...]), 0)
    for span in (slice(0, split), slice(split, hidden)):
        u = dot(h, up[:, span], 0, 0) + bias_ref[:, span]
        grad_act = dot(g, down[:, span], 0, 0)
        square = u * u
        t = jnp.tanh(u * (root + (root * 0.044715) * square))
        half = 0.5 + 0.5 * t
        mid_ref[0, :, span] = (u * half).astype(BF16)
        slope = half + (0.5 * u) * (1 - t * t) * (root + (3 * root * 0.044715) * square)
        gup = (grad_act * slope).astype(BF16)
        mid_ref[1, :, span] = gup
        gb_ref[:, span] += jnp.sum(gup.astype(F32), axis=0, keepdims=True)
    gh_ref[...] = dot(up[...], mid_ref[1], 1, 1).astype(BF16)
    out = dot(down[...], mid_ref[0], 1, 1).astype(BF16)
    n = own_ref.shape[0]
    own_ref[...], other_ref[...] = out[:n], out[n:]


def feed(spot, count, h_two, g_own, g_other, weights, bias_up, tile, old):
    depth, length = h_two.shape
    own = g_own.shape[0]
    hidden = bias_up.shape[1]
    column = lambda rows: pl.BlockSpec((rows, tile), lambda i, s: (0, s[0] + i))
    anywhere = pl.BlockSpec(memory_space=pl.ANY)
    vector = pl.BlockSpec((1, hidden), lambda i, s: (0, 0))
    local = lambda rows: pl.BlockSpec((rows, tile), lambda i, s: (0, i))
    aliases = {} if old is None else {9: 0}
    return pl.pallas_call(
        feed_kernel,
        grid_spec=pltpu.PrefetchScalarGridSpec(
            num_scalar_prefetch=1,
            grid=(count,),
            in_specs=[column(depth), column(own), column(own)]
            + [anywhere] * 4
            + [vector]
            + [anywhere] * len(aliases),
            out_specs=[
                pl.BlockSpec((2, tile, hidden), lambda i, s: (0, s[0] + i, 0)),
                local(own),
                local(own),
                local(depth),
                vector,
                pl.BlockSpec((1, own), lambda i, s: (0, 0)),
            ],
            scratch_shapes=[
                pltpu.VMEM((depth, hidden), BF16),
                pltpu.VMEM((depth, hidden), BF16),
                pltpu.VMEM((own, LANES), F32),
                pltpu.SemaphoreType.DMA((8,)),
            ],
        ),
        out_shape=[
            jax.ShapeDtypeStruct((2, length, hidden), BF16),
            *(jax.ShapeDtypeStruct((n, count * tile), BF16) for n in (own, own, depth)),
            jax.ShapeDtypeStruct((1, hidden), F32),
            jax.ShapeDtypeStruct((1, own), F32),
        ],
        input_output_aliases=aliases,
        compiler_params=params(50),
        cost_estimate=cost(8 * depth * count * tile * hidden, 12 * depth * hidden),
        name="feed",
    )(spot, h_two, g_own, g_other, *weights, bias_up, *([] if old is None else [old]))


def weight_grad_kernel(which_ref, h_ref, go_ref, gt_ref, m_ref, *rest):
    rest, (lhs, rhs, sems) = rest[:-3], rest[-3:]
    half = lhs.shape[1]
    step = pl.program_id(0)
    split = rest[0].shape[1]
    columns = (slice(0, split), slice(split, rhs.shape[1]))
    which = which_ref[0]

    def part(i):
        return pltpu.make_async_copy(h_ref.at[pl.ds(half * i, half)], lhs.at[i], sems.at[i])

    def column(i):
        return pltpu.make_async_copy(m_ref.at[which, :, columns[i]], rhs.at[:, columns[i]], sems.at[2 + i])

    @pl.when(first_step())
    def _():
        @pl.when(which == 0)
        def _():
            for i, g in enumerate((go_ref, gt_ref)):
                pltpu.make_async_copy(g, lhs.at[i], sems.at[i]).start()

        @pl.when(which == 1)
        def _():
            for i in range(2):
                part(i).start()

        column(0).start()
        column(1).start()
        part(0).wait()
        column(0).wait()

    @pl.when(last_step())
    def _():
        part(1).wait()

    rows = lhs[step]
    p = dot(rows, rhs[:, columns[0]], 1, 0)

    @pl.when(first_step())
    def _():
        column(1).wait()

    q = dot(rows, rhs[:, columns[1]], 1, 0)
    if len(rest) == 2:
        rest[0][...], rest[1][...] = p.astype(BF16), q.astype(BF16)
        return
    pg_ref, qg_ref, pk_ref, pa_ref, qk_ref, qa_ref = rest
    p = (p + pg_ref[...].astype(F32)).astype(BF16)
    q = (q + qg_ref[...].astype(F32)).astype(BF16)
    n = p.shape[0] // 4
    low = jnp.concatenate((p[:n], p[2 * n : 3 * n]), 0)
    high = jnp.concatenate((p[n : 2 * n], p[3 * n :]), 0)
    pk_ref[...], pa_ref[...] = unit(which_ref[1], low, high)
    qk_ref[...], qa_ref[...] = unit(which_ref[2], q[: 2 * n], q[2 * n :])


def weight_grad(which, h_two, g_own, g_other, middle, split, got=None):
    depth, length = h_two.shape
    hidden = middle.shape[2]
    steps = 2
    rows = depth // steps
    parts = (split, hidden - split)
    blocks = [pl.BlockSpec((rows, n), lambda i, s: (i, 0)) for n in parts]
    in_specs = [pl.BlockSpec(memory_space=pl.ANY)] * 4
    out_specs, shapes = blocks, [jax.ShapeDtypeStruct((depth, n), BF16) for n in parts]
    if got is not None:
        in_specs += blocks
        out_specs = [pl.BlockSpec((rows // 2, n), lambda i, s: (i, 0)) for n in parts for _ in range(2)]
        shapes = [jax.ShapeDtypeStruct((depth // 2, n), BF16) for n in parts for _ in range(2)]
    return pl.pallas_call(
        weight_grad_kernel,
        grid_spec=pltpu.PrefetchScalarGridSpec(
            num_scalar_prefetch=1,
            grid=(steps,),
            in_specs=in_specs,
            out_specs=out_specs,
            scratch_shapes=[
                pltpu.VMEM((steps, rows, length), BF16),
                pltpu.VMEM((length, hidden), BF16),
                pltpu.SemaphoreType.DMA((4,)),
            ],
        ),
        out_shape=shapes,
        compiler_params=params(60),
        cost_estimate=cost(2 * depth * length * hidden, 2 * (2 * depth + hidden) * length),
        name="weight_grad",
    )(which, h_two, g_own, g_other, middle, *(got or ()))


def mid_back_kernel(
    spot_ref, xo_ref, xt_ref, p_ref, go_ref, gt_ref, keep_ref, got_ref, m_ref, g_ref, v_ref,
    gp_ref, gq_ref, ma_ref, mb_ref, sa_ref, sb_ref, n_ref, w_own, w_other, gc, sums,
):
    @pl.when(first_step())
    def _():
        n = w_own.shape[1]
        parts = [own_first(spot_ref[2], w[:, :n]) for w in (m_ref, g_ref)]
        w_own[...], w_other[...] = unit(spot_ref[1], *parts)
        sums[...] = jnp.zeros_like(sums)

    own = xo_ref.shape[0]
    rank = spot_ref[2]
    keep, got = keep_ref[...].astype(F32), got_ref[...].astype(F32)
    gh = keep + jnp.concatenate((got[own:], got[:own]), 0)
    mid = jnp.concatenate((xo_ref[...], xt_ref[...]), 0).astype(F32) + p_ref[...].astype(F32)
    hat, inv = norm_rows(mid)
    e = gh * v_ref[:, 2:3]
    grad = jnp.concatenate((go_ref[...], gt_ref[...]), 0).astype(F32) + inv * (
        e - jnp.mean(e, axis=0, keepdims=True) - hat * jnp.mean(e * hat, axis=0, keepdims=True)
    )
    gp = grad.astype(BF16)
    gp_ref[...], gq_ref[...] = gp[:own], gp[own:]
    gc[...] = (dot(w_own[...], gp[:own], 1, 0) + dot(w_other[...], gp[own:], 1, 0)).astype(BF16)
    half = HEAD // 2
    a, b = ma_ref.shape[0], mb_ref.shape[0] - HEAD
    near, away = half * rank, own + half * (1 - rank)
    own_half = gc[rows_at((a + b) * (1 - rank), half)]
    other_half = gc[rows_at(own + (a + b) * rank, half)]
    ma_ref[...] = gc[rows_at(near, a)]
    mb_ref[:b] = gc[rows_at(near + a, b)]
    mb_ref[b : b + half] = own_half
    mb_ref[b + half :] = other_half
    sa_ref[...] = gc[rows_at(away, a)]
    sb_ref[:b] = gc[rows_at(away + a, b)]
    sb_ref[b : b + half] = other_half
    sb_ref[b + half :] = own_half
    sums[...] += jnp.concatenate(
        (lane_sums(gh * hat), lane_sums(gh), lane_sums(gp.astype(F32))), 1
    )

    @pl.when(last_step())
    def _():
        n_ref[...] = row_sums(sums[...])


def mid_back(spot, x_own, x_other, projected, g_own, g_other, keep, got, mine, got_w, vectors, rows_a, rows_b):
    own, length = x_own.shape
    depth = 2 * own
    share = length // 2
    column = lambda rows: pl.BlockSpec((rows, TILE), lambda i, s: (0, s[0] + i))
    local = lambda rows: pl.BlockSpec((rows, TILE), lambda i, s: (0, i))
    whole = lambda a: pl.BlockSpec(a.shape, lambda i, s: (0, 0))
    out = lambda rows: jax.ShapeDtypeStruct((rows, share), BF16)
    sizes = (own, own, rows_a, rows_b, rows_a, rows_b)
    return pl.pallas_call(
        mid_back_kernel,
        grid_spec=pltpu.PrefetchScalarGridSpec(
            num_scalar_prefetch=1,
            grid=(share // TILE,),
            in_specs=[column(own), column(own), column(depth), column(own), column(own)]
            + [local(depth)] * 2
            + [out_columns(depth)] * 2
            + [whole(vectors)],
            out_specs=[local(r) for r in sizes] + [pl.BlockSpec((3, depth), lambda i, s: (0, 0))],
            scratch_shapes=[pltpu.VMEM((depth, own), BF16)] * 2
            + [pltpu.VMEM((depth, TILE), BF16), pltpu.VMEM((depth, 3 * LANES), F32)],
        ),
        out_shape=[out(r) for r in sizes] + [jax.ShapeDtypeStruct((3, depth), F32)],
        compiler_params=params(60),
        cost_estimate=cost(2 * depth * depth * share, depth * share * 16),
        name="mid_back",
    )(spot, x_own, x_other, projected, g_own, g_other, keep, got, mine, got_w, vectors)


def half_lanes(columns):
    return -(-columns // (2 * LANES)) * LANES


def grads_kernel(place_ref, h_ref, g_ref, send_ref, keep_ref):
    cols = send_ref.shape[1]
    low = dot(h_ref[...], g_ref[:cols], 1, 1).astype(BF16)
    high = dot(h_ref[...], g_ref[g_ref.shape[0] - cols :], 1, 1).astype(BF16)
    keep_ref[...], send_ref[...] = unit(place_ref[1], low, high)


def grads_out_kernel(place_ref, h_ref, c_ref, g_ref, pm_ref, pg_ref, send_ref, keep_ref, gp):
    @pl.when(first_step())
    def _():
        share = pm_ref.shape[1]
        gp[:, :share], gp[:, share:] = unit(place_ref[0], pm_ref[...], pg_ref[...])

    out = half_lanes(gp.shape[0])
    cols = send_ref.shape[1] - out
    for lhs, rhs, n, to in (
        (h_ref, g_ref, cols, slice(0, cols)),
        (c_ref, gp, out, slice(cols, cols + out)),
    ):
        low = dot(lhs[...], rhs[:n], 1, 1).astype(BF16)
        high = dot(lhs[...], rhs[rhs.shape[0] - n :], 1, 1).astype(BF16)
        keep_ref[:, to], send_ref[:, to] = unit(place_ref[1], low, high)


def column_grads(places, cols, h_one, grad, context=None, gp=None, gp_got=None):
    depth, length = h_one.shape
    kernel, total, scratch = grads_kernel, cols, []
    part = pl.BlockSpec((depth // 2, length), lambda i, s: (i, 0))
    whole = lambda a: pl.BlockSpec(a.shape, lambda i, s: (0, 0))
    args, specs = [h_one, grad], [part, whole(grad)]
    if context is not None:
        kernel, total = grads_out_kernel, cols + half_lanes(gp.shape[0])
        args = [h_one, context, grad, gp, gp_got]
        specs = [part, part] + [whole(a) for a in args[2:]]
        scratch = [pltpu.VMEM((gp.shape[0], length), BF16)]
    return pl.pallas_call(
        kernel,
        grid_spec=pltpu.PrefetchScalarGridSpec(
            num_scalar_prefetch=1,
            grid=(2,),
            in_specs=specs,
            out_specs=[pl.BlockSpec((depth // 2, total), lambda i, s: (i, 0))] * 2,
            scratch_shapes=scratch,
        ),
        out_shape=[jax.ShapeDtypeStruct((depth, total), BF16)] * 2,
        compiler_params=params(32),
        cost_estimate=cost(4 * depth * total * length, 6 * depth * length),
        name="column_grads",
    )(places, *args)


def output_kernel(
    place_ref, x_ref, p_ref, b_ref, low_ref, high_ref, low_got_ref, high_got_ref, o_ref
):
    mine = pl.program_id(0) // (pl.num_programs(0) // 2) == place_ref[0]
    pick = lambda a, b: jnp.where(mine, a[...], b[...]).astype(F32)
    down = pick(high_ref, low_ref) + pick(low_got_ref, high_got_ref)
    o_ref[...] = (
        x_ref[...].astype(F32) + p_ref[...].astype(F32) + (down + b_ref[...])
    ).astype(BF16)


def close_output(places, x_own, projected, bias, low, high, low_got, high_got):
    own, length = x_own.shape
    column = pl.BlockSpec((own, TILE), lambda i, s: (0, i))
    steps = length // 2 // TILE
    half = pl.BlockSpec((own, TILE), lambda i, s: (0, lax.rem(i, steps)))
    return pl.pallas_call(
        output_kernel,
        grid_spec=pltpu.PrefetchScalarGridSpec(
            num_scalar_prefetch=1,
            grid=(2 * steps,),
            in_specs=[column] * 2 + [pl.BlockSpec((own, 1), lambda i, s: (0, 0))] + [half] * 4,
            out_specs=column,
        ),
        out_shape=jax.ShapeDtypeStruct((own, length), BF16),
        compiler_params=params(60),
        cost_estimate=cost(0, 0),
        name="close_output",
    )(places, x_own, projected, bias, low, high, low_got, high_got)


def tokens_kernel(place_ref, x_ref, gp_ref, gq_ref, keep_ref, got_ref, s_ref, v_ref, o_ref):
    own = x_ref.shape[0]
    mine = pl.program_id(0) // (pl.num_programs(0) // 2) == place_ref[0]
    gp = jnp.where(mine, gp_ref[...], gq_ref[...]).astype(F32)
    e = (keep_ref[...].astype(F32) + got_ref[:own].astype(F32)) * v_ref[:own, 0:1]
    others = got_ref[own:].astype(F32)
    mean, inv = s_ref[2:3], s_ref[3:4]
    total = (s_ref[:2] + (others[:2] + others[2:4])) * (0.5 / own)
    hat = (x_ref[...].astype(F32) - mean) * inv
    o_ref[...] = gp + inv * (e - total[:1] - hat * total[1:])


def close_tokens(places, x_own, gp, gp_got, keep, got, stats, vectors):
    own, length = x_own.shape
    steps = length // 2 // TILE
    column = lambda rows: pl.BlockSpec((rows, TILE), lambda i, s: (0, i))
    half = pl.BlockSpec((own, TILE), lambda i, s: (0, lax.rem(i, steps)))
    return pl.pallas_call(
        tokens_kernel,
        grid_spec=pltpu.PrefetchScalarGridSpec(
            num_scalar_prefetch=1,
            grid=(2 * steps,),
            in_specs=[column(own), half, half, column(own), column(own + SPARE), column(4)]
            + [pl.BlockSpec(vectors.shape, lambda i, s: (0, 0))],
            out_specs=column(own),
        ),
        out_shape=jax.ShapeDtypeStruct((own, length), F32),
        compiler_params=params(60),
        cost_estimate=cost(0, 0),
        name="close_tokens",
    )(places, x_own, gp, gp_got, keep, got, stats, vectors)


def qkv_back_kernel(
    core_ref, xo_ref, xt_ref, gb_ref, ga_ref, bm_ref, bg_ref, am_ref, ag_ref, v_ref,
    keep_ref, send_ref, s_ref, n_ref, db_ref, da_ref, b_low, b_high, a_low, a_high, n_sum, b_sum, a_sum,
):
    @pl.when(first_step())
    def _():
        b_low[...], b_high[...] = unit(core_ref[0], bm_ref[...], bg_ref[...])
        a_low[...], a_high[...] = unit(core_ref[0], am_ref[...], ag_ref[...])
        for r in (n_sum, b_sum, a_sum):
            r[...] = jnp.zeros_like(r)

    own = xo_ref.shape[0]
    gb, ga = gb_ref[...], ga_ref[...]
    cols_b, cols_a = b_low.shape[1], a_low.shape[1]
    twice = 2 * cols_b - gb.shape[0]
    rest = jnp.concatenate((jnp.zeros((twice, gb.shape[1]), BF16), gb[cols_b:]), 0)
    gh = (dot(b_low[...], gb[:cols_b], 1, 0) + dot(b_high[...], rest, 1, 0)) + (
        dot(a_low[...], ga[:cols_a], 1, 0) + dot(a_high[...], ga[cols_a:], 1, 0)
    )
    keep_ref[...] = gh[:own].astype(BF16)
    send_ref[:own] = gh[own:].astype(BF16)
    x = jnp.concatenate((xo_ref[...], xt_ref[...]), 0).astype(F32)
    hat, inv = norm_rows(x)
    both = gh * hat
    gain = v_ref[:, 0:1]
    mine = jnp.concatenate(
        (jnp.sum(gh * gain, axis=0, keepdims=True), jnp.sum(both * gain, axis=0, keepdims=True)), 0
    )
    s_ref[...] = jnp.concatenate((mine, jnp.mean(x, axis=0, keepdims=True), inv), 0)
    high = mine.astype(BF16).astype(F32)
    parts = jnp.concatenate((high, mine - high, jnp.zeros((SPARE - 4, mine.shape[1]), F32)), 0)
    send_ref[own:] = parts.astype(BF16)
    n_sum[...] += jnp.concatenate((lane_sums(both), lane_sums(gh)), 1)
    b_sum[...] += lane_sums(gb.astype(F32))
    a_sum[...] += lane_sums(ga.astype(F32))

    @pl.when(last_step())
    def _():
        n_ref[...] = row_sums(n_sum[...])
        db_ref[...] = row_sums(b_sum[...])
        da_ref[...] = row_sums(a_sum[...])


def qkv_back(core, x_own, x_other, grad_b, grad_a, w_b, w_a, vectors):
    own = x_own.shape[0]
    depth = 2 * own
    column = lambda rows: pl.BlockSpec((rows, TILE), lambda i, s: (0, i))
    whole = lambda a: pl.BlockSpec(a.shape, lambda i, s: (0, 0))
    span = x_own.shape[1]
    out = jax.ShapeDtypeStruct
    rows = (depth, grad_b.shape[0], grad_a.shape[0])
    flat = [out((n, r), F32) for n, r in zip((2, 1, 1), rows)]
    return pl.pallas_call(
        qkv_back_kernel,
        grid_spec=pltpu.PrefetchScalarGridSpec(
            num_scalar_prefetch=1,
            grid=(span // TILE,),
            in_specs=[column(own)] * 2
            + [column(grad_b.shape[0]), column(grad_a.shape[0])]
            + [whole(a) for a in (*w_b, *w_a, vectors)],
            out_specs=[column(own), column(own + SPARE), column(4)] + [whole(t) for t in flat],
            scratch_shapes=[pltpu.VMEM(w.shape, BF16) for w in (*w_b, *w_a)]
            + [pltpu.VMEM((r, n * LANES), F32) for n, r in zip((2, 1, 1), rows)],
        ),
        out_shape=[out((own, span), BF16), out((own + SPARE, span), BF16), out((4, span), F32)]
        + flat,
        compiler_params=params(36),
        cost_estimate=cost(2 * depth * span * (rows[1] + rows[2]), depth * span * 12),
        name="qkv_back",
    )(core, x_own, x_other, grad_b, grad_a, *w_b, *w_a, vectors)


def by_bit(bit, a, b):
    return jnp.where(lax.axis_index("wide") & bit == 0, a, b)


def flip(a, bit):
    size = lax.axis_size("wide")
    return lax.ppermute(a, "wide", [(i, i ^ bit) for i in range(size)])


def join_kernel(place_ref, kept_ref, got_ref, out_ref):
    first = place_ref[0] == 0
    if out_ref.ndim == 2:
        half = kept_ref.shape[0]
        out_ref[:half] = jnp.where(first, kept_ref[...], got_ref[...])
        out_ref[half:] = jnp.where(first, got_ref[...], kept_ref[...])
    else:
        out_ref[:, 0:1] = jnp.where(first, kept_ref[...], got_ref[...])
        out_ref[:, 1:2] = jnp.where(first, got_ref[...], kept_ref[...])


def join(kept, got, place, axis):
    rows, cols = kept.shape[-2:]
    call = dict(compiler_params=params(16), cost_estimate=cost(0, 0), name="join")
    place = place.astype(jnp.int32)[None]
    if axis is None:
        spec = lambda n: pl.BlockSpec((n, cols), lambda i, s: (0, 0))
        grid_spec = pltpu.PrefetchScalarGridSpec(
            num_scalar_prefetch=1, grid=(1,), in_specs=[spec(rows)] * 2, out_specs=spec(2 * rows)
        )
        shape = jax.ShapeDtypeStruct((2 * rows, cols), kept.dtype)
        return pl.pallas_call(join_kernel, grid_spec=grid_spec, out_shape=shape, **call)(place, kept, got)
    outer, inner = math.prod(kept.shape[:axis]), math.prod(kept.shape[axis:-1])
    spec = lambda n: pl.BlockSpec((outer, n, inner, cols), lambda i, s: (0, 0, 0, 0))
    grid_spec = pltpu.PrefetchScalarGridSpec(
        num_scalar_prefetch=1, grid=(1,), in_specs=[spec(1)] * 2, out_specs=spec(2)
    )
    shape = jax.ShapeDtypeStruct((outer, 2, inner, cols), kept.dtype)
    args = [a.reshape(outer, 1, inner, cols) for a in (kept, got)]
    out = pl.pallas_call(join_kernel, grid_spec=grid_spec, out_shape=shape, **call)(place, *args)
    return out.reshape(kept.shape[:axis] + (2,) + kept.shape[axis:])


def fold_kernel(index_ref, kept_ref, got_ref, keep_ref, away_ref):
    total = kept_ref[...].astype(F32) + got_ref[...].astype(F32)
    if kept_ref.ndim == 2:
        half = keep_ref.shape[0]
        low, high = total[:half], total[half:]
        first = index_ref[0] == 0
        keep_ref[...], away_ref[...] = jnp.where(first, low, high), jnp.where(first, high, low)
        return
    total = total.astype(BF16)
    if kept_ref.shape[1] == 2:
        keep_ref[...], away_ref[...] = unit(index_ref[0], total[:, 0], total[:, 1])
        return
    total = total.reshape(keep_ref.shape)

    @pl.when(pl.program_id(1) == 0)
    def _():
        keep_ref[...] = total

    @pl.when(pl.program_id(1) == 1)
    def _():
        away_ref[...] = total


def fold(kept, got, index, axis):
    rows, cols = kept.shape[-2:]
    call = dict(compiler_params=params(16), cost_estimate=cost(0, 0), name="fold")
    index = index.astype(jnp.int32)[None]
    if axis is None:
        spec = lambda n: pl.BlockSpec((n, cols), lambda i, s: (0, 0))
        grid_spec = pltpu.PrefetchScalarGridSpec(
            num_scalar_prefetch=1, grid=(1,), in_specs=[spec(rows)] * 2, out_specs=[spec(rows // 2)] * 2
        )
        shape = [jax.ShapeDtypeStruct((rows // 2, cols), F32)] * 2
        return pl.pallas_call(fold_kernel, grid_spec=grid_spec, out_shape=shape, **call)(index, kept, got)
    outer, inner = math.prod(kept.shape[:axis]), math.prod(kept.shape[axis + 1 : -1])
    if kept.size <= 1 << 19:
        whole = pl.BlockSpec((outer, 2, inner, cols), lambda i, s: (0, 0, 0, 0))
        part = pl.BlockSpec((outer, inner, cols), lambda i, s: (0, 0, 0))
        grid, in_spec, out_spec = (1,), whole, part
    else:
        in_spec = pl.BlockSpec((1, 1, inner, cols), lambda a, j, s: (a, j ^ s[0], 0, 0))
        out_spec = pl.BlockSpec((1, inner, cols), lambda a, j, s: (a, 0, 0))
        grid = (outer, 2)
    grid_spec = pltpu.PrefetchScalarGridSpec(
        num_scalar_prefetch=1,
        grid=grid,
        in_specs=[in_spec] * 2,
        out_specs=[out_spec] * 2,
    )
    shape = [jax.ShapeDtypeStruct((outer, inner, cols), BF16)] * 2
    args = [a.reshape(outer, 2, inner, cols) for a in (kept, got)]
    out = pl.pallas_call(fold_kernel, grid_spec=grid_spec, out_shape=shape, **call)(index, *args)
    return [o.reshape(kept.shape[:axis] + kept.shape[axis + 1 :]) for o in out]


class Gather:
    def __init__(self, a, b, order):
        self.kept = by_bit(1, a, b)
        self.got = flip(by_bit(1, b, a), 1)
        self.order = list(order)
        self.bits = []
        self.last = None

    def merge(self):
        if self.last is None:
            axis, place = None, lax.axis_index("wide") & 1
        else:
            axis = sum(1 for b in self.bits if b > self.last)
            place = (lax.axis_index("wide") & self.last != 0).astype(jnp.int32)
            if self.last == max(self.order + self.bits + [self.last]):
                place = place ^ lax.axis_index("narrow")
            self.bits.append(self.last)
        self.cur = join(self.kept, self.got, place, axis)

    def came(self):
        return self.got

    def come(self, value):
        self.got = value

    def held(self):
        return self.cur

    def hold(self, value):
        self.cur = value

    def send(self):
        self.last = self.order.pop(0) if self.order else 1
        if self.last == 1:
            self.cur = self.cur.reshape(-1, self.cur.shape[-1])
        self.kept, self.got = self.cur, flip(self.cur, self.last)


class Whole:
    def __init__(self, a, b):
        self.kept = by_bit(1, a, b)
        self.got = flip(by_bit(1, b, a), 1)
        self.stage = 0

    def merge(self):
        if self.stage == 0:
            low = lax.axis_index("wide") & 1 == 0
            kept, got = self.kept, self.got
            self.cur = jnp.where(
                low, jnp.concatenate((kept, got), 0), jnp.concatenate((got, kept), 0)
            )

    def came(self):
        return self.got if self.stage == 0 else self.cur

    def come(self, value):
        if self.stage == 0:
            self.got = value
        else:
            self.cur = value

    def held(self):
        return self.cur

    def hold(self, value):
        self.cur = value

    def send(self):
        if self.stage == 0:
            size = lax.axis_size("wide")
            groups = [list(range(c, size, 2)) for c in range(2)]
            self.cur = lax.all_gather(
                self.cur, "wide", axis=0, tiled=True, axis_index_groups=groups
            )
        else:
            self.got = flip(self.cur, 1)
        self.stage += 1


class Scatter:
    def __init__(self, send, order):
        self.got = flip(send, 1)
        self.order = list(order)
        self.axes = sorted(order, reverse=True)
        self.top = self.axes[0]

    def merge(self):
        kept, got = self.kept, self.got
        if self.order:
            if kept.ndim == 2:
                shape = (2,) * len(self.axes) + (-1, kept.shape[-1])
                kept, got = kept.reshape(shape), got.reshape(shape)
            bit = self.order.pop(0)
            axis = self.axes.index(bit)
            self.axes.remove(bit)
            index = (lax.axis_index("wide") & bit != 0).astype(jnp.int32)
            if bit == self.top:
                index = index ^ lax.axis_index("narrow")
        else:
            bit, axis, index = 1, None, lax.axis_index("wide") & 1
        self.bit = bit
        self.keep, self.away = fold(kept, got, index, axis)

    def next_index(self):
        index = (lax.axis_index("wide") & self.order[0] != 0).astype(jnp.int32)
        return index ^ lax.axis_index("narrow") if self.order[0] == self.top else index

    def start(self, other, *halves):
        for m, keep, away in ((self, *halves[:2]), (other, *halves[2:])):
            m.bit = m.order.pop(0)
            m.axes.remove(m.bit)
            shape = (2,) * len(m.axes) + (-1, keep.shape[-1])
            m.keep, m.away = keep.reshape(shape), away.reshape(shape)

    def came(self):
        return self.got

    def come(self, value):
        self.got = value

    def held(self):
        return self.keep, self.away

    def hold(self, value):
        self.keep, self.away = value

    def send(self):
        self.kept, self.got = self.keep, flip(self.away, self.bit)

    def result(self):
        return by_bit(1, self.kept, self.got), by_bit(1, self.got, self.kept)


def meet(values, *moves, wait=()):
    moves = list(moves) + list(wait)
    values, came = lax.optimization_barrier((values, [m.came() for m in moves]))
    for m, c in zip(moves, came):
        m.come(c)
        m.merge()
    values, held = lax.optimization_barrier((values, [m.held() for m in moves]))
    for m, h in zip(moves, held):
        m.hold(h)
        if m not in wait:
            m.send()
    return values


def send_now(values, *moves):
    values, held = lax.optimization_barrier((values, [m.held() for m in moves]))
    for m, h in zip(moves, held):
        m.hold(h)
        m.send()
    return values


def pair_plan(
    tokens,
    piece_starts,
    ln1_gain,
    ln1_bias,
    w_qkv,
    bias_qv,
    w_out,
    bias_out,
    ln2_gain,
    ln2_bias,
    w_up,
    bias_up,
    w_down,
    bias_down,
    cotangent,
):
    rank = lax.axis_index("narrow")
    first = rank == 0
    core = lax.axis_index("wide") & 1
    own, length = tokens.shape
    depth = 2 * own
    whole = own // HEAD * HEAD
    rest = own - whole
    rows_a = whole // 2
    rows_b = whole - rows_a + 2 * rest
    heads_a, heads_b = rows_a // HEAD, rows_b // HEAD
    block = w_out.shape[0]
    hidden = w_up.shape[1]
    tile = length // 4
    part = -(-(hidden + own) // 256) * LANES
    split = hidden - part
    split_back = hidden // 256 * LANES + 2 * LANES
    rank_arg = rank.astype(jnp.int32)[None]

    def swap(a):
        return lax.ppermute(a, "narrow", [(0, 1), (1, 0)])

    def heads_first(a):
        return jnp.where(first, a, jnp.concatenate((a[..., rest:], a[..., :rest]), -1))

    def heads_back(a):
        return jnp.where(first, a, jnp.concatenate((a[..., whole:], a[..., :whole]), -1))

    def at_rows(bias):
        return jnp.stack((bias[0], jnp.zeros_like(bias[0]), bias[1])).reshape(-1, 1)

    far, near, side = 8, 4, 2
    inward, outward = (far, near, side), (side, far, near)
    w_out_other = swap(w_out)
    w_heads = heads_first(w_qkv)
    shard_a = w_heads[:, :, :rows_a].reshape(block, -1)
    cols_a = shard_a.shape[1] // 2
    get_a = Gather(shard_a[:, :cols_a], shard_a[:, cols_a:], inward)
    pad = jnp.zeros((block, part - split - own), BF16)
    get_p = Whole(
        jnp.concatenate((w_out, pad, w_up[:, :split]), 1),
        jnp.concatenate((w_out_other, pad, w_down.T[:, :split]), 1),
    )
    get_p.merge()
    get_p.send()
    bias_local = heads_first(bias_qv)
    own_vectors = jnp.concatenate(
        (jnp.stack((ln1_gain, ln1_bias, ln2_gain, ln2_bias, bias_out)), bias_local), 0
    )
    half_rows = w_heads[:, :, whole:].reshape(-1, own)
    count = own_vectors.shape[0]
    small_swap = swap(jnp.concatenate((own_vectors, half_rows), 0))
    w_up_in, w_down_in, g_own = meet((w_up, w_down, cotangent), get_a)
    small_swap, x_own = lax.optimization_barrier((small_swap, tokens))
    x_other = swap(x_own)
    other_half = small_swap[count:].reshape(block, 3, rest)
    shard_b = jnp.concatenate((w_heads[:, :, rows_a:], other_half), 2).reshape(block, -1)
    cols_b = -(-shard_b.shape[1] // 256) * 128
    skip = shard_b.shape[1] - cols_b
    get_b = Gather(shard_b[:, :cols_b], shard_b[:, skip:], inward)
    other_vectors = small_swap[:count]
    vectors = jnp.concatenate((own_vectors[:5], other_vectors[:5]), 1).astype(F32).T
    gain_one, shift_one = vectors[:, 0:1], vectors[:, 1:2]
    bias_f = bias_local.astype(F32)
    bias_a = bias_f[:, :rows_a]
    bias_b = jnp.concatenate((bias_f[:, rows_a:], other_vectors[5:, whole:].astype(F32)), 1)
    bias_a, bias_b = at_rows(bias_a), at_rows(bias_b)
    w_down_t = w_down_in.T
    get_q = Whole(w_up_in[:, split:], w_down_t[:, split:])
    meet((), get_a, get_b, get_q)
    starts, g_own = meet((piece_starts[0], g_own), get_a, get_b)
    g_other = swap(g_own)
    seen = mask_bias(starts, length)
    seen, x_other, bias_a, bias_b, vectors = meet((seen, x_other, bias_a, bias_b, vectors), get_a, get_b)
    x_other, get_a.got = meet((x_other, get_a.got))

    core_arg = core[None]
    w_a = (get_a.cur, get_a.got)
    h_one, qkv_a = norm_qkv(core_arg, tokens, x_other, *w_a, vectors, bias_a)
    qkv_a = qkv_a.reshape(3, rows_a, length)

    context_a, lse_a = attend(seen, qkv_a, 0, heads_a)
    context_a, h_one = meet((context_a, h_one), get_b, get_p)
    h_b, get_b.got = meet((h_one, get_b.got))

    context_a_other = swap(after(context_a, g_other))
    w_b = (get_b.cur, get_b.got)
    qkv_b = qkv_of(core_arg, h_b, *w_b, bias_b).reshape(3, rows_b, length)
    whole_b = heads_b - 1
    half_b = whole_b // 2
    context_b, lse_b = attend(seen, qkv_b, 0, half_b)
    context_b, qkv_d = meet((context_b, qkv_b))
    context_b_other = swap(after(context_b, context_a_other))
    context_d, lse_d = attend(seen, qkv_d, half_b, whole_b - half_b)
    context_d, qkv_c = meet((context_d, qkv_d))

    context_d_other = swap(after(context_d, context_b_other))
    context_c, lse_c = attend(seen, qkv_c, whole_b, 1)
    lse_b = jnp.concatenate((lse_b, lse_d, lse_c), 0)
    context_a_other, context_b_other, context_d_other, context_c, get_p.got = meet(
        (context_a_other, context_b_other, context_d_other, context_c, get_p.got), get_q
    )

    pieces = (
        context_a, context_b, context_d, context_a_other, context_b_other, context_d_other, context_c
    )
    w_o = (get_p.cur, get_p.got)
    places = jnp.stack((rank, core)).astype(jnp.int32)
    projected, h_two, context = project(places, tokens, x_other, pieces, *w_o, vectors)
    projected, h_two, context, get_q.got = meet((projected, h_two, context, get_q.got))

    weights = (get_p.cur, get_p.got, get_q.cur, get_q.got)
    bias_up_f = bias_up.astype(F32)[None]
    steps = length // 2 // TILE

    def spot(at):
        return jnp.stack((at, core, rank)).astype(jnp.int32)

    old, low_own, low_other, gh_send, gb_send, gs_send = feed(
        spot(steps * (1 - rank)), steps, h_two, cotangent, g_other, weights, bias_up_f, TILE, None
    )
    old, gh_send = meet((old, gh_send))
    gh_got = swap(gh_send)
    middle, high_own, high_other, gh_keep, gb_keep, gs_keep = feed(
        spot(steps * rank), steps, h_two, cotangent, g_other, weights, bias_up_f, TILE, old
    )
    grad_bias_up = gb_send + gb_keep
    send_p, send_q = weight_grad(core[None], h_two, cotangent, g_other, middle, split_back)
    gh_got, gh_keep, send_p, send_q, middle, low_other = meet(
        (gh_got, gh_keep, send_p, send_q, middle, low_other)
    )

    put_p = Scatter(send_p, (side, near, far))
    put_q = Scatter(send_q, (near, far, side))
    low_got = swap(low_other)
    gp, gp_away, mine_a, mine_b, send_a, send_b, grad_two = mid_back(
        spot(steps * rank), tokens, x_other, projected, cotangent, g_other, gh_keep,
        gh_got, *w_o, vectors, rows_a, rows_b,
    )
    gp, gp_away, mine_a, mine_b, send_a, send_b, middle, put_p.got, put_q.got = meet(
        (gp, gp_away, mine_a, mine_b, send_a, send_b, middle, put_p.got, put_q.got)
    )

    got_b = swap(send_b)
    put_p.start(put_q, *weight_grad(
        jnp.stack((1 - core, put_p.next_index(), put_q.next_index())).astype(jnp.int32),
        h_two, cotangent, g_other, middle, split_back, (put_p.got, put_q.got),
    ))
    got_b, mine_b, send_a, gp_away, low_got = send_now(
        meet((got_b, mine_b, send_a, gp_away, low_got)), put_p, put_q
    )

    got_a = swap(send_a)
    gp_got = swap(gp_away)
    back_b = attend_back(seen, rank_arg, qkv_b, mine_b, got_b, lse_b, 0, heads_b, True)
    back_b, got_a, gp_got, high_other = meet((back_b, got_a, gp_got, high_other), put_p, put_q)

    high_got = swap(high_other)
    grad_b = back_b.reshape(3 * rows_b, length)

    half_a = heads_a // 2
    back_a = attend_back(seen, rank_arg, qkv_a, mine_a, got_a, lse_a, 0, half_a, False)
    send_b, keep_b = column_grads(places, cols_b, h_one, grad_b, context, gp, gp_got)
    back_a, send_b, keep_b, high_got = meet(
        (back_a, send_b, keep_b, high_got), wait=(put_p, put_q)
    )
    put_b = Scatter(send_b, (side, near, far))
    put_b.kept = keep_b
    back_a = attend_back(
        seen, rank_arg, qkv_a, mine_a, got_a, lse_a, half_a, heads_a - half_a, False, back_a
    )
    back_a = send_now(meet(back_a, put_b), put_p, put_q)
    grad_a = back_a.reshape(3 * rows_a, length)

    def vector_parts(sums):
        def row(a):
            return jnp.pad(a, ((0, 0), (0, depth - a.shape[1])))

        low = [grad_bias_up[:, :depth], grad_bias_up[:, depth:]]
        return jnp.concatenate(
            (sums[0], grad_two, row(sums[1]), row(sums[2]), row(gs_send + gs_keep), *map(row, low))
        )

    send_a, keep_a = column_grads(places, cols_a, h_one, grad_a)
    put_a = Scatter(send_a, (side, near, far))
    put_a.kept = keep_a
    keep, send, stats, *sums = qkv_back(
        core_arg, tokens, x_other, grad_b, grad_a, w_b, w_a, vectors
    )
    got = swap(send)
    keep, stats, sums, low_got = meet((keep, stats, sums, low_got), put_a, put_b, put_p, put_q)
    total = vector_parts(sums)
    total = total + flip(total, 1)
    output = close_output(
        places, tokens, projected, bias_down.astype(F32)[:, None], low_own, high_own, low_got, high_got
    )
    total, output = meet((total, output), put_a, put_b)
    total = total + flip(total, side)
    total = meet(total, put_a)
    total = total + flip(total, near)
    total, got = meet((total, got), put_a, put_b)
    total = total + flip(total, far)
    grad_tokens = close_tokens(places, tokens, gp, gp_got, keep, got, stats, vectors)
    sum_up_p, sum_down_p = put_p.result()
    sum_up_q, sum_down_q = put_q.result()
    low_b, high_b = put_b.result()
    sum_a = jnp.concatenate(put_a.result(), 1).reshape(block, 3, rows_a)
    out_cols = half_lanes(own)
    sum_out = jnp.concatenate((low_b[:, cols_b:], high_b[:, cols_b + 2 * out_cols - own :]), 1)
    sum_b = jnp.concatenate((low_b[:, :cols_b], high_b[:, cols_b - skip : cols_b]), 1)
    sum_b = sum_b.reshape(block, 3, rows_b)[:, :, : rows_b - rest]
    sum_w_qkv = heads_back(jnp.concatenate((sum_a, sum_b), 2))

    two = total[:5, :own] + swap(total[:5, own:])
    vec = [
        jnp.concatenate(
            (total[6, i * rows_a : (i + 1) * rows_a], total[5, i * rows_b : (i + 1) * rows_b - rest])
        )
        for i in (0, 2)
    ]
    return (
        output,
        grad_tokens,
        two[0],
        two[1],
        sum_w_qkv,
        heads_back(jnp.stack(vec)),
        sum_out,
        two[4],
        two[2],
        two[3],
        jnp.concatenate((sum_up_p, sum_up_q), 1),
        jnp.concatenate((total[8], total[9]))[:hidden],
        jnp.concatenate((sum_down_p, sum_down_q), 1).T,
        total[7, :own],
    )


def solution(mesh):
    in_specs = (
        P("narrow", "wide"),
        P("wide", None),
        P("narrow"),
        P("narrow"),
        P("wide", None, "narrow"),
        P(None, "narrow"),
        P("wide", "narrow"),
        P("narrow"),
        P("narrow"),
        P("narrow"),
        P("wide", "narrow"),
        P("narrow"),
        P("narrow", "wide"),
        P("narrow"),
        P("narrow", "wide"),
    )
    out_specs = (
        P("narrow", "wide"),
        P("narrow", "wide"),
        P("narrow"),
        P("narrow"),
        P("wide", None, "narrow"),
        P(None, "narrow"),
        P("wide", "narrow"),
        P("narrow"),
        P("narrow"),
        P("narrow"),
        P("wide", "narrow"),
        P("narrow"),
        P("narrow", "wide"),
        P("narrow"),
    )
    paired = mesh.shape["narrow"] == 2 and mesh.shape["wide"] == 16
    return jax.shard_map(
        pair_plan if paired else any_mesh, mesh=mesh, in_specs=in_specs, out_specs=out_specs, check_vma=False
    )
```
